32 devices in a mesh: pipe: 4 (over y, x), dp: 8 (over z, core).
Axes of the slice: x: 2, y: 2, z: 4, core: 2. Of those that a mesh axis runs over, the one named last changes fastest.
Arguments:
- block_input: bfloat16 [2, 3072, 2048], P(None, 'dp', 'pipe'), may hold values from -6 to 6
- cotangent: bfloat16 [2, 3072, 2048], P(None, 'dp', 'pipe'), may hold values from -6 to 6
- weight_wide: bfloat16 [4, 2048, 512], P('pipe'), may hold values from -0.125 to 0.125
- weight_taps: bfloat16 [4, 2304, 512], P('pipe'), may hold values from -0.09375 to 0.09375
- norm_mid: float32 [4, 2, 512], P('pipe'), may hold values from 0.5 to 1.5
- norm_out: float32 [4, 2, 1024], P('pipe'), may hold values from 0.5 to 1.5
- group_counts: int32 [2, 8, 4], replicated, may hold values from 0 to 96, as said below
Outputs:
- mixed: bfloat16 [2, 3072, 2048], P(None, 'dp', 'pipe')
- grad_input: float32 [2, 3072, 2048], P(None, 'dp', 'pipe')
- grad_wide: float32 [4, 2048, 512], P('pipe')
- grad_taps: float32 [4, 2304, 512], P('pipe')
- grad_mid: float32 [4, 2, 512], P('pipe')
- grad_out: float32 [4, 2, 1024], P('pipe')
The draws below stay inside these ranges and needn't reach their ends.
Inputs may be any that keep to these rules, and one draw needn't show every extreme that they name: group_counts[m, j] are counts of maps of 49, 36 and 25 pixels and of 4-pixel tiles that together fill at most 384 rows; some device holds 96 tiles.
All inputs are finite; a program needn't handle non-finite values.
Results may differ from the reference program's by a relative error of at most 0.023.
Values may be sent and summed in bfloat16 or wider, within the bound.
A program may use at most 320 MiB of HBM per device.

```python
import jax
import jax.numpy as jnp
from jax import lax

D = 2048
C = 512
ROWS = 384
M = 2
SECTIONS = 4
HALF = 2304
TOKENS = 3072
N_DP = 8


def draw_group_counts(key, part):
    key = jax.random.fold_in(key, 11)
    key_list = jax.random.split(key, 4)
    grid_shape = (M, N_DP)
    device_rank = jnp.arange(N_DP, dtype=jnp.int32)[None, :]
    micro_rank = jnp.arange(M, dtype=jnp.int32)[:, None]
    only_tiles = (micro_rank == 0) & (device_rank == N_DP - 1)
    lowest_rows = ROWS // 3
    base_rows = lowest_rows + (ROWS - lowest_rows) * device_rank // max(N_DP - 1, 1)
    jitter = jax.random.randint(key_list[0], grid_shape, -(ROWS // 16), ROWS // 16 + 1)
    target_rows = jnp.clip(base_rows + jitter, ROWS // 4, ROWS)
    target_rows = jnp.where(device_rank == N_DP - 1, ROWS, target_rows)
    target_rows = target_rows - target_rows % 4
    big_maps = jax.random.randint(key_list[1], grid_shape, 0, jnp.maximum((target_rows - 75) // 98, 0) + 1)
    big_maps = jnp.where(only_tiles, 0, big_maps)
    leftover = target_rows - 49 * big_maps
    mid_maps = jax.random.randint(key_list[2], grid_shape, 0, jnp.maximum((leftover - 75) // 72, 0) + 1)
    mid_maps = jnp.where(only_tiles, 0, mid_maps)
    leftover = leftover - 36 * mid_maps
    small_maps = (4 - big_maps % 4) % 4
    small_maps = small_maps + 4 * jax.random.randint(key_list[3], grid_shape, 0, jnp.maximum((leftover - 25 * small_maps) // 200, 0) + 1)
    small_maps = jnp.where(only_tiles, 0, small_maps)
    leftover = leftover - 25 * small_maps
    tile_count = leftover // 4
    return jnp.stack([big_maps, mid_maps, small_maps, tile_count], -1).astype(jnp.int32)


def block_levels(stream_key, dims, cuts, smallest, largest):
    factor_of = 1.0
    for dim, parts in cuts:
        draws = jax.random.uniform(jax.random.fold_in(jax.random.fold_in(stream_key, 6), dim), (parts,), jnp.float32, smallest / len(cuts), largest / len(cuts))
        factor_of = factor_of * jnp.repeat(jnp.exp(draws), dims[dim] // parts).reshape((-1,) + (1,) * (len(dims) - 1 - dim))
    return factor_of


def gaussian(own_key, extent, deviation, most, shards=(), held_as=jnp.bfloat16):
    values = jax.random.normal(own_key, extent, jnp.float32) * deviation
    if len(shards) > 0:
        values = block_levels(own_key, extent, shards, -0.22, 0.18) * values
    return jnp.clip(values, min=-most, max=most).astype(held_as)


def setup_inputs(seed: int = 0) -> dict:
    key_of = jax.random.split(jax.random.key(seed), 8)
    block_input = gaussian(key_of[0], (M, TOKENS, D), 1.0, 6.0, ((1, 8), (2, 4)))
    cotangent = gaussian(key_of[1], (M, TOKENS, D), 1.0, 6.0, ((1, 8), (2, 4)))
    weight_wide = gaussian(key_of[2], (SECTIONS, D, C), D ** -0.5, 0.125, ((0, 4),))
    weight_taps = gaussian(key_of[3], (SECTIONS, HALF, C), (9 * C) ** -0.5, 0.09375, ((0, 4),))
    norm_mid = jnp.clip(0.5 + 1.0 * jax.random.uniform(key_of[4], (SECTIONS, 2, C), jnp.float32) ** block_levels(key_of[4], (SECTIONS, 2, C), ((0, 4),), -0.2, 0.2), 0.5, 1.5)
    norm_out = jnp.clip(0.5 + 1.0 * jax.random.uniform(key_of[5], (SECTIONS, 2, D // 2), jnp.float32) ** block_levels(key_of[5], (SECTIONS, 2, D // 2), ((0, 4),), -0.2, 0.2), 0.5, 1.5)
    group_counts = draw_group_counts(jax.random.fold_in(key_of[7], 71), 0)
    return {"block_input": block_input, "cotangent": cotangent, "weight_wide": weight_wide, "weight_taps": weight_taps, "norm_mid": norm_mid, "norm_out": norm_out, "group_counts": group_counts}


@jax.custom_vjp
def low(v):
    return lax.optimization_barrier(v.astype(jnp.bfloat16)).astype(jnp.float32)

@jax.custom_vjp
def low_back(v):
    return v

def low_keep(v):
    return (low(v), None)

def low_pass(kept, grad):
    return (grad,)

def back_keep(v):
    return (v, None)

def back_low(kept, grad):
    return (low(grad),)
low.defvjp(low_keep, low_pass)
low_back.defvjp(back_keep, back_low)
highest = lax.Precision.HIGHEST

def neighbour_table(group_row, row_count):
    row_index = jnp.arange(row_count, dtype=jnp.int32)
    first_end = 49 * group_row[0]
    second_end = first_end + 36 * group_row[1]
    third_end = second_end + 25 * group_row[2]
    fourth_end = third_end + 4 * group_row[3]
    side_length = jnp.where(row_index < first_end, 7, jnp.where(row_index < second_end, 6, jnp.where(row_index < third_end, 5, jnp.where(row_index < fourth_end, 2, 1)))).astype(jnp.int32)
    group_start = jnp.where(row_index < first_end, 0, jnp.where(row_index < second_end, first_end, jnp.where(row_index < third_end, second_end, jnp.where(row_index < fourth_end, third_end, row_index)))).astype(jnp.int32)
    within = (row_index - group_start) % (side_length * side_length)
    image_start = row_index - within
    map_row = within // side_length
    map_column = within % side_length
    inside = row_index < fourth_end
    neighbours = []
    usable_list = []
    for shift_row in (-1, 0, 1):
        for shift_column in (-1, 0, 1):
            new_row = map_row + shift_row
            new_column = map_column + shift_column
            usable = inside & (new_row >= 0) & (new_row < side_length) & (new_column >= 0) & (new_column < side_length)
            neighbours.append(jnp.where(usable, image_start + new_row * side_length + new_column, 0).astype(jnp.int32))
            usable_list.append(usable)
    return (jnp.stack(neighbours, 1), jnp.stack(usable_list, 1).astype(jnp.float32), inside.astype(jnp.float32))

def batch_norm(values, insides, pixel_total, gain_row, bias_row):
    mean_value = lax.optimization_barrier(jnp.sum(values * insides[:, None], 0)) / pixel_total
    centred = (values - mean_value) * insides[:, None]
    variance = lax.optimization_barrier(jnp.sum(centred * centred, 0)) / pixel_total
    return gain_row * (values - mean_value) * lax.rsqrt(variance + 1e-05) + bias_row

def patch_rows(hidden, tables, usables):
    return jnp.concatenate([jnp.take(hidden, tables[:, tap_id], axis=0) * usables[:, tap_id, None] for tap_id in range(9)], 1)

def bottleneck(stream, layer_pos, wide_weight, tap_weight, mid_norm, out_norm, tables, usables, insides, pixel_total):
    front_id = 2 * layer_pos
    back_id = front_id + 1
    row_mask = insides[:, None]
    conv_input = low_back(stream)
    first = low_back(jnp.dot(conv_input, wide_weight[front_id], precision=highest))
    hidden_one = low(row_mask * jax.nn.silu(batch_norm(first, insides, pixel_total, mid_norm[front_id, 0], mid_norm[front_id, 1])))
    kernel = jnp.concatenate([tap_weight[front_id], tap_weight[back_id]], 0)
    second = low_back(jnp.dot(patch_rows(hidden_one, tables, usables), kernel, precision=highest))
    hidden_two = low(row_mask * jax.nn.silu(batch_norm(second, insides, pixel_total, mid_norm[back_id, 0], mid_norm[back_id, 1])))
    third = low_back(jnp.dot(hidden_two, wide_weight[back_id].T, precision=highest))
    out_gains = jnp.concatenate([out_norm[front_id], out_norm[back_id]], -1)
    summed = low_back(batch_norm(third, insides, pixel_total, out_gains[0], out_gains[1]) + stream)
    return row_mask * jax.nn.silu(summed)

def reference(block_input, cotangent, weight_wide, weight_taps, norm_mid, norm_out, group_counts):
    pixel_sizes = jnp.array([49, 36, 25, 4], jnp.int32)
    device_offsets = (jnp.arange(N_DP, dtype=jnp.int32) * ROWS)[:, None, None]
    layouts = []
    for micro_index in range(M):
        tables, usables, insides = jax.vmap(lambda counts_row: neighbour_table(counts_row, ROWS))(group_counts[micro_index])
        tables = (tables + device_offsets).reshape(N_DP * ROWS, 9).astype(jnp.int32)
        pixel_total = jnp.sum(group_counts[micro_index] * pixel_sizes).astype(jnp.float32)
        layouts.append((tables, usables.reshape(N_DP * ROWS, 9), insides.reshape(N_DP * ROWS), pixel_total))

    def forward(inputs, wide_weight, tap_weight, mid_norm, out_norm):
        outputs = []
        for micro_index in range(M):
            tables, usables, insides, pixel_total = layouts[micro_index]
            stream = inputs[micro_index]
            for layer_pos in range(2):
                stream = bottleneck(stream, layer_pos, wide_weight, tap_weight, mid_norm, out_norm, tables, usables, insides, pixel_total)
                if layer_pos == 0:
                    stream = low(stream)
            outputs.append(stream)
        return jnp.stack(outputs)
    result, pullback = jax.vjp(forward, block_input.astype(jnp.float32), weight_wide.astype(jnp.float32), weight_taps.astype(jnp.float32), norm_mid, norm_out)
    grads = pullback(cotangent.astype(jnp.float32))
    return (result.astype(jnp.bfloat16), grads[0], grads[1], grads[2], grads[3], grads[4])
```

```python
import functools
from types import SimpleNamespace

import jax
import jax.numpy as jnp
from jax import lax
from jax.experimental import pallas as pl
from jax.experimental.pallas import tpu as pltpu
from jax.sharding import PartitionSpec as P

MESH = pl.DeviceIdType.MESH
F32 = jnp.float32
BF16 = jnp.bfloat16
EPS = 1e-05
LANES = 128
N_PIPE = 4
NEAR = [k for k in range(9) if k != 4]


def slot_of(tap):
    return tap if tap < 4 else tap - 1


def dot_nn(a, b):
    return jnp.dot(a, b, preferred_element_type=F32)


def dot_nt(a, b):
    return lax.dot_general(a, b, (((1,), (1,)), ((), ())), preferred_element_type=F32)


def sigmoid(v):
    return jax.nn.sigmoid(v)


def sizes(n_dp, rows):
    n_z = n_dp // 2
    n_own = min(n_z, 16)
    return n_z, n_own, 256 // n_own, 2304 // n_own


def scratch_list(n_dp, rows):
    n_z, n_own, wr, kr = sizes(n_dp, rows)
    dma = pltpu.SemaphoreType.DMA

    def half(*shape):
        return pltpu.VMEM(shape, BF16)

    def full(*shape):
        return pltpu.VMEM(shape, F32)

    return dict(
        wt=half(4, 512, 512),
        k2=half(2, 512, 1152),
        gm=full(4, 2, 128),
        go=full(4, 2, 2, 512),
        msk=full(2, rows, 128),
        pm=half(2, 8, rows, rows),
        part=half(2, 2, 4, rows, 128),
        rsr=half(6, 2, 3, rows, 128),
        ag=half(6, 2, 4, rows, 128),
        stm=full(8, 2, n_dp, 2, 128),
        stw=full(4, 2, n_dp, 2, 512),
        midv=full(4, 2, rows, 128),
        dzm=full(2, rows, 128),
        inv_mid=full(4, 2, 1, 128),
        inv_wide=full(2, 2, 1, 512),
        widv=full(2, 2, rows, 512),
        pre0=full(2, rows, 512),
        s1=half(2, rows, 512),
        mix=half(2, rows, 512),
        gp=half(2, 2, rows, 512),
        cv=half(2, rows, 512),
        gt=half(2, rows, 512),
        gb=half(2, rows, 1152),
        yb=half(8, rows, 128),
        tb=half(512, 2 * rows),
        dw=half(4, 2, 256, 512),
        prw=half(4, 256, 512),
        zsw=half(4, 256, 512),
        zrw=half(4, n_z - 1, wr, 512),
        fiw=half(4, wr, 512),
        ow=half(4, 2, n_own, wr, 512),
        dk=half(2, 4608, 128),
        prk=half(2, 2304, 128),
        zsk=half(2, 2304, 128),
        zrk=half(2, n_z - 1, kr, 128),
        fik=half(2, kr, 128),
        ok=half(2304, 512),
        gsm=full(4, 4, 2, 128),
        gsw=full(2, 4, 2, 512),
        cnt=pltpu.SMEM((2, n_dp), F32),
        w_s=dma((3,)),
        w_r=dma((4,)),
        w_f=dma((4,)),
        k_s=dma((3, 5)),
        k_r=dma((4, 5)),
        k_f=dma((4, 5)),
        n_s=dma((3, 3)),
        n_r=dma((3, 3)),
        loc=dma((8,)),
        rs_s=dma((6, 2, 3)),
        rs_r=dma((6, 2, 3)),
        ag_s=dma((6, 2, 3)),
        ag_r=dma((6, 2, 3)),
        stm_s=dma((8, 2)),
        stm_r=dma((8, 2)),
        stw_s=dma((4, 2)),
        stw_r=dma((4, 2)),
        pw_s=dma((6,)),
        pw_r=dma((6,)),
        zw_s=dma((6,)),
        zw_r=dma((6,)),
        fw_s=dma((6,)),
        fw_r=dma((2, 4)),
        aw_s=dma((2,)),
        aw_r=dma((2,)),
        bw_s=dma((2,)),
        bw_r=dma((2,)),
        g_s=dma((3, 2)),
        g_r=dma((3, 2)),
        out=dma((8,)),
    )


def kernel(names, n, *refs):
    (x_ref, cot_ref, wide_ref, taps_ref, nmid_ref, nout_ref, counts_ref) = refs[:7]
    (mixed_ref, gpre_ref, conv_ref, gwide_ref, gtaps_ref, gmid_ref, gout_ref) = refs[7:14]
    sc = SimpleNamespace(**dict(zip(names, refs[14:])))
    rows = x_ref.shape[1]
    n_z, n_own, wr, kr = sizes(n, rows)
    p = lax.axis_index("pipe")
    d = lax.axis_index("dp")
    z = lax.div(d, 2)
    c = lax.rem(d, 2)
    parity = lax.rem(p, 2)
    sibling = (p, 2 * z + 1 - c)
    finish = []

    def pipe_at(off):
        return lax.rem(p + off, N_PIPE)

    def remote(src, dst, ss, rs, dev):
        return pltpu.make_async_remote_copy(
            src_ref=src, dst_ref=dst, send_sem=ss, recv_sem=rs, device_id=dev, device_id_type=MESH
        )

    def each(count, first, body):
        if count - first <= 8:
            for k in range(first, count):
                body(k)
        else:

            def step(k, carry):
                body(k)
                return carry

            lax.fori_loop(first, count, step, 0)

    def bytes_wait(view, sem):
        pltpu.make_async_copy(view, view, sem).wait()

    barrier = pltpu.get_barrier_semaphore()
    for off in range(1, N_PIPE):
        pl.semaphore_signal(barrier, inc=1, device_id=(pipe_at(off), d), device_id_type=MESH)

    def greet(k):
        pl.semaphore_signal(
            barrier, inc=1, device_id=(p, lax.rem(d + k, n)), device_id_type=MESH
        )

    each(n, 1, greet)

    own_w = pltpu.make_async_copy(
        wide_ref.at[0, pl.ds(pl.multiple_of(512 * p, 512), 512), :], sc.wt.at[p], sc.loc.at[0]
    )
    own_w.start()

    def tap_parts(h, column):
        layer = h // 2
        odd = h % 2
        listed = [
            (
                taps_ref.at[0, pl.ds(512 * i + 256 * odd, 512), column],
                (layer, pl.ds(0, 512), pl.ds(128 * (i + 5 * odd), 128)),
            )
            for i in range(4)
        ]
        listed.append(
            (
                taps_ref.at[0, pl.ds(2048 * (1 - odd), 256), column],
                (layer, pl.ds(256 * odd, 256), pl.ds(512, 128)),
            )
        )
        return listed

    def columns_of(q):
        return pl.ds(pl.multiple_of(128 * q, 128), 128)

    for s in range(4):

        @pl.when(p == s)
        def _(s=s):
            for i, (src, dst) in enumerate(tap_parts(s, columns_of(p))):
                pltpu.make_async_copy(src, sc.k2.at[dst], sc.loc.at[1 + i]).start()

    own_n = pltpu.make_async_copy(
        nmid_ref.at[0, :, columns_of(p)], sc.gm.at[p], sc.loc.at[6]
    )
    own_n.start()
    for e in range(2):
        sc.go[p, e] = nout_ref[0, :, 512 * e : 512 * e + 512]

    def used_rows(m, j):
        return (
            49 * counts_ref[m, j, 0]
            + 36 * counts_ref[m, j, 1]
            + 25 * counts_ref[m, j, 2]
            + 4 * counts_ref[m, j, 3]
        )

    totals = []
    for m in range(2):

        def count_up(j, acc, m=m):
            used = used_rows(m, j)
            sc.cnt[m, j] = used.astype(F32)
            return acc + used

        totals.append(lax.fori_loop(0, n, count_up, jnp.int32(0)).astype(F32))

    pl.semaphore_wait(barrier, N_PIPE - 1 + n - 1)

    def send_wide(off):
        q = pipe_at(off)
        return remote(
            wide_ref.at[0, pl.ds(pl.multiple_of(512 * q, 512), 512), :],
            sc.wt.at[p],
            sc.w_s.at[off - 1],
            sc.w_r.at[p],
            (q, d),
        )

    def send_taps(s, off):
        q = pipe_at(off)
        return [
            remote(
                src, sc.k2.at[dst], sc.k_s.at[off - 1, i], sc.k_r.at[p, i], (q, d)
            )
            for i, (src, dst) in enumerate(tap_parts(s, columns_of(q)))
        ]

    def send_norm(off):
        q = pipe_at(off)
        listed = [
            remote(
                nmid_ref.at[0, :, columns_of(q)],
                sc.gm.at[p],
                sc.n_s.at[off - 1, 0],
                sc.n_r.at[off - 1, 0],
                (q, d),
            )
        ]
        for e in range(2):
            listed.append(
                remote(
                    nout_ref.at[0, :, pl.ds(512 * e, 512)],
                    sc.go.at[p, e],
                    sc.n_s.at[off - 1, 1 + e],
                    sc.n_r.at[off - 1, 1 + e],
                    (q, d),
                )
            )
        return listed

    def start_wide(s):
        @pl.when((p == s) & (c == s % 2))
        def _():
            for off in range(1, 4):
                send_wide(off).start()

    def start_taps(s):
        @pl.when((p == s) & (c == s % 2))
        def _():
            for off in range(1, 4):
                for copy in send_taps(s, off):
                    copy.start()

    def finish_weights():
        for s in range(4):

            @pl.when((p == s) & (c == s % 2))
            def _(s=s):
                for off in range(1, 4):
                    send_wide(off).wait_send()
                    for copy in send_taps(s, off):
                        copy.wait_send()

            @pl.when((p != s) & (c == s % 2))
            def _(s=s):
                pass_wide(s).wait_send()
                for copy in pass_taps(s):
                    copy.wait_send()

    finish.append(finish_weights)

    def pass_wide(s):
        return remote(sc.wt.at[s], sc.wt.at[s], sc.w_f.at[s], sc.w_r.at[s], sibling)

    def pass_taps(s):
        return [
            remote(
                sc.k2.at[dst], sc.k2.at[dst], sc.k_f.at[s, i], sc.k_r.at[s, i], sibling
            )
            for i, (_, dst) in enumerate(tap_parts(s, pl.ds(0, 128)))
        ]

    def relay_wide(s):
        @pl.when((p != s) & (c == s % 2))
        def _():
            copy = pass_wide(s)
            copy.wait_recv()
            copy.start()

    def ready_wide(s):
        @pl.when((p != s) & (c != s % 2))
        def _():
            pass_wide(s).wait_recv()

        if s == 0:
            own_w.wait()

    def relay_taps(s):
        @pl.when((p != s) & (c == s % 2))
        def _():
            for copy in pass_taps(s):
                copy.wait_recv()
                copy.start()

    def ready_taps(s):
        @pl.when((p != s) & (c != s % 2))
        def _():
            for copy in pass_taps(s):
                copy.wait_recv()

        @pl.when(p == s)
        def _():
            for i, (src, dst) in enumerate(tap_parts(s, columns_of(p))):
                pltpu.make_async_copy(src, sc.k2.at[dst], sc.loc.at[1 + i]).wait()

    start_wide(0)
    for off in range(1, 4):
        for copy in send_norm(off):
            copy.start()
    start_taps(0)
    start_taps(1)
    start_wide(1)

    def finish_norm():
        for off in range(1, 4):
            for copy in send_norm(off):
                copy.wait_send()

    finish.append(finish_norm)

    row_id = lax.broadcasted_iota(jnp.int32, (rows, LANES), 0).astype(F32)
    lane_id = lax.broadcasted_iota(jnp.int32, (rows, LANES), 1).astype(F32)

    def build(m):
        ends = []
        total = jnp.int32(0)
        for g, area in enumerate((49, 36, 25, 4)):
            total = total + area * counts_ref[m, d, g]
            ends.append(total.astype(F32))
        sc.msk[m] = jnp.where(row_id < ends[3], 1.0, 0.0)

        def pick(values):
            out = values[4]
            for g in (3, 2, 1, 0):
                out = jnp.where(row_id < ends[g], values[g], out)
            return out

        zero = jnp.zeros((rows, LANES), F32)
        side = pick([zero + 7.0, zero + 6.0, zero + 5.0, zero + 2.0, zero + 1.0])
        begin = pick([zero, zero + ends[0], zero + ends[1], zero + ends[2], row_id])
        one_over = pick(
            [zero + 1.0 / 7.0, zero + 1.0 / 6.0, zero + 1.0 / 5.0, zero + 0.5, zero + 1.0]
        )
        within = row_id - begin
        within = within - side * side * jnp.floor((within + 0.5) * one_over * one_over)
        map_row = jnp.floor((within + 0.5) * one_over)
        map_col = within - side * map_row
        for k in NEAR:
            du, dv = k // 3 - 1, k % 3 - 1
            usable = row_id < ends[3]
            if du == -1:
                usable = usable & (map_row > 0.5)
            if du == 1:
                usable = usable & (map_row < side - 1.5)
            if dv == -1:
                usable = usable & (map_col > 0.5)
            if dv == 1:
                usable = usable & (map_col < side - 1.5)
            target = jnp.where(usable, row_id + du * side + dv, -1000.0)
            for t in range(rows // LANES):
                hit = jnp.where(target == lane_id + float(LANES * t), 1.0, 0.0)
                sc.pm[m, slot_of(k), :, LANES * t : LANES * (t + 1)] = hit.astype(BF16)

    for m in range(2):
        build(m)

    rs_last = {0: None, 1: None}
    rs_turn = [0]

    def rs_copies(rid, m, par):
        listed = []
        for off in range(1, 4):
            q = pipe_at(off)
            listed.append(
                remote(
                    sc.part.at[par, m, q],
                    sc.rsr.at[rid, m, off - 1],
                    sc.rs_s.at[rid, m, off - 1],
                    sc.rs_r.at[rid, m, off - 1],
                    (q, d),
                )
            )
        return listed

    def rs_open(rid, m, par):
        if rs_last[par] is not None:
            for copy in rs_copies(rs_last[par], m, par):
                copy.wait_send()

    def rs_start(rid, m, par):
        for copy in rs_copies(rid, m, par):
            copy.start()

    def rs_sum(rid, m, par):
        for copy in rs_copies(rid, m, par):
            copy.wait_recv()
        total = sc.part[par, m, p].astype(F32)
        for k in range(3):
            total = total + sc.rsr[rid, m, k].astype(F32)
        return total

    def ag_copies(aid, m):
        listed = []
        for off in range(1, 4):
            listed.append(
                remote(
                    sc.ag.at[aid, m, p],
                    sc.ag.at[aid, m, p],
                    sc.ag_s.at[aid, m, off - 1],
                    sc.ag_r.at[aid, m, off - 1],
                    (pipe_at(off), d),
                )
            )
        return listed

    def ag_start(aid, m, value):
        sc.ag[aid, m, p] = value
        for copy in ag_copies(aid, m):
            copy.start()

    def ag_wait(aid, m):
        for copy in ag_copies(aid, m):
            copy.wait_recv()

    def ag_value(aid, m):
        return jnp.concatenate([sc.ag[aid, m, q] for q in range(4)], axis=1)

    def finish_ag():
        for aid in range(6):
            for m in range(2):
                for copy in ag_copies(aid, m):
                    copy.wait_send()

    finish.append(finish_ag)

    def st_refs(wide, i, m):
        if wide:
            return sc.stw.at[i, m], sc.stw_s.at[i, m], sc.stw_r.at[i, m]
        return sc.stm.at[i, m], sc.stm_s.at[i, m], sc.stm_r.at[i, m]

    def st_start(wide, i, m):
        buf, ss, rs = st_refs(wide, i, m)

        def go(k):
            remote(buf.at[d], buf.at[d], ss, rs, (p, lax.rem(d + k, n))).start()

        each(n, 1, go)

    def st_wait(wide, i, m):
        buf, ss, rs = st_refs(wide, i, m)
        bytes_wait(buf.at[pl.ds(0, n - 1)], rs)

    def finish_st():
        for wide, count in ((True, 4), (False, 8)):
            for i in range(count):
                for m in range(2):
                    buf, ss, rs = st_refs(wide, i, m)
                    bytes_wait(buf.at[pl.ds(0, n - 1)], ss)

    finish.append(finish_st)

    def over_devices(body, init):
        if n <= 8:
            for j in range(n):
                init = body(j, init)
            return init
        return lax.fori_loop(0, n, body, init)

    def combine(wide, i, m):
        st_wait(wide, i, m)
        ref = sc.stw if wide else sc.stm
        blank = jnp.zeros((1, ref.shape[-1]), F32)
        mean = over_devices(
            lambda j, acc: acc + sc.cnt[m, j] * ref[i, m, j, 0:1, :], blank
        )
        mean = mean / totals[m]

        def spread(j, acc):
            gap = ref[i, m, j, 0:1, :] - mean
            return acc + ref[i, m, j, 1:2, :] + sc.cnt[m, j] * (gap * gap)

        var = over_devices(spread, blank) / totals[m]
        return mean, lax.rsqrt(var + EPS)

    def back_sums(wide, i, m):
        st_wait(wide, i, m)
        ref = sc.stw if wide else sc.stm
        return over_devices(
            lambda j, acc: acc + ref[i, m, j], jnp.zeros((2, ref.shape[-1]), F32)
        )

    def local_moments(v, m):
        mask = sc.msk[m]
        own = jnp.maximum(sc.cnt[m, d], 1.0)
        mean = jnp.sum(v * mask, 0, keepdims=True) / own
        gap = (v - mean) * mask
        return jnp.concatenate([mean, jnp.sum(gap * gap, 0, keepdims=True)], 0)

    def local_sums(dz, vhat):
        return jnp.concatenate(
            [jnp.sum(dz * vhat, 0, keepdims=True), jnp.sum(dz, 0, keepdims=True)], 0
        )

    def lanes(j):
        return slice(LANES * j, LANES * (j + 1))

    def stream(layer, m):
        return x_ref[m] if layer == 0 else sc.s1[m]

    def stream_part(layer, m, j):
        return (x_ref[m, :, lanes(j)] if layer == 0 else sc.s1[m, :, lanes(j)]).astype(F32)

    rs_par = {0: 0, 1: 1, 3: 0, 5: 1, 2: 0, 4: 1}
    rs_before = {0: None, 1: None, 3: 0, 5: 1, 2: 3, 4: 5}

    def rs_send(rid, m, values):
        par = rs_par[rid]
        if rs_before[rid] is not None:
            for copy in rs_copies(rs_before[rid], m, par):
                copy.wait_send()
        for j, value in enumerate(values):
            half = value.astype(BF16)
            sc.part[par, m, 2 * j] = half[:, :LANES]
            sc.part[par, m, 2 * j + 1] = half[:, LANES:]
        rs_start(rid, m, par)

    def finish_rs():
        for rid in (2, 4):
            for m in range(2):
                for copy in rs_copies(rid, m, rs_par[rid]):
                    copy.wait_send()

    finish.append(finish_rs)

    def first_part(layer, m):
        s = stream(layer, m)
        rs_send(
            layer,
            m,
            [dot_nn(s, sc.wt[2 * layer, :, 256 * j : 256 * j + 256]) for j in range(2)],
        )

    def mid_moments(i, m, v):
        sc.midv[i, m] = v
        sc.stm[i, m, d] = local_moments(v, m)
        st_start(False, i, m)

    def first_norm(layer, m):
        mid_moments(2 * layer, m, rs_sum(layer, m, rs_par[layer]))

    def mid_hidden(i, m):
        mean, inv = combine(False, i, m)
        sc.inv_mid[i, m] = inv
        vhat = (sc.midv[i, m] - mean) * inv
        sc.midv[i, m] = vhat
        u = sc.gm[i, 0:1, :] * vhat + sc.gm[i, 1:2, :]
        return (sc.msk[m] * (u * sigmoid(u))).astype(BF16)

    def hidden_one(layer, m):
        ag_start(layer, m, mid_hidden(2 * layer, m))

    def second_part(layer, m):
        ag_wait(layer, m)
        h = ag_value(layer, m)
        centre = None
        for j in range(5):
            width = 256 if j < 4 else 128
            y = dot_nn(h, sc.k2[layer, :, 256 * j : 256 * j + width])
            for e in range(width // LANES):
                tap = 2 * j + e
                if tap == 4:
                    centre = y[:, lanes(e)]
                    sc.midv[2 * layer + 1, m] = centre
                else:
                    sc.yb[slot_of(tap)] = y[:, lanes(e)].astype(BF16)
        total = sc.midv[2 * layer + 1, m]
        for k in range(8):
            total = total + dot_nn(sc.pm[m, k], sc.yb[k])
        mid_moments(2 * layer + 1, m, total)

    def hidden_two(layer, m):
        ag_start(2 + layer, m, mid_hidden(2 * layer + 1, m))

    def third_part(layer, m):
        ag_wait(2 + layer, m)
        h = ag_value(2 + layer, m)
        for j in range(2):
            sc.widv[layer, m, :, 256 * j : 256 * j + 256] = dot_nt(
                h, sc.wt[2 * layer + 1, 256 * j : 256 * j + 256, :]
            )
        for j in range(4):
            sc.stw[layer, m, d, :, lanes(j)] = local_moments(sc.widv[layer, m, :, lanes(j)], m)
        st_start(True, layer, m)

    def out_gain(layer, j):
        both = sc.go[2 * layer + lax.div(p, 2), lax.rem(p, 2)]
        return both[0:1, lanes(j)], both[1:2, lanes(j)]

    def pre_values(layer, m):
        mean, inv = combine(True, layer, m)
        sc.inv_wide[layer, m] = inv
        mask = sc.msk[m]
        for j in range(4):
            gain, bias = out_gain(layer, j)
            vhat = (sc.widv[layer, m, :, lanes(j)] - mean[:, lanes(j)]) * inv[:, lanes(j)]
            sc.widv[layer, m, :, lanes(j)] = vhat
            pre = gain * vhat + bias + stream_part(layer, m, j)
            sig = sigmoid(pre)
            out = (mask * (pre * sig)).astype(BF16)
            if layer == 0:
                sc.pre0[m, :, lanes(j)] = pre
                sc.s1[m, :, lanes(j)] = out
            else:
                sc.mix[m, :, lanes(j)] = out
                slope = sig * (1.0 + pre * (1.0 - sig))
                grad = (cot_ref[m, :, lanes(j)].astype(F32) * mask * slope).astype(BF16)
                sc.gp[1, m, :, lanes(j)] = grad
                sc.stw[3, m, d, :, lanes(j)] = local_sums(grad.astype(F32), vhat)
        if layer == 1:
            st_start(True, 3, m)

    def put_out(k, src, dst):
        copy = pltpu.make_async_copy(src, dst, sc.out.at[k])
        copy.start()
        return copy

    def grad_out_norm(layer, m):
        sums = back_sums(True, 2 + layer, m)
        if m == 0:
            sc.gsw[layer, p] = sums
        else:
            sc.gsw[layer, p] = sc.gsw[layer, p] + sums
        mask = sc.msk[m]
        inv = sc.inv_wide[layer, m]
        for j in range(4):
            gain, _ = out_gain(layer, j)
            dz = sc.gp[layer, m, :, lanes(j)].astype(F32)
            vhat = sc.widv[layer, m, :, lanes(j)]
            s1 = sums[0:1, lanes(j)] / totals[m]
            s0 = sums[1:2, lanes(j)] / totals[m]
            dv = mask * (gain * inv[:, lanes(j)]) * (dz - s0 - vhat * s1)
            sc.gt[m, :, lanes(j)] = dv.astype(BF16)
        g = sc.gt[m]
        rs_send(
            2 + layer,
            m,
            [dot_nn(g, sc.wt[2 * layer + 1, :, 256 * j : 256 * j + 256]) for j in range(2)],
        )

    def mid_grad(i, m, upstream):
        vhat = sc.midv[i, m]
        u = sc.gm[i, 0:1, :] * vhat + sc.gm[i, 1:2, :]
        sig = sigmoid(u)
        dz = upstream * sc.msk[m] * (sig * (1.0 + u * (1.0 - sig)))
        sc.dzm[m] = dz
        sc.stm[4 + i, m, d] = local_sums(dz, vhat)
        st_start(False, 4 + i, m)

    def mid_back(i, m):
        sums = back_sums(False, 4 + i, m)
        if m == 0:
            sc.gsm[i, p] = sums
        else:
            sc.gsm[i, p] = sc.gsm[i, p] + sums
        s1 = sums[0:1, :] / totals[m]
        s0 = sums[1:2, :] / totals[m]
        scale = sc.gm[i, 0:1, :] * sc.inv_mid[i, m]
        return (sc.msk[m] * scale * (sc.dzm[m] - s0 - sc.midv[i, m] * s1)).astype(BF16)

    def grad_two(layer, m):
        mid_grad(2 * layer + 1, m, rs_sum(2 + layer, m, rs_par[2 + layer]))

    def grad_second(layer, m):
        gs = mid_back(2 * layer + 1, m)
        for k in range(9):
            if k == 4:
                sc.gb[m, :, lanes(k)] = gs
            else:
                sc.gb[m, :, lanes(k)] = dot_nn(sc.pm[m, slot_of(8 - k)], gs).astype(BF16)
        g = sc.gb[m]
        rs_send(
            4 + layer,
            m,
            [dot_nt(g, sc.k2[layer, 256 * j : 256 * j + 256, :]) for j in range(2)],
        )

    def grad_one(layer, m):
        mid_grad(2 * layer, m, rs_sum(4 + layer, m, rs_par[4 + layer]))

    def grad_first(layer, m):
        ag_start(4 + layer, m, mid_back(2 * layer, m))

    def conv_grad(layer, m):
        ag_wait(4 + layer, m)
        g = ag_value(4 + layer, m)
        mask = sc.msk[m]
        for j in range(2):
            r = dot_nt(g, sc.wt[2 * layer, 256 * j : 256 * j + 256, :]).astype(BF16)
            if layer == 0:
                sc.cv[m, :, 256 * j : 256 * j + 256] = r
                continue
            for e in range(2):
                i = 2 * j + e
                pre = sc.pre0[m, :, lanes(i)]
                sig = sigmoid(pre)
                slope = sig * (1.0 + pre * (1.0 - sig))
                up = sc.gp[1, m, :, lanes(i)].astype(F32) + r[:, lanes(e)].astype(F32)
                grad = (up * mask * slope).astype(BF16)
                sc.gp[0, m, :, lanes(i)] = grad
                sc.stw[2, m, d, :, lanes(i)] = local_sums(
                    grad.astype(F32), sc.widv[0, m, :, lanes(i)]
                )
        if layer == 1:
            st_start(True, 2, m)

    def turned(blocks):
        for m, block in enumerate(blocks):
            sc.tb[:, rows * m : rows * (m + 1)] = block.T

    def both(get):
        return jnp.concatenate([get(0), get(1)], axis=0)

    def wide_grad(s, left, right):
        turned([left(0), left(1)])
        for j in range(2):
            cols = slice(256 * j, 256 * j + 256)
            rhs = both(lambda m: right(m)[:, cols])
            for h in range(2):
                r = dot_nn(sc.tb[256 * h : 256 * h + 256, :], rhs)
                sc.dw[s, h, :, cols] = r.astype(BF16)
        pair_w(s).start()

    def taps_grad(layer):
        turned([ag_value(layer, 0), ag_value(layer, 1)])
        for j in range(5):
            width = 256 if j < 4 else 128
            rhs = both(lambda m: sc.gb[m, :, 256 * j : 256 * j + width])
            r = dot_nn(sc.tb[...], rhs).astype(BF16)
            for e in range(width // LANES):
                tap = 2 * j + e
                sc.dk[layer, 512 * tap : 512 * tap + 512, :] = r[:, lanes(e)]
        pair_k(layer).start()

    def pair_w(s):
        return remote(
            sc.dw.at[s, 1 - c], sc.prw.at[s], sc.pw_s.at[s], sc.pw_r.at[s], sibling
        )

    def other_half():
        return pl.ds(pl.multiple_of(2304 * (1 - c), 2304), 2304)

    def own_half():
        return pl.ds(pl.multiple_of(2304 * c, 2304), 2304)

    def pair_k(layer):
        return remote(
            sc.dk.at[layer, other_half()],
            sc.prk.at[layer],
            sc.pw_s.at[4 + layer],
            sc.pw_r.at[4 + layer],
            sibling,
        )

    def owner(index, body):
        if n_own == n_z:
            body()
        else:
            pl.when(index < n_own)(body)

    def z_copy(wide, s, k):
        j = lax.rem(z + k, n_z)
        if wide:
            src = sc.zsw.at[s, pl.ds(pl.multiple_of(wr * j, wr), wr)]
            dst, sem = sc.zrw.at[s, k - 1], s
        else:
            src = sc.zsk.at[s, pl.ds(pl.multiple_of(kr * j, kr), kr)]
            dst, sem = sc.zrk.at[s, k - 1], 4 + s
        return j, remote(src, dst, sc.zw_s.at[sem], sc.zw_r.at[sem], (p, 2 * j + c))

    def z_start(wide, s):
        def go(k):
            j, copy = z_copy(wide, s, k)
            owner(j, lambda: copy.start())

        each(n_z, 1, go)

    def wide_z(s):
        pair_w(s).wait_recv()
        sc.zsw[s] = (sc.dw[s, c].astype(F32) + sc.prw[s].astype(F32)).astype(BF16)
        z_start(True, s)

    def taps_z(layer):
        pair_k(layer).wait_recv()
        for i in range(4):
            part = slice(576 * i, 576 * i + 576)
            mine = pl.ds(pl.multiple_of(2304 * c + 576 * i, 576), 576)
            sc.zsk[layer, part] = (
                sc.dk[layer, mine].astype(F32) + sc.prk[layer, part].astype(F32)
            ).astype(BF16)
        z_start(False, layer)

    def wide_fin_copy(s):
        return remote(
            sc.fiw.at[s], sc.ow.at[p, c, z], sc.fw_s.at[s], sc.fw_r.at[0, p], (s, d)
        )

    def wide_pipe(s):
        def go():
            bytes_wait(sc.zrw.at[s], sc.zw_r.at[s])
            total = sc.zsw[s, pl.ds(pl.multiple_of(wr * z, wr), wr)].astype(F32)
            for k in range(n_z - 1):
                total = total + sc.zrw[s, k].astype(F32)
            sc.fiw[s] = total.astype(BF16)

            @pl.when(p == s)
            def _():
                sc.ow[p, c, z] = sc.fiw[s]

            @pl.when(p != s)
            def _():
                wide_fin_copy(s).start()

        owner(z, go)

    def wide_ag_copy(k):
        j = lax.rem(z + k, n_z)
        view = sc.ow.at[:, c, lax.rem(z, n_own)]
        return remote(view, view, sc.aw_s.at[0], sc.aw_r.at[0], (p, 2 * j + c))

    def wide_ag(s):
        def go():
            for q in range(4):
                if q != s:
                    copy = remote(
                        sc.fiw.at[s],
                        sc.ow.at[q, c, z],
                        sc.fw_s.at[s],
                        sc.fw_r.at[0, q],
                        (s, d),
                    )
                    copy.wait_recv()
            each(n_z, 1, lambda k: wide_ag_copy(k).start())

        @pl.when(p == s)
        def _():
            owner(z, go)

    def wait_pieces(view_of, sem):
        if n_own == n_z:
            bytes_wait(view_of(n_own - 1), sem)
        else:

            @pl.when(z < n_own)
            def _():
                bytes_wait(view_of(n_own - 1), sem)

            @pl.when(z >= n_own)
            def _():
                bytes_wait(view_of(n_own), sem)

    def wide_pair_copy():
        return remote(sc.ow.at[:, c], sc.ow.at[:, c], sc.bw_s.at[0], sc.bw_r.at[0], sibling)

    def wide_pair(s):
        @pl.when(p == s)
        def _():
            wait_pieces(lambda count: sc.ow.at[:, 0, pl.ds(0, count)], sc.aw_r.at[0])
            wide_pair_copy().start()

    def wide_done():
        wide_pair_copy().wait_recv()
        return [
            put_out(
                0,
                sc.ow.at[...],
                gwide_ref.at[...],
            )
        ]

    def taps_fin_copy(layer, q):
        return remote(
            sc.fik.at[layer],
            sc.ok.at[pl.ds(pl.multiple_of(kr * z, kr), kr), pl.ds(128 * q, 128)],
            sc.fw_s.at[4 + layer],
            sc.fw_r.at[1, q],
            (2 * layer + c, d),
        )

    def taps_pipe(layer):
        def go():
            bytes_wait(sc.zrk.at[layer], sc.zw_r.at[4 + layer])
            total = sc.zsk[layer, pl.ds(pl.multiple_of(kr * z, kr), kr)].astype(F32)
            for k in range(n_z - 1):
                total = total + sc.zrk[layer, k].astype(F32)
            sc.fik[layer] = total.astype(BF16)
            for q in range(4):
                if q // 2 == layer:

                    @pl.when((p == q) & (c == q % 2))
                    def _(q=q):
                        sc.ok[pl.ds(pl.multiple_of(kr * z, kr), kr), 128 * q : 128 * q + 128] = (
                            sc.fik[layer]
                        )

                    @pl.when((p == q) & (c != q % 2))
                    def _(q=q):
                        taps_fin_copy(layer, q).start()

                else:

                    @pl.when(p == q)
                    def _(q=q):
                        taps_fin_copy(layer, q).start()

        owner(z, go)

    def taps_ag_copy(k):
        j = lax.rem(z + k, n_z)
        view = sc.ok.at[pl.ds(pl.multiple_of(kr * lax.rem(z, n_own), kr), kr)]
        return remote(view, view, sc.aw_s.at[1], sc.aw_r.at[1], (p, 2 * j + c))

    def taps_ag(layer):
        for h in range(2):
            s = 2 * layer + h

            def go(s=s):
                for q in range(4):
                    if q != s:
                        taps_fin_copy(layer, q).wait_recv()
                each(n_z, 1, lambda k: taps_ag_copy(k).start())

            @pl.when((p == s) & (c == h))
            def _(go=go):
                owner(z, go)

    def taps_pair_copy():
        return remote(sc.ok.at[...], sc.ok.at[...], sc.bw_s.at[1], sc.bw_r.at[1], sibling)

    def taps_pair(layer):
        @pl.when((lax.div(p, 2) == layer) & (c == parity))
        def _():
            wait_pieces(lambda count: sc.ok.at[pl.ds(0, kr * count)], sc.aw_r.at[1])
            taps_pair_copy().start()

    def taps_done():
        @pl.when(c != parity)
        def _():
            taps_pair_copy().wait_recv()

        return [put_out(1, sc.ok.at[...], gtaps_ref.at[...])]

    def finish_grads():
        for wide, s in [(True, s) for s in range(4)] + [(False, layer) for layer in range(2)]:
            (pair_w if wide else pair_k)(s).wait_send()

            def sent(k, wide=wide, s=s):
                j, copy = z_copy(wide, s, k)
                owner(j, lambda: copy.wait_send())

            each(n_z, 1, sent)

        def pieces():
            for s in range(4):

                @pl.when(p != s)
                def _(s=s):
                    wide_fin_copy(s).wait_send()

            for layer in range(2):

                @pl.when(p != 2 * layer + c)
                def _(layer=layer):
                    taps_fin_copy(layer, 0).wait_send()

            each(n_z, 1, lambda k: wide_ag_copy(k).wait_send())

            @pl.when(c == parity)
            def _():
                each(n_z, 1, lambda k: taps_ag_copy(k).wait_send())

        owner(z, pieces)
        wide_pair_copy().wait_send()

        @pl.when(c == parity)
        def _():
            taps_pair_copy().wait_send()

    finish.append(finish_grads)

    def gain_copies(off):
        dev = (pipe_at(off), d)
        return [
            remote(
                sc.gsm.at[:, p], sc.gsm.at[:, p], sc.g_s.at[off - 1, 0], sc.g_r.at[off - 1, 0], dev
            ),
            remote(
                sc.gsw.at[:, p], sc.gsw.at[:, p], sc.g_s.at[off - 1, 1], sc.g_r.at[off - 1, 1], dev
            ),
        ]

    def gains_start():
        for off in range(1, 4):
            for copy in gain_copies(off):
                copy.start()

    def gains_done():
        for off in range(1, 4):
            for copy in gain_copies(off):
                copy.wait_recv()
        for q in range(4):
            gmid_ref[0, :, lanes(q)] = sc.gsm[p, q]
        layer = lax.div(p, 2)
        for e in range(2):
            gout_ref[0, :, 512 * e : 512 * e + 512] = sc.gsw[layer, 2 * parity + e]

    def finish_gains():
        for off in range(1, 4):
            for copy in gain_copies(off):
                copy.wait_send()

    finish.append(finish_gains)

    def phase(body, layer):
        for m in range(2):
            body(layer, m)

    relay_wide(0)
    ready_wide(0)
    phase(first_part, 0)
    own_n.wait()
    for off in range(1, 4):
        for copy in send_norm(off):
            copy.wait_recv()
    phase(first_norm, 0)
    phase(hidden_one, 0)
    start_wide(2)
    start_taps(2)
    start_taps(3)
    start_wide(3)
    relay_taps(0)
    relay_taps(1)
    ready_taps(0)
    ready_taps(1)
    phase(second_part, 0)
    relay_wide(1)
    phase(hidden_two, 0)
    ready_wide(1)
    phase(third_part, 0)
    relay_wide(2)
    ready_wide(2)

    def turn(layer, m):
        pre_values(0, m)
        first_part(1, m)

    phase(turn, 0)
    phase(first_norm, 1)
    relay_taps(2)
    relay_taps(3)
    phase(hidden_one, 1)
    ready_taps(2)
    ready_taps(3)
    phase(second_part, 1)
    relay_wide(3)
    phase(hidden_two, 1)
    ready_wide(3)
    phase(third_part, 1)
    phase(pre_values, 1)
    outs = [put_out(2, sc.mix.at[...], mixed_ref.at[...])]

    phase(grad_out_norm, 1)
    wide_grad(3, lambda m: sc.gt[m], lambda m: ag_value(3, m))
    phase(grad_two, 1)
    wide_z(3)
    phase(grad_second, 1)
    taps_grad(1)
    phase(grad_one, 1)
    wide_pipe(3)
    taps_z(1)
    phase(grad_first, 1)
    wide_ag(3)
    phase(conv_grad, 1)
    outs.append(put_out(3, sc.gp.at[0], gpre_ref.at[...]))
    wide_grad(2, lambda m: sc.s1[m], lambda m: ag_value(5, m))
    phase(grad_out_norm, 0)
    wide_grad(1, lambda m: sc.gt[m], lambda m: ag_value(2, m))
    wide_z(2)
    phase(grad_two, 0)
    wide_z(1)
    taps_pipe(1)
    phase(grad_second, 0)
    taps_grad(0)
    wide_pipe(2)
    phase(grad_one, 0)
    taps_z(0)
    wide_pipe(1)
    taps_ag(1)
    phase(grad_first, 0)
    gains_start()
    wide_ag(2)
    wide_ag(1)
    phase(conv_grad, 0)
    outs.append(put_out(4, sc.cv.at[...], conv_ref.at[...]))
    wide_grad(0, lambda m: x_ref[m], lambda m: ag_value(4, m))
    taps_pipe(0)
    wide_z(0)
    gains_done()
    taps_ag(0)
    wide_pipe(0)
    taps_pair(1)
    wide_pair(3)
    wide_ag(0)
    wide_pair(2)
    wide_pair(1)
    taps_pair(0)
    outs.extend(taps_done())
    wide_pair(0)
    outs.extend(wide_done())
    for copy in outs:
        copy.wait()
    for body in finish:
        body()


def local(block_input, cotangent, weight_wide, weight_taps, norm_mid, norm_out, group_counts):
    n_dp = group_counts.shape[1]
    micro, rows, width = block_input.shape
    n_z, n_own, wr, kr = sizes(n_dp, rows)
    scratch = scratch_list(n_dp, rows)
    vmem = pl.BlockSpec(memory_space=pltpu.VMEM)
    smem = pl.BlockSpec(memory_space=pltpu.SMEM)
    anywhere = pl.BlockSpec(memory_space=pl.ANY)

    def shape(dims, dtype):
        return jax.ShapeDtypeStruct(dims, dtype)

    stream = (micro, rows, width)
    mixed, gpre, conv, gwide, gtaps, gmid, gout = pl.pallas_call(
        functools.partial(kernel, list(scratch), n_dp),
        out_shape=[
            shape(stream, BF16),
            shape(stream, BF16),
            shape(stream, BF16),
            shape((4, 2, n_own, wr, 512), BF16),
            shape((2304, 512), BF16),
            shape(norm_mid.shape, F32),
            shape(norm_out.shape, F32),
        ],
        in_specs=[vmem, vmem, anywhere, anywhere, vmem, vmem, smem],
        out_specs=[anywhere] * 5 + [vmem] * 2,
        scratch_shapes=list(scratch.values()),
        compiler_params=pltpu.CompilerParams(
            collective_id=0, has_side_effects=True, vmem_limit_bytes=62 * 2**20
        ),
        name="layers",
    )(block_input, cotangent, weight_wide, weight_taps, norm_mid, norm_out, group_counts)
    grad_input = gpre.astype(F32) + conv.astype(F32)
    return (
        mixed,
        grad_input,
        gwide.astype(F32).reshape(weight_wide.shape),
        gtaps.astype(F32).reshape(weight_taps.shape),
        gmid,
        gout,
    )


def solution(mesh):
    split = P(None, "dp", "pipe")
    section = P("pipe", None, None)
    return jax.shard_map(
        local,
        mesh=mesh,
        in_specs=(split, split, section, section, section, section, P()),
        out_specs=(split, split, section, section, section, section),
        check_vma=False,
    )
```

```python
import functools
from types import SimpleNamespace

import jax
import jax.numpy as jnp
from jax import lax
from jax.experimental import pallas as pl
from jax.experimental.pallas import tpu as pltpu
from jax.sharding import PartitionSpec as P

MESH = pl.DeviceIdType.MESH
F32 = jnp.float32
BF16 = jnp.bfloat16
EPS = 1e-05
LANES = 128
N_PIPE = 4
NEAR = [k for k in range(9) if k != 4]


def slot_of(tap):
    return tap if tap < 4 else tap - 1


def dot_nn(a, b):
    return jnp.dot(a, b, preferred_element_type=F32)


def dot_nt(a, b):
    return lax.dot_general(a, b, (((1,), (1,)), ((), ())), preferred_element_type=F32)


def sigmoid(v):
    return jax.nn.sigmoid(v)


def sizes(n_dp):
    n_z = n_dp // 2
    n_own = min(n_z, 16)
    return n_z, n_own


def gradient_items(n_dp):
    line = n_dp // 2 == 4
    listed = []
    for kind, index, chunks in (
        ("w", 3, 1),
        ("k", 1, 2 if line else 1),
        ("w", 2, 1),
        ("w", 1, 1),
        ("k", 0, 4 if line else 1),
        ("w", 0, 2 if line else 1),
    ):
        total = 256 if kind == "w" else 2304
        for part in range(chunks):
            listed.append(
                SimpleNamespace(
                    kind=kind,
                    t=index,
                    r0=total // chunks * part,
                    nr=total // chunks,
                    i=len(listed),
                )
            )
    return listed


def scratch_list(n_dp, rows):
    n_z, n_own = sizes(n_dp)
    items = len(gradient_items(n_dp))
    line = n_z == 4
    dma = pltpu.SemaphoreType.DMA

    def half(*shape):
        return pltpu.VMEM(shape, BF16)

    def full(*shape):
        return pltpu.VMEM(shape, F32)

    return dict(
        wt=half(4, 512, 512),
        k2=half(2, 18, 256, 128),
        gm=full(4, 2, 128),
        go=full(4, 2, 2, 512),
        msk=full(2, rows, 128),
        pm=half(2, 8, rows, rows),
        part=half(2, 2, 4, rows, 128),
        rsr=half(6, 2, 3, rows, 128),
        ag=half(6, 2, 4, rows, 128),
        stm=full(8, 2, n_dp, 2, 128),
        stw=full(4, 2, n_dp, 2, 512),
        midv=full(4, 2, rows, 128),
        dzm=full(2, rows, 128),
        inv_mid=full(4, 2, 1, 128),
        inv_wide=full(2, 2, 1, 512),
        widv=full(2, 2, rows, 512),
        pre0=full(2, rows, 512),
        s1=half(2, rows, 512),
        mix=half(2, rows, 512),
        gp=half(2, 2, rows, 512),
        cv=half(2, rows, 512),
        gt=half(2, rows, 512),
        gb=half(2, rows, 1152),
        yb=half(8, rows, 128),
        tb=half(512, 2 * rows),
        dw=half(4, 2, 256, 512),
        prw=half(4, 256, 512),
        zsw=half(4, 256, 512),
        fzw=half(4, 256, 512),
        ow=half(4, 2, 256, 512),
        dk=half(2, 4608, 128),
        prk=half(2, 2304, 128),
        zsk=half(2, 2304, 128),
        fzk=half(2, 2304, 128),
        ok=half(2304, 512),
        zow=half(4, 256, 512) if line else half(4, n_z - 1, 256 // n_own, 512),
        ziw=half(4, 128, 512),
        zok=half(2, 2304, 128) if line else half(2, n_z - 1, 2304 // n_own, 128),
        zik=half(2, 1152, 128),
        gsm=full(4, 4, 2, 128),
        gsw=full(2, 4, 2, 512),
        cnt=pltpu.SMEM((2, n_dp), F32),
        f_s=dma((2, 3)),
        f_r=dma((2, 4)),
        z_s=dma((2, 4)),
        z_r=dma((2, 4)),
        b_s=dma((2, 4, 2)),
        b_r=dma((2, 4, 2)),
        n_s=dma((3, 3)),
        n_r=dma((3, 3)),
        loc=dma((8,)),
        rs_s=dma((6, 2, 3)),
        rs_r=dma((6, 2, 3)),
        ag_s=dma((6, 2, 3)),
        ag_r=dma((6, 2, 3)),
        stm_s=dma((8, 2)),
        stm_r=dma((8, 2)),
        stw_s=dma((4, 2)),
        stw_r=dma((4, 2)),
        pw_s=dma((6,)),
        pw_r=dma((6,)),
        up_s=dma((items,)),
        up_r=dma((items,)),
        mid_s=dma((items,)),
        mid_r=dma((items,)),
        inn_s=dma((items,)),
        inn_r=dma((items,)),
        dn_s=dma((items, 2)),
        dn_r=dma((items, 2)),
        to_s=dma((items,)),
        to_r=dma((items, 4)),
        sib_s=dma((items, 4)),
        sib_r=dma((items, 4)),
        g_s=dma((3, 2)),
        g_r=dma((3, 2)),
        out=dma((8,)),
    )


def kernel(names, n, *refs):
    (x_ref, cot_ref, wide_ref, taps_ref, nmid_ref, nout_ref, counts_ref) = refs[:7]
    (mixed_ref, gpre_ref, conv_ref, gwide_ref, gtaps_ref, gmid_ref, gout_ref) = refs[7:14]
    sc = SimpleNamespace(**dict(zip(names, refs[14:])))
    rows = x_ref.shape[1]
    n_z, n_own = sizes(n)
    p = lax.axis_index("pipe")
    d = lax.axis_index("dp")
    z = lax.div(d, 2)
    c = lax.rem(d, 2)
    parity = lax.rem(p, 2)
    sibling = (p, 2 * z + 1 - c)
    z_odd = lax.rem(z, 2)
    z_pair = (p, 2 * (z + 1 - 2 * z_odd) + c)
    quarter = 2 * z_odd + c
    quarter_z = 2 * (1 - z_odd) + c
    finish = []

    def pipe_at(off):
        return lax.rem(p + off, N_PIPE)

    def remote(src, dst, ss, rs, dev):
        return pltpu.make_async_remote_copy(
            src_ref=src, dst_ref=dst, send_sem=ss, recv_sem=rs, device_id=dev, device_id_type=MESH
        )

    def each(count, first, body):
        if count - first <= 8:
            for k in range(first, count):
                body(k)
        else:

            def step(k, carry):
                body(k)
                return carry

            lax.fori_loop(first, count, step, 0)

    def bytes_wait(view, sem):
        pltpu.make_async_copy(view, view, sem).wait()

    barrier = pltpu.get_barrier_semaphore()
    for off in range(1, N_PIPE):
        pl.semaphore_signal(barrier, inc=1, device_id=(pipe_at(off), d), device_id_type=MESH)

    def greet(k):
        pl.semaphore_signal(
            barrier, inc=1, device_id=(p, lax.rem(d + k, n)), device_id_type=MESH
        )

    each(n, 1, greet)

    def columns_of(q):
        return pl.ds(pl.multiple_of(128 * q, 128), 128)

    own_w = pltpu.make_async_copy(
        wide_ref.at[0, pl.ds(pl.multiple_of(512 * p, 512), 512), :], sc.wt.at[p], sc.loc.at[0]
    )
    own_k = pltpu.make_async_copy(
        taps_ref.at[:, :, columns_of(p)],
        sc.k2.at[lax.div(p, 2), pl.ds(9 * parity, 9)],
        sc.loc.at[1],
    )
    own_w.start()
    own_k.start()
    own_n = pltpu.make_async_copy(
        nmid_ref.at[0, :, columns_of(p)], sc.gm.at[p], sc.loc.at[6]
    )
    own_n.start()
    for e in range(2):
        sc.go[p, e] = nout_ref[0, :, 512 * e : 512 * e + 512]

    def used_rows(m, j):
        return (
            49 * counts_ref[m, j, 0]
            + 36 * counts_ref[m, j, 1]
            + 25 * counts_ref[m, j, 2]
            + 4 * counts_ref[m, j, 3]
        )

    totals = []
    for m in range(2):

        def count_up(j, acc, m=m):
            used = used_rows(m, j)
            sc.cnt[m, j] = used.astype(F32)
            return acc + used

        totals.append(lax.fori_loop(0, n, count_up, jnp.int32(0)).astype(F32))

    pl.semaphore_wait(barrier, N_PIPE - 1 + n - 1)

    def held(kind, s, part):
        if kind == 0:
            return sc.wt.at[s, pl.ds(pl.multiple_of(128 * part, 128), 128)]
        layer, odd = (s // 2, s % 2) if isinstance(s, int) else (lax.div(s, 2), lax.rem(s, 2))
        return sc.k2.at[
            layer, pl.ds(9 * odd, 9), pl.ds(pl.multiple_of(64 * part, 64), 64)
        ]

    def fetch(kind, off):
        q = pipe_at(off)
        if kind == 0:
            src = wide_ref.at[0, pl.ds(pl.multiple_of(512 * q + 128 * quarter, 128), 128), :]
        else:
            src = taps_ref.at[:, pl.ds(pl.multiple_of(64 * quarter, 64), 64), columns_of(q)]
        return remote(
            src, held(kind, p, quarter), sc.f_s.at[kind, off - 1], sc.f_r.at[kind, p], (q, d)
        )

    def send_norm(off):
        q = pipe_at(off)
        listed = [
            remote(
                nmid_ref.at[0, :, columns_of(q)],
                sc.gm.at[p],
                sc.n_s.at[off - 1, 0],
                sc.n_r.at[off - 1, 0],
                (q, d),
            )
        ]
        for e in range(2):
            listed.append(
                remote(
                    nout_ref.at[0, :, pl.ds(512 * e, 512)],
                    sc.go.at[p, e],
                    sc.n_s.at[off - 1, 1 + e],
                    sc.n_r.at[off - 1, 1 + e],
                    (q, d),
                )
            )
        return listed

    def pass_z(kind, s):
        view = held(kind, s, quarter)
        return remote(view, view, sc.z_s.at[kind, s], sc.z_r.at[kind, s], z_pair)

    def pass_sibling(kind, s, e):
        view = held(kind, s, quarter if e == 0 else quarter_z)
        return remote(view, view, sc.b_s.at[kind, s, e], sc.b_r.at[kind, s, e], sibling)

    def spread_first(kind, s):
        @pl.when(p != s)
        def _():
            view = held(kind, s, quarter)
            bytes_wait(view, sc.f_r.at[kind, s])
            pass_z(kind, s).start()
            pass_sibling(kind, s, 0).start()

    def spread_second(kind, s):
        @pl.when(p != s)
        def _():
            pass_z(kind, s).wait_recv()
            pass_sibling(kind, s, 1).start()

    def ready(kind, s):
        @pl.when(p != s)
        def _():
            for e in range(2):
                pass_sibling(kind, s, e).wait_recv()

        @pl.when(p == s)
        def _():
            (own_w if kind == 0 else own_k).wait()

    def finish_weights():
        for kind in range(2):
            for off in range(1, 4):
                fetch(kind, off).wait_send()
            for s in range(4):

                @pl.when(p != s)
                def _(kind=kind, s=s):
                    pass_z(kind, s).wait_send()
                    for e in range(2):
                        pass_sibling(kind, s, e).wait_send()

    finish.append(finish_weights)

    for even in range(2):

        @pl.when(parity == even)
        def _(even=even):
            for kind in (even, 1 - even):
                for off in range(1, 4):
                    fetch(kind, off).start()
                if kind == even:
                    for off in range(1, 4):
                        for copy in send_norm(off):
                            copy.start()

    def finish_norm():
        for off in range(1, 4):
            for copy in send_norm(off):
                copy.wait_send()

    finish.append(finish_norm)

    row_id = lax.broadcasted_iota(jnp.int32, (rows, LANES), 0).astype(F32)
    lane_id = lax.broadcasted_iota(jnp.int32, (rows, LANES), 1).astype(F32)

    def build(m):
        ends = []
        total = jnp.int32(0)
        for g, area in enumerate((49, 36, 25, 4)):
            total = total + area * counts_ref[m, d, g]
            ends.append(total.astype(F32))
        sc.msk[m] = jnp.where(row_id < ends[3], 1.0, 0.0)

        def pick(values):
            out = values[4]
            for g in (3, 2, 1, 0):
                out = jnp.where(row_id < ends[g], values[g], out)
            return out

        zero = jnp.zeros((rows, LANES), F32)
        side = pick([zero + 7.0, zero + 6.0, zero + 5.0, zero + 2.0, zero + 1.0])
        begin = pick([zero, zero + ends[0], zero + ends[1], zero + ends[2], row_id])
        one_over = pick(
            [zero + 1.0 / 7.0, zero + 1.0 / 6.0, zero + 1.0 / 5.0, zero + 0.5, zero + 1.0]
        )
        within = row_id - begin
        within = within - side * side * jnp.floor((within + 0.5) * one_over * one_over)
        map_row = jnp.floor((within + 0.5) * one_over)
        map_col = within - side * map_row
        for k in NEAR:
            du, dv = k // 3 - 1, k % 3 - 1
            usable = row_id < ends[3]
            if du == -1:
                usable = usable & (map_row > 0.5)
            if du == 1:
                usable = usable & (map_row < side - 1.5)
            if dv == -1:
                usable = usable & (map_col > 0.5)
            if dv == 1:
                usable = usable & (map_col < side - 1.5)
            target = jnp.where(usable, row_id + du * side + dv, -1000.0)
            for t in range(rows // LANES):
                hit = jnp.where(target == lane_id + float(LANES * t), 1.0, 0.0)
                sc.pm[m, slot_of(k), :, LANES * t : LANES * (t + 1)] = hit.astype(BF16)

    for m in range(2):
        build(m)


    def rs_copies(rid, m, par):
        listed = []
        for off in range(1, 4):
            q = pipe_at(off)
            listed.append(
                remote(
                    sc.part.at[par, m, q],
                    sc.rsr.at[rid, m, off - 1],
                    sc.rs_s.at[rid, m, off - 1],
                    sc.rs_r.at[rid, m, off - 1],
                    (q, d),
                )
            )
        return listed

    def rs_start(rid, m, par):
        for copy in rs_copies(rid, m, par):
            copy.start()

    def rs_sum(rid, m, par):
        for copy in rs_copies(rid, m, par):
            copy.wait_recv()
        total = sc.part[par, m, p].astype(F32)
        for k in range(3):
            total = total + sc.rsr[rid, m, k].astype(F32)
        return total

    def ag_copies(aid, m):
        listed = []
        for off in range(1, 4):
            listed.append(
                remote(
                    sc.ag.at[aid, m, p],
                    sc.ag.at[aid, m, p],
                    sc.ag_s.at[aid, m, off - 1],
                    sc.ag_r.at[aid, m, off - 1],
                    (pipe_at(off), d),
                )
            )
        return listed

    def ag_start(aid, m, value):
        sc.ag[aid, m, p] = value
        for copy in ag_copies(aid, m):
            copy.start()

    def ag_wait(aid, m):
        for copy in ag_copies(aid, m):
            copy.wait_recv()

    def ag_value(aid, m):
        return jnp.concatenate([sc.ag[aid, m, q] for q in range(4)], axis=1)

    def finish_ag():
        for aid in range(6):
            for m in range(2):
                for copy in ag_copies(aid, m):
                    copy.wait_send()

    finish.append(finish_ag)

    def st_refs(wide, i, m):
        if wide:
            return sc.stw.at[i, m], sc.stw_s.at[i, m], sc.stw_r.at[i, m]
        return sc.stm.at[i, m], sc.stm_s.at[i, m], sc.stm_r.at[i, m]

    def st_start(wide, i, m):
        buf, ss, rs = st_refs(wide, i, m)

        def go(k):
            remote(buf.at[d], buf.at[d], ss, rs, (p, lax.rem(d + k, n))).start()

        each(n, 1, go)

    def st_wait(wide, i, m):
        buf, ss, rs = st_refs(wide, i, m)
        bytes_wait(buf.at[pl.ds(0, n - 1)], rs)

    def finish_st():
        for wide, count in ((True, 4), (False, 8)):
            for i in range(count):
                for m in range(2):
                    buf, ss, rs = st_refs(wide, i, m)
                    bytes_wait(buf.at[pl.ds(0, n - 1)], ss)

    finish.append(finish_st)

    def over_devices(body, init):
        if n <= 8:
            for j in range(n):
                init = body(j, init)
            return init
        return lax.fori_loop(0, n, body, init)

    def combine(wide, i, m):
        st_wait(wide, i, m)
        ref = sc.stw if wide else sc.stm
        blank = jnp.zeros((1, ref.shape[-1]), F32)
        mean = over_devices(
            lambda j, acc: acc + sc.cnt[m, j] * ref[i, m, j, 0:1, :], blank
        )
        mean = mean / totals[m]

        def spread(j, acc):
            gap = ref[i, m, j, 0:1, :] - mean
            return acc + ref[i, m, j, 1:2, :] + sc.cnt[m, j] * (gap * gap)

        var = over_devices(spread, blank) / totals[m]
        return mean, lax.rsqrt(var + EPS)

    def back_sums(wide, i, m):
        st_wait(wide, i, m)
        ref = sc.stw if wide else sc.stm
        return over_devices(
            lambda j, acc: acc + ref[i, m, j], jnp.zeros((2, ref.shape[-1]), F32)
        )

    def local_moments(v, m):
        mask = sc.msk[m]
        own = jnp.maximum(sc.cnt[m, d], 1.0)
        mean = jnp.sum(v * mask, 0, keepdims=True) / own
        gap = (v - mean) * mask
        return jnp.concatenate([mean, jnp.sum(gap * gap, 0, keepdims=True)], 0)

    def local_sums(dz, vhat):
        return jnp.concatenate(
            [jnp.sum(dz * vhat, 0, keepdims=True), jnp.sum(dz, 0, keepdims=True)], 0
        )

    def lanes(j):
        return slice(LANES * j, LANES * (j + 1))

    def stream(layer, m):
        return x_ref[m] if layer == 0 else sc.s1[m]

    def stream_part(layer, m, j):
        return (x_ref[m, :, lanes(j)] if layer == 0 else sc.s1[m, :, lanes(j)]).astype(F32)

    rs_par = {0: 0, 1: 1, 3: 0, 5: 1, 2: 0, 4: 1}
    rs_before = {0: None, 1: None, 3: 0, 5: 1, 2: 3, 4: 5}

    def rs_send(rid, m, values):
        par = rs_par[rid]
        if rs_before[rid] is not None:
            for copy in rs_copies(rs_before[rid], m, par):
                copy.wait_send()
        for j, value in enumerate(values):
            half = value.astype(BF16)
            sc.part[par, m, 2 * j] = half[:, :LANES]
            sc.part[par, m, 2 * j + 1] = half[:, LANES:]
        rs_start(rid, m, par)

    def finish_rs():
        for rid in (2, 4):
            for m in range(2):
                for copy in rs_copies(rid, m, rs_par[rid]):
                    copy.wait_send()

    finish.append(finish_rs)

    def first_part(layer, m):
        s = stream(layer, m)
        rs_send(
            layer,
            m,
            [dot_nn(s, sc.wt[2 * layer, :, 256 * j : 256 * j + 256]) for j in range(2)],
        )

    def mid_moments(i, m, v):
        sc.midv[i, m] = v
        sc.stm[i, m, d] = local_moments(v, m)
        st_start(False, i, m)

    def first_norm(layer, m):
        mid_moments(2 * layer, m, rs_sum(layer, m, rs_par[layer]))

    def mid_hidden(i, m):
        mean, inv = combine(False, i, m)
        sc.inv_mid[i, m] = inv
        vhat = (sc.midv[i, m] - mean) * inv
        sc.midv[i, m] = vhat
        u = sc.gm[i, 0:1, :] * vhat + sc.gm[i, 1:2, :]
        return (sc.msk[m] * (u * sigmoid(u))).astype(BF16)

    def hidden_one(layer, m):
        ag_start(layer, m, mid_hidden(2 * layer, m))

    def taps_of(layer, taps):
        return jnp.concatenate(
            [
                jnp.concatenate([sc.k2[layer, 2 * k], sc.k2[layer, 2 * k + 1]], axis=0)
                for k in taps
            ],
            axis=1,
        )

    def second_part(layer, m):
        ag_wait(layer, m)
        h = ag_value(layer, m)
        centre = None
        for j in range(5):
            width = 256 if j < 4 else 128
            y = dot_nn(h, taps_of(layer, [2 * j + e for e in range(width // LANES)]))
            for e in range(width // LANES):
                tap = 2 * j + e
                if tap == 4:
                    centre = y[:, lanes(e)]
                    sc.midv[2 * layer + 1, m] = centre
                else:
                    sc.yb[slot_of(tap)] = y[:, lanes(e)].astype(BF16)
        total = sc.midv[2 * layer + 1, m]
        for k in range(8):
            total = total + dot_nn(sc.pm[m, k], sc.yb[k])
        mid_moments(2 * layer + 1, m, total)

    def hidden_two(layer, m):
        ag_start(2 + layer, m, mid_hidden(2 * layer + 1, m))

    def third_part(layer, m):
        ag_wait(2 + layer, m)
        h = ag_value(2 + layer, m)
        for j in range(2):
            sc.widv[layer, m, :, 256 * j : 256 * j + 256] = dot_nt(
                h, sc.wt[2 * layer + 1, 256 * j : 256 * j + 256, :]
            )
        for j in range(4):
            sc.stw[layer, m, d, :, lanes(j)] = local_moments(sc.widv[layer, m, :, lanes(j)], m)
        st_start(True, layer, m)

    def out_gain(layer, j):
        both = sc.go[2 * layer + lax.div(p, 2), lax.rem(p, 2)]
        return both[0:1, lanes(j)], both[1:2, lanes(j)]

    def pre_values(layer, m):
        mean, inv = combine(True, layer, m)
        sc.inv_wide[layer, m] = inv
        mask = sc.msk[m]
        for j in range(4):
            gain, bias = out_gain(layer, j)
            vhat = (sc.widv[layer, m, :, lanes(j)] - mean[:, lanes(j)]) * inv[:, lanes(j)]
            sc.widv[layer, m, :, lanes(j)] = vhat
            pre = gain * vhat + bias + stream_part(layer, m, j)
            sig = sigmoid(pre)
            out = (mask * (pre * sig)).astype(BF16)
            if layer == 0:
                sc.pre0[m, :, lanes(j)] = pre
                sc.s1[m, :, lanes(j)] = out
            else:
                sc.mix[m, :, lanes(j)] = out
                slope = sig * (1.0 + pre * (1.0 - sig))
                grad = (cot_ref[m, :, lanes(j)].astype(F32) * mask * slope).astype(BF16)
                sc.gp[1, m, :, lanes(j)] = grad
                sc.stw[3, m, d, :, lanes(j)] = local_sums(grad.astype(F32), vhat)
        if layer == 1:
            st_start(True, 3, m)

    def put_out(k, src, dst):
        copy = pltpu.make_async_copy(src, dst, sc.out.at[k])
        copy.start()
        return copy

    def grad_out_norm(layer, m):
        sums = back_sums(True, 2 + layer, m)
        if m == 0:
            sc.gsw[layer, p] = sums
        else:
            sc.gsw[layer, p] = sc.gsw[layer, p] + sums
        mask = sc.msk[m]
        inv = sc.inv_wide[layer, m]
        for j in range(4):
            gain, _ = out_gain(layer, j)
            dz = sc.gp[layer, m, :, lanes(j)].astype(F32)
            vhat = sc.widv[layer, m, :, lanes(j)]
            s1 = sums[0:1, lanes(j)] / totals[m]
            s0 = sums[1:2, lanes(j)] / totals[m]
            dv = mask * (gain * inv[:, lanes(j)]) * (dz - s0 - vhat * s1)
            sc.gt[m, :, lanes(j)] = dv.astype(BF16)
        g = sc.gt[m]
        rs_send(
            2 + layer,
            m,
            [dot_nn(g, sc.wt[2 * layer + 1, :, 256 * j : 256 * j + 256]) for j in range(2)],
        )

    def mid_grad(i, m, upstream):
        vhat = sc.midv[i, m]
        u = sc.gm[i, 0:1, :] * vhat + sc.gm[i, 1:2, :]
        sig = sigmoid(u)
        dz = upstream * sc.msk[m] * (sig * (1.0 + u * (1.0 - sig)))
        sc.dzm[m] = dz
        sc.stm[4 + i, m, d] = local_sums(dz, vhat)
        st_start(False, 4 + i, m)

    def mid_back(i, m):
        sums = back_sums(False, 4 + i, m)
        if m == 0:
            sc.gsm[i, p] = sums
        else:
            sc.gsm[i, p] = sc.gsm[i, p] + sums
        s1 = sums[0:1, :] / totals[m]
        s0 = sums[1:2, :] / totals[m]
        scale = sc.gm[i, 0:1, :] * sc.inv_mid[i, m]
        return (sc.msk[m] * scale * (sc.dzm[m] - s0 - sc.midv[i, m] * s1)).astype(BF16)

    def grad_two(layer, m):
        mid_grad(2 * layer + 1, m, rs_sum(2 + layer, m, rs_par[2 + layer]))

    def grad_second(layer, m):
        gs = mid_back(2 * layer + 1, m)
        for k in range(9):
            if k == 4:
                sc.gb[m, :, lanes(k)] = gs
            else:
                sc.gb[m, :, lanes(k)] = dot_nn(sc.pm[m, slot_of(8 - k)], gs).astype(BF16)
        g = sc.gb[m]
        rs_send(
            4 + layer,
            m,
            [
                dot_nt(
                    g, jnp.concatenate([sc.k2[layer, 2 * k + j] for k in range(9)], axis=1)
                )
                for j in range(2)
            ],
        )

    def grad_one(layer, m):
        mid_grad(2 * layer, m, rs_sum(4 + layer, m, rs_par[4 + layer]))

    def grad_first(layer, m):
        ag_start(4 + layer, m, mid_back(2 * layer, m))

    def conv_grad(layer, m):
        ag_wait(4 + layer, m)
        g = ag_value(4 + layer, m)
        mask = sc.msk[m]
        for j in range(2):
            r = dot_nt(g, sc.wt[2 * layer, 256 * j : 256 * j + 256, :]).astype(BF16)
            if layer == 0:
                sc.cv[m, :, 256 * j : 256 * j + 256] = r
                continue
            for e in range(2):
                i = 2 * j + e
                pre = sc.pre0[m, :, lanes(i)]
                sig = sigmoid(pre)
                slope = sig * (1.0 + pre * (1.0 - sig))
                up = sc.gp[1, m, :, lanes(i)].astype(F32) + r[:, lanes(e)].astype(F32)
                grad = (up * mask * slope).astype(BF16)
                sc.gp[0, m, :, lanes(i)] = grad
                sc.stw[2, m, d, :, lanes(i)] = local_sums(
                    grad.astype(F32), sc.widv[0, m, :, lanes(i)]
                )
        if layer == 1:
            st_start(True, 2, m)

    def turned(blocks):
        for m, block in enumerate(blocks):
            sc.tb[:, rows * m : rows * (m + 1)] = block.T

    def both(get):
        return jnp.concatenate([get(0), get(1)], axis=0)

    def wide_grad(s, left, right):
        turned([left(0), left(1)])
        for j in range(2):
            cols = slice(256 * j, 256 * j + 256)
            rhs = both(lambda m: right(m)[:, cols])
            for h in range(2):
                r = dot_nn(sc.tb[256 * h : 256 * h + 256, :], rhs)
                sc.dw[s, h, :, cols] = r.astype(BF16)
        pair_copy("w", s).start()

    def taps_grad(layer):
        turned([ag_value(layer, 0), ag_value(layer, 1)])
        for j in range(5):
            width = 256 if j < 4 else 128
            rhs = both(lambda m: sc.gb[m, :, 256 * j : 256 * j + width])
            r = dot_nn(sc.tb[...], rhs).astype(BF16)
            for e in range(width // LANES):
                tap = 2 * j + e
                sc.dk[layer, 512 * tap : 512 * tap + 512, :] = r[:, lanes(e)]
        pair_copy("k", layer).start()

    def half_rows(which):
        return pl.ds(pl.multiple_of(2304 * which, 2304), 2304)

    def pair_copy(kind, t):
        if kind == "w":
            src, dst, i = sc.dw.at[t, 1 - c], sc.prw.at[t], t
        else:
            src, dst, i = sc.dk.at[t, half_rows(1 - c)], sc.prk.at[t], 4 + t
        return remote(src, dst, sc.pw_s.at[i], sc.pw_r.at[i], sibling)

    def pair_sum(kind, t):
        pair_copy(kind, t).wait_recv()
        if kind == "w":
            sc.zsw[t] = (sc.dw[t, c].astype(F32) + sc.prw[t].astype(F32)).astype(BF16)
            return
        for i in range(4):
            part = slice(576 * i, 576 * i + 576)
            mine = pl.ds(pl.multiple_of(2304 * c + 576 * i, 576), 576)
            sc.zsk[t, part] = (
                sc.dk[t, mine].astype(F32) + sc.prk[t, part].astype(F32)
            ).astype(BF16)

    items = gradient_items(n)
    line = n_z == 4
    inner = (z == 1) | (z == 2)

    def tile(it, name):
        return getattr(sc, name + it.kind)

    def some(it, name, start, count):
        return tile(it, name).at[it.t, pl.ds(start, count)]

    def part_rows(it, which):
        half = it.nr // 2
        return pl.ds(pl.multiple_of(it.r0 + half * which, half), half)

    def up_copy(it):
        rows_of = pl.ds(it.r0, it.nr)
        return remote(
            tile(it, "zs").at[it.t, rows_of],
            tile(it, "zo").at[it.t, rows_of],
            sc.up_s.at[it.i],
            sc.up_r.at[it.i],
            (p, 2 * (1 + lax.div(z, 3)) + c),
        )

    def mid_copy(it):
        return remote(
            tile(it, "zs").at[it.t, part_rows(it, 2 - z)],
            tile(it, "zi").at[it.t, pl.ds(it.r0 // 2, it.nr // 2)],
            sc.mid_s.at[it.i],
            sc.mid_r.at[it.i],
            (p, 2 * (3 - z) + c),
        )

    def inn_copy(it):
        view = tile(it, "fz").at[it.t, part_rows(it, z - 1)]
        return remote(
            view, view, sc.inn_s.at[it.i], sc.inn_r.at[it.i], (p, 2 * (3 - z) + c)
        )

    def down_copy(it, e):
        view = tile(it, "fz").at[it.t, part_rows(it, z - 1 if e == 0 else 2 - z)]
        return remote(
            view, view, sc.dn_s.at[it.i, e], sc.dn_r.at[it.i, e], (p, 2 * (3 * (z - 1)) + c)
        )

    def direct_rows(it, j):
        count = it.nr // n_own
        return pl.ds(pl.multiple_of(it.r0 + count * j, count), count)

    def owner(index, body):
        if n_own == n_z:
            body()
        else:
            pl.when(index < n_own)(body)

    def scatter_copy(it, k):
        j = lax.rem(z + k, n_z)
        return j, remote(
            tile(it, "zs").at[it.t, direct_rows(it, lax.rem(j, n_own))],
            tile(it, "zo").at[it.t, k - 1],
            sc.up_s.at[it.i],
            sc.up_r.at[it.i],
            (p, 2 * j + c),
        )

    def gather_copy(it, k):
        j = lax.rem(z + k, n_z)
        view = tile(it, "fz").at[it.t, direct_rows(it, lax.rem(z, n_own))]
        return remote(view, view, sc.dn_s.at[it.i, 0], sc.dn_r.at[it.i, 0], (p, 2 * j + c))

    def add_rows(target, first, second):
        target[...] = (first[...].astype(F32) + second[...].astype(F32)).astype(BF16)

    def step_up(it):
        if line:

            @pl.when((z == 0) | (z == 3))
            def _():
                up_copy(it).start()

        else:

            def go(k):
                j, copy = scatter_copy(it, k)
                owner(j, lambda: copy.start())

            each(n_z, 1, go)

    def step_mid(it):
        if not line:
            return

        @pl.when(inner)
        def _():
            up_copy(it).wait_recv()
            mine = some(it, "zs", it.r0, it.nr)
            add_rows(mine, mine, some(it, "zo", it.r0, it.nr))
            mid_copy(it).start()

    def step_down(it):
        if line:

            @pl.when(inner)
            def _():
                mid_copy(it).wait_recv()
                keep = part_rows(it, z - 1)
                add_rows(
                    tile(it, "fz").at[it.t, keep],
                    tile(it, "zs").at[it.t, keep],
                    some(it, "zi", it.r0 // 2, it.nr // 2),
                )
                inn_copy(it).start()
                down_copy(it, 0).start()

            return

        def go():
            bytes_wait(tile(it, "zo").at[it.t], sc.up_r.at[it.i])
            mine = direct_rows(it, z)
            total = tile(it, "zs")[it.t, mine].astype(F32)
            total = lax.fori_loop(
                0, n_z - 1, lambda k, acc: acc + tile(it, "zo")[it.t, k].astype(F32), total
            )
            tile(it, "fz")[it.t, mine] = total.astype(BF16)
            each(n_z, 1, lambda k: gather_copy(it, k).start())

        owner(z, go)

    def step_last(it):
        if not line:
            return

        @pl.when(inner)
        def _():
            inn_copy(it).wait_recv()
            down_copy(it, 1).start()

    def owner_of(it):
        return it.t if it.kind == "w" else 2 * it.t + c

    def landing(it, q, core):
        if it.kind == "w":
            return sc.ow.at[q, core, pl.ds(it.r0, it.nr)]
        lane = pl.ds(128 * q, 128) if isinstance(q, int) else columns_of(q)
        return sc.ok.at[pl.ds(it.r0, it.nr), lane]

    def to_copy(it):
        return remote(
            some(it, "fz", it.r0, it.nr),
            landing(it, p, c),
            sc.to_s.at[it.i],
            sc.to_r.at[it.i, p],
            (owner_of(it), d),
        )

    def step_out(it):
        if line:

            @pl.when((z == 0) | (z == 3))
            def _():
                for e in range(2):
                    bytes_wait(some(it, "fz", it.r0, it.nr // 2), sc.dn_r.at[it.i, e])

        else:
            count = it.nr // n_own
            if n_own == n_z:
                bytes_wait(some(it, "fz", it.r0, count * (n_own - 1)), sc.dn_r.at[it.i, 0])
            else:

                @pl.when(z < n_own)
                def _():
                    bytes_wait(some(it, "fz", it.r0, count * (n_own - 1)), sc.dn_r.at[it.i, 0])

                @pl.when(z >= n_own)
                def _():
                    bytes_wait(some(it, "fz", it.r0, count * n_own), sc.dn_r.at[it.i, 0])

        @pl.when(p != owner_of(it))
        def _():
            to_copy(it).start()

        def place(q):
            landing(it, q, c)[...] = some(it, "fz", it.r0, it.nr)[...]

        if it.kind == "w":
            pl.when(p == it.t)(lambda: place(it.t))
        else:
            for core in range(2):
                pl.when((p == 2 * it.t + core) & (c == core))(
                    functools.partial(place, 2 * it.t + core)
                )

    def sibling_copy(it, q):
        view = landing(it, q, c)
        return remote(view, view, sc.sib_s.at[it.i, q], sc.sib_r.at[it.i, q], sibling)

    def step_sibling(it):
        def go(own):
            for q in range(4):
                if q != own:
                    bytes_wait(landing(it, q, 0), sc.to_r.at[it.i, q])
                sibling_copy(it, q).start()

        if it.kind == "w":
            pl.when(p == it.t)(lambda: go(it.t))
        else:
            for core in range(2):
                pl.when((p == 2 * it.t + core) & (c == core))(
                    functools.partial(go, 2 * it.t + core)
                )

    def step_done(it):
        def go():
            for q in range(4):
                bytes_wait(landing(it, q, 0), sc.sib_r.at[it.i, q])

        if it.kind == "w":
            pl.when(p == it.t)(go)
        else:
            for core in range(2):
                pl.when((p == 2 * it.t + core) & (c != core))(go)

    def finish_grads():
        for kind, t in [("w", s) for s in range(4)] + [("k", layer) for layer in range(2)]:
            pair_copy(kind, t).wait_send()
        for it in items:
            if line:

                @pl.when(inner)
                def _(it=it):
                    mid_copy(it).wait_send()
                    inn_copy(it).wait_send()
                    for e in range(2):
                        down_copy(it, e).wait_send()

                @pl.when((z == 0) | (z == 3))
                def _(it=it):
                    up_copy(it).wait_send()

            else:

                def sent(k, it=it):
                    j, copy = scatter_copy(it, k)
                    owner(j, lambda: copy.wait_send())

                each(n_z, 1, sent)
                owner(z, lambda: each(n_z, 1, lambda k: gather_copy(it, k).wait_send()))

            @pl.when(p != owner_of(it))
            def _(it=it):
                to_copy(it).wait_send()

            def passed(it=it):
                for q in range(4):
                    sibling_copy(it, q).wait_send()

            if it.kind == "w":
                pl.when(p == it.t)(passed)
            else:
                pl.when(p == 2 * it.t + c)(passed)

    finish.append(finish_grads)

    def gain_copies(off):
        dev = (pipe_at(off), d)
        return [
            remote(
                sc.gsm.at[:, p], sc.gsm.at[:, p], sc.g_s.at[off - 1, 0], sc.g_r.at[off - 1, 0], dev
            ),
            remote(
                sc.gsw.at[:, p], sc.gsw.at[:, p], sc.g_s.at[off - 1, 1], sc.g_r.at[off - 1, 1], dev
            ),
        ]

    def gains_start():
        for off in range(1, 4):
            for copy in gain_copies(off):
                copy.start()

    def gains_done():
        for off in range(1, 4):
            for copy in gain_copies(off):
                copy.wait_recv()
        for q in range(4):
            gmid_ref[0, :, lanes(q)] = sc.gsm[p, q]
        layer = lax.div(p, 2)
        for e in range(2):
            gout_ref[0, :, 512 * e : 512 * e + 512] = sc.gsw[layer, 2 * parity + e]

    def finish_gains():
        for off in range(1, 4):
            for copy in gain_copies(off):
                copy.wait_send()

    finish.append(finish_gains)

    def phase(body, layer):
        for m in range(2):
            body(layer, m)

    def of(kind, t, part=None):
        chosen = [it for it in items if it.kind == kind and it.t == t]
        return chosen

    def run(step, kind, t):
        for it in of(kind, t):
            step(it)

    wide, taps = 0, 1
    spread_first(wide, 0)
    spread_second(wide, 0)
    ready(wide, 0)
    phase(first_part, 0)
    own_n.wait()
    for off in range(1, 4):
        for copy in send_norm(off):
            copy.wait_recv()
    spread_first(taps, 0)
    spread_first(taps, 1)
    phase(first_norm, 0)
    spread_second(taps, 0)
    spread_second(taps, 1)
    phase(hidden_one, 0)
    spread_first(wide, 1)
    spread_first(wide, 2)
    ready(taps, 0)
    ready(taps, 1)
    phase(second_part, 0)
    spread_second(wide, 1)
    spread_second(wide, 2)
    phase(hidden_two, 0)
    spread_first(taps, 2)
    spread_first(taps, 3)
    ready(wide, 1)
    phase(third_part, 0)
    spread_second(taps, 2)
    spread_second(taps, 3)
    ready(wide, 2)

    def turn(layer, m):
        pre_values(0, m)
        first_part(1, m)

    phase(turn, 0)
    spread_first(wide, 3)
    phase(first_norm, 1)
    spread_second(wide, 3)
    phase(hidden_one, 1)
    ready(taps, 2)
    ready(taps, 3)
    phase(second_part, 1)
    phase(hidden_two, 1)
    ready(wide, 3)
    phase(third_part, 1)
    phase(pre_values, 1)
    outs = [put_out(2, sc.mix.at[...], mixed_ref.at[...])]

    phase(grad_out_norm, 1)
    wide_grad(3, lambda m: sc.gt[m], lambda m: ag_value(3, m))
    phase(grad_two, 1)
    pair_sum("w", 3)
    run(step_up, "w", 3)
    phase(grad_second, 1)
    taps_grad(1)
    run(step_mid, "w", 3)
    phase(grad_one, 1)
    pair_sum("k", 1)
    run(step_up, "k", 1)
    run(step_down, "w", 3)
    phase(grad_first, 1)
    run(step_last, "w", 3)
    phase(conv_grad, 1)
    outs.append(put_out(3, sc.gp.at[0], gpre_ref.at[...]))
    wide_grad(2, lambda m: sc.s1[m], lambda m: ag_value(5, m))
    run(step_mid, "k", 1)
    phase(grad_out_norm, 0)
    wide_grad(1, lambda m: sc.gt[m], lambda m: ag_value(2, m))
    run(step_out, "w", 3)
    phase(grad_two, 0)
    pair_sum("w", 2)
    run(step_up, "w", 2)
    pair_sum("w", 1)
    run(step_up, "w", 1)
    run(step_down, "k", 1)
    phase(grad_second, 0)
    taps_grad(0)
    run(step_mid, "w", 2)
    run(step_last, "k", 1)
    phase(grad_one, 0)
    pair_sum("k", 0)
    run(step_up, "k", 0)
    run(step_mid, "w", 1)
    run(step_down, "w", 2)
    phase(grad_first, 0)
    run(step_out, "k", 1)
    run(step_last, "w", 2)
    run(step_down, "w", 1)
    gains_start()
    phase(conv_grad, 0)
    outs.append(put_out(4, sc.cv.at[...], conv_ref.at[...]))
    wide_grad(0, lambda m: x_ref[m], lambda m: ag_value(4, m))
    run(step_out, "w", 2)
    run(step_mid, "k", 0)
    run(step_last, "w", 1)
    pair_sum("w", 0)
    run(step_up, "w", 0)
    run(step_down, "k", 0)
    run(step_out, "w", 1)
    gains_done()
    run(step_sibling, "w", 3)
    run(step_sibling, "k", 1)
    run(step_last, "k", 0)
    run(step_mid, "w", 0)
    run(step_sibling, "w", 2)
    run(step_out, "k", 0)
    run(step_down, "w", 0)
    run(step_sibling, "w", 1)
    run(step_last, "w", 0)
    run(step_sibling, "k", 0)
    run(step_out, "w", 0)
    run(step_done, "k", 1)
    run(step_done, "k", 0)
    outs.append(put_out(1, sc.ok.at[...], gtaps_ref.at[...]))
    run(step_sibling, "w", 0)
    for s in (3, 2, 1, 0):
        run(step_done, "w", s)
    outs.append(put_out(0, sc.ow.at[...], gwide_ref.at[...]))
    for copy in outs:
        copy.wait()
    for body in finish:
        body()


def local(block_input, cotangent, weight_wide, weight_taps, norm_mid, norm_out, group_counts):
    n_dp = group_counts.shape[1]
    micro, rows, width = block_input.shape
    scratch = scratch_list(n_dp, rows)
    vmem = pl.BlockSpec(memory_space=pltpu.VMEM)
    smem = pl.BlockSpec(memory_space=pltpu.SMEM)
    anywhere = pl.BlockSpec(memory_space=pl.ANY)

    def shape(dims, dtype):
        return jax.ShapeDtypeStruct(dims, dtype)

    stream = (micro, rows, width)
    mixed, gpre, conv, gwide, gtaps, gmid, gout = pl.pallas_call(
        functools.partial(kernel, list(scratch), n_dp),
        out_shape=[
            shape(stream, BF16),
            shape(stream, BF16),
            shape(stream, BF16),
            shape((4, 2, 256, 512), BF16),
            shape((2304, 512), BF16),
            shape(norm_mid.shape, F32),
            shape(norm_out.shape, F32),
        ],
        in_specs=[vmem, vmem, anywhere, anywhere, vmem, vmem, smem],
        out_specs=[anywhere] * 5 + [vmem] * 2,
        scratch_shapes=list(scratch.values()),
        compiler_params=pltpu.CompilerParams(
            collective_id=0, has_side_effects=True, vmem_limit_bytes=62 * 2**20
        ),
        name="layers",
    )(block_input, cotangent, weight_wide, weight_taps.reshape(9, 256, 512), norm_mid, norm_out, group_counts)
    grad_input = gpre.astype(F32) + conv.astype(F32)
    return (
        mixed,
        grad_input,
        gwide.astype(F32).reshape(weight_wide.shape),
        gtaps.astype(F32).reshape(weight_taps.shape),
        gmid,
        gout,
    )


def solution(mesh):
    split = P(None, "dp", "pipe")
    section = P("pipe", None, None)
    return jax.shard_map(
        local,
        mesh=mesh,
        in_specs=(split, split, section, section, section, section, P()),
        out_specs=(split, split, section, section, section, section),
        check_vma=False,
    )
```

```python
import functools
from types import SimpleNamespace

import jax
import jax.numpy as jnp
from jax import lax
from jax.experimental import pallas as pl
from jax.experimental.pallas import tpu as pltpu
from jax.sharding import PartitionSpec as P

MESH = pl.DeviceIdType.MESH
F32 = jnp.float32
BF16 = jnp.bfloat16
EPS = 1e-05
LANES = 128
N_PIPE = 4
NEAR = [k for k in range(9) if k != 4]


def slot_of(tap):
    return tap if tap < 4 else tap - 1


def dot_nn(a, b):
    return jnp.dot(a, b, preferred_element_type=F32)


def dot_nt(a, b):
    return lax.dot_general(a, b, (((1,), (1,)), ((), ())), preferred_element_type=F32)


def sigmoid(v):
    return jax.nn.sigmoid(v)


def sizes(n_dp):
    n_z = n_dp // 2
    n_own = min(n_z, 16)
    return n_z, n_own


def gradient_items(n_dp):
    line = n_dp // 2 == 4
    listed = []
    for kind, index, parts in (
        ("w", 3, [256]),
        ("k", 1, [576] * 4),
        ("w", 2, [256]),
        ("w", 1, [256]),
        ("k", 0, [288, 576, 576, 576, 288]),
        ("w", 0, [64] * 4),
    ):
        start = 0
        for part, rows in enumerate(parts if line else [sum(parts)]):
            listed.append(
                SimpleNamespace(
                    kind=kind, t=index, r0=start, nr=rows, i=len(listed), part=part
                )
            )
            start += rows
    return listed


def scratch_list(n_dp, rows):
    n_z, n_own = sizes(n_dp)
    items = len(gradient_items(n_dp))
    line = n_z == 4
    dma = pltpu.SemaphoreType.DMA

    def half(*shape):
        return pltpu.VMEM(shape, BF16)

    def full(*shape):
        return pltpu.VMEM(shape, F32)

    return dict(
        wt=half(4, 512, 512),
        k2=half(2, 18, 256, 128),
        gm=full(4, 2, 128),
        go=full(4, 2, 2, 512),
        msk=full(2, rows, 128),
        pm=half(2, 8, rows, rows),
        part=half(2, 2, 4, rows, 128),
        rsr=half(6, 2, 3, rows, 128),
        ag=half(6, 2, 4, rows, 128),
        stm=full(8, 2, n_dp, 2, 128),
        stw=full(4, 2, n_dp, 2, 512),
        midv=full(4, 2, rows, 128),
        dzm=full(2, rows, 128),
        inv_mid=full(4, 2, 1, 128),
        inv_wide=full(2, 2, 1, 512),
        widv=full(2, 2, rows, 512),
        pre0=full(2, rows, 512),
        s1=half(2, rows, 512),
        mix=half(2, rows, 512),
        gp=half(2, 2, rows, 512),
        cv=half(2, rows, 512),
        gt=half(2, rows, 512),
        gb=half(2, rows, 1152),
        yb=half(8, rows, 128),
        tb=half(512, 2 * rows),
        dw=half(4, 2, 256, 512),
        prw=half(4, 256, 512),
        zsw=half(4, 256, 512),
        fzw=half(4, 256, 512),
        ow=half(4, 2, 256, 512),
        dk=half(2, 4608, 128),
        prk=half(2, 2304, 128),
        zsk=half(2, 2304, 128),
        fzk=half(2, 2304, 128),
        ok=half(2304, 512),
        zow=half(4, 256, 512) if line else half(4, n_z - 1, 256 // n_own, 512),
        ziw=half(4, 128, 512),
        zok=half(2, 2304, 128) if line else half(2, n_z - 1, 2304 // n_own, 128),
        zik=half(2, 1152, 128),
        gsm=full(4, 4, 2, 128),
        gsw=full(2, 4, 2, 512),
        cnt=pltpu.SMEM((2, n_dp), F32),
        counts=pltpu.SMEM((2, 4, n_dp), jnp.int32),
        f_s=dma((2,)),
        f_r=dma((2, 4)),
        z_r=dma((2, 4)),
        b_s=dma((2, 4)),
        b_r=dma((2, 4)),
        n_s=dma((2,)),
        n_r=dma((2,)),
        loc=dma((4,)),
        ex_s=dma((2, 2)),
        ex_r=dma((2, 2)),
        st_s=dma((2, 2)),
        st_r=dma((2, 2)),
        pw_s=dma((6,)),
        pw_r=dma((6,)),
        it_s=dma((items,)),
        one_r=dma((items,)),
        mid_r=dma((items,)),
        inn_r=dma((items,)),
        to_s=dma((items,)),
        to_r=dma((2, 5)),
        sib_s=dma((2, 5)),
        sib_r=dma((2, 5)),
        g_s=dma((2,)),
        g_r=dma((2,)),
        out=dma((7,)),
    )


def kernel(names, n, *refs):
    (x_ref, cot_ref, wide_ref, taps_ref, nmid_ref, nout_ref, counts_hbm) = refs[:7]
    (mixed_ref, gpre_ref, conv_ref, gwide_ref, gtaps_ref, gmid_ref, gout_ref) = refs[7:14]
    sc = SimpleNamespace(**dict(zip(names, refs[14:])))
    counts_ref = sc.counts
    rows = x_ref.shape[1]
    n_z, n_own = sizes(n)
    p = lax.axis_index("pipe")
    d = lax.axis_index("dp")
    z = lax.div(d, 2)
    c = lax.rem(d, 2)
    parity = lax.rem(p, 2)
    sibling = (p, 2 * z + 1 - c)
    z_odd = lax.rem(z, 2)
    z_pair = (p, 2 * (z + 1 - 2 * z_odd) + c)
    quarter = 2 * z_odd + c
    quarter_z = 2 * (1 - z_odd) + c
    finish = []

    def pipe_at(off):
        return lax.rem(p + N_PIPE + (2 * parity - 1) * off, N_PIPE)

    def remote(src, dst, ss, rs, dev):
        return pltpu.make_async_remote_copy(
            src_ref=src, dst_ref=dst, send_sem=ss, recv_sem=rs, device_id=dev, device_id_type=MESH
        )

    def each(count, first, body):
        if count - first <= 8:
            for k in range(first, count):
                body(k)
        else:

            def step(k, carry):
                body(k)
                return carry

            lax.fori_loop(first, count, step, 0)

    def bytes_wait(view, sem):
        pltpu.make_async_copy(view, view, sem).wait()

    barrier = pltpu.get_barrier_semaphore()
    for off in range(1, N_PIPE):
        pl.semaphore_signal(barrier, inc=1, device_id=(pipe_at(off), d), device_id_type=MESH)

    def greet(k):
        pl.semaphore_signal(
            barrier, inc=1, device_id=(p, lax.rem(d + k, n)), device_id_type=MESH
        )

    each(n, 1, greet)

    def columns_of(q):
        return pl.ds(pl.multiple_of(128 * q, 128), 128)

    own_w = pltpu.make_async_copy(
        wide_ref.at[0, pl.ds(pl.multiple_of(512 * p, 512), 512), :], sc.wt.at[p], sc.loc.at[0]
    )
    own_k = pltpu.make_async_copy(
        taps_ref.at[:, :, columns_of(p)],
        sc.k2.at[lax.div(p, 2), pl.ds(9 * parity, 9)],
        sc.loc.at[1],
    )
    own_c = pltpu.make_async_copy(counts_hbm, counts_ref, sc.loc.at[2])
    own_c.start()
    own_w.start()
    own_k.start()
    own_n = pltpu.make_async_copy(
        nmid_ref.at[0, :, columns_of(p)], sc.gm.at[p], sc.loc.at[3]
    )
    own_n.start()
    for e in range(2):
        sc.go[p, e] = nout_ref[0, :, 512 * e : 512 * e + 512]

    own_c.wait()

    def used_rows(m, j):
        return (
            49 * counts_ref[m, 0, j]
            + 36 * counts_ref[m, 1, j]
            + 25 * counts_ref[m, 2, j]
            + 4 * counts_ref[m, 3, j]
        )

    totals = []
    for m in range(2):

        def count_up(j, acc, m=m):
            used = used_rows(m, j)
            sc.cnt[m, j] = used.astype(F32)
            return acc + used

        totals.append(lax.fori_loop(0, n, count_up, jnp.int32(0)).astype(F32))

    pl.semaphore_wait(barrier, N_PIPE - 1 + n - 1)

    def held(kind, s, part):
        if kind == 0:
            return sc.wt.at[s, pl.ds(pl.multiple_of(128 * part, 128), 128)]
        layer, odd = (s // 2, s % 2) if isinstance(s, int) else (lax.div(s, 2), lax.rem(s, 2))
        return sc.k2.at[
            layer, pl.ds(9 * odd, 9), pl.ds(pl.multiple_of(64 * part, 64), 64)
        ]

    def fetch(kind, off):
        q = pipe_at(off)
        if kind == 0:
            src = wide_ref.at[0, pl.ds(pl.multiple_of(512 * q + 128 * quarter, 128), 128), :]
        else:
            src = taps_ref.at[:, pl.ds(pl.multiple_of(64 * quarter, 64), 64), columns_of(q)]
        return remote(
            src, held(kind, p, quarter), sc.f_s.at[kind], sc.f_r.at[kind, p], (q, d)
        )

    def send_norm(off):
        q = pipe_at(off)
        listed = [
            remote(
                nmid_ref.at[0, :, columns_of(q)],
                sc.gm.at[p],
                sc.n_s.at[0],
                sc.n_r.at[0],
                (q, d),
            )
        ]
        for e in range(2):
            listed.append(
                remote(
                    nout_ref.at[0, :, pl.ds(512 * e, 512)],
                    sc.go.at[p, e],
                    sc.n_s.at[1],
                    sc.n_r.at[1],
                    (q, d),
                )
            )
        return listed

    def norm_wait(sems):
        bytes_wait(sc.gm.at[pl.ds(0, 3)], sems.at[0])
        bytes_wait(sc.go.at[pl.ds(0, 3)], sems.at[1])

    def pass_z(kind, s):
        view = held(kind, s, quarter)
        return remote(view, view, sc.b_s.at[kind, s], sc.z_r.at[kind, s], z_pair)

    def pass_sibling(kind, s, e):
        view = held(kind, s, quarter if e == 0 else quarter_z)
        return remote(view, view, sc.b_s.at[kind, s], sc.b_r.at[kind, s], sibling)

    def spread_first(kind, s):
        @pl.when(p != s)
        def _():
            view = held(kind, s, quarter)
            bytes_wait(view, sc.f_r.at[kind, s])
            pass_z(kind, s).start()
            pass_sibling(kind, s, 0).start()

    def spread_second(kind, s):
        @pl.when(p != s)
        def _():
            pass_z(kind, s).wait_recv()
            pass_sibling(kind, s, 1).start()

    def quarters(kind, s, count):
        if kind == 0:
            return sc.wt.at[s, pl.ds(0, 128 * count)]
        return sc.k2.at[s // 2, pl.ds(9 * (s % 2), 9), pl.ds(0, 64 * count)]

    def ready(kind, s):
        @pl.when(p != s)
        def _():
            bytes_wait(quarters(kind, s, 2), sc.b_r.at[kind, s])

        @pl.when(p == s)
        def _():
            (own_w if kind == 0 else own_k).wait()

    def finish_weights():
        for kind in range(2):
            bytes_wait(quarters(kind, 0, 3), sc.f_s.at[kind])
            for s in range(4):

                @pl.when(p != s)
                def _(kind=kind, s=s):
                    bytes_wait(quarters(kind, s, 3), sc.b_s.at[kind, s])

    finish.append(finish_weights)

    for even in range(2):

        @pl.when(parity == even)
        def _(even=even):
            for kind in (even, 1 - even):
                for off in range(1, 4):
                    fetch(kind, off).start()
                if kind == even:
                    for off in range(1, 4):
                        for copy in send_norm(off):
                            copy.start()

    def finish_norm():
        norm_wait(sc.n_s)

    finish.append(finish_norm)

    row_id = lax.broadcasted_iota(jnp.int32, (rows, LANES), 0).astype(F32)
    lane_id = lax.broadcasted_iota(jnp.int32, (rows, LANES), 1).astype(F32)

    def build(m):
        ends = []
        total = jnp.int32(0)
        for g, area in enumerate((49, 36, 25, 4)):
            total = total + area * counts_ref[m, g, d]
            ends.append(total.astype(F32))
        sc.msk[m] = jnp.where(row_id < ends[3], 1.0, 0.0)

        def pick(values):
            out = values[4]
            for g in (3, 2, 1, 0):
                out = jnp.where(row_id < ends[g], values[g], out)
            return out

        zero = jnp.zeros((rows, LANES), F32)
        side = pick([zero + 7.0, zero + 6.0, zero + 5.0, zero + 2.0, zero + 1.0])
        begin = pick([zero, zero + ends[0], zero + ends[1], zero + ends[2], row_id])
        one_over = pick(
            [zero + 1.0 / 7.0, zero + 1.0 / 6.0, zero + 1.0 / 5.0, zero + 0.5, zero + 1.0]
        )
        within = row_id - begin
        within = within - side * side * jnp.floor((within + 0.5) * one_over * one_over)
        map_row = jnp.floor((within + 0.5) * one_over)
        map_col = within - side * map_row
        for k in NEAR:
            du, dv = k // 3 - 1, k % 3 - 1
            usable = row_id < ends[3]
            if du == -1:
                usable = usable & (map_row > 0.5)
            if du == 1:
                usable = usable & (map_row < side - 1.5)
            if dv == -1:
                usable = usable & (map_col > 0.5)
            if dv == 1:
                usable = usable & (map_col < side - 1.5)
            target = jnp.where(usable, row_id + du * side + dv, -1000.0)
            for t in range(rows // LANES):
                hit = jnp.where(target == lane_id + float(LANES * t), 1.0, 0.0)
                sc.pm[m, slot_of(k), :, LANES * t : LANES * (t + 1)] = hit.astype(BF16)

    for m in range(2):
        build(m)


    exchange_order = [
        ("rs", 0), ("ag", 0), ("ag", 2), ("rs", 1), ("ag", 1), ("ag", 3),
        ("rs", 3), ("rs", 5), ("ag", 5), ("rs", 2), ("rs", 4), ("ag", 4),
    ]

    def three(kind, i, m):
        return sc.rsr.at[i, m] if kind == "rs" else sc.ag.at[i, m, pl.ds(0, 3)]

    def exchange_wait(sems, kind, i, m):
        turn = exchange_order.index((kind, i))
        bytes_wait(three(kind, i, m), sems.at[turn % 2, m])

    def exchange_open(kind, i, m):
        turn = exchange_order.index((kind, i))
        if turn >= 2:
            exchange_wait(sc.ex_s, *exchange_order[turn - 2], m)
        return sc.ex_s.at[turn % 2, m], sc.ex_r.at[turn % 2, m]

    def rs_sum(rid, m, par):
        exchange_wait(sc.ex_r, "rs", rid, m)
        total = sc.part[par, m, p].astype(F32)
        for k in range(3):
            total = total + sc.rsr[rid, m, k].astype(F32)
        return total

    def ag_start(aid, m, value):
        ss, rs = exchange_open("ag", aid, m)
        sc.ag[aid, m, p] = value
        own = sc.ag.at[aid, m, p]
        for off in range(1, 4):
            remote(own, own, ss, rs, (pipe_at(off), d)).start()

    def ag_wait(aid, m):
        exchange_wait(sc.ex_r, "ag", aid, m)

    def ag_value(aid, m):
        return jnp.concatenate([sc.ag[aid, m, q] for q in range(4)], axis=1)

    def finish_exchanges():
        for kind, i in exchange_order[-2:]:
            for m in range(2):
                exchange_wait(sc.ex_s, kind, i, m)

    finish.append(finish_exchanges)

    sum_order = [
        (False, 0), (False, 1), (True, 0), (False, 2), (False, 3), (True, 1),
        (True, 3), (False, 7), (False, 6), (True, 2), (False, 5), (False, 4),
    ]

    def st_buffer(wide, i, m):
        return (sc.stw if wide else sc.stm).at[i, m]

    def st_bytes(sems, wide, i, m):
        turn = sum_order.index((wide, i))
        bytes_wait(st_buffer(wide, i, m).at[pl.ds(0, n - 1)], sems.at[turn % 2, m])

    def st_start(wide, i, m):
        turn = sum_order.index((wide, i))
        if turn >= 2:
            st_bytes(sc.st_s, *sum_order[turn - 2], m)
        own = st_buffer(wide, i, m).at[d]
        ss, rs = sc.st_s.at[turn % 2, m], sc.st_r.at[turn % 2, m]

        def go(k):
            remote(own, own, ss, rs, (p, lax.rem(d + k, n))).start()

        each(n, 1, go)

    def st_wait(wide, i, m):
        st_bytes(sc.st_r, wide, i, m)

    def finish_st():
        for wide, i in sum_order[-2:]:
            for m in range(2):
                st_bytes(sc.st_s, wide, i, m)

    finish.append(finish_st)

    def over_devices(body, init):
        if n <= 8:
            for j in range(n):
                init = body(j, init)
            return init
        return lax.fori_loop(0, n, body, init)

    def combine(wide, i, m):
        st_wait(wide, i, m)
        ref = sc.stw if wide else sc.stm
        blank = jnp.zeros((1, ref.shape[-1]), F32)
        mean = over_devices(
            lambda j, acc: acc + sc.cnt[m, j] * ref[i, m, j, 0:1, :], blank
        )
        mean = mean / totals[m]

        def spread(j, acc):
            gap = ref[i, m, j, 0:1, :] - mean
            return acc + ref[i, m, j, 1:2, :] + sc.cnt[m, j] * (gap * gap)

        var = over_devices(spread, blank) / totals[m]
        return mean, lax.rsqrt(var + EPS)

    def back_sums(wide, i, m):
        st_wait(wide, i, m)
        ref = sc.stw if wide else sc.stm
        return over_devices(
            lambda j, acc: acc + ref[i, m, j], jnp.zeros((2, ref.shape[-1]), F32)
        )

    def local_moments(v, m):
        mask = sc.msk[m]
        own = jnp.maximum(sc.cnt[m, d], 1.0)
        mean = jnp.sum(v * mask, 0, keepdims=True) / own
        gap = (v - mean) * mask
        return jnp.concatenate([mean, jnp.sum(gap * gap, 0, keepdims=True)], 0)

    def local_sums(dz, vhat):
        return jnp.concatenate(
            [jnp.sum(dz * vhat, 0, keepdims=True), jnp.sum(dz, 0, keepdims=True)], 0
        )

    def lanes(j):
        return slice(LANES * j, LANES * (j + 1))

    def stream(layer, m):
        return x_ref[m] if layer == 0 else sc.s1[m]

    def stream_part(layer, m, j):
        return (x_ref[m, :, lanes(j)] if layer == 0 else sc.s1[m, :, lanes(j)]).astype(F32)

    rs_par = {0: 0, 1: 1, 3: 0, 5: 1, 2: 0, 4: 1}

    def rs_send(rid, m, values):
        par = rs_par[rid]
        ss, rs = exchange_open("rs", rid, m)
        for j, value in enumerate(values):
            half = value.astype(BF16)
            sc.part[par, m, 2 * j] = half[:, :LANES]
            sc.part[par, m, 2 * j + 1] = half[:, LANES:]
        for off in range(1, 4):
            q = pipe_at(off)
            remote(sc.part.at[par, m, q], sc.rsr.at[rid, m, off - 1], ss, rs, (q, d)).start()

    def first_part(layer, m):
        s = stream(layer, m)
        rs_send(
            layer,
            m,
            [dot_nn(s, sc.wt[2 * layer, :, 256 * j : 256 * j + 256]) for j in range(2)],
        )

    def mid_moments(i, m, v):
        sc.midv[i, m] = v
        sc.stm[i, m, d] = local_moments(v, m)
        st_start(False, i, m)

    def first_norm(layer, m):
        mid_moments(2 * layer, m, rs_sum(layer, m, rs_par[layer]))

    def mid_hidden(i, m):
        mean, inv = combine(False, i, m)
        sc.inv_mid[i, m] = inv
        vhat = (sc.midv[i, m] - mean) * inv
        sc.midv[i, m] = vhat
        u = sc.gm[i, 0:1, :] * vhat + sc.gm[i, 1:2, :]
        return (sc.msk[m] * (u * sigmoid(u))).astype(BF16)

    def hidden_one(layer, m):
        ag_start(layer, m, mid_hidden(2 * layer, m))

    def taps_of(layer, taps):
        return jnp.concatenate(
            [
                jnp.concatenate([sc.k2[layer, 2 * k], sc.k2[layer, 2 * k + 1]], axis=0)
                for k in taps
            ],
            axis=1,
        )

    def second_part(layer, m):
        ag_wait(layer, m)
        h = ag_value(layer, m)
        centre = None
        for j in range(5):
            width = 256 if j < 4 else 128
            y = dot_nn(h, taps_of(layer, [2 * j + e for e in range(width // LANES)]))
            for e in range(width // LANES):
                tap = 2 * j + e
                if tap == 4:
                    centre = y[:, lanes(e)]
                    sc.midv[2 * layer + 1, m] = centre
                else:
                    sc.yb[slot_of(tap)] = y[:, lanes(e)].astype(BF16)
        total = sc.midv[2 * layer + 1, m]
        for k in range(8):
            total = total + dot_nn(sc.pm[m, k], sc.yb[k])
        mid_moments(2 * layer + 1, m, total)

    def hidden_two(layer, m):
        ag_start(2 + layer, m, mid_hidden(2 * layer + 1, m))

    def third_part(layer, m):
        ag_wait(2 + layer, m)
        h = ag_value(2 + layer, m)
        for j in range(2):
            sc.widv[layer, m, :, 256 * j : 256 * j + 256] = dot_nt(
                h, sc.wt[2 * layer + 1, 256 * j : 256 * j + 256, :]
            )
        for j in range(4):
            sc.stw[layer, m, d, :, lanes(j)] = local_moments(sc.widv[layer, m, :, lanes(j)], m)
        st_start(True, layer, m)

    def out_gain(layer, j):
        both = sc.go[2 * layer + lax.div(p, 2), lax.rem(p, 2)]
        return both[0:1, lanes(j)], both[1:2, lanes(j)]

    def pre_values(layer, m):
        mean, inv = combine(True, layer, m)
        sc.inv_wide[layer, m] = inv
        mask = sc.msk[m]
        for j in range(4):
            gain, bias = out_gain(layer, j)
            vhat = (sc.widv[layer, m, :, lanes(j)] - mean[:, lanes(j)]) * inv[:, lanes(j)]
            sc.widv[layer, m, :, lanes(j)] = vhat
            pre = gain * vhat + bias + stream_part(layer, m, j)
            sig = sigmoid(pre)
            out = (mask * (pre * sig)).astype(BF16)
            if layer == 0:
                sc.pre0[m, :, lanes(j)] = pre
                sc.s1[m, :, lanes(j)] = out
            else:
                sc.mix[m, :, lanes(j)] = out
                slope = sig * (1.0 + pre * (1.0 - sig))
                grad = (cot_ref[m, :, lanes(j)].astype(F32) * mask * slope).astype(BF16)
                sc.gp[1, m, :, lanes(j)] = grad
                sc.stw[3, m, d, :, lanes(j)] = local_sums(grad.astype(F32), vhat)
        if layer == 1:
            st_start(True, 3, m)

    def put_out(k, src, dst):
        copy = pltpu.make_async_copy(src, dst, sc.out.at[k])
        copy.start()
        return copy

    def grad_out_norm(layer, m):
        sums = back_sums(True, 2 + layer, m)
        if m == 0:
            sc.gsw[layer, p] = sums
        else:
            sc.gsw[layer, p] = sc.gsw[layer, p] + sums
        mask = sc.msk[m]
        inv = sc.inv_wide[layer, m]
        for j in range(4):
            gain, _ = out_gain(layer, j)
            dz = sc.gp[layer, m, :, lanes(j)].astype(F32)
            vhat = sc.widv[layer, m, :, lanes(j)]
            s1 = sums[0:1, lanes(j)] / totals[m]
            s0 = sums[1:2, lanes(j)] / totals[m]
            dv = mask * (gain * inv[:, lanes(j)]) * (dz - s0 - vhat * s1)
            sc.gt[m, :, lanes(j)] = dv.astype(BF16)
        g = sc.gt[m]
        rs_send(
            2 + layer,
            m,
            [dot_nn(g, sc.wt[2 * layer + 1, :, 256 * j : 256 * j + 256]) for j in range(2)],
        )

    def mid_grad(i, m, upstream):
        vhat = sc.midv[i, m]
        u = sc.gm[i, 0:1, :] * vhat + sc.gm[i, 1:2, :]
        sig = sigmoid(u)
        dz = upstream * sc.msk[m] * (sig * (1.0 + u * (1.0 - sig)))
        sc.dzm[m] = dz
        sc.stm[4 + i, m, d] = local_sums(dz, vhat)
        st_start(False, 4 + i, m)

    def mid_back(i, m):
        sums = back_sums(False, 4 + i, m)
        if m == 0:
            sc.gsm[i, p] = sums
        else:
            sc.gsm[i, p] = sc.gsm[i, p] + sums
        s1 = sums[0:1, :] / totals[m]
        s0 = sums[1:2, :] / totals[m]
        scale = sc.gm[i, 0:1, :] * sc.inv_mid[i, m]
        return (sc.msk[m] * scale * (sc.dzm[m] - s0 - sc.midv[i, m] * s1)).astype(BF16)

    def grad_two(layer, m):
        mid_grad(2 * layer + 1, m, rs_sum(2 + layer, m, rs_par[2 + layer]))

    def grad_second(layer, m):
        gs = mid_back(2 * layer + 1, m)
        for k in range(9):
            if k == 4:
                sc.gb[m, :, lanes(k)] = gs
            else:
                sc.gb[m, :, lanes(k)] = dot_nn(sc.pm[m, slot_of(8 - k)], gs).astype(BF16)
        g = sc.gb[m]
        rs_send(
            4 + layer,
            m,
            [
                dot_nt(
                    g, jnp.concatenate([sc.k2[layer, 2 * k + j] for k in range(9)], axis=1)
                )
                for j in range(2)
            ],
        )

    def grad_one(layer, m):
        mid_grad(2 * layer, m, rs_sum(4 + layer, m, rs_par[4 + layer]))

    def grad_first(layer, m):
        ag_start(4 + layer, m, mid_back(2 * layer, m))

    def conv_grad(layer, m):
        ag_wait(4 + layer, m)
        g = ag_value(4 + layer, m)
        mask = sc.msk[m]
        for j in range(2):
            r = dot_nt(g, sc.wt[2 * layer, 256 * j : 256 * j + 256, :]).astype(BF16)
            if layer == 0:
                sc.cv[m, :, 256 * j : 256 * j + 256] = r
                continue
            for e in range(2):
                i = 2 * j + e
                pre = sc.pre0[m, :, lanes(i)]
                sig = sigmoid(pre)
                slope = sig * (1.0 + pre * (1.0 - sig))
                up = sc.gp[1, m, :, lanes(i)].astype(F32) + r[:, lanes(e)].astype(F32)
                grad = (up * mask * slope).astype(BF16)
                sc.gp[0, m, :, lanes(i)] = grad
                sc.stw[2, m, d, :, lanes(i)] = local_sums(
                    grad.astype(F32), sc.widv[0, m, :, lanes(i)]
                )
        if layer == 1:
            st_start(True, 2, m)

    def turned(blocks):
        for m, block in enumerate(blocks):
            sc.tb[:, rows * m : rows * (m + 1)] = block.T

    def both(get):
        return jnp.concatenate([get(0), get(1)], axis=0)

    def wide_grad(s, left, right):
        turned([left(0), left(1)])
        for j in range(2):
            cols = slice(256 * j, 256 * j + 256)
            rhs = both(lambda m: right(m)[:, cols])
            for h in range(2):
                r = dot_nn(sc.tb[256 * h : 256 * h + 256, :], rhs)
                sc.dw[s, h, :, cols] = r.astype(BF16)
        pair_copy("w", s).start()

    def taps_grad(layer):
        turned([ag_value(layer, 0), ag_value(layer, 1)])
        for j in range(5):
            width = 256 if j < 4 else 128
            rhs = both(lambda m: sc.gb[m, :, 256 * j : 256 * j + width])
            r = dot_nn(sc.tb[...], rhs).astype(BF16)
            for e in range(width // LANES):
                tap = 2 * j + e
                sc.dk[layer, 512 * tap : 512 * tap + 512, :] = r[:, lanes(e)]
        pair_copy("k", layer).start()

    def half_rows(which):
        return pl.ds(pl.multiple_of(2304 * which, 2304), 2304)

    def pair_copy(kind, t):
        if kind == "w":
            src, dst, i = sc.dw.at[t, 1 - c], sc.prw.at[t], t
        else:
            src, dst, i = sc.dk.at[t, half_rows(1 - c)], sc.prk.at[t], 4 + t
        return remote(src, dst, sc.pw_s.at[i], sc.pw_r.at[i], sibling)

    def pair_sum(kind, t):
        pair_copy(kind, t).wait_recv()
        if kind == "w":
            sc.zsw[t] = (sc.dw[t, c].astype(F32) + sc.prw[t].astype(F32)).astype(BF16)
            return
        for i in range(4):
            part = slice(576 * i, 576 * i + 576)
            mine = pl.ds(pl.multiple_of(2304 * c + 576 * i, 576), 576)
            sc.zsk[t, part] = (
                sc.dk[t, mine].astype(F32) + sc.prk[t, part].astype(F32)
            ).astype(BF16)

    items = gradient_items(n)
    line = n_z == 4
    inner = (z == 1) | (z == 2)

    def tile(it, name):
        return getattr(sc, name + it.kind)

    def some(it, name, start, count):
        return tile(it, name).at[it.t, pl.ds(start, count)]

    def part_rows(it, which):
        half = it.nr // 2
        return pl.ds(pl.multiple_of(it.r0 + half * which, half), half)

    def up_copy(it):
        rows_of = pl.ds(it.r0, it.nr)
        return remote(
            tile(it, "zs").at[it.t, rows_of],
            tile(it, "zo").at[it.t, rows_of],
            sc.it_s.at[it.i],
            sc.one_r.at[it.i],
            (p, 2 * (1 + lax.div(z, 3)) + c),
        )

    def mid_copy(it):
        return remote(
            tile(it, "zs").at[it.t, part_rows(it, 2 - z)],
            tile(it, "zi").at[it.t, pl.ds(it.r0 // 2, it.nr // 2)],
            sc.it_s.at[it.i],
            sc.mid_r.at[it.i],
            (p, 2 * (3 - z) + c),
        )

    def inn_copy(it):
        view = tile(it, "fz").at[it.t, part_rows(it, z - 1)]
        return remote(
            view, view, sc.it_s.at[it.i], sc.inn_r.at[it.i], (p, 2 * (3 - z) + c)
        )

    def down_copy(it, e):
        view = tile(it, "fz").at[it.t, part_rows(it, z - 1 if e == 0 else 2 - z)]
        return remote(
            view, view, sc.it_s.at[it.i], sc.one_r.at[it.i], (p, 2 * (3 * (z - 1)) + c)
        )

    def direct_rows(it, j):
        count = it.nr // n_own
        return pl.ds(pl.multiple_of(it.r0 + count * j, count), count)

    def owner(index, body):
        if n_own == n_z:
            body()
        else:
            pl.when(index < n_own)(body)

    def scatter_copy(it, k):
        j = lax.rem(z + k, n_z)
        return j, remote(
            tile(it, "zs").at[it.t, direct_rows(it, lax.rem(j, n_own))],
            tile(it, "zo").at[it.t, k - 1],
            sc.it_s.at[it.i],
            sc.one_r.at[it.i],
            (p, 2 * j + c),
        )

    def gather_copy(it, k):
        j = lax.rem(z + k, n_z)
        view = tile(it, "fz").at[it.t, direct_rows(it, lax.rem(z, n_own))]
        return remote(view, view, sc.to_s.at[it.i], sc.mid_r.at[it.i], (p, 2 * j + c))

    def add_rows(target, first, second):
        target[...] = (first[...].astype(F32) + second[...].astype(F32)).astype(BF16)

    def step_up(it):
        if line:

            @pl.when((z == 0) | (z == 3))
            def _():
                up_copy(it).start()

        else:

            def go(k):
                j, copy = scatter_copy(it, k)
                owner(j, lambda: copy.start())

            each(n_z, 1, go)

    def step_mid(it):
        if not line:
            return

        @pl.when(inner)
        def _():
            up_copy(it).wait_recv()
            mine = some(it, "zs", it.r0, it.nr)
            add_rows(mine, mine, some(it, "zo", it.r0, it.nr))
            mid_copy(it).start()

    def step_down(it):
        if line:

            @pl.when(inner)
            def _():
                mid_copy(it).wait_recv()
                keep = part_rows(it, z - 1)
                add_rows(
                    tile(it, "fz").at[it.t, keep],
                    tile(it, "zs").at[it.t, keep],
                    some(it, "zi", it.r0 // 2, it.nr // 2),
                )
                inn_copy(it).start()
                down_copy(it, 0).start()

            return

        def go():
            bytes_wait(tile(it, "zo").at[it.t], sc.one_r.at[it.i])
            mine = direct_rows(it, z)
            total = tile(it, "zs")[it.t, mine].astype(F32)
            total = lax.fori_loop(
                0, n_z - 1, lambda k, acc: acc + tile(it, "zo")[it.t, k].astype(F32), total
            )
            tile(it, "fz")[it.t, mine] = total.astype(BF16)
            each(n_z, 1, lambda k: gather_copy(it, k).start())

        owner(z, go)

    def step_last(it):
        if not line:
            return

        @pl.when(inner)
        def _():
            inn_copy(it).wait_recv()
            down_copy(it, 1).start()

    def owner_of(it):
        return it.t if it.kind == "w" else 2 * it.t + c

    def landing(it, q, core):
        if it.kind == "w":
            return sc.ow.at[q, core, pl.ds(it.r0, it.nr)]
        lane = pl.ds(128 * q, 128) if isinstance(q, int) else columns_of(q)
        return sc.ok.at[pl.ds(it.r0, it.nr), lane]

    def to_sem(it, sems):
        return sems.at[0 if it.kind == "w" else 1, it.part]

    def to_copy(it):
        return remote(
            some(it, "fz", it.r0, it.nr),
            landing(it, p, c),
            sc.to_s.at[it.i],
            to_sem(it, sc.to_r),
            (owner_of(it), d),
        )

    def step_out(it):
        if line:

            @pl.when((z == 0) | (z == 3))
            def _():
                bytes_wait(some(it, "fz", it.r0, it.nr), sc.one_r.at[it.i])

        else:
            count = it.nr // n_own
            if n_own == n_z:
                bytes_wait(some(it, "fz", it.r0, count * (n_own - 1)), sc.mid_r.at[it.i])
            else:

                @pl.when(z < n_own)
                def _():
                    bytes_wait(some(it, "fz", it.r0, count * (n_own - 1)), sc.mid_r.at[it.i])

                @pl.when(z >= n_own)
                def _():
                    bytes_wait(some(it, "fz", it.r0, count * n_own), sc.mid_r.at[it.i])

        @pl.when(p != owner_of(it))
        def _():
            to_copy(it).start()

        def place(q):
            landing(it, q, c)[...] = some(it, "fz", it.r0, it.nr)[...]

        if it.kind == "w":
            pl.when(p == it.t)(lambda: place(it.t))
        else:
            for core in range(2):
                pl.when((p == 2 * it.t + core) & (c == core))(
                    functools.partial(place, 2 * it.t + core)
                )

    def sibling_copy(it, q):
        view = landing(it, q, c)
        return remote(
            view, view, to_sem(it, sc.sib_s), to_sem(it, sc.sib_r), sibling
        )

    def slices(it, count):
        if it.kind == "w":
            return sc.ow.at[pl.ds(0, count), 0, pl.ds(it.r0, it.nr)]
        return sc.ok.at[pl.ds(it.r0, it.nr), pl.ds(0, 128 * count)]

    def step_sibling(it):
        def go():
            bytes_wait(slices(it, 3), to_sem(it, sc.to_r))
            for q in range(4):
                sibling_copy(it, q).start()

        pl.when(p == owner_of(it))(go)

    def step_done(it):
        def go():
            bytes_wait(slices(it, 4), to_sem(it, sc.sib_r))

        pl.when(p == (it.t if it.kind == "w" else 2 * it.t + 1 - c))(go)

    def twice(it):
        if it.kind == "w":
            return sc.dw.at[it.t, :, pl.ds(0, it.nr)]
        return sc.dk.at[it.t, pl.ds(0, 2 * it.nr)]

    def finish_grads():
        for kind, t in [("w", s) for s in range(4)] + [("k", layer) for layer in range(2)]:
            pair_copy(kind, t).wait_send()
        for it in items:
            if line:

                @pl.when(inner)
                def _(it=it):
                    bytes_wait(twice(it), sc.it_s.at[it.i])

                @pl.when((z == 0) | (z == 3))
                def _(it=it):
                    up_copy(it).wait_send()

            else:

                def sent(k, it=it):
                    j, copy = scatter_copy(it, k)
                    owner(j, lambda: copy.wait_send())

                each(n_z, 1, sent)
                owner(z, lambda: each(n_z, 1, lambda k: gather_copy(it, k).wait_send()))

            @pl.when(p != owner_of(it))
            def _(it=it):
                to_copy(it).wait_send()

            @pl.when(p == owner_of(it))
            def _(it=it):
                bytes_wait(slices(it, 4), to_sem(it, sc.sib_s))

    finish.append(finish_grads)

    def gain_copies(off):
        dev = (pipe_at(off), d)
        return [
            remote(sc.gsm.at[:, p], sc.gsm.at[:, p], sc.g_s.at[0], sc.g_r.at[0], dev),
            remote(sc.gsw.at[:, p], sc.gsw.at[:, p], sc.g_s.at[1], sc.g_r.at[1], dev),
        ]

    def gains_wait(sems):
        bytes_wait(sc.gsm.at[:, pl.ds(0, 3)], sems.at[0])
        bytes_wait(sc.gsw.at[:, pl.ds(0, 3)], sems.at[1])

    def gains_start():
        for off in range(1, 4):
            for copy in gain_copies(off):
                copy.start()

    def gains_done():
        gains_wait(sc.g_r)
        for q in range(4):
            gmid_ref[0, :, lanes(q)] = sc.gsm[p, q]
        layer = lax.div(p, 2)
        for e in range(2):
            gout_ref[0, :, 512 * e : 512 * e + 512] = sc.gsw[layer, 2 * parity + e]

    def finish_gains():
        gains_wait(sc.g_s)

    finish.append(finish_gains)

    def phase(body, layer, between=None):
        body(layer, 0)
        if between is not None:
            between()
        body(layer, 1)

    def of(kind, t):
        return [it for it in items if it.kind == kind and it.t == t]

    def one(step, kind, t, part):
        for it in of(kind, t)[part : part + 1]:
            step(it)

    def run(step, kind, t):
        for it in of(kind, t):
            step(it)

    wide, taps = 0, 1
    spread_first(wide, 0)
    spread_second(wide, 0)
    ready(wide, 0)
    phase(first_part, 0)
    own_n.wait()
    norm_wait(sc.n_r)
    spread_first(taps, 0)
    spread_first(taps, 1)
    phase(first_norm, 0)
    spread_second(taps, 0)
    spread_second(taps, 1)
    phase(hidden_one, 0)
    spread_first(wide, 1)
    spread_first(wide, 2)
    ready(taps, 0)
    ready(taps, 1)
    phase(second_part, 0)
    spread_second(wide, 1)
    spread_second(wide, 2)
    phase(hidden_two, 0)
    spread_first(taps, 2)
    spread_first(taps, 3)
    ready(wide, 1)
    phase(third_part, 0)
    spread_second(taps, 2)
    spread_second(taps, 3)
    ready(wide, 2)

    def turn(layer, m):
        pre_values(0, m)
        first_part(1, m)

    phase(turn, 0)
    spread_first(wide, 3)
    phase(first_norm, 1)
    spread_second(wide, 3)
    phase(hidden_one, 1)
    ready(taps, 2)
    ready(taps, 3)
    phase(second_part, 1)
    phase(hidden_two, 1)
    ready(wide, 3)
    phase(third_part, 1)
    phase(pre_values, 1)
    outs = [put_out(2, sc.mix.at[...], mixed_ref.at[...])]

    phase(grad_out_norm, 1)
    wide_grad(3, lambda m: sc.gt[m], lambda m: ag_value(3, m))
    phase(grad_two, 1)
    pair_sum("w", 3)
    run(step_up, "w", 3)
    phase(grad_second, 1)
    taps_grad(1)
    phase(grad_one, 1, lambda: run(step_mid, "w", 3))
    pair_sum("k", 1)
    run(step_up, "k", 1)
    run(step_down, "w", 3)
    phase(grad_first, 1)
    run(step_last, "w", 3)
    one(step_mid, "k", 1, 0)
    phase(conv_grad, 1, lambda: one(step_mid, "k", 1, 1))
    outs.append(put_out(3, sc.gp.at[0], gpre_ref.at[...]))
    wide_grad(2, lambda m: sc.s1[m], lambda m: ag_value(5, m))
    one(step_mid, "k", 1, 2)
    one(step_down, "k", 1, 0)
    one(step_down, "k", 1, 1)

    def early_zero():
        one(step_mid, "k", 1, 3)
        one(step_down, "k", 1, 2)
        pair_sum("w", 2)
        run(step_up, "w", 2)

    phase(grad_out_norm, 0, early_zero)
    wide_grad(1, lambda m: sc.gt[m], lambda m: ag_value(2, m))
    one(step_last, "k", 1, 0)
    one(step_last, "k", 1, 1)
    def early_two():
        one(step_down, "k", 1, 3)
        run(step_mid, "w", 2)

    phase(grad_two, 0, early_two)
    pair_sum("w", 1)
    run(step_up, "w", 1)
    one(step_last, "k", 1, 2)
    one(step_last, "k", 1, 3)
    phase(grad_second, 0, lambda: run(step_down, "w", 2))
    taps_grad(0)

    def early_one():
        run(step_last, "w", 2)
        run(step_mid, "w", 1)
        pair_sum("k", 0)
        one(step_up, "k", 0, 0)

    phase(grad_one, 0, early_one)
    for part in range(1, 5):
        one(step_up, "k", 0, part)
    run(step_down, "w", 1)
    phase(grad_first, 0)
    gains_start()
    one(step_mid, "k", 0, 0)
    run(step_last, "w", 1)
    one(step_mid, "k", 0, 1)
    one(step_down, "k", 0, 0)
    conv_grad(0, 0)
    one(step_mid, "k", 0, 2)
    one(step_down, "k", 0, 1)
    one(step_last, "k", 0, 0)
    run(step_out, "k", 1)
    conv_grad(0, 1)
    wide_grad(0, lambda m: x_ref[m], lambda m: ag_value(4, m))
    one(step_mid, "k", 0, 3)
    one(step_down, "k", 0, 2)
    one(step_last, "k", 0, 1)
    one(step_out, "k", 0, 0)
    outs.append(put_out(4, sc.cv.at[...], conv_ref.at[...]))
    one(step_mid, "k", 0, 4)
    pair_sum("w", 0)
    run(step_up, "w", 0)
    one(step_down, "k", 0, 3)
    one(step_last, "k", 0, 2)
    one(step_out, "k", 0, 1)
    run(step_out, "w", 3)
    one(step_down, "k", 0, 4)
    one(step_mid, "w", 0, 0)
    one(step_last, "k", 0, 3)
    one(step_out, "k", 0, 2)
    one(step_mid, "w", 0, 1)
    one(step_last, "k", 0, 4)
    one(step_down, "w", 0, 0)
    one(step_mid, "w", 0, 2)
    one(step_out, "k", 0, 3)
    one(step_down, "w", 0, 1)
    one(step_mid, "w", 0, 3)
    one(step_last, "w", 0, 0)
    one(step_out, "k", 0, 4)
    one(step_down, "w", 0, 2)
    one(step_last, "w", 0, 1)
    one(step_out, "w", 0, 0)
    run(step_out, "w", 2)
    one(step_down, "w", 0, 3)
    one(step_last, "w", 0, 2)
    one(step_out, "w", 0, 1)
    one(step_last, "w", 0, 3)
    run(step_out, "w", 1)
    one(step_out, "w", 0, 2)
    one(step_out, "w", 0, 3)
    gains_done()
    run(step_sibling, "w", 3)
    run(step_sibling, "k", 1)
    run(step_sibling, "k", 0)
    run(step_sibling, "w", 2)
    run(step_sibling, "w", 1)
    one(step_sibling, "w", 0, 0)
    one(step_sibling, "w", 0, 1)
    run(step_done, "k", 1)
    run(step_done, "k", 0)
    outs.append(put_out(1, sc.ok.at[...], gtaps_ref.at[...]))
    for s in (3, 2, 1):
        run(step_done, "w", s)
    last = of("w", 0)
    for group, part in enumerate((last[:-1], last[-1:]) if len(last) > 1 else (last,)):
        first, count = part[0].r0, sum(it.nr for it in part)
        for it in part:
            if it.i >= last[0].i + 2:
                step_sibling(it)
        for it in part:
            step_done(it)
        part_rows_of = pl.ds(first, count)
        outs.append(
            put_out(
                5 + group, sc.ow.at[:, :, part_rows_of], gwide_ref.at[:, :, part_rows_of]
            )
        )
    for copy in outs:
        copy.wait()
    for body in finish:
        body()


def cast_pieces(rows):
    pieces = [("taps", pl.ds(576 * i, 576)) for i in range(4)]
    pieces += [("wide", pl.ds(512 * i, 512)) for i in range(4)]
    return pieces + [("stream", m) for m in range(2)]


def cast_kernel(mixed, gpre, conv, gwide, gtaps, gmid, gout, *refs):
    o_mixed, o_input, o_wide, o_taps, o_mid, o_out = refs[:6]
    b_taps, b_wide, b_gpre, b_conv, f_taps, f_wide, f_stream = refs[6:13]
    b_mixed, b_mid, b_out, r_sem, w_sem, d_sem = refs[13:]
    pieces = cast_pieces(gpre.shape[1])
    same = ((mixed, b_mixed, o_mixed), (gmid, b_mid, o_mid), (gout, b_out, o_out))
    arrive = [pltpu.make_async_copy(a, b, d_sem.at[i]) for i, (a, b, _) in enumerate(same)]
    leave = [pltpu.make_async_copy(b, o, d_sem.at[i]) for i, (_, b, o) in enumerate(same)]
    reads, writes = [], []
    for i, (kind, part) in enumerate(pieces):
        if kind == "stream":
            reads.append(
                [
                    pltpu.make_async_copy(gpre.at[part], b_gpre.at[part], r_sem.at[i]),
                    pltpu.make_async_copy(conv.at[part], b_conv.at[part], r_sem.at[i + 2]),
                ]
            )
            writes.append(
                pltpu.make_async_copy(f_stream.at[part], o_input.at[part], w_sem.at[i])
            )
            continue
        src, low, high, dst = (
            (gtaps, b_taps, f_taps, o_taps)
            if kind == "taps"
            else (gwide, b_wide, f_wide, o_wide)
        )
        reads.append([pltpu.make_async_copy(src.at[part], low.at[part], r_sem.at[i])])
        writes.append(pltpu.make_async_copy(high.at[part], dst.at[part], w_sem.at[i]))
    for group in reads:
        for copy in group:
            copy.start()
    for copy in arrive:
        copy.start()
    for (kind, part), group, write in zip(pieces, reads, writes):
        for copy in group:
            copy.wait()
        size = 64

        def strip(i, carry, kind=kind, part=part):
            if kind == "stream":
                at = pl.ds(pl.multiple_of(i * size, size), size)
                f_stream[part, at] = b_gpre[part, at].astype(F32) + b_conv[part, at].astype(F32)
                return carry
            at = pl.ds(pl.multiple_of(part.start + i * size, size), size)
            if kind == "taps":
                f_taps[at] = b_taps[at].astype(F32)
            else:
                f_wide[at] = b_wide[at].astype(F32)
            return carry

        lax.fori_loop(0, (gpre.shape[1] if kind == "stream" else part.size) // size, strip, 0)
        write.start()
    for first, second in zip(arrive, leave):
        first.wait()
        second.start()
    for copy in writes + leave:
        copy.wait()


def cast_all(mixed, gpre, conv, gwide, gtaps, gmid, gout):
    anywhere = pl.BlockSpec(memory_space=pl.ANY)
    shape = jax.ShapeDtypeStruct
    count = len(cast_pieces(gpre.shape[1]))
    return pl.pallas_call(
        cast_kernel,
        in_specs=[anywhere] * 7,
        out_specs=[anywhere] * 6,
        out_shape=[
            shape(mixed.shape, BF16),
            shape(mixed.shape, F32),
            shape(gwide.shape, F32),
            shape(gtaps.shape, F32),
            shape(gmid.shape, F32),
            shape(gout.shape, F32),
        ],
        scratch_shapes=[
            pltpu.VMEM(gtaps.shape, BF16),
            pltpu.VMEM(gwide.shape, BF16),
            pltpu.VMEM(gpre.shape, BF16),
            pltpu.VMEM(gpre.shape, BF16),
            pltpu.VMEM(gtaps.shape, F32),
            pltpu.VMEM(gwide.shape, F32),
            pltpu.VMEM(gpre.shape, F32),
            pltpu.VMEM(mixed.shape, BF16),
            pltpu.VMEM(gmid.shape, F32),
            pltpu.VMEM(gout.shape, F32),
            pltpu.SemaphoreType.DMA((count + 2,)),
            pltpu.SemaphoreType.DMA((count,)),
            pltpu.SemaphoreType.DMA((3,)),
        ],
        compiler_params=pltpu.CompilerParams(vmem_limit_bytes=60 * 2**20),
        name="casts",
    )(mixed, gpre, conv, gwide, gtaps, gmid, gout)


def local(block_input, cotangent, weight_wide, weight_taps, norm_mid, norm_out, group_counts):
    n_dp = group_counts.shape[1]
    micro, rows, width = block_input.shape
    scratch = scratch_list(n_dp, rows)
    vmem = pl.BlockSpec(memory_space=pltpu.VMEM)
    anywhere = pl.BlockSpec(memory_space=pl.ANY)

    def shape(dims, dtype):
        return jax.ShapeDtypeStruct(dims, dtype)

    stream = (micro, rows, width)
    mixed, gpre, conv, gwide, gtaps, gmid, gout = pl.pallas_call(
        functools.partial(kernel, list(scratch), n_dp),
        out_shape=[
            shape(stream, BF16),
            shape(stream, BF16),
            shape(stream, BF16),
            shape((4, 2, 256, 512), BF16),
            shape((2304, 512), BF16),
            shape(norm_mid.shape, F32),
            shape(norm_out.shape, F32),
        ],
        in_specs=[vmem, vmem, anywhere, anywhere, vmem, vmem, anywhere],
        out_specs=[anywhere] * 5 + [vmem] * 2,
        scratch_shapes=list(scratch.values()),
        compiler_params=pltpu.CompilerParams(
            collective_id=0, has_side_effects=True, vmem_limit_bytes=62 * 2**20
        ),
        name="layers",
    )(block_input, cotangent, weight_wide, weight_taps.reshape(9, 256, 512), norm_mid, norm_out, jnp.swapaxes(group_counts, 1, 2))
    results = cast_all(mixed, gpre, conv, gwide.reshape(2048, 512), gtaps, gmid, gout)
    mixed, grad_input, gwide, gtaps, gmid, gout = results
    return (
        mixed,
        grad_input,
        gwide.reshape(weight_wide.shape),
        gtaps.reshape(weight_taps.shape),
        gmid,
        gout,
    )


def solution(mesh):
    split = P(None, "dp", "pipe")
    section = P("pipe", None, None)
    return jax.shard_map(
        local,
        mesh=mesh,
        in_specs=(split, split, section, section, section, section, P()),
        out_specs=(split, split, section, section, section, section),
        check_vma=False,
    )
```

```python
import functools
from types import SimpleNamespace

import jax
import jax.numpy as jnp
from jax import lax
from jax.experimental import pallas as pl
from jax.experimental.pallas import tpu as pltpu
from jax.sharding import PartitionSpec as P

MESH = pl.DeviceIdType.MESH
F32 = jnp.float32
BF16 = jnp.bfloat16
EPS = 1e-05
LANES = 128
N_PIPE = 4
NEAR = [k for k in range(9) if k != 4]


def slot_of(tap):
    return tap if tap < 4 else tap - 1


def dot_nn(a, b):
    return jnp.dot(a, b, preferred_element_type=F32)


def dot_nt(a, b):
    return lax.dot_general(a, b, (((1,), (1,)), ((), ())), preferred_element_type=F32)


def sigmoid(v):
    return jax.nn.sigmoid(v)


def sizes(n_dp):
    n_z = n_dp // 2
    n_own = min(n_z, 16)
    return n_z, n_own


def gradient_items(n_dp):
    line = n_dp // 2 == 4
    listed = []
    for kind, index, parts in (
        ("w", 3, [128, 128]),
        ("k", 1, [576] * 4),
        ("w", 2, [128, 128]),
        ("w", 1, [128, 128]),
        ("k", 0, [576] * 4),
        ("w", 0, [64] * 4),
    ):
        start = 0
        for part, rows in enumerate(parts if line else [sum(parts)]):
            listed.append(
                SimpleNamespace(
                    kind=kind, t=index, r0=start, nr=rows, i=len(listed), part=part
                )
            )
            start += rows
    return listed


def scratch_list(n_dp, rows):
    n_z, n_own = sizes(n_dp)
    items = len(gradient_items(n_dp))
    line = n_z == 4
    dma = pltpu.SemaphoreType.DMA

    def half(*shape):
        return pltpu.VMEM(shape, BF16)

    def full(*shape):
        return pltpu.VMEM(shape, F32)

    return dict(
        wt=half(4, 512, 512),
        k2=half(2, 18, 256, 128),
        gm=full(4, 2, 128),
        go=full(4, 2, 2, 512),
        msk=full(2, rows, 128),
        pm=half(2, 8, rows, rows),
        part=half(2, 2, 4, rows, 128),
        rsr=half(6, 2, 3, rows, 128),
        ag=half(6, 2, 4, rows, 128),
        stm=full(8, 2, n_dp, 2, 128),
        stw=full(4, 2, n_dp, 2, 512),
        midv=full(4, 2, rows, 128),
        dzm=full(2, rows, 128),
        inv_mid=full(4, 2, 1, 128),
        inv_wide=full(2, 2, 1, 512),
        widv=full(2, 2, rows, 512),
        pre0=full(2, rows, 512),
        s1=half(2, rows, 512),
        mix=half(2, rows, 512),
        gp=half(2, 2, rows, 512),
        cv=half(2, rows, 512),
        gt=half(2, rows, 512),
        gb=half(2, rows, 1152),
        yb=half(8, rows, 128),
        tb=half(512, 2 * rows),
        dw=half(4, 2, 256, 512),
        prw=half(4, 256, 512),
        zsw=half(4, 256, 512),
        fzw=half(4, 256, 512),
        ow=half(4, 2, 256, 512),
        dk=half(2, 4608, 128),
        prk=half(2, 2304, 128),
        zsk=half(2, 2304, 128),
        fzk=half(2, 2304, 128),
        ok=half(2304, 512),
        zow=half(4, 256, 512) if line else half(4, n_z - 1, 256 // n_own, 512),
        ziw=half(4, 128, 512),
        zok=half(2, 2304, 128) if line else half(2, n_z - 1, 2304 // n_own, 128),
        zik=half(2, 1152, 128),
        gsm=full(4, 4, 2, 128),
        gsw=full(2, 4, 2, 512),
        cnt=pltpu.SMEM((2, n_dp), F32),
        counts=pltpu.SMEM((2, 4, n_dp), jnp.int32),
        f_s=dma((2,)),
        f_r=dma((2, 4)),
        z_r=dma((2, 4)),
        b_s=dma((2, 4)),
        b_r=dma((2, 4)),
        n_s=dma((2,)),
        n_r=dma((2,)),
        loc=dma((4,)),
        ex_s=dma((2, 2)),
        ex_r=dma((2, 2)),
        st_s=dma((2, 2)),
        st_r=dma((2, 2)),
        pw_s=dma((6,)),
        pw_r=dma((6,)),
        it_s=dma((items,)),
        one_r=dma((items,)),
        mid_r=dma((items,)),
        inn_r=dma((items,)),
        to_s=dma((items,)),
        to_r=dma((2, 5)),
        sib_s=dma((2, 5)),
        sib_r=dma((2, 5)),
        g_s=dma((2,)),
        g_r=dma((2,)),
        out=dma((7,)),
    )


def kernel(names, n, *refs):
    (x_ref, cot_ref, wide_ref, taps_ref, nmid_ref, nout_ref, counts_hbm) = refs[:7]
    (mixed_ref, gpre_ref, conv_ref, gwide_ref, gtaps_ref, gmid_ref, gout_ref) = refs[7:14]
    sc = SimpleNamespace(**dict(zip(names, refs[14:])))
    counts_ref = sc.counts
    rows = x_ref.shape[1]
    n_z, n_own = sizes(n)
    p = lax.axis_index("pipe")
    d = lax.axis_index("dp")
    z = lax.div(d, 2)
    c = lax.rem(d, 2)
    parity = lax.rem(p, 2)
    sibling = (p, 2 * z + 1 - c)
    z_odd = lax.rem(z, 2)
    z_pair = (p, 2 * (z + 1 - 2 * z_odd) + c)
    quarter = 2 * z_odd + c
    quarter_z = 2 * (1 - z_odd) + c
    finish = []

    def pipe_at(off):
        return lax.rem(p + N_PIPE + (2 * parity - 1) * off, N_PIPE)

    def remote(src, dst, ss, rs, dev):
        return pltpu.make_async_remote_copy(
            src_ref=src, dst_ref=dst, send_sem=ss, recv_sem=rs, device_id=dev, device_id_type=MESH
        )

    def each(count, first, body):
        if count - first <= 8:
            for k in range(first, count):
                body(k)
        else:

            def step(k, carry):
                body(k)
                return carry

            lax.fori_loop(first, count, step, 0)

    def bytes_wait(view, sem):
        pltpu.make_async_copy(view, view, sem).wait()

    barrier = pltpu.get_barrier_semaphore()
    for off in range(1, N_PIPE):
        pl.semaphore_signal(barrier, inc=1, device_id=(pipe_at(off), d), device_id_type=MESH)

    def greet(k):
        pl.semaphore_signal(
            barrier, inc=1, device_id=(p, lax.rem(d + k, n)), device_id_type=MESH
        )

    each(n, 1, greet)

    def columns_of(q):
        return pl.ds(pl.multiple_of(128 * q, 128), 128)

    own_w = pltpu.make_async_copy(
        wide_ref.at[0, pl.ds(pl.multiple_of(512 * p, 512), 512), :], sc.wt.at[p], sc.loc.at[0]
    )
    own_k = pltpu.make_async_copy(
        taps_ref.at[:, :, columns_of(p)],
        sc.k2.at[lax.div(p, 2), pl.ds(9 * parity, 9)],
        sc.loc.at[1],
    )
    own_c = pltpu.make_async_copy(counts_hbm, counts_ref, sc.loc.at[2])
    own_c.start()
    own_w.start()
    own_k.start()
    own_n = pltpu.make_async_copy(
        nmid_ref.at[0, :, columns_of(p)], sc.gm.at[p], sc.loc.at[3]
    )
    own_n.start()
    for e in range(2):
        sc.go[p, e] = nout_ref[0, :, 512 * e : 512 * e + 512]

    own_c.wait()

    def used_rows(m, j):
        return (
            49 * counts_ref[m, 0, j]
            + 36 * counts_ref[m, 1, j]
            + 25 * counts_ref[m, 2, j]
            + 4 * counts_ref[m, 3, j]
        )

    totals = []
    for m in range(2):

        def count_up(j, acc, m=m):
            used = used_rows(m, j)
            sc.cnt[m, j] = used.astype(F32)
            return acc + used

        totals.append(lax.fori_loop(0, n, count_up, jnp.int32(0)).astype(F32))

    pl.semaphore_wait(barrier, N_PIPE - 1 + n - 1)

    def held(kind, s, part):
        if kind == 0:
            return sc.wt.at[s, pl.ds(pl.multiple_of(128 * part, 128), 128)]
        layer, odd = (s // 2, s % 2) if isinstance(s, int) else (lax.div(s, 2), lax.rem(s, 2))
        return sc.k2.at[
            layer, pl.ds(9 * odd, 9), pl.ds(pl.multiple_of(64 * part, 64), 64)
        ]

    def fetch(kind, off):
        q = pipe_at(off)
        if kind == 0:
            src = wide_ref.at[0, pl.ds(pl.multiple_of(512 * q + 128 * quarter, 128), 128), :]
        else:
            src = taps_ref.at[:, pl.ds(pl.multiple_of(64 * quarter, 64), 64), columns_of(q)]
        return remote(
            src, held(kind, p, quarter), sc.f_s.at[kind], sc.f_r.at[kind, p], (q, d)
        )

    def send_norm(off):
        q = pipe_at(off)
        listed = [
            remote(
                nmid_ref.at[0, :, columns_of(q)],
                sc.gm.at[p],
                sc.n_s.at[0],
                sc.n_r.at[0],
                (q, d),
            )
        ]
        for e in range(2):
            listed.append(
                remote(
                    nout_ref.at[0, :, pl.ds(512 * e, 512)],
                    sc.go.at[p, e],
                    sc.n_s.at[1],
                    sc.n_r.at[1],
                    (q, d),
                )
            )
        return listed

    def norm_wait(sems):
        bytes_wait(sc.gm.at[pl.ds(0, 3)], sems.at[0])
        bytes_wait(sc.go.at[pl.ds(0, 3)], sems.at[1])

    def pass_z(kind, s):
        view = held(kind, s, quarter)
        return remote(view, view, sc.b_s.at[kind, s], sc.z_r.at[kind, s], z_pair)

    def pass_sibling(kind, s, e):
        view = held(kind, s, quarter if e == 0 else quarter_z)
        return remote(view, view, sc.b_s.at[kind, s], sc.b_r.at[kind, s], sibling)

    def spread_first(kind, s):
        @pl.when(p != s)
        def _():
            view = held(kind, s, quarter)
            bytes_wait(view, sc.f_r.at[kind, s])
            pass_z(kind, s).start()
            pass_sibling(kind, s, 0).start()

    def spread_second(kind, s):
        @pl.when(p != s)
        def _():
            pass_z(kind, s).wait_recv()
            pass_sibling(kind, s, 1).start()

    def quarters(kind, s, count):
        if kind == 0:
            return sc.wt.at[s, pl.ds(0, 128 * count)]
        return sc.k2.at[s // 2, pl.ds(9 * (s % 2), 9), pl.ds(0, 64 * count)]

    def ready(kind, s):
        @pl.when(p != s)
        def _():
            bytes_wait(quarters(kind, s, 2), sc.b_r.at[kind, s])

        @pl.when(p == s)
        def _():
            (own_w if kind == 0 else own_k).wait()

    def finish_weights():
        for kind in range(2):
            bytes_wait(quarters(kind, 0, 3), sc.f_s.at[kind])
            for s in range(4):

                @pl.when(p != s)
                def _(kind=kind, s=s):
                    bytes_wait(quarters(kind, s, 3), sc.b_s.at[kind, s])

    finish.append(finish_weights)

    for even in range(2):

        @pl.when(parity == even)
        def _(even=even):
            for kind in (even, 1 - even):
                for off in range(1, 4):
                    fetch(kind, off).start()
                if kind == even:
                    for off in range(1, 4):
                        for copy in send_norm(off):
                            copy.start()

    def finish_norm():
        norm_wait(sc.n_s)

    finish.append(finish_norm)

    row_id = lax.broadcasted_iota(jnp.int32, (rows, LANES), 0).astype(F32)
    lane_id = lax.broadcasted_iota(jnp.int32, (rows, LANES), 1).astype(F32)

    def build(m):
        ends = []
        total = jnp.int32(0)
        for g, area in enumerate((49, 36, 25, 4)):
            total = total + area * counts_ref[m, g, d]
            ends.append(total.astype(F32))
        sc.msk[m] = jnp.where(row_id < ends[3], 1.0, 0.0)

        def pick(values):
            out = values[4]
            for g in (3, 2, 1, 0):
                out = jnp.where(row_id < ends[g], values[g], out)
            return out

        zero = jnp.zeros((rows, LANES), F32)
        side = pick([zero + 7.0, zero + 6.0, zero + 5.0, zero + 2.0, zero + 1.0])
        begin = pick([zero, zero + ends[0], zero + ends[1], zero + ends[2], row_id])
        one_over = pick(
            [zero + 1.0 / 7.0, zero + 1.0 / 6.0, zero + 1.0 / 5.0, zero + 0.5, zero + 1.0]
        )
        within = row_id - begin
        within = within - side * side * jnp.floor((within + 0.5) * one_over * one_over)
        map_row = jnp.floor((within + 0.5) * one_over)
        map_col = within - side * map_row
        for k in NEAR:
            du, dv = k // 3 - 1, k % 3 - 1
            usable = row_id < ends[3]
            if du == -1:
                usable = usable & (map_row > 0.5)
            if du == 1:
                usable = usable & (map_row < side - 1.5)
            if dv == -1:
                usable = usable & (map_col > 0.5)
            if dv == 1:
                usable = usable & (map_col < side - 1.5)
            target = jnp.where(usable, row_id + du * side + dv, -1000.0)
            for t in range(rows // LANES):
                hit = jnp.where(target == lane_id + float(LANES * t), 1.0, 0.0)
                sc.pm[m, slot_of(k), :, LANES * t : LANES * (t + 1)] = hit.astype(BF16)

    for m in range(2):
        build(m)


    exchange_order = [
        ("rs", 0), ("ag", 0), ("ag", 2), ("rs", 1), ("ag", 1), ("ag", 3),
        ("rs", 3), ("rs", 5), ("ag", 5), ("rs", 2), ("rs", 4), ("ag", 4),
    ]

    def three(kind, i, m):
        return sc.rsr.at[i, m] if kind == "rs" else sc.ag.at[i, m, pl.ds(0, 3)]

    def exchange_wait(sems, kind, i, m):
        turn = exchange_order.index((kind, i))
        bytes_wait(three(kind, i, m), sems.at[turn % 2, m])

    def exchange_open(kind, i, m):
        turn = exchange_order.index((kind, i))
        if turn >= 2:
            exchange_wait(sc.ex_s, *exchange_order[turn - 2], m)
        return sc.ex_s.at[turn % 2, m], sc.ex_r.at[turn % 2, m]

    def rs_sum(rid, m, par):
        exchange_wait(sc.ex_r, "rs", rid, m)
        total = sc.part[par, m, p].astype(F32)
        for k in range(3):
            total = total + sc.rsr[rid, m, k].astype(F32)
        return total

    def ag_start(aid, m, value):
        ss, rs = exchange_open("ag", aid, m)
        sc.ag[aid, m, p] = value
        own = sc.ag.at[aid, m, p]
        for off in range(1, 4):
            remote(own, own, ss, rs, (pipe_at(off), d)).start()

    def ag_wait(aid, m):
        exchange_wait(sc.ex_r, "ag", aid, m)

    def ag_value(aid, m):
        return jnp.concatenate([sc.ag[aid, m, q] for q in range(4)], axis=1)

    def finish_exchanges():
        for kind, i in exchange_order[-2:]:
            for m in range(2):
                exchange_wait(sc.ex_s, kind, i, m)

    finish.append(finish_exchanges)

    sum_order = [
        (False, 0), (False, 1), (True, 0), (False, 2), (False, 3), (True, 1),
        (True, 3), (False, 7), (False, 6), (True, 2), (False, 5), (False, 4),
    ]

    def st_buffer(wide, i, m):
        return (sc.stw if wide else sc.stm).at[i, m]

    def st_bytes(sems, wide, i, m):
        turn = sum_order.index((wide, i))
        bytes_wait(st_buffer(wide, i, m).at[pl.ds(0, n - 1)], sems.at[turn % 2, m])

    def st_start(wide, i, m):
        turn = sum_order.index((wide, i))
        if turn >= 2:
            st_bytes(sc.st_s, *sum_order[turn - 2], m)
        own = st_buffer(wide, i, m).at[d]
        ss, rs = sc.st_s.at[turn % 2, m], sc.st_r.at[turn % 2, m]

        def go(k):
            remote(own, own, ss, rs, (p, lax.rem(d + k, n))).start()

        each(n, 1, go)

    def st_wait(wide, i, m):
        st_bytes(sc.st_r, wide, i, m)

    def finish_st():
        for wide, i in sum_order[-2:]:
            for m in range(2):
                st_bytes(sc.st_s, wide, i, m)

    finish.append(finish_st)

    def over_devices(body, init):
        if n <= 8:
            for j in range(n):
                init = body(j, init)
            return init
        return lax.fori_loop(0, n, body, init)

    def combine(wide, i, m):
        st_wait(wide, i, m)
        ref = sc.stw if wide else sc.stm
        blank = jnp.zeros((1, ref.shape[-1]), F32)
        mean = over_devices(
            lambda j, acc: acc + sc.cnt[m, j] * ref[i, m, j, 0:1, :], blank
        )
        mean = mean / totals[m]

        def spread(j, acc):
            gap = ref[i, m, j, 0:1, :] - mean
            return acc + ref[i, m, j, 1:2, :] + sc.cnt[m, j] * (gap * gap)

        var = over_devices(spread, blank) / totals[m]
        return mean, lax.rsqrt(var + EPS)

    def back_sums(wide, i, m):
        st_wait(wide, i, m)
        ref = sc.stw if wide else sc.stm
        return over_devices(
            lambda j, acc: acc + ref[i, m, j], jnp.zeros((2, ref.shape[-1]), F32)
        )

    def local_moments(v, m):
        mask = sc.msk[m]
        own = jnp.maximum(sc.cnt[m, d], 1.0)
        mean = jnp.sum(v * mask, 0, keepdims=True) / own
        gap = (v - mean) * mask
        return jnp.concatenate([mean, jnp.sum(gap * gap, 0, keepdims=True)], 0)

    def local_sums(dz, vhat):
        return jnp.concatenate(
            [jnp.sum(dz * vhat, 0, keepdims=True), jnp.sum(dz, 0, keepdims=True)], 0
        )

    def lanes(j):
        return slice(LANES * j, LANES * (j + 1))

    def stream(layer, m):
        return x_ref[m] if layer == 0 else sc.s1[m]

    def stream_part(layer, m, j):
        return (x_ref[m, :, lanes(j)] if layer == 0 else sc.s1[m, :, lanes(j)]).astype(F32)

    rs_par = {0: 0, 1: 1, 3: 0, 5: 1, 2: 0, 4: 1}

    def rs_send(rid, m, values):
        par = rs_par[rid]
        ss, rs = exchange_open("rs", rid, m)
        for j, value in enumerate(values):
            half = value.astype(BF16)
            sc.part[par, m, 2 * j] = half[:, :LANES]
            sc.part[par, m, 2 * j + 1] = half[:, LANES:]
        for off in range(1, 4):
            q = pipe_at(off)
            remote(sc.part.at[par, m, q], sc.rsr.at[rid, m, off - 1], ss, rs, (q, d)).start()

    def first_part(layer, m):
        s = stream(layer, m)
        rs_send(
            layer,
            m,
            [dot_nn(s, sc.wt[2 * layer, :, 256 * j : 256 * j + 256]) for j in range(2)],
        )

    def mid_moments(i, m, v):
        sc.midv[i, m] = v
        sc.stm[i, m, d] = local_moments(v, m)
        st_start(False, i, m)

    def first_norm(layer, m):
        mid_moments(2 * layer, m, rs_sum(layer, m, rs_par[layer]))

    def mid_hidden(i, m):
        mean, inv = combine(False, i, m)
        sc.inv_mid[i, m] = inv
        vhat = (sc.midv[i, m] - mean) * inv
        sc.midv[i, m] = vhat
        u = sc.gm[i, 0:1, :] * vhat + sc.gm[i, 1:2, :]
        return (sc.msk[m] * (u * sigmoid(u))).astype(BF16)

    def hidden_one(layer, m):
        ag_start(layer, m, mid_hidden(2 * layer, m))

    def taps_of(layer, taps):
        return jnp.concatenate(
            [
                jnp.concatenate([sc.k2[layer, 2 * k], sc.k2[layer, 2 * k + 1]], axis=0)
                for k in taps
            ],
            axis=1,
        )

    def second_part(layer, m):
        ag_wait(layer, m)
        h = ag_value(layer, m)
        centre = None
        for j in range(5):
            width = 256 if j < 4 else 128
            y = dot_nn(h, taps_of(layer, [2 * j + e for e in range(width // LANES)]))
            for e in range(width // LANES):
                tap = 2 * j + e
                if tap == 4:
                    centre = y[:, lanes(e)]
                    sc.midv[2 * layer + 1, m] = centre
                else:
                    sc.yb[slot_of(tap)] = y[:, lanes(e)].astype(BF16)
        total = sc.midv[2 * layer + 1, m]
        for k in range(8):
            total = total + dot_nn(sc.pm[m, k], sc.yb[k])
        mid_moments(2 * layer + 1, m, total)

    def hidden_two(layer, m):
        ag_start(2 + layer, m, mid_hidden(2 * layer + 1, m))

    def third_part(layer, m):
        ag_wait(2 + layer, m)
        h = ag_value(2 + layer, m)
        for j in range(2):
            sc.widv[layer, m, :, 256 * j : 256 * j + 256] = dot_nt(
                h, sc.wt[2 * layer + 1, 256 * j : 256 * j + 256, :]
            )
        for j in range(4):
            sc.stw[layer, m, d, :, lanes(j)] = local_moments(sc.widv[layer, m, :, lanes(j)], m)
        st_start(True, layer, m)

    def out_gain(layer, j):
        both = sc.go[2 * layer + lax.div(p, 2), lax.rem(p, 2)]
        return both[0:1, lanes(j)], both[1:2, lanes(j)]

    def pre_values(layer, m):
        mean, inv = combine(True, layer, m)
        sc.inv_wide[layer, m] = inv
        mask = sc.msk[m]
        for j in range(4):
            gain, bias = out_gain(layer, j)
            vhat = (sc.widv[layer, m, :, lanes(j)] - mean[:, lanes(j)]) * inv[:, lanes(j)]
            sc.widv[layer, m, :, lanes(j)] = vhat
            pre = gain * vhat + bias + stream_part(layer, m, j)
            sig = sigmoid(pre)
            out = (mask * (pre * sig)).astype(BF16)
            if layer == 0:
                sc.pre0[m, :, lanes(j)] = pre
                sc.s1[m, :, lanes(j)] = out
            else:
                sc.mix[m, :, lanes(j)] = out
                slope = sig * (1.0 + pre * (1.0 - sig))
                grad = (cot_ref[m, :, lanes(j)].astype(F32) * mask * slope).astype(BF16)
                sc.gp[1, m, :, lanes(j)] = grad
                sc.stw[3, m, d, :, lanes(j)] = local_sums(grad.astype(F32), vhat)
        if layer == 1:
            st_start(True, 3, m)

    def put_out(k, src, dst):
        copy = pltpu.make_async_copy(src, dst, sc.out.at[k])
        copy.start()
        return copy

    def grad_out_norm(layer, m):
        sums = back_sums(True, 2 + layer, m)
        if m == 0:
            sc.gsw[layer, p] = sums
        else:
            sc.gsw[layer, p] = sc.gsw[layer, p] + sums
        mask = sc.msk[m]
        inv = sc.inv_wide[layer, m]
        for j in range(4):
            gain, _ = out_gain(layer, j)
            dz = sc.gp[layer, m, :, lanes(j)].astype(F32)
            vhat = sc.widv[layer, m, :, lanes(j)]
            s1 = sums[0:1, lanes(j)] / totals[m]
            s0 = sums[1:2, lanes(j)] / totals[m]
            dv = mask * (gain * inv[:, lanes(j)]) * (dz - s0 - vhat * s1)
            sc.gt[m, :, lanes(j)] = dv.astype(BF16)
        g = sc.gt[m]
        rs_send(
            2 + layer,
            m,
            [dot_nn(g, sc.wt[2 * layer + 1, :, 256 * j : 256 * j + 256]) for j in range(2)],
        )

    def mid_grad(i, m, upstream):
        vhat = sc.midv[i, m]
        u = sc.gm[i, 0:1, :] * vhat + sc.gm[i, 1:2, :]
        sig = sigmoid(u)
        dz = upstream * sc.msk[m] * (sig * (1.0 + u * (1.0 - sig)))
        sc.dzm[m] = dz
        sc.stm[4 + i, m, d] = local_sums(dz, vhat)
        st_start(False, 4 + i, m)

    def mid_back(i, m):
        sums = back_sums(False, 4 + i, m)
        if m == 0:
            sc.gsm[i, p] = sums
        else:
            sc.gsm[i, p] = sc.gsm[i, p] + sums
        s1 = sums[0:1, :] / totals[m]
        s0 = sums[1:2, :] / totals[m]
        scale = sc.gm[i, 0:1, :] * sc.inv_mid[i, m]
        return (sc.msk[m] * scale * (sc.dzm[m] - s0 - sc.midv[i, m] * s1)).astype(BF16)

    def grad_two(layer, m):
        mid_grad(2 * layer + 1, m, rs_sum(2 + layer, m, rs_par[2 + layer]))

    def grad_second(layer, m):
        gs = mid_back(2 * layer + 1, m)
        for k in range(9):
            if k == 4:
                sc.gb[m, :, lanes(k)] = gs
            else:
                sc.gb[m, :, lanes(k)] = dot_nn(sc.pm[m, slot_of(8 - k)], gs).astype(BF16)
        g = sc.gb[m]
        rs_send(
            4 + layer,
            m,
            [
                dot_nt(
                    g, jnp.concatenate([sc.k2[layer, 2 * k + j] for k in range(9)], axis=1)
                )
                for j in range(2)
            ],
        )

    def grad_one(layer, m):
        mid_grad(2 * layer, m, rs_sum(4 + layer, m, rs_par[4 + layer]))

    def grad_first(layer, m):
        ag_start(4 + layer, m, mid_back(2 * layer, m))

    def conv_grad(layer, m):
        ag_wait(4 + layer, m)
        g = ag_value(4 + layer, m)
        mask = sc.msk[m]
        for j in range(2):
            r = dot_nt(g, sc.wt[2 * layer, 256 * j : 256 * j + 256, :]).astype(BF16)
            if layer == 0:
                sc.cv[m, :, 256 * j : 256 * j + 256] = r
                continue
            for e in range(2):
                i = 2 * j + e
                pre = sc.pre0[m, :, lanes(i)]
                sig = sigmoid(pre)
                slope = sig * (1.0 + pre * (1.0 - sig))
                up = sc.gp[1, m, :, lanes(i)].astype(F32) + r[:, lanes(e)].astype(F32)
                grad = (up * mask * slope).astype(BF16)
                sc.gp[0, m, :, lanes(i)] = grad
                sc.stw[2, m, d, :, lanes(i)] = local_sums(
                    grad.astype(F32), sc.widv[0, m, :, lanes(i)]
                )
        if layer == 1:
            st_start(True, 2, m)

    def turned(blocks):
        for m, block in enumerate(blocks):
            sc.tb[:, rows * m : rows * (m + 1)] = block.T

    def both(get):
        return jnp.concatenate([get(0), get(1)], axis=0)

    def wide_grad(s, left, right):
        turned([left(0), left(1)])
        for j in range(2):
            cols = slice(256 * j, 256 * j + 256)
            rhs = both(lambda m: right(m)[:, cols])
            for h in range(2):
                r = dot_nn(sc.tb[256 * h : 256 * h + 256, :], rhs)
                sc.dw[s, h, :, cols] = r.astype(BF16)
        pair_copy("w", s).start()

    def taps_grad(layer):
        turned([ag_value(layer, 0), ag_value(layer, 1)])
        for j in range(5):
            width = 256 if j < 4 else 128
            rhs = both(lambda m: sc.gb[m, :, 256 * j : 256 * j + width])
            r = dot_nn(sc.tb[...], rhs).astype(BF16)
            for e in range(width // LANES):
                tap = 2 * j + e
                sc.dk[layer, 512 * tap : 512 * tap + 512, :] = r[:, lanes(e)]
        pair_copy("k", layer).start()

    def half_rows(which):
        return pl.ds(pl.multiple_of(2304 * which, 2304), 2304)

    def pair_copy(kind, t):
        if kind == "w":
            src, dst, i = sc.dw.at[t, 1 - c], sc.prw.at[t], t
        else:
            src, dst, i = sc.dk.at[t, half_rows(1 - c)], sc.prk.at[t], 4 + t
        return remote(src, dst, sc.pw_s.at[i], sc.pw_r.at[i], sibling)

    def pair_sum(kind, t):
        pair_copy(kind, t).wait_recv()
        if kind == "w":
            sc.zsw[t] = (sc.dw[t, c].astype(F32) + sc.prw[t].astype(F32)).astype(BF16)
            return
        for i in range(4):
            part = slice(576 * i, 576 * i + 576)
            mine = pl.ds(pl.multiple_of(2304 * c + 576 * i, 576), 576)
            sc.zsk[t, part] = (
                sc.dk[t, mine].astype(F32) + sc.prk[t, part].astype(F32)
            ).astype(BF16)

    items = gradient_items(n)
    line = n_z == 4
    inner = (z == 1) | (z == 2)

    def tile(it, name):
        return getattr(sc, name + it.kind)

    def some(it, name, start, count):
        return tile(it, name).at[it.t, pl.ds(start, count)]

    def part_rows(it, which):
        half = it.nr // 2
        return pl.ds(pl.multiple_of(it.r0 + half * which, half), half)

    def up_copy(it):
        rows_of = pl.ds(it.r0, it.nr)
        return remote(
            tile(it, "zs").at[it.t, rows_of],
            tile(it, "zo").at[it.t, rows_of],
            sc.it_s.at[it.i],
            sc.one_r.at[it.i],
            (p, 2 * (1 + lax.div(z, 3)) + c),
        )

    def mid_copy(it):
        return remote(
            tile(it, "zs").at[it.t, part_rows(it, 2 - z)],
            tile(it, "zi").at[it.t, pl.ds(it.r0 // 2, it.nr // 2)],
            sc.it_s.at[it.i],
            sc.mid_r.at[it.i],
            (p, 2 * (3 - z) + c),
        )

    def inn_copy(it):
        view = tile(it, "fz").at[it.t, part_rows(it, z - 1)]
        return remote(
            view, view, sc.it_s.at[it.i], sc.inn_r.at[it.i], (p, 2 * (3 - z) + c)
        )

    def down_copy(it, e):
        view = tile(it, "fz").at[it.t, part_rows(it, z - 1 if e == 0 else 2 - z)]
        return remote(
            view, view, sc.it_s.at[it.i], sc.one_r.at[it.i], (p, 2 * (3 * (z - 1)) + c)
        )

    def direct_rows(it, j):
        count = it.nr // n_own
        return pl.ds(pl.multiple_of(it.r0 + count * j, count), count)

    def owner(index, body):
        if n_own == n_z:
            body()
        else:
            pl.when(index < n_own)(body)

    def scatter_copy(it, k):
        j = lax.rem(z + k, n_z)
        return j, remote(
            tile(it, "zs").at[it.t, direct_rows(it, lax.rem(j, n_own))],
            tile(it, "zo").at[it.t, k - 1],
            sc.it_s.at[it.i],
            sc.one_r.at[it.i],
            (p, 2 * j + c),
        )

    def gather_copy(it, k):
        j = lax.rem(z + k, n_z)
        view = tile(it, "fz").at[it.t, direct_rows(it, lax.rem(z, n_own))]
        return remote(view, view, sc.to_s.at[it.i], sc.mid_r.at[it.i], (p, 2 * j + c))

    def add_rows(target, first, second):
        target[...] = (first[...].astype(F32) + second[...].astype(F32)).astype(BF16)

    def step_up(it):
        if line:

            @pl.when((z == 0) | (z == 3))
            def _():
                up_copy(it).start()

        else:

            def go(k):
                j, copy = scatter_copy(it, k)
                owner(j, lambda: copy.start())

            each(n_z, 1, go)

    def step_mid(it):
        if not line:
            return

        @pl.when(inner)
        def _():
            up_copy(it).wait_recv()
            mine = some(it, "zs", it.r0, it.nr)
            add_rows(mine, mine, some(it, "zo", it.r0, it.nr))
            mid_copy(it).start()

    def step_down(it):
        if line:

            @pl.when(inner)
            def _():
                mid_copy(it).wait_recv()
                keep = part_rows(it, z - 1)
                add_rows(
                    tile(it, "fz").at[it.t, keep],
                    tile(it, "zs").at[it.t, keep],
                    some(it, "zi", it.r0 // 2, it.nr // 2),
                )
                inn_copy(it).start()
                down_copy(it, 0).start()

            return

        def go():
            bytes_wait(tile(it, "zo").at[it.t], sc.one_r.at[it.i])
            mine = direct_rows(it, z)
            total = tile(it, "zs")[it.t, mine].astype(F32)
            total = lax.fori_loop(
                0, n_z - 1, lambda k, acc: acc + tile(it, "zo")[it.t, k].astype(F32), total
            )
            tile(it, "fz")[it.t, mine] = total.astype(BF16)
            each(n_z, 1, lambda k: gather_copy(it, k).start())

        owner(z, go)

    def step_last(it):
        if not line:
            return

        @pl.when(inner)
        def _():
            inn_copy(it).wait_recv()
            down_copy(it, 1).start()

    def owner_of(it):
        return it.t if it.kind == "w" else 2 * it.t + c

    def landing(it, q, core):
        if it.kind == "w":
            return sc.ow.at[q, core, pl.ds(it.r0, it.nr)]
        lane = pl.ds(128 * q, 128) if isinstance(q, int) else columns_of(q)
        return sc.ok.at[pl.ds(it.r0, it.nr), lane]

    def to_sem(it, sems):
        return sems.at[0 if it.kind == "w" else 1, it.part]

    def to_copy(it):
        return remote(
            some(it, "fz", it.r0, it.nr),
            landing(it, p, c),
            sc.to_s.at[it.i],
            to_sem(it, sc.to_r),
            (owner_of(it), d),
        )

    def step_out(it):
        if line:

            @pl.when((z == 0) | (z == 3))
            def _():
                bytes_wait(some(it, "fz", it.r0, it.nr), sc.one_r.at[it.i])

        else:
            count = it.nr // n_own
            if n_own == n_z:
                bytes_wait(some(it, "fz", it.r0, count * (n_own - 1)), sc.mid_r.at[it.i])
            else:

                @pl.when(z < n_own)
                def _():
                    bytes_wait(some(it, "fz", it.r0, count * (n_own - 1)), sc.mid_r.at[it.i])

                @pl.when(z >= n_own)
                def _():
                    bytes_wait(some(it, "fz", it.r0, count * n_own), sc.mid_r.at[it.i])

        @pl.when(p != owner_of(it))
        def _():
            to_copy(it).start()

        def place(q):
            landing(it, q, c)[...] = some(it, "fz", it.r0, it.nr)[...]

        if it.kind == "w":
            pl.when(p == it.t)(lambda: place(it.t))
        else:
            for core in range(2):
                pl.when((p == 2 * it.t + core) & (c == core))(
                    functools.partial(place, 2 * it.t + core)
                )

    def sibling_copy(it, q):
        view = landing(it, q, c)
        return remote(
            view, view, to_sem(it, sc.sib_s), to_sem(it, sc.sib_r), sibling
        )

    def slices(it, count):
        if it.kind == "w":
            return sc.ow.at[pl.ds(0, count), 0, pl.ds(it.r0, it.nr)]
        return sc.ok.at[pl.ds(it.r0, it.nr), pl.ds(0, 128 * count)]

    def step_sibling(it):
        def go():
            bytes_wait(slices(it, 3), to_sem(it, sc.to_r))
            for q in range(4):
                sibling_copy(it, q).start()

        pl.when(p == owner_of(it))(go)

    def step_done(it):
        def go():
            bytes_wait(slices(it, 4), to_sem(it, sc.sib_r))

        pl.when(p == (it.t if it.kind == "w" else 2 * it.t + 1 - c))(go)

    def twice(it):
        if it.kind == "w":
            return sc.dw.at[it.t, :, pl.ds(0, it.nr)]
        return sc.dk.at[it.t, pl.ds(0, 2 * it.nr)]

    def finish_grads():
        for kind, t in [("w", s) for s in range(4)] + [("k", layer) for layer in range(2)]:
            pair_copy(kind, t).wait_send()
        for it in items:
            if line:

                @pl.when(inner)
                def _(it=it):
                    bytes_wait(twice(it), sc.it_s.at[it.i])

                @pl.when((z == 0) | (z == 3))
                def _(it=it):
                    up_copy(it).wait_send()

            else:

                def sent(k, it=it):
                    j, copy = scatter_copy(it, k)
                    owner(j, lambda: copy.wait_send())

                each(n_z, 1, sent)
                owner(z, lambda: each(n_z, 1, lambda k: gather_copy(it, k).wait_send()))

            @pl.when(p != owner_of(it))
            def _(it=it):
                to_copy(it).wait_send()

            @pl.when(p == owner_of(it))
            def _(it=it):
                bytes_wait(slices(it, 4), to_sem(it, sc.sib_s))

    finish.append(finish_grads)

    def gain_copies(off):
        dev = (pipe_at(off), d)
        return [
            remote(sc.gsm.at[:, p], sc.gsm.at[:, p], sc.g_s.at[0], sc.g_r.at[0], dev),
            remote(sc.gsw.at[:, p], sc.gsw.at[:, p], sc.g_s.at[1], sc.g_r.at[1], dev),
        ]

    def gains_wait(sems):
        bytes_wait(sc.gsm.at[:, pl.ds(0, 3)], sems.at[0])
        bytes_wait(sc.gsw.at[:, pl.ds(0, 3)], sems.at[1])

    def gains_start():
        for off in range(1, 4):
            for copy in gain_copies(off):
                copy.start()

    def gains_done():
        gains_wait(sc.g_r)
        for q in range(4):
            gmid_ref[0, :, lanes(q)] = sc.gsm[p, q]
        layer = lax.div(p, 2)
        for e in range(2):
            gout_ref[0, :, 512 * e : 512 * e + 512] = sc.gsw[layer, 2 * parity + e]

    def finish_gains():
        gains_wait(sc.g_s)

    finish.append(finish_gains)

    def of(kind, t):
        return [it for it in items if it.kind == kind and it.t == t]

    def one(step, kind, t, part):
        for it in of(kind, t)[part : part + 1]:
            step(it)

    def run(step, kind, t):
        for it in of(kind, t):
            step(it)

    def nothing():
        return None

    def paired(arrival, reply, layer, hooks=(nothing, nothing)):
        for m in range(2):
            arrival(layer, m)
            hooks[m]()
            reply(layer, m)

    def steps(*listed):
        def go():
            for body, *rest in listed:
                body(*rest)

        return go

    up, mid, down, last, out = step_up, step_mid, step_down, step_last, step_out
    wide, taps = 0, 1
    spread_first(wide, 0)
    spread_second(wide, 0)
    ready(wide, 0)
    first_part(0, 0)
    first_part(0, 1)
    own_n.wait()
    norm_wait(sc.n_r)
    spread_first(taps, 0)
    spread_first(taps, 1)
    paired(
        first_norm,
        hidden_one,
        0,
        (
            steps((spread_second, taps, 0), (spread_second, taps, 1)),
            steps((spread_first, wide, 1)),
        ),
    )
    ready(taps, 0)
    ready(taps, 1)
    paired(
        second_part,
        hidden_two,
        0,
        (steps((spread_first, wide, 2), (spread_second, wide, 1)), steps((spread_first, taps, 2))),
    )
    ready(wide, 1)

    def turn(layer, m):
        pre_values(0, m)
        if m == 0:
            ready(wide, 2)
        first_part(1, m)

    paired(
        third_part,
        turn,
        0,
        (
            steps((spread_second, wide, 2), (spread_first, taps, 3), (spread_second, taps, 2)),
            steps((spread_first, wide, 3)),
        ),
    )
    paired(
        first_norm,
        hidden_one,
        1,
        (steps((spread_second, taps, 3)), steps((spread_second, wide, 3))),
    )
    ready(taps, 2)
    ready(taps, 3)
    paired(second_part, hidden_two, 1)
    ready(wide, 3)
    third_part(1, 0)
    pre_values(1, 0)
    third_part(1, 1)
    grad_out_norm(1, 0)
    pre_values(1, 1)
    outs = [put_out(2, sc.mix.at[...], mixed_ref.at[...])]
    grad_out_norm(1, 1)
    wide_grad(3, lambda m: sc.gt[m], lambda m: ag_value(3, m))

    paired(
        grad_two,
        grad_second,
        1,
        (
            steps((pair_sum, "w", 3), (one, up, "w", 3, 0)),
            steps((one, up, "w", 3, 1), (one, mid, "w", 3, 0)),
        ),
    )
    taps_grad(1)
    paired(
        grad_one,
        grad_first,
        1,
        (
            steps(
                (pair_sum, "k", 1),
                (one, up, "k", 1, 0),
                (one, mid, "w", 3, 1),
                (one, down, "w", 3, 0),
            ),
            steps(
                (one, up, "k", 1, 1),
                (one, down, "w", 3, 1),
                (one, last, "w", 3, 0),
                (one, mid, "k", 1, 0),
            ),
        ),
    )

    def fold(layer, m):
        conv_grad(1, m)
        if m == 1:
            outs.append(put_out(3, sc.gp.at[0], gpre_ref.at[...]))

    paired(
        fold,
        grad_out_norm,
        0,
        (
            steps(
                (one, up, "k", 1, 2),
                (one, last, "w", 3, 1),
                (one, mid, "k", 1, 1),
                (one, down, "k", 1, 0),
            ),
            steps(
                (one, up, "k", 1, 3),
                (one, mid, "k", 1, 2),
                (one, down, "k", 1, 1),
                (one, last, "k", 1, 0),
            ),
        ),
    )
    wide_grad(2, lambda m: sc.s1[m], lambda m: ag_value(5, m))
    wide_grad(1, lambda m: sc.gt[m], lambda m: ag_value(2, m))
    paired(
        grad_two,
        grad_second,
        0,
        (
            steps(
                (pair_sum, "w", 2),
                (one, up, "w", 2, 0),
                (one, mid, "k", 1, 3),
                (one, down, "k", 1, 2),
                (one, last, "k", 1, 1),
            ),
            steps(
                (one, up, "w", 2, 1),
                (pair_sum, "w", 1),
                (one, mid, "w", 2, 0),
                (one, down, "k", 1, 3),
                (one, last, "k", 1, 2),
            ),
        ),
    )
    taps_grad(0)
    paired(
        grad_one,
        grad_first,
        0,
        (
            steps(
                (pair_sum, "k", 0),
                (one, up, "k", 0, 0),
                (one, mid, "w", 2, 1),
                (one, down, "w", 2, 0),
                (one, last, "k", 1, 3),
            ),
            steps(
                (one, up, "k", 0, 1),
                (one, up, "k", 0, 2),
                (one, up, "k", 0, 3),
                (one, mid, "k", 0, 0),
                (one, down, "w", 2, 1),
                (one, last, "w", 2, 0),
            ),
        ),
    )
    gains_start()
    one(mid, "k", 0, 1)
    one(down, "k", 0, 0)
    one(last, "w", 2, 1)
    conv_grad(0, 0)
    one(up, "w", 1, 0)
    one(mid, "k", 0, 2)
    one(down, "k", 0, 1)
    one(last, "k", 0, 0)
    run(out, "k", 1)
    conv_grad(0, 1)
    wide_grad(0, lambda m: x_ref[m], lambda m: ag_value(4, m))
    one(mid, "k", 0, 3)
    one(down, "k", 0, 2)
    one(last, "k", 0, 1)
    one(out, "k", 0, 0)
    outs.append(put_out(4, sc.cv.at[...], conv_ref.at[...]))
    pair_sum("w", 0)
    run(up, "w", 0)
    one(up, "w", 1, 1)
    one(mid, "w", 1, 0)
    one(down, "k", 0, 3)
    one(last, "k", 0, 2)
    one(out, "k", 0, 1)
    run(out, "w", 3)
    one(mid, "w", 0, 0)
    one(last, "k", 0, 3)
    one(out, "k", 0, 2)
    one(mid, "w", 0, 1)
    one(down, "w", 0, 0)
    one(mid, "w", 0, 2)
    one(down, "w", 1, 0)
    one(out, "k", 0, 3)
    one(down, "w", 0, 1)
    one(mid, "w", 0, 3)
    one(last, "w", 0, 0)
    one(mid, "w", 1, 1)
    one(down, "w", 0, 2)
    one(last, "w", 0, 1)
    one(last, "w", 1, 0)
    one(out, "w", 0, 0)
    one(down, "w", 0, 3)
    one(last, "w", 0, 2)
    one(out, "w", 0, 1)
    one(down, "w", 1, 1)
    one(last, "w", 0, 3)
    run(out, "w", 2)
    one(out, "w", 1, 0)
    one(out, "w", 0, 2)
    one(last, "w", 1, 1)
    one(out, "w", 0, 3)
    one(out, "w", 1, 1)
    gains_done()
    run(step_sibling, "w", 3)
    run(step_sibling, "k", 1)
    run(step_sibling, "k", 0)
    run(step_sibling, "w", 2)
    run(step_sibling, "w", 1)
    one(step_sibling, "w", 0, 0)
    one(step_sibling, "w", 0, 1)
    run(step_done, "k", 1)
    run(step_done, "k", 0)
    outs.append(put_out(1, sc.ok.at[...], gtaps_ref.at[...]))
    for s in (3, 2, 1):
        run(step_done, "w", s)
    final = of("w", 0)
    for group, part in enumerate((final[:-1], final[-1:]) if len(final) > 1 else (final,)):
        first, count = part[0].r0, sum(it.nr for it in part)
        for it in part:
            if it.i >= final[0].i + 2:
                step_sibling(it)
        for it in part:
            step_done(it)
        part_rows_of = pl.ds(first, count)
        outs.append(
            put_out(
                5 + group, sc.ow.at[:, :, part_rows_of], gwide_ref.at[:, :, part_rows_of]
            )
        )
    for copy in outs:
        copy.wait()
    for body in finish:
        body()


def cast_pieces(rows):
    pieces = [("taps", pl.ds(576 * i, 576)) for i in range(4)]
    pieces += [("wide", pl.ds(512 * i, 512)) for i in range(4)]
    return pieces + [("stream", m) for m in range(2)]


def cast_kernel(mixed, gpre, conv, gwide, gtaps, gmid, gout, *refs):
    o_mixed, o_input, o_wide, o_taps, o_mid, o_out = refs[:6]
    b_taps, b_wide, b_gpre, b_conv, f_taps, f_wide, f_stream = refs[6:13]
    b_mixed, b_mid, b_out, r_sem, w_sem, d_sem = refs[13:]
    pieces = cast_pieces(gpre.shape[1])
    same = ((mixed, b_mixed, o_mixed), (gmid, b_mid, o_mid), (gout, b_out, o_out))
    arrive = [pltpu.make_async_copy(a, b, d_sem.at[i]) for i, (a, b, _) in enumerate(same)]
    leave = [pltpu.make_async_copy(b, o, d_sem.at[i]) for i, (_, b, o) in enumerate(same)]
    reads, writes = [], []
    for i, (kind, part) in enumerate(pieces):
        if kind == "stream":
            reads.append(
                [
                    pltpu.make_async_copy(gpre.at[part], b_gpre.at[part], r_sem.at[i]),
                    pltpu.make_async_copy(conv.at[part], b_conv.at[part], r_sem.at[i + 2]),
                ]
            )
            writes.append(
                pltpu.make_async_copy(f_stream.at[part], o_input.at[part], w_sem.at[i])
            )
            continue
        src, low, high, dst = (
            (gtaps, b_taps, f_taps, o_taps)
            if kind == "taps"
            else (gwide, b_wide, f_wide, o_wide)
        )
        reads.append([pltpu.make_async_copy(src.at[part], low.at[part], r_sem.at[i])])
        writes.append(pltpu.make_async_copy(high.at[part], dst.at[part], w_sem.at[i]))
    for group in reads:
        for copy in group:
            copy.start()
    for copy in arrive:
        copy.start()
    for (kind, part), group, write in zip(pieces, reads, writes):
        for copy in group:
            copy.wait()
        size = 64

        def strip(i, carry, kind=kind, part=part):
            if kind == "stream":
                at = pl.ds(pl.multiple_of(i * size, size), size)
                f_stream[part, at] = b_gpre[part, at].astype(F32) + b_conv[part, at].astype(F32)
                return carry
            at = pl.ds(pl.multiple_of(part.start + i * size, size), size)
            if kind == "taps":
                f_taps[at] = b_taps[at].astype(F32)
            else:
                f_wide[at] = b_wide[at].astype(F32)
            return carry

        lax.fori_loop(0, (gpre.shape[1] if kind == "stream" else part.size) // size, strip, 0)
        write.start()
    for first, second in zip(arrive, leave):
        first.wait()
        second.start()
    for copy in writes + leave:
        copy.wait()


def cast_all(mixed, gpre, conv, gwide, gtaps, gmid, gout):
    anywhere = pl.BlockSpec(memory_space=pl.ANY)
    shape = jax.ShapeDtypeStruct
    count = len(cast_pieces(gpre.shape[1]))
    return pl.pallas_call(
        cast_kernel,
        in_specs=[anywhere] * 7,
        out_specs=[anywhere] * 6,
        out_shape=[
            shape(mixed.shape, BF16),
            shape(mixed.shape, F32),
            shape(gwide.shape, F32),
            shape(gtaps.shape, F32),
            shape(gmid.shape, F32),
            shape(gout.shape, F32),
        ],
        scratch_shapes=[
            pltpu.VMEM(gtaps.shape, BF16),
            pltpu.VMEM(gwide.shape, BF16),
            pltpu.VMEM(gpre.shape, BF16),
            pltpu.VMEM(gpre.shape, BF16),
            pltpu.VMEM(gtaps.shape, F32),
            pltpu.VMEM(gwide.shape, F32),
            pltpu.VMEM(gpre.shape, F32),
            pltpu.VMEM(mixed.shape, BF16),
            pltpu.VMEM(gmid.shape, F32),
            pltpu.VMEM(gout.shape, F32),
            pltpu.SemaphoreType.DMA((count + 2,)),
            pltpu.SemaphoreType.DMA((count,)),
            pltpu.SemaphoreType.DMA((3,)),
        ],
        compiler_params=pltpu.CompilerParams(vmem_limit_bytes=60 * 2**20),
        name="casts",
    )(mixed, gpre, conv, gwide, gtaps, gmid, gout)


def local(block_input, cotangent, weight_wide, weight_taps, norm_mid, norm_out, group_counts):
    n_dp = group_counts.shape[1]
    micro, rows, width = block_input.shape
    scratch = scratch_list(n_dp, rows)
    vmem = pl.BlockSpec(memory_space=pltpu.VMEM)
    anywhere = pl.BlockSpec(memory_space=pl.ANY)

    def shape(dims, dtype):
        return jax.ShapeDtypeStruct(dims, dtype)

    stream = (micro, rows, width)
    mixed, gpre, conv, gwide, gtaps, gmid, gout = pl.pallas_call(
        functools.partial(kernel, list(scratch), n_dp),
        out_shape=[
            shape(stream, BF16),
            shape(stream, BF16),
            shape(stream, BF16),
            shape((4, 2, 256, 512), BF16),
            shape((2304, 512), BF16),
            shape(norm_mid.shape, F32),
            shape(norm_out.shape, F32),
        ],
        in_specs=[vmem, vmem, anywhere, anywhere, vmem, vmem, anywhere],
        out_specs=[anywhere] * 5 + [vmem] * 2,
        scratch_shapes=list(scratch.values()),
        compiler_params=pltpu.CompilerParams(
            collective_id=0, has_side_effects=True, vmem_limit_bytes=62 * 2**20
        ),
        name="layers",
    )(block_input, cotangent, weight_wide, weight_taps.reshape(9, 256, 512), norm_mid, norm_out, jnp.swapaxes(group_counts, 1, 2))
    results = cast_all(mixed, gpre, conv, gwide.reshape(2048, 512), gtaps, gmid, gout)
    mixed, grad_input, gwide, gtaps, gmid, gout = results
    return (
        mixed,
        grad_input,
        gwide.reshape(weight_wide.shape),
        gtaps.reshape(weight_taps.shape),
        gmid,
        gout,
    )


def solution(mesh):
    split = P(None, "dp", "pipe")
    section = P("pipe", None, None)
    return jax.shard_map(
        local,
        mesh=mesh,
        in_specs=(split, split, section, section, section, section, P()),
        out_specs=(split, split, section, section, section, section),
        check_vma=False,
    )
```

```python
import functools
from types import SimpleNamespace

import jax
import jax.numpy as jnp
from jax import lax
from jax.experimental import pallas as pl
from jax.experimental.pallas import tpu as pltpu
from jax.sharding import PartitionSpec as P

MESH = pl.DeviceIdType.MESH
F32 = jnp.float32
BF16 = jnp.bfloat16
EPS = 1e-05
LANES = 128
N_PIPE = 4
SIDES = (7, 6, 5, 2)


def dot_nn(a, b):
    return jnp.dot(a, b, preferred_element_type=F32)


def dot_nt(a, b):
    return lax.dot_general(a, b, (((1,), (1,)), ((), ())), preferred_element_type=F32)


def sigmoid(v):
    return jax.nn.sigmoid(v)


def sizes(n_dp):
    n_z = n_dp // 2
    n_own = min(n_z, 16)
    return n_z, n_own


def gradient_items(n_dp):
    line = n_dp // 2 == 4
    listed = []
    for kind, index, parts in (
        ("w", 3, [128, 128]),
        ("k", 1, [576] * 4),
        ("w", 2, [128, 128]),
        ("w", 1, [128, 128]),
        ("k", 0, [576] * 4),
        ("w", 0, [64] * 4),
    ):
        start = 0
        for part, rows in enumerate(parts if line else [sum(parts)]):
            listed.append(
                SimpleNamespace(
                    kind=kind, t=index, r0=start, nr=rows, i=len(listed), part=part
                )
            )
            start += rows
    return listed


def scratch_list(n_dp, rows):
    n_z, n_own = sizes(n_dp)
    items = len(gradient_items(n_dp))
    line = n_z == 4
    dma = pltpu.SemaphoreType.DMA

    def half(*shape):
        return pltpu.VMEM(shape, BF16)

    def full(*shape):
        return pltpu.VMEM(shape, F32)

    return dict(
        wt=half(4, 512, 512),
        k2=half(2, 18, 256, 128),
        gm=full(4, 2, 128),
        go=full(4, 2, 2, 512),
        msk=full(2, rows, 128),
        beside=full(2, 2, rows, 128),
        above=full(2, 4, 2, rows, 128),
        yf=full(9, rows, 128),
        part=half(2, 2, 4, rows, 128),
        rsr=half(6, 2, 3, rows, 128),
        ag=half(6, 2, 4, rows, 128),
        stm=full(8, 2, n_dp, 2, 128),
        stw=full(4, 2, n_dp, 2, 512),
        midv=full(4, 2, rows, 128),
        dzm=full(2, rows, 128),
        inv_mid=full(4, 2, 1, 128),
        inv_wide=full(2, 2, 1, 512),
        widv=full(2, 2, rows, 512),
        pre0=full(2, rows, 512),
        s1=half(2, rows, 512),
        mix=half(2, rows, 512),
        gp=half(2, 2, rows, 512),
        cv=half(2, rows, 512),
        gt=half(2, rows, 512),
        gb=half(2, rows, 1152),
        tb=half(512, 2 * rows),
        dw=half(4, 2, 256, 512),
        prw=half(4, 256, 512),
        zsw=half(4, 256, 512),
        fzw=half(4, 256, 512),
        ow=half(4, 2, 256, 512),
        dk=half(2, 4608, 128),
        prk=half(2, 2304, 128),
        zsk=half(2, 2304, 128),
        fzk=half(2, 2304, 128),
        ok=half(2304, 512),
        zow=half(4, 256, 512) if line else half(4, n_z - 1, 256 // n_own, 512),
        ziw=half(4, 128, 512),
        zok=half(2, 2304, 128) if line else half(2, n_z - 1, 2304 // n_own, 128),
        zik=half(2, 1152, 128),
        gsm=full(4, 4, 2, 128),
        gsw=full(2, 4, 2, 512),
        cnt=pltpu.SMEM((2, n_dp), F32),
        xin=half(2, rows, 512),
        cin=half(2, rows, 512),
        gmo=full(1, 2, 512),
        goo=full(1, 2, 1024),
        counts=pltpu.SMEM((2, 4, n_dp), jnp.int32),
        f_s=dma((2,)),
        f_r=dma((2, 4)),
        z_r=dma((2, 4)),
        b_s=dma((2, 4)),
        b_r=dma((2, 4)),
        n_s=dma((2,)),
        n_r=dma((2,)),
        loc=dma((7,)),
        ex_s=dma((2, 2)),
        ex_r=dma((2, 2)),
        st_s=dma((2, 2)),
        st_r=dma((2, 2)),
        pw_s=dma((6,)),
        pw_r=dma((6,)),
        it_s=dma((items,)),
        one_r=dma((items,)),
        mid_r=dma((items,)),
        inn_r=dma((items,)),
        to_s=dma((items,)),
        to_r=dma((2, 5)),
        sib_s=dma((2, 5)),
        sib_r=dma((2, 5)),
        g_s=dma((2,)),
        g_r=dma((2,)),
        out=dma((8,)),
    )


def kernel(names, n, *refs):
    (x_hbm, cot_hbm, wide_ref, taps_ref, nmid_ref, nout_ref, counts_hbm) = refs[:7]
    (mixed_ref, gpre_ref, conv_ref, gwide_ref, gtaps_ref, gmid_ref, gout_ref) = refs[7:14]
    sc = SimpleNamespace(**dict(zip(names, refs[14:])))
    counts_ref = sc.counts
    x_ref, cot_ref = sc.xin, sc.cin
    rows = x_ref.shape[1]
    n_z, n_own = sizes(n)
    p = lax.axis_index("pipe")
    d = lax.axis_index("dp")
    z = lax.div(d, 2)
    c = lax.rem(d, 2)
    parity = lax.rem(p, 2)
    sibling = (p, 2 * z + 1 - c)
    z_odd = lax.rem(z, 2)
    z_pair = (p, 2 * (z + 1 - 2 * z_odd) + c)
    quarter = 2 * z_odd + c
    quarter_z = 2 * (1 - z_odd) + c
    finish = []

    def pipe_at(off):
        return lax.rem(p + N_PIPE + (2 * parity - 1) * off, N_PIPE)

    def remote(src, dst, ss, rs, dev):
        return pltpu.make_async_remote_copy(
            src_ref=src, dst_ref=dst, send_sem=ss, recv_sem=rs, device_id=dev, device_id_type=MESH
        )

    def each(count, first, body):
        if count - first <= 8:
            for k in range(first, count):
                body(k)
        else:

            def step(k, carry):
                body(k)
                return carry

            lax.fori_loop(first, count, step, 0)

    def bytes_wait(view, sem):
        pltpu.make_async_copy(view, view, sem).wait()

    barrier = pltpu.get_barrier_semaphore()
    for off in range(1, N_PIPE):
        pl.semaphore_signal(barrier, inc=1, device_id=(pipe_at(off), d), device_id_type=MESH)

    def greet(k):
        pl.semaphore_signal(
            barrier, inc=1, device_id=(p, lax.rem(d + k, n)), device_id_type=MESH
        )

    each(n, 1, greet)

    def columns_of(q):
        return pl.ds(pl.multiple_of(128 * q, 128), 128)

    own_w = pltpu.make_async_copy(
        wide_ref.at[0, pl.ds(pl.multiple_of(512 * p, 512), 512), :], sc.wt.at[p], sc.loc.at[0]
    )
    own_k = pltpu.make_async_copy(
        taps_ref.at[:, :, columns_of(p)],
        sc.k2.at[lax.div(p, 2), pl.ds(9 * parity, 9)],
        sc.loc.at[1],
    )
    own_c = pltpu.make_async_copy(counts_hbm, counts_ref, sc.loc.at[2])
    own_c.start()
    own_x = pltpu.make_async_copy(x_hbm, sc.xin, sc.loc.at[4])
    own_cot = pltpu.make_async_copy(cot_hbm, sc.cin, sc.loc.at[5])
    own_x.start()
    own_w.start()
    own_k.start()
    own_n = pltpu.make_async_copy(
        nmid_ref.at[0, :, columns_of(p)], sc.gm.at[p], sc.loc.at[3]
    )
    own_n.start()
    for e in range(2):
        pltpu.make_async_copy(
            nout_ref.at[0, :, pl.ds(512 * e, 512)], sc.go.at[p, e], sc.loc.at[6]
        ).start()
    own_cot.start()

    own_c.wait()

    def used_rows(m, j):
        return (
            49 * counts_ref[m, 0, j]
            + 36 * counts_ref[m, 1, j]
            + 25 * counts_ref[m, 2, j]
            + 4 * counts_ref[m, 3, j]
        )

    totals = []
    for m in range(2):

        def count_up(j, acc, m=m):
            used = used_rows(m, j)
            sc.cnt[m, j] = used.astype(F32)
            return acc + used

        totals.append(lax.fori_loop(0, n, count_up, jnp.int32(0)).astype(F32))

    pl.semaphore_wait(barrier, N_PIPE - 1 + n - 1)

    def held(kind, s, part):
        if kind == 0:
            return sc.wt.at[s, pl.ds(pl.multiple_of(128 * part, 128), 128)]
        layer, odd = (s // 2, s % 2) if isinstance(s, int) else (lax.div(s, 2), lax.rem(s, 2))
        return sc.k2.at[
            layer, pl.ds(9 * odd, 9), pl.ds(pl.multiple_of(64 * part, 64), 64)
        ]

    def fetch(kind, off):
        q = pipe_at(off)
        if kind == 0:
            src = wide_ref.at[0, pl.ds(pl.multiple_of(512 * q + 128 * quarter, 128), 128), :]
        else:
            src = taps_ref.at[:, pl.ds(pl.multiple_of(64 * quarter, 64), 64), columns_of(q)]
        return remote(
            src, held(kind, p, quarter), sc.f_s.at[kind], sc.f_r.at[kind, p], (q, d)
        )

    def send_norm(off):
        q = pipe_at(off)
        listed = [
            remote(
                nmid_ref.at[0, :, columns_of(q)],
                sc.gm.at[p],
                sc.n_s.at[0],
                sc.n_r.at[0],
                (q, d),
            )
        ]
        for e in range(2):
            listed.append(
                remote(
                    nout_ref.at[0, :, pl.ds(512 * e, 512)],
                    sc.go.at[p, e],
                    sc.n_s.at[1],
                    sc.n_r.at[1],
                    (q, d),
                )
            )
        return listed

    def norm_wait(sems):
        bytes_wait(sc.gm.at[pl.ds(0, 3)], sems.at[0])
        bytes_wait(sc.go.at[pl.ds(0, 3)], sems.at[1])

    def pass_z(kind, s):
        view = held(kind, s, quarter)
        return remote(view, view, sc.b_s.at[kind, s], sc.z_r.at[kind, s], z_pair)

    def pass_sibling(kind, s, e):
        view = held(kind, s, quarter if e == 0 else quarter_z)
        return remote(view, view, sc.b_s.at[kind, s], sc.b_r.at[kind, s], sibling)

    def spread_first(kind, s):
        @pl.when(p != s)
        def _():
            view = held(kind, s, quarter)
            bytes_wait(view, sc.f_r.at[kind, s])
            pass_z(kind, s).start()
            pass_sibling(kind, s, 0).start()

    def spread_second(kind, s):
        @pl.when(p != s)
        def _():
            pass_z(kind, s).wait_recv()
            pass_sibling(kind, s, 1).start()

    def quarters(kind, s, count):
        if kind == 0:
            return sc.wt.at[s, pl.ds(0, 128 * count)]
        return sc.k2.at[s // 2, pl.ds(9 * (s % 2), 9), pl.ds(0, 64 * count)]

    def ready(kind, s):
        @pl.when(p != s)
        def _():
            bytes_wait(quarters(kind, s, 2), sc.b_r.at[kind, s])

        @pl.when(p == s)
        def _():
            (own_w if kind == 0 else own_k).wait()

    def finish_weights():
        for kind in range(2):
            bytes_wait(quarters(kind, 0, 3), sc.f_s.at[kind])
            for s in range(4):

                @pl.when(p != s)
                def _(kind=kind, s=s):
                    bytes_wait(quarters(kind, s, 3), sc.b_s.at[kind, s])

    finish.append(finish_weights)

    for even in range(2):

        @pl.when(parity == even)
        def _(even=even):
            for kind in (even, 1 - even):
                for off in range(1, 4):
                    fetch(kind, off).start()
                if kind == even:
                    for off in range(1, 4):
                        for copy in send_norm(off):
                            copy.start()

    def finish_norm():
        norm_wait(sc.n_s)

    finish.append(finish_norm)

    row_id = lax.broadcasted_iota(jnp.int32, (rows, LANES), 0).astype(F32)

    def build(m):
        ends = [jnp.float32(0.0)]
        total = jnp.int32(0)
        for g, side in enumerate(SIDES):
            total = total + side * side * counts_ref[m, g, d]
            ends.append(total.astype(F32))
        sc.msk[m] = jnp.where(row_id < ends[4], 1.0, 0.0)
        left = jnp.zeros((rows, LANES), F32)
        right = left
        for g, side in enumerate(SIDES):
            inside = (row_id >= ends[g]) & (row_id < ends[g + 1])
            within = row_id - ends[g]
            within = within - side * side * jnp.floor((within + 0.5) / (side * side))
            map_row = jnp.floor((within + 0.5) / side)
            map_col = within - side * map_row
            left = jnp.where(inside & (map_col > 0.5), 1.0, left)
            right = jnp.where(inside & (map_col < side - 1.5), 1.0, right)
            sc.above[m, g, 0] = jnp.where(inside & (map_row > 0.5), 1.0, 0.0)
            sc.above[m, g, 1] = jnp.where(inside & (map_row < side - 1.5), 1.0, 0.0)
        sc.beside[m, 0] = left
        sc.beside[m, 1] = right

    def shifted(values, count):
        return pltpu.roll(values, count % rows, 0)

    def from_above(values, m):
        return sum(
            sc.above[m, g, 0] * shifted(values, side) for g, side in enumerate(SIDES)
        )

    def from_below(values, m):
        return sum(
            sc.above[m, g, 1] * shifted(values, -side) for g, side in enumerate(SIDES)
        )

    for m in range(2):
        build(m)


    exchange_order = [
        ("rs", 0), ("ag", 0), ("ag", 2), ("rs", 1), ("ag", 1), ("ag", 3),
        ("rs", 3), ("rs", 5), ("ag", 5), ("rs", 2), ("rs", 4), ("ag", 4),
    ]

    def three(kind, i, m):
        return sc.rsr.at[i, m] if kind == "rs" else sc.ag.at[i, m, pl.ds(0, 3)]

    def exchange_wait(sems, kind, i, m):
        turn = exchange_order.index((kind, i))
        bytes_wait(three(kind, i, m), sems.at[turn % 2, m])

    def exchange_open(kind, i, m):
        turn = exchange_order.index((kind, i))
        if turn >= 2:
            exchange_wait(sc.ex_s, *exchange_order[turn - 2], m)
        return sc.ex_s.at[turn % 2, m], sc.ex_r.at[turn % 2, m]

    def rs_sum(rid, m, par):
        exchange_wait(sc.ex_r, "rs", rid, m)
        total = sc.part[par, m, p].astype(F32)
        for k in range(3):
            total = total + sc.rsr[rid, m, k].astype(F32)
        return total

    def ag_start(aid, m, value):
        ss, rs = exchange_open("ag", aid, m)
        sc.ag[aid, m, p] = value
        own = sc.ag.at[aid, m, p]
        for off in range(1, 4):
            remote(own, own, ss, rs, (pipe_at(off), d)).start()

    def ag_wait(aid, m):
        exchange_wait(sc.ex_r, "ag", aid, m)

    def ag_value(aid, m):
        return jnp.concatenate([sc.ag[aid, m, q] for q in range(4)], axis=1)

    def finish_exchanges():
        for kind, i in exchange_order[-2:]:
            for m in range(2):
                exchange_wait(sc.ex_s, kind, i, m)

    finish.append(finish_exchanges)

    sum_order = [
        (False, 0), (False, 1), (True, 0), (False, 2), (False, 3), (True, 1),
        (True, 3), (False, 7), (False, 6), (True, 2), (False, 5), (False, 4),
    ]

    def st_buffer(wide, i, m):
        return (sc.stw if wide else sc.stm).at[i, m]

    def st_bytes(sems, wide, i, m):
        turn = sum_order.index((wide, i))
        bytes_wait(st_buffer(wide, i, m).at[pl.ds(0, n - 1)], sems.at[turn % 2, m])

    def st_start(wide, i, m):
        turn = sum_order.index((wide, i))
        if turn >= 2:
            st_bytes(sc.st_s, *sum_order[turn - 2], m)
        own = st_buffer(wide, i, m).at[d]
        ss, rs = sc.st_s.at[turn % 2, m], sc.st_r.at[turn % 2, m]

        def go(k):
            remote(own, own, ss, rs, (p, lax.rem(d + k, n))).start()

        if n > 8:
            each(n, 1, go)
            return
        high = lax.div(2 * z, n_z)
        for i in range(n_z - 1):
            low_far = n_z - 1 - i - lax.div(z + i + 1, n_z)
            high_far = i + lax.div(i - z + n_z, n_z)
            far = high * high_far + (1 - high) * low_far
            for e in range(2):
                remote(own, own, ss, rs, (p, 2 * far + e)).start()
        remote(own, own, ss, rs, sibling).start()

    def st_wait(wide, i, m):
        st_bytes(sc.st_r, wide, i, m)

    def finish_st():
        for wide, i in sum_order[-2:]:
            for m in range(2):
                st_bytes(sc.st_s, wide, i, m)

    finish.append(finish_st)

    def over_devices(body, init):
        if n <= 8:
            for j in range(n):
                init = body(j, init)
            return init
        return lax.fori_loop(0, n, body, init)

    def combine(wide, i, m):
        st_wait(wide, i, m)
        ref = sc.stw if wide else sc.stm
        blank = jnp.zeros((1, ref.shape[-1]), F32)
        mean = over_devices(
            lambda j, acc: acc + sc.cnt[m, j] * ref[i, m, j, 0:1, :], blank
        )
        mean = mean / totals[m]

        def spread(j, acc):
            gap = ref[i, m, j, 0:1, :] - mean
            return acc + ref[i, m, j, 1:2, :] + sc.cnt[m, j] * (gap * gap)

        var = over_devices(spread, blank) / totals[m]
        return mean, lax.rsqrt(var + EPS)

    def back_sums(wide, i, m):
        st_wait(wide, i, m)
        ref = sc.stw if wide else sc.stm
        return over_devices(
            lambda j, acc: acc + ref[i, m, j], jnp.zeros((2, ref.shape[-1]), F32)
        )

    def local_moments(v, m):
        mask = sc.msk[m]
        own = jnp.maximum(sc.cnt[m, d], 1.0)
        mean = jnp.sum(v * mask, 0, keepdims=True) / own
        gap = (v - mean) * mask
        return jnp.concatenate([mean, jnp.sum(gap * gap, 0, keepdims=True)], 0)

    def local_sums(dz, vhat):
        return jnp.concatenate(
            [jnp.sum(dz * vhat, 0, keepdims=True), jnp.sum(dz, 0, keepdims=True)], 0
        )

    def lanes(j):
        return slice(LANES * j, LANES * (j + 1))

    def stream(layer, m):
        return x_ref[m] if layer == 0 else sc.s1[m]

    def stream_part(layer, m, j):
        return (x_ref[m, :, lanes(j)] if layer == 0 else sc.s1[m, :, lanes(j)]).astype(F32)

    rs_par = {0: 0, 1: 1, 3: 0, 5: 1, 2: 0, 4: 1}

    def rs_send(rid, m, values):
        par = rs_par[rid]
        ss, rs = exchange_open("rs", rid, m)
        for j, value in enumerate(values):
            half = value.astype(BF16)
            sc.part[par, m, 2 * j] = half[:, :LANES]
            sc.part[par, m, 2 * j + 1] = half[:, LANES:]
        for off in range(1, 4):
            q = pipe_at(off)
            remote(sc.part.at[par, m, q], sc.rsr.at[rid, m, off - 1], ss, rs, (q, d)).start()

    def first_part(layer, m):
        s = stream(layer, m)
        rs_send(
            layer,
            m,
            [dot_nn(s, sc.wt[2 * layer, :, 256 * j : 256 * j + 256]) for j in range(2)],
        )

    def mid_moments(i, m, v):
        sc.midv[i, m] = v
        sc.stm[i, m, d] = local_moments(v, m)
        st_start(False, i, m)

    def first_norm(layer, m):
        mid_moments(2 * layer, m, rs_sum(layer, m, rs_par[layer]))

    def mid_hidden(i, m):
        mean, inv = combine(False, i, m)
        sc.inv_mid[i, m] = inv
        vhat = (sc.midv[i, m] - mean) * inv
        sc.midv[i, m] = vhat
        u = sc.gm[i, 0:1, :] * vhat + sc.gm[i, 1:2, :]
        return (sc.msk[m] * (u * sigmoid(u))).astype(BF16)

    def hidden_one(layer, m):
        ag_start(layer, m, mid_hidden(2 * layer, m))

    def taps_of(layer, taps):
        return jnp.concatenate(
            [
                jnp.concatenate([sc.k2[layer, 2 * k], sc.k2[layer, 2 * k + 1]], axis=0)
                for k in taps
            ],
            axis=1,
        )

    def second_part(layer, m):
        ag_wait(layer, m)
        h = ag_value(layer, m)
        for j in range(5):
            width = 256 if j < 4 else 128
            y = dot_nn(h, taps_of(layer, [2 * j + e for e in range(width // LANES)]))
            for e in range(width // LANES):
                sc.yf[2 * j + e] = y[:, lanes(e)]

        def across(k):
            return (
                sc.yf[k + 1]
                + sc.beside[m, 0] * shifted(sc.yf[k], 1)
                + sc.beside[m, 1] * shifted(sc.yf[k + 2], -1)
            )

        total = across(3) + from_above(across(0), m) + from_below(across(6), m)
        mid_moments(2 * layer + 1, m, total)

    def hidden_two(layer, m):
        ag_start(2 + layer, m, mid_hidden(2 * layer + 1, m))

    def third_part(layer, m):
        ag_wait(2 + layer, m)
        h = ag_value(2 + layer, m)
        for j in range(2):
            sc.widv[layer, m, :, 256 * j : 256 * j + 256] = dot_nt(
                h, sc.wt[2 * layer + 1, 256 * j : 256 * j + 256, :]
            )
        for j in range(4):
            sc.stw[layer, m, d, :, lanes(j)] = local_moments(sc.widv[layer, m, :, lanes(j)], m)
        st_start(True, layer, m)

    def out_gain(layer, j):
        both = sc.go[2 * layer + lax.div(p, 2), lax.rem(p, 2)]
        return both[0:1, lanes(j)], both[1:2, lanes(j)]

    def pre_values(layer, m):
        mean, inv = combine(True, layer, m)
        sc.inv_wide[layer, m] = inv
        mask = sc.msk[m]
        for j in range(4):
            gain, bias = out_gain(layer, j)
            vhat = (sc.widv[layer, m, :, lanes(j)] - mean[:, lanes(j)]) * inv[:, lanes(j)]
            sc.widv[layer, m, :, lanes(j)] = vhat
            pre = gain * vhat + bias + stream_part(layer, m, j)
            sig = sigmoid(pre)
            out = (mask * (pre * sig)).astype(BF16)
            if layer == 0:
                sc.pre0[m, :, lanes(j)] = pre
                sc.s1[m, :, lanes(j)] = out
            else:
                sc.mix[m, :, lanes(j)] = out
                slope = sig * (1.0 + pre * (1.0 - sig))
                grad = (cot_ref[m, :, lanes(j)].astype(F32) * mask * slope).astype(BF16)
                sc.gp[1, m, :, lanes(j)] = grad
                sc.stw[3, m, d, :, lanes(j)] = local_sums(grad.astype(F32), vhat)
        if layer == 1:
            st_start(True, 3, m)

    def put_out(k, src, dst):
        copy = pltpu.make_async_copy(src, dst, sc.out.at[k])
        copy.start()
        return copy

    def grad_out_norm(layer, m):
        sums = back_sums(True, 2 + layer, m)
        if m == 0:
            sc.gsw[layer, p] = sums
        else:
            sc.gsw[layer, p] = sc.gsw[layer, p] + sums
        mask = sc.msk[m]
        inv = sc.inv_wide[layer, m]
        for j in range(4):
            gain, _ = out_gain(layer, j)
            dz = sc.gp[layer, m, :, lanes(j)].astype(F32)
            vhat = sc.widv[layer, m, :, lanes(j)]
            s1 = sums[0:1, lanes(j)] / totals[m]
            s0 = sums[1:2, lanes(j)] / totals[m]
            dv = mask * (gain * inv[:, lanes(j)]) * (dz - s0 - vhat * s1)
            sc.gt[m, :, lanes(j)] = dv.astype(BF16)
        g = sc.gt[m]
        rs_send(
            2 + layer,
            m,
            [dot_nn(g, sc.wt[2 * layer + 1, :, 256 * j : 256 * j + 256]) for j in range(2)],
        )

    def mid_grad(i, m, upstream):
        vhat = sc.midv[i, m]
        u = sc.gm[i, 0:1, :] * vhat + sc.gm[i, 1:2, :]
        sig = sigmoid(u)
        dz = upstream * sc.msk[m] * (sig * (1.0 + u * (1.0 - sig)))
        sc.dzm[m] = dz
        sc.stm[4 + i, m, d] = local_sums(dz, vhat)
        st_start(False, 4 + i, m)

    def mid_back(i, m):
        sums = back_sums(False, 4 + i, m)
        if m == 0:
            sc.gsm[i, p] = sums
        else:
            sc.gsm[i, p] = sc.gsm[i, p] + sums
        s1 = sums[0:1, :] / totals[m]
        s0 = sums[1:2, :] / totals[m]
        scale = sc.gm[i, 0:1, :] * sc.inv_mid[i, m]
        return (sc.msk[m] * scale * (sc.dzm[m] - s0 - sc.midv[i, m] * s1)).astype(BF16)

    def grad_two(layer, m):
        mid_grad(2 * layer + 1, m, rs_sum(2 + layer, m, rs_par[2 + layer]))

    def grad_second(layer, m):
        gs = mid_back(2 * layer + 1, m)
        own = gs.astype(F32)
        for du, moved in ((0, own), (1, from_above(own, m)), (-1, from_below(own, m))):
            k = 3 * (du + 1)
            sc.gb[m, :, lanes(k + 1)] = moved.astype(BF16)
            sc.gb[m, :, lanes(k + 2)] = (sc.beside[m, 0] * shifted(moved, 1)).astype(BF16)
            sc.gb[m, :, lanes(k)] = (sc.beside[m, 1] * shifted(moved, -1)).astype(BF16)
        g = sc.gb[m]
        rs_send(
            4 + layer,
            m,
            [
                dot_nt(
                    g, jnp.concatenate([sc.k2[layer, 2 * k + j] for k in range(9)], axis=1)
                )
                for j in range(2)
            ],
        )

    def grad_one(layer, m):
        mid_grad(2 * layer, m, rs_sum(4 + layer, m, rs_par[4 + layer]))

    def grad_first(layer, m):
        ag_start(4 + layer, m, mid_back(2 * layer, m))

    def conv_grad(layer, m):
        ag_wait(4 + layer, m)
        g = ag_value(4 + layer, m)
        mask = sc.msk[m]
        for j in range(2):
            r = dot_nt(g, sc.wt[2 * layer, 256 * j : 256 * j + 256, :]).astype(BF16)
            if layer == 0:
                sc.cv[m, :, 256 * j : 256 * j + 256] = r
                continue
            for e in range(2):
                i = 2 * j + e
                pre = sc.pre0[m, :, lanes(i)]
                sig = sigmoid(pre)
                slope = sig * (1.0 + pre * (1.0 - sig))
                up = sc.gp[1, m, :, lanes(i)].astype(F32) + r[:, lanes(e)].astype(F32)
                grad = (up * mask * slope).astype(BF16)
                sc.gp[0, m, :, lanes(i)] = grad
                sc.stw[2, m, d, :, lanes(i)] = local_sums(
                    grad.astype(F32), sc.widv[0, m, :, lanes(i)]
                )
        if layer == 1:
            st_start(True, 2, m)

    def turned(blocks):
        for m, block in enumerate(blocks):
            sc.tb[:, rows * m : rows * (m + 1)] = block.T

    def both(get):
        return jnp.concatenate([get(0), get(1)], axis=0)

    def wide_grad(s, left, right):
        turned([left(0), left(1)])
        for j in range(2):
            cols = slice(256 * j, 256 * j + 256)
            rhs = both(lambda m: right(m)[:, cols])
            for h in range(2):
                r = dot_nn(sc.tb[256 * h : 256 * h + 256, :], rhs)
                sc.dw[s, h, :, cols] = r.astype(BF16)
        pair_copy("w", s).start()

    def taps_grad(layer):
        turned([ag_value(layer, 0), ag_value(layer, 1)])
        for j in range(5):
            width = 256 if j < 4 else 128
            rhs = both(lambda m: sc.gb[m, :, 256 * j : 256 * j + width])
            r = dot_nn(sc.tb[...], rhs).astype(BF16)
            for e in range(width // LANES):
                tap = 2 * j + e
                sc.dk[layer, 512 * tap : 512 * tap + 512, :] = r[:, lanes(e)]
        pair_copy("k", layer).start()

    def half_rows(which):
        return pl.ds(pl.multiple_of(2304 * which, 2304), 2304)

    def pair_copy(kind, t):
        if kind == "w":
            src, dst, i = sc.dw.at[t, 1 - c], sc.prw.at[t], t
        else:
            src, dst, i = sc.dk.at[t, half_rows(1 - c)], sc.prk.at[t], 4 + t
        return remote(src, dst, sc.pw_s.at[i], sc.pw_r.at[i], sibling)

    def pair_sum(kind, t):
        pair_copy(kind, t).wait_recv()
        if kind == "w":
            sc.zsw[t] = (sc.dw[t, c].astype(F32) + sc.prw[t].astype(F32)).astype(BF16)
            return
        for i in range(4):
            part = slice(576 * i, 576 * i + 576)
            mine = pl.ds(pl.multiple_of(2304 * c + 576 * i, 576), 576)
            sc.zsk[t, part] = (
                sc.dk[t, mine].astype(F32) + sc.prk[t, part].astype(F32)
            ).astype(BF16)

    items = gradient_items(n)
    line = n_z == 4
    inner = (z == 1) | (z == 2)

    def tile(it, name):
        return getattr(sc, name + it.kind)

    def some(it, name, start, count):
        return tile(it, name).at[it.t, pl.ds(start, count)]

    def part_rows(it, which):
        half = it.nr // 2
        return pl.ds(pl.multiple_of(it.r0 + half * which, half), half)

    def up_copy(it):
        rows_of = pl.ds(it.r0, it.nr)
        return remote(
            tile(it, "zs").at[it.t, rows_of],
            tile(it, "zo").at[it.t, rows_of],
            sc.it_s.at[it.i],
            sc.one_r.at[it.i],
            (p, 2 * (1 + lax.div(z, 3)) + c),
        )

    def mid_copy(it):
        return remote(
            tile(it, "zs").at[it.t, part_rows(it, 2 - z)],
            tile(it, "zi").at[it.t, pl.ds(it.r0 // 2, it.nr // 2)],
            sc.it_s.at[it.i],
            sc.mid_r.at[it.i],
            (p, 2 * (3 - z) + c),
        )

    def inn_copy(it):
        view = tile(it, "fz").at[it.t, part_rows(it, z - 1)]
        return remote(
            view, view, sc.it_s.at[it.i], sc.inn_r.at[it.i], (p, 2 * (3 - z) + c)
        )

    def down_copy(it, e):
        view = tile(it, "fz").at[it.t, part_rows(it, z - 1 if e == 0 else 2 - z)]
        return remote(
            view, view, sc.it_s.at[it.i], sc.one_r.at[it.i], (p, 2 * (3 * (z - 1)) + c)
        )

    def direct_rows(it, j):
        count = it.nr // n_own
        return pl.ds(pl.multiple_of(it.r0 + count * j, count), count)

    def owner(index, body):
        if n_own == n_z:
            body()
        else:
            pl.when(index < n_own)(body)

    def scatter_copy(it, k):
        j = lax.rem(z + k, n_z)
        return j, remote(
            tile(it, "zs").at[it.t, direct_rows(it, lax.rem(j, n_own))],
            tile(it, "zo").at[it.t, k - 1],
            sc.it_s.at[it.i],
            sc.one_r.at[it.i],
            (p, 2 * j + c),
        )

    def gather_copy(it, k):
        j = lax.rem(z + k, n_z)
        view = tile(it, "fz").at[it.t, direct_rows(it, lax.rem(z, n_own))]
        return remote(view, view, sc.to_s.at[it.i], sc.mid_r.at[it.i], (p, 2 * j + c))

    def add_rows(target, first, second):
        target[...] = (first[...].astype(F32) + second[...].astype(F32)).astype(BF16)

    def step_up(it):
        if line:

            @pl.when((z == 0) | (z == 3))
            def _():
                up_copy(it).start()

        else:

            def go(k):
                j, copy = scatter_copy(it, k)
                owner(j, lambda: copy.start())

            each(n_z, 1, go)

    def step_mid(it):
        if not line:
            return

        @pl.when(inner)
        def _():
            up_copy(it).wait_recv()
            mine = some(it, "zs", it.r0, it.nr)
            add_rows(mine, mine, some(it, "zo", it.r0, it.nr))
            mid_copy(it).start()

    def step_down(it):
        if line:

            @pl.when(inner)
            def _():
                mid_copy(it).wait_recv()
                keep = part_rows(it, z - 1)
                add_rows(
                    tile(it, "fz").at[it.t, keep],
                    tile(it, "zs").at[it.t, keep],
                    some(it, "zi", it.r0 // 2, it.nr // 2),
                )
                inn_copy(it).start()
                down_copy(it, 0).start()

            return

        def go():
            bytes_wait(tile(it, "zo").at[it.t], sc.one_r.at[it.i])
            mine = direct_rows(it, z)
            total = tile(it, "zs")[it.t, mine].astype(F32)
            total = lax.fori_loop(
                0, n_z - 1, lambda k, acc: acc + tile(it, "zo")[it.t, k].astype(F32), total
            )
            tile(it, "fz")[it.t, mine] = total.astype(BF16)
            each(n_z, 1, lambda k: gather_copy(it, k).start())

        owner(z, go)

    def step_last(it):
        if not line:
            return

        @pl.when(inner)
        def _():
            inn_copy(it).wait_recv()
            down_copy(it, 1).start()

    def owner_of(it):
        return it.t if it.kind == "w" else 2 * it.t + c

    def landing(it, q, core):
        if it.kind == "w":
            return sc.ow.at[q, core, pl.ds(it.r0, it.nr)]
        lane = pl.ds(128 * q, 128) if isinstance(q, int) else columns_of(q)
        return sc.ok.at[pl.ds(it.r0, it.nr), lane]

    def to_sem(it, sems):
        return sems.at[0 if it.kind == "w" else 1, it.part]

    def to_copy(it):
        return remote(
            some(it, "fz", it.r0, it.nr),
            landing(it, p, c),
            sc.to_s.at[it.i],
            to_sem(it, sc.to_r),
            (owner_of(it), d),
        )

    def step_out(it):
        if line:

            @pl.when((z == 0) | (z == 3))
            def _():
                bytes_wait(some(it, "fz", it.r0, it.nr), sc.one_r.at[it.i])

        else:
            count = it.nr // n_own
            if n_own == n_z:
                bytes_wait(some(it, "fz", it.r0, count * (n_own - 1)), sc.mid_r.at[it.i])
            else:

                @pl.when(z < n_own)
                def _():
                    bytes_wait(some(it, "fz", it.r0, count * (n_own - 1)), sc.mid_r.at[it.i])

                @pl.when(z >= n_own)
                def _():
                    bytes_wait(some(it, "fz", it.r0, count * n_own), sc.mid_r.at[it.i])

        @pl.when(p != owner_of(it))
        def _():
            to_copy(it).start()

        def place(q):
            landing(it, q, c)[...] = some(it, "fz", it.r0, it.nr)[...]

        if it.kind == "w":
            pl.when(p == it.t)(lambda: place(it.t))
        else:
            for core in range(2):
                pl.when((p == 2 * it.t + core) & (c == core))(
                    functools.partial(place, 2 * it.t + core)
                )

    def sibling_copy(it, q):
        view = landing(it, q, c)
        return remote(
            view, view, to_sem(it, sc.sib_s), to_sem(it, sc.sib_r), sibling
        )

    def slices(it, count):
        if it.kind == "w":
            return sc.ow.at[pl.ds(0, count), 0, pl.ds(it.r0, it.nr)]
        return sc.ok.at[pl.ds(it.r0, it.nr), pl.ds(0, 128 * count)]

    def step_sibling(it):
        def go():
            bytes_wait(slices(it, 3), to_sem(it, sc.to_r))
            for q in range(4):
                sibling_copy(it, q).start()

        pl.when(p == owner_of(it))(go)

    def step_done(it):
        def go():
            bytes_wait(slices(it, 4), to_sem(it, sc.sib_r))

        pl.when(p == (it.t if it.kind == "w" else 2 * it.t + 1 - c))(go)

    def twice(it):
        if it.kind == "w":
            return sc.dw.at[it.t, :, pl.ds(0, it.nr)]
        return sc.dk.at[it.t, pl.ds(0, 2 * it.nr)]

    def finish_grads():
        for kind, t in [("w", s) for s in range(4)] + [("k", layer) for layer in range(2)]:
            pair_copy(kind, t).wait_send()
        for it in items:
            if line:

                @pl.when(inner)
                def _(it=it):
                    bytes_wait(twice(it), sc.it_s.at[it.i])

                @pl.when((z == 0) | (z == 3))
                def _(it=it):
                    up_copy(it).wait_send()

            else:

                def sent(k, it=it):
                    j, copy = scatter_copy(it, k)
                    owner(j, lambda: copy.wait_send())

                each(n_z, 1, sent)
                owner(z, lambda: each(n_z, 1, lambda k: gather_copy(it, k).wait_send()))

            @pl.when(p != owner_of(it))
            def _(it=it):
                to_copy(it).wait_send()

            @pl.when(p == owner_of(it))
            def _(it=it):
                bytes_wait(slices(it, 4), to_sem(it, sc.sib_s))

    finish.append(finish_grads)

    def gain_copies(off):
        dev = (pipe_at(off), d)
        return [
            remote(sc.gsm.at[:, p], sc.gsm.at[:, p], sc.g_s.at[0], sc.g_r.at[0], dev),
            remote(sc.gsw.at[:, p], sc.gsw.at[:, p], sc.g_s.at[1], sc.g_r.at[1], dev),
        ]

    def gains_wait(sems):
        bytes_wait(sc.gsm.at[:, pl.ds(0, 3)], sems.at[0])
        bytes_wait(sc.gsw.at[:, pl.ds(0, 3)], sems.at[1])

    def gains_start():
        for off in range(1, 4):
            for copy in gain_copies(off):
                copy.start()

    def gains_done():
        gains_wait(sc.g_r)
        for q in range(4):
            sc.gmo[0, :, lanes(q)] = sc.gsm[p, q]
        layer = lax.div(p, 2)
        for e in range(2):
            sc.goo[0, :, 512 * e : 512 * e + 512] = sc.gsw[layer, 2 * parity + e]
        outs.append(put_out(0, sc.gmo.at[...], gmid_ref.at[...]))
        outs.append(put_out(7, sc.goo.at[...], gout_ref.at[...]))

    def finish_gains():
        gains_wait(sc.g_s)

    finish.append(finish_gains)

    def of(kind, t):
        return [it for it in items if it.kind == kind and it.t == t]

    def one(step, kind, t, part):
        for it in of(kind, t)[part : part + 1]:
            step(it)

    def run(step, kind, t):
        for it in of(kind, t):
            step(it)

    def nothing():
        return None

    def paired(arrival, reply, layer, hooks=(nothing, nothing)):
        for m in range(2):
            arrival(layer, m)
            hooks[m]()
            reply(layer, m)

    def steps(*listed):
        def go():
            for body, *rest in listed:
                body(*rest)

        return go

    up, mid, down, last, out = step_up, step_mid, step_down, step_last, step_out
    wide, taps = 0, 1
    spread_first(wide, 0)
    spread_second(wide, 0)
    ready(wide, 0)
    own_x.wait()
    first_part(0, 0)
    first_part(0, 1)
    own_n.wait()
    bytes_wait(sc.go.at[0], sc.loc.at[6])
    own_cot.wait()
    norm_wait(sc.n_r)
    spread_first(taps, 0)
    spread_first(taps, 1)
    paired(
        first_norm,
        hidden_one,
        0,
        (
            steps((spread_second, taps, 0), (spread_second, taps, 1)),
            steps((spread_first, wide, 1)),
        ),
    )
    ready(taps, 0)
    ready(taps, 1)
    paired(
        second_part,
        hidden_two,
        0,
        (steps((spread_first, wide, 2), (spread_second, wide, 1)), steps((spread_first, taps, 2))),
    )
    ready(wide, 1)

    def turn(layer, m):
        pre_values(0, m)
        if m == 0:
            ready(wide, 2)
        first_part(1, m)

    paired(
        third_part,
        turn,
        0,
        (
            steps((spread_second, wide, 2), (spread_first, taps, 3), (spread_second, taps, 2)),
            steps((spread_first, wide, 3)),
        ),
    )
    paired(
        first_norm,
        hidden_one,
        1,
        (steps((spread_second, taps, 3)), steps((spread_second, wide, 3))),
    )
    ready(taps, 2)
    ready(taps, 3)
    paired(second_part, hidden_two, 1)
    ready(wide, 3)
    third_part(1, 0)
    pre_values(1, 0)
    third_part(1, 1)
    grad_out_norm(1, 0)
    pre_values(1, 1)
    outs = [put_out(2, sc.mix.at[...], mixed_ref.at[...])]
    grad_out_norm(1, 1)
    wide_grad(3, lambda m: sc.gt[m], lambda m: ag_value(3, m))

    paired(
        grad_two,
        grad_second,
        1,
        (
            steps((pair_sum, "w", 3), (one, up, "w", 3, 0)),
            steps((one, up, "w", 3, 1), (one, mid, "w", 3, 0)),
        ),
    )
    taps_grad(1)
    paired(
        grad_one,
        grad_first,
        1,
        (
            steps(
                (pair_sum, "k", 1),
                (one, up, "k", 1, 0),
                (one, mid, "w", 3, 1),
                (one, down, "w", 3, 0),
            ),
            steps(
                (one, up, "k", 1, 1),
                (one, down, "w", 3, 1),
                (one, last, "w", 3, 0),
                (one, mid, "k", 1, 0),
            ),
        ),
    )

    def fold(layer, m):
        conv_grad(1, m)
        if m == 1:
            outs.append(put_out(3, sc.gp.at[0], gpre_ref.at[...]))

    paired(
        fold,
        grad_out_norm,
        0,
        (
            steps(
                (one, up, "k", 1, 2),
                (one, last, "w", 3, 1),
                (one, mid, "k", 1, 1),
                (one, down, "k", 1, 0),
            ),
            steps(
                (one, up, "k", 1, 3),
                (one, mid, "k", 1, 2),
                (one, down, "k", 1, 1),
                (one, last, "k", 1, 0),
            ),
        ),
    )
    wide_grad(2, lambda m: sc.s1[m], lambda m: ag_value(5, m))
    wide_grad(1, lambda m: sc.gt[m], lambda m: ag_value(2, m))
    paired(
        grad_two,
        grad_second,
        0,
        (
            steps(
                (pair_sum, "w", 2),
                (one, up, "w", 2, 0),
                (one, mid, "k", 1, 3),
                (one, down, "k", 1, 2),
                (one, last, "k", 1, 1),
            ),
            steps(
                (one, up, "w", 2, 1),
                (pair_sum, "w", 1),
                (one, mid, "w", 2, 0),
                (one, down, "k", 1, 3),
                (one, last, "k", 1, 2),
            ),
        ),
    )
    taps_grad(0)
    paired(
        grad_one,
        grad_first,
        0,
        (
            steps(
                (pair_sum, "k", 0),
                (one, up, "k", 0, 0),
                (one, mid, "w", 2, 1),
                (one, down, "w", 2, 0),
                (one, last, "k", 1, 3),
            ),
            steps(
                (one, up, "k", 0, 1),
                (one, up, "k", 0, 2),
                (one, up, "k", 0, 3),
                (one, mid, "k", 0, 0),
                (one, down, "w", 2, 1),
                (one, last, "w", 2, 0),
            ),
        ),
    )
    gains_start()
    one(mid, "k", 0, 1)
    one(down, "k", 0, 0)
    one(last, "w", 2, 1)
    conv_grad(0, 0)
    one(up, "w", 1, 0)
    one(mid, "k", 0, 2)
    one(down, "k", 0, 1)
    one(last, "k", 0, 0)
    run(out, "k", 1)
    conv_grad(0, 1)
    wide_grad(0, lambda m: x_ref[m], lambda m: ag_value(4, m))
    one(mid, "k", 0, 3)
    one(down, "k", 0, 2)
    one(last, "k", 0, 1)
    one(out, "k", 0, 0)
    outs.append(put_out(4, sc.cv.at[...], conv_ref.at[...]))
    pair_sum("w", 0)
    run(up, "w", 0)
    one(up, "w", 1, 1)
    one(mid, "w", 1, 0)
    one(down, "k", 0, 3)
    one(last, "k", 0, 2)
    one(out, "k", 0, 1)
    run(out, "w", 3)
    one(mid, "w", 0, 0)
    one(last, "k", 0, 3)
    one(out, "k", 0, 2)
    one(mid, "w", 0, 1)
    one(down, "w", 0, 0)
    one(mid, "w", 0, 2)
    one(down, "w", 1, 0)
    one(out, "k", 0, 3)
    one(down, "w", 0, 1)
    one(mid, "w", 0, 3)
    one(last, "w", 0, 0)
    one(mid, "w", 1, 1)
    one(down, "w", 0, 2)
    one(last, "w", 0, 1)
    one(last, "w", 1, 0)
    one(out, "w", 0, 0)
    one(down, "w", 0, 3)
    one(last, "w", 0, 2)
    one(out, "w", 0, 1)
    one(down, "w", 1, 1)
    one(last, "w", 0, 3)
    run(out, "w", 2)
    one(out, "w", 1, 0)
    one(out, "w", 0, 2)
    one(last, "w", 1, 1)
    one(out, "w", 0, 3)
    one(out, "w", 1, 1)
    gains_done()
    run(step_sibling, "w", 3)
    run(step_sibling, "k", 1)
    run(step_sibling, "k", 0)
    run(step_sibling, "w", 2)
    run(step_sibling, "w", 1)
    one(step_sibling, "w", 0, 0)
    one(step_sibling, "w", 0, 1)
    run(step_done, "k", 1)
    run(step_done, "k", 0)
    outs.append(put_out(1, sc.ok.at[...], gtaps_ref.at[...]))
    for s in (3, 2, 1):
        run(step_done, "w", s)
    final = of("w", 0)
    for group, part in enumerate((final[:-1], final[-1:]) if len(final) > 1 else (final,)):
        first, count = part[0].r0, sum(it.nr for it in part)
        for it in part:
            if it.i >= final[0].i + 2:
                step_sibling(it)
        for it in part:
            step_done(it)
        part_rows_of = pl.ds(first, count)
        outs.append(
            put_out(
                5 + group, sc.ow.at[:, :, part_rows_of], gwide_ref.at[:, :, part_rows_of]
            )
        )
    for copy in outs:
        copy.wait()
    for body in finish:
        body()


def cast_pieces(rows):
    pieces = [("taps", pl.ds(576 * i, 576)) for i in range(4)]
    pieces += [("wide", pl.ds(512 * i, 512)) for i in range(4)]
    return pieces + [("stream", m) for m in range(2)]


def cast_kernel(mixed, gpre, conv, gwide, gtaps, gmid, gout, *refs):
    o_mixed, o_input, o_wide, o_taps, o_mid, o_out = refs[:6]
    b_taps, b_wide, b_gpre, b_conv, f_taps, f_wide, f_stream = refs[6:13]
    b_mixed, b_mid, b_out, r_sem, w_sem, d_sem = refs[13:]
    pieces = cast_pieces(gpre.shape[1])
    same = ((mixed, b_mixed, o_mixed), (gmid, b_mid, o_mid), (gout, b_out, o_out))
    arrive = [pltpu.make_async_copy(a, b, d_sem.at[i]) for i, (a, b, _) in enumerate(same)]
    leave = [pltpu.make_async_copy(b, o, d_sem.at[i]) for i, (_, b, o) in enumerate(same)]
    reads, writes = [], []
    for i, (kind, part) in enumerate(pieces):
        if kind == "stream":
            reads.append(
                [
                    pltpu.make_async_copy(gpre.at[part], b_gpre.at[part], r_sem.at[i]),
                    pltpu.make_async_copy(conv.at[part], b_conv.at[part], r_sem.at[i + 2]),
                ]
            )
            writes.append(
                pltpu.make_async_copy(f_stream.at[part], o_input.at[part], w_sem.at[i])
            )
            continue
        src, low, high, dst = (
            (gtaps, b_taps, f_taps, o_taps)
            if kind == "taps"
            else (gwide, b_wide, f_wide, o_wide)
        )
        reads.append([pltpu.make_async_copy(src.at[part], low.at[part], r_sem.at[i])])
        writes.append(pltpu.make_async_copy(high.at[part], dst.at[part], w_sem.at[i]))
    for group in reads:
        for copy in group:
            copy.start()
    for copy in arrive:
        copy.start()
    for (kind, part), group, write in zip(pieces, reads, writes):
        for copy in group:
            copy.wait()
        size = 64

        def strip(i, carry, kind=kind, part=part):
            if kind == "stream":
                at = pl.ds(pl.multiple_of(i * size, size), size)
                f_stream[part, at] = b_gpre[part, at].astype(F32) + b_conv[part, at].astype(F32)
                return carry
            at = pl.ds(pl.multiple_of(part.start + i * size, size), size)
            if kind == "taps":
                f_taps[at] = b_taps[at].astype(F32)
            else:
                f_wide[at] = b_wide[at].astype(F32)
            return carry

        lax.fori_loop(0, (gpre.shape[1] if kind == "stream" else part.size) // size, strip, 0)
        write.start()
    for first, second in zip(arrive, leave):
        first.wait()
        second.start()
    for copy in writes + leave:
        copy.wait()


def cast_all(mixed, gpre, conv, gwide, gtaps, gmid, gout):
    anywhere = pl.BlockSpec(memory_space=pl.ANY)
    shape = jax.ShapeDtypeStruct
    count = len(cast_pieces(gpre.shape[1]))
    return pl.pallas_call(
        cast_kernel,
        in_specs=[anywhere] * 7,
        out_specs=[anywhere] * 6,
        out_shape=[
            shape(mixed.shape, BF16),
            shape(mixed.shape, F32),
            shape(gwide.shape, F32),
            shape(gtaps.shape, F32),
            shape(gmid.shape, F32),
            shape(gout.shape, F32),
        ],
        scratch_shapes=[
            pltpu.VMEM(gtaps.shape, BF16),
            pltpu.VMEM(gwide.shape, BF16),
            pltpu.VMEM(gpre.shape, BF16),
            pltpu.VMEM(gpre.shape, BF16),
            pltpu.VMEM(gtaps.shape, F32),
            pltpu.VMEM(gwide.shape, F32),
            pltpu.VMEM(gpre.shape, F32),
            pltpu.VMEM(mixed.shape, BF16),
            pltpu.VMEM(gmid.shape, F32),
            pltpu.VMEM(gout.shape, F32),
            pltpu.SemaphoreType.DMA((count + 2,)),
            pltpu.SemaphoreType.DMA((count,)),
            pltpu.SemaphoreType.DMA((3,)),
        ],
        compiler_params=pltpu.CompilerParams(vmem_limit_bytes=60 * 2**20),
        name="casts",
    )(mixed, gpre, conv, gwide, gtaps, gmid, gout)


def local(block_input, cotangent, weight_wide, weight_taps, norm_mid, norm_out, group_counts):
    n_dp = group_counts.shape[1]
    micro, rows, width = block_input.shape
    scratch = scratch_list(n_dp, rows)
    anywhere = pl.BlockSpec(memory_space=pl.ANY)

    def shape(dims, dtype):
        return jax.ShapeDtypeStruct(dims, dtype)

    stream = (micro, rows, width)
    mixed, gpre, conv, gwide, gtaps, gmid, gout = pl.pallas_call(
        functools.partial(kernel, list(scratch), n_dp),
        out_shape=[
            shape(stream, BF16),
            shape(stream, BF16),
            shape(stream, BF16),
            shape((4, 2, 256, 512), BF16),
            shape((2304, 512), BF16),
            shape(norm_mid.shape, F32),
            shape(norm_out.shape, F32),
        ],
        in_specs=[anywhere] * 7,
        out_specs=[anywhere] * 7,
        scratch_shapes=list(scratch.values()),
        compiler_params=pltpu.CompilerParams(
            collective_id=0, has_side_effects=True, vmem_limit_bytes=62 * 2**20
        ),
        name="layers",
    )(block_input, cotangent, weight_wide, weight_taps.reshape(9, 256, 512), norm_mid, norm_out, jnp.swapaxes(group_counts, 1, 2))
    results = cast_all(mixed, gpre, conv, gwide.reshape(2048, 512), gtaps, gmid, gout)
    mixed, grad_input, gwide, gtaps, gmid, gout = results
    return (
        mixed,
        grad_input,
        gwide.reshape(weight_wide.shape),
        gtaps.reshape(weight_taps.shape),
        gmid,
        gout,
    )


def solution(mesh):
    split = P(None, "dp", "pipe")
    section = P("pipe", None, None)
    return jax.shard_map(
        local,
        mesh=mesh,
        in_specs=(split, split, section, section, section, section, P()),
        out_specs=(split, split, section, section, section, section),
        check_vma=False,
    )
```

```python
import functools
from types import SimpleNamespace

import jax
import jax.numpy as jnp
from jax import lax
from jax.experimental import pallas as pl
from jax.experimental.pallas import tpu as pltpu
from jax.sharding import PartitionSpec as P

MESH = pl.DeviceIdType.MESH
F32 = jnp.float32
BF16 = jnp.bfloat16
EPS = 1e-05
LANES = 128
N_PIPE = 4
SIDES = (7, 6, 5, 2)


def dot_nn(a, b):
    return jnp.dot(a, b, preferred_element_type=F32)


def dot_nt(a, b):
    return lax.dot_general(a, b, (((1,), (1,)), ((), ())), preferred_element_type=F32)


def sigmoid(v):
    return jax.nn.sigmoid(v)


def sizes(n_dp):
    n_z = n_dp // 2
    n_own = min(n_z, 16)
    return n_z, n_own


def gradient_items(n_dp):
    line = n_dp // 2 == 4
    listed = []
    for kind, index, parts in (
        ("w", 3, [128, 128]),
        ("k", 1, [768] * 3),
        ("w", 2, [128, 128]),
        ("w", 1, [128, 128]),
        ("k", 0, [288, 288, 288, 288, 576, 576]),
        ("w", 0, [64] * 4),
    ):
        start = 0
        for part, rows in enumerate(parts if line else [sum(parts)]):
            listed.append(
                SimpleNamespace(
                    kind=kind, t=index, r0=start, nr=rows, i=len(listed), part=part
                )
            )
            start += rows
    return listed


def scratch_list(n_dp, rows):
    n_z, n_own = sizes(n_dp)
    items = len(gradient_items(n_dp))
    line = n_z == 4
    dma = pltpu.SemaphoreType.DMA

    def half(*shape):
        return pltpu.VMEM(shape, BF16)

    def full(*shape):
        return pltpu.VMEM(shape, F32)

    return dict(
        wt=half(4, 512, 512),
        k2=half(2, 18, 256, 128),
        gm=full(4, 2, 128),
        gmf=full(4, 2, 512),
        hf=half(2, 2, rows, 512),
        gff=half(2, 2, rows, 512),
        sml=full(2, 2, 4, 4, 128),
        go=full(4, 2, 2, 512),
        msk=full(2, rows, 128),
        beside=full(2, 2, rows, 128),
        above=full(2, 4, 2, rows, 128),
        yf=full(9, rows, 128),
        part=half(2, 2, 4, rows, 128),
        rsr=half(6 if line else 2, 2, 3, rows, 128),
        ag=half(6, 2, 4, rows, 128),
        stm=full(8, 2, n_dp, 2, 128),
        stw=full(4, 2, n_dp, 2, 512),
        midv=full(4, 2, rows, 128),
        dzm=full(2, rows, 128),
        inv_mid=full(4, 2, 1, 128),
        inv_wide=full(2, 2, 1, 512),
        widv=full(2, 2, rows, 512),
        pre0=full(2, rows, 512),
        s1=half(2, rows, 512),
        mix=half(2, rows, 512),
        gp=half(2, 2, rows, 512),
        gt=half(2, rows, 512),
        gb=half(2, rows, 1152),
        tb=half(512, 2 * rows),
        ack=full(512, 1152),
        dw=half(4, 2, 256, 512),
        prw=half(4, 256, 512),
        zsw=half(4, 256, 512),
        fzw=half(4, 256, 512),
        ow=half(4, 2, 256, 512),
        dk=half(2, 4608, 128),
        prk=half(2, 2304, 128),
        zsk=half(2, 2304, 128),
        fzk=half(2, 2304, 128),
        ok=half(2304, 512),
        zow=half(4, 256, 512) if line else half(4, n_z - 1, 256 // n_own, 512),
        ziw=half(4, 128, 512) if line else half(1, 16, 128),
        zok=half(2, 2304, 128) if line else half(2, n_z - 1, 2304 // n_own, 128),
        zik=half(2, 1152, 128) if line else half(1, 16, 128),
        gsm=full(4, 4, 2, 128),
        gsw=full(2, 4, 2, 512),
        cnt=pltpu.SMEM((2, n_dp), F32),
        xin=half(2, rows, 512),
        cin=half(2, rows, 512),
        gmo=full(1, 2, 512),
        goo=full(1, 2, 1024),
        counts=pltpu.SMEM((2, 4, n_dp), jnp.int32),
        f_s=dma((2,)),
        f_r=dma((2, 4)),
        z_r=dma((2, 4)),
        b_s=dma((2, 4)),
        b_r=dma((2, 4)),
        n_s=dma((3,)),
        n_r=dma((3,)),
        sm_s=dma((2, 2)),
        sm_r=dma((2, 2)),
        loc=dma((8,)),
        ex_s=dma((2, 2)),
        ex_r=dma((2, 2)),
        st_s=dma((2, 2)),
        st_r=dma((2, 2)),
        pw_s=dma((6,)),
        pw_r=dma((6,)),
        it_s=dma((6,)),
        one_r=dma((items,)),
        mid_r=dma((items,)),
        inn_r=dma((items,)),
        to_s=dma((6,)),
        ga_s=dma((6 if n_z != 4 else 1,)),
        sh_s=dma((4,)),
        sh_r=dma((4,)),
        to_r=dma((2, 6)),
        sib_s=dma((2,)),
        sib_r=dma((2, 6)),
        g_s=dma((2,)),
        g_r=dma((2,)),
        out=dma((8,)),
    )


def kernel(names, n, *refs):
    (x_hbm, cot_hbm, wide_ref, taps_ref, nmid_ref, nout_ref, counts_hbm) = refs[:7]
    (mixed_ref, gpre_ref, conv_ref, gwide_ref, gtaps_ref, gmid_ref, gout_ref) = refs[7:14]
    sc = SimpleNamespace(**dict(zip(names, refs[14:])))
    counts_ref = sc.counts
    x_ref, cot_ref = sc.xin, sc.cin
    rows = x_ref.shape[1]
    n_z, n_own = sizes(n)
    p = lax.axis_index("pipe")
    d = lax.axis_index("dp")
    z = lax.div(d, 2)
    c = lax.rem(d, 2)
    parity = lax.rem(p, 2)
    sibling = (p, 2 * z + 1 - c)
    z_odd = lax.rem(z, 2)
    z_pair = (p, 2 * (z + 1 - 2 * z_odd) + c)
    quarter = 2 * z_odd + c
    quarter_z = 2 * (1 - z_odd) + c
    finish = []

    def pipe_at(off):
        return lax.rem(p + N_PIPE + (2 * parity - 1) * off, N_PIPE)

    def remote(src, dst, ss, rs, dev):
        return pltpu.make_async_remote_copy(
            src_ref=src, dst_ref=dst, send_sem=ss, recv_sem=rs, device_id=dev, device_id_type=MESH
        )

    def each(count, first, body):
        if count - first <= 8:
            for k in range(first, count):
                body(k)
        else:

            def step(k, carry):
                body(k)
                return carry

            lax.fori_loop(first, count, step, 0)

    def bytes_wait(view, sem):
        pltpu.make_async_copy(view, view, sem).wait()

    barrier = pltpu.get_barrier_semaphore()
    for off in range(1, N_PIPE):
        pl.semaphore_signal(barrier, inc=1, device_id=(pipe_at(off), d), device_id_type=MESH)

    def greet(k):
        pl.semaphore_signal(
            barrier, inc=1, device_id=(p, lax.rem(d + k, n)), device_id_type=MESH
        )

    each(n, 1, greet)

    def columns_of(q):
        return pl.ds(pl.multiple_of(128 * q, 128), 128)

    own_w = pltpu.make_async_copy(
        wide_ref.at[0, pl.ds(pl.multiple_of(512 * p, 512), 512), :], sc.wt.at[p], sc.loc.at[0]
    )
    own_k = pltpu.make_async_copy(
        taps_ref.at[:, :, columns_of(p)],
        sc.k2.at[lax.div(p, 2), pl.ds(9 * parity, 9)],
        sc.loc.at[1],
    )
    own_c = pltpu.make_async_copy(counts_hbm, counts_ref, sc.loc.at[2])
    own_c.start()
    own_x = pltpu.make_async_copy(x_hbm, sc.xin, sc.loc.at[4])
    own_cot = pltpu.make_async_copy(cot_hbm, sc.cin, sc.loc.at[5])
    own_x.start()
    own_w.start()
    own_k.start()
    own_n = pltpu.make_async_copy(
        nmid_ref.at[0, :, columns_of(p)], sc.gm.at[p], sc.loc.at[3]
    )
    own_n.start()
    for e in range(2):
        pltpu.make_async_copy(
            nout_ref.at[0, :, pl.ds(512 * e, 512)], sc.go.at[p, e], sc.loc.at[6]
        ).start()
    own_cot.start()
    own_g = pltpu.make_async_copy(nmid_ref.at[0], sc.gmf.at[p], sc.loc.at[7])
    own_g.start()

    own_c.wait()

    def used_rows(m, j):
        return (
            49 * counts_ref[m, 0, j]
            + 36 * counts_ref[m, 1, j]
            + 25 * counts_ref[m, 2, j]
            + 4 * counts_ref[m, 3, j]
        )

    totals = []
    for m in range(2):

        def count_up(j, acc, m=m):
            used = used_rows(m, j)
            sc.cnt[m, j] = used.astype(F32)
            return acc + used

        totals.append(lax.fori_loop(0, n, count_up, jnp.int32(0)).astype(F32))

    pl.semaphore_wait(barrier, N_PIPE - 1 + n - 1)

    def held(kind, s, part):
        if kind == 0:
            return sc.wt.at[s, pl.ds(pl.multiple_of(128 * part, 128), 128)]
        layer, odd = (s // 2, s % 2) if isinstance(s, int) else (lax.div(s, 2), lax.rem(s, 2))
        return sc.k2.at[
            layer, pl.ds(9 * odd, 9), pl.ds(pl.multiple_of(64 * part, 64), 64)
        ]

    def fetch(kind, off):
        q = pipe_at(off)
        if kind == 0:
            src = wide_ref.at[0, pl.ds(pl.multiple_of(512 * q + 128 * quarter, 128), 128), :]
        else:
            src = taps_ref.at[:, pl.ds(pl.multiple_of(64 * quarter, 64), 64), columns_of(q)]
        return remote(
            src, held(kind, p, quarter), sc.f_s.at[kind], sc.f_r.at[kind, p], (q, d)
        )

    def send_norm(off):
        q = pipe_at(off)
        listed = [
            remote(
                nmid_ref.at[0, :, columns_of(q)],
                sc.gm.at[p],
                sc.n_s.at[0],
                sc.n_r.at[0],
                (q, d),
            ),
            remote(nmid_ref.at[0], sc.gmf.at[p], sc.n_s.at[2], sc.n_r.at[2], (q, d)),
        ]
        for e in range(2):
            listed.append(
                remote(
                    nout_ref.at[0, :, pl.ds(512 * e, 512)],
                    sc.go.at[p, e],
                    sc.n_s.at[1],
                    sc.n_r.at[1],
                    (q, d),
                )
            )
        return listed

    def norm_wait(sems):
        bytes_wait(sc.gm.at[pl.ds(0, 3)], sems.at[0])
        bytes_wait(sc.go.at[pl.ds(0, 3)], sems.at[1])
        bytes_wait(sc.gmf.at[pl.ds(0, 3)], sems.at[2])

    def pass_z(kind, s):
        view = held(kind, s, quarter)
        return remote(view, view, sc.b_s.at[kind, s], sc.z_r.at[kind, s], z_pair)

    def pass_sibling(kind, s, e):
        view = held(kind, s, quarter if e == 0 else quarter_z)
        return remote(view, view, sc.b_s.at[kind, s], sc.b_r.at[kind, s], sibling)

    def spread_first(kind, s):
        @pl.when(p != s)
        def _():
            view = held(kind, s, quarter)
            bytes_wait(view, sc.f_r.at[kind, s])
            pass_z(kind, s).start()
            pass_sibling(kind, s, 0).start()

    def spread_second(kind, s):
        @pl.when(p != s)
        def _():
            pass_z(kind, s).wait_recv()
            pass_sibling(kind, s, 1).start()

    def quarters(kind, s, count):
        if kind == 0:
            return sc.wt.at[s, pl.ds(0, 128 * count)]
        return sc.k2.at[s // 2, pl.ds(9 * (s % 2), 9), pl.ds(0, 64 * count)]

    def ready(kind, s):
        @pl.when(p != s)
        def _():
            bytes_wait(quarters(kind, s, 2), sc.b_r.at[kind, s])

        @pl.when(p == s)
        def _():
            (own_w if kind == 0 else own_k).wait()

    def finish_weights():
        for kind in range(2):
            bytes_wait(quarters(kind, 0, 3), sc.f_s.at[kind])
            for s in range(4):

                @pl.when(p != s)
                def _(kind=kind, s=s):
                    bytes_wait(quarters(kind, s, 3), sc.b_s.at[kind, s])

    finish.append(finish_weights)

    for even in range(2):

        @pl.when(parity == even)
        def _(even=even):
            for kind in (even, 1 - even):
                for off in range(1, 4):
                    fetch(kind, off).start()
                if kind == even:
                    for off in range(1, 4):
                        for copy in send_norm(off):
                            copy.start()

    def finish_norm():
        norm_wait(sc.n_s)

    finish.append(finish_norm)

    row_id = lax.broadcasted_iota(jnp.int32, (rows, LANES), 0).astype(F32)

    def build(m):
        ends = [jnp.float32(0.0)]
        total = jnp.int32(0)
        for g, side in enumerate(SIDES):
            total = total + side * side * counts_ref[m, g, d]
            ends.append(total.astype(F32))
        sc.msk[m] = jnp.where(row_id < ends[4], 1.0, 0.0)
        left = jnp.zeros((rows, LANES), F32)
        right = left
        for g, side in enumerate(SIDES):
            inside = (row_id >= ends[g]) & (row_id < ends[g + 1])
            within = row_id - ends[g]
            within = within - side * side * jnp.floor((within + 0.5) / (side * side))
            map_row = jnp.floor((within + 0.5) / side)
            map_col = within - side * map_row
            left = jnp.where(inside & (map_col > 0.5), 1.0, left)
            right = jnp.where(inside & (map_col < side - 1.5), 1.0, right)
            sc.above[m, g, 0] = jnp.where(inside & (map_row > 0.5), 1.0, 0.0)
            sc.above[m, g, 1] = jnp.where(inside & (map_row < side - 1.5), 1.0, 0.0)
        sc.beside[m, 0] = left
        sc.beside[m, 1] = right

    def shifted(values, count):
        return pltpu.roll(values, count % rows, 0)

    def from_above(values, m):
        return sum(
            sc.above[m, g, 0] * shifted(values, side) for g, side in enumerate(SIDES)
        )

    def from_below(values, m):
        return sum(
            sc.above[m, g, 1] * shifted(values, -side) for g, side in enumerate(SIDES)
        )

    for m in range(2):
        build(m)


    exchange_order = [
        ("rs", 0), ("ag", 0), ("ag", 2), ("rs", 1), ("ag", 1), ("ag", 3),
        ("rs", 3), ("rs", 5), ("ag", 5), ("rs", 2), ("rs", 4), ("ag", 4),
    ]

    def rs_slot(rid):
        return rid if sc.rsr.shape[0] == 6 else rs_par[rid]

    def three(kind, i, m):
        return sc.rsr.at[rs_slot(i), m] if kind == "rs" else sc.ag.at[i, m, pl.ds(0, 3)]

    def exchange_wait(sems, kind, i, m):
        turn = exchange_order.index((kind, i))
        bytes_wait(three(kind, i, m), sems.at[turn % 2, m])

    def exchange_open(kind, i, m):
        turn = exchange_order.index((kind, i))
        if turn >= 2:
            exchange_wait(sc.ex_s, *exchange_order[turn - 2], m)
        return sc.ex_s.at[turn % 2, m], sc.ex_r.at[turn % 2, m]

    def rs_sum(rid, m, par):
        exchange_wait(sc.ex_r, "rs", rid, m)
        total = sc.part[par, m, p].astype(F32)
        for k in range(3):
            total = total + sc.rsr[rs_slot(rid), m, k].astype(F32)
        return total

    def ag_start(aid, m, value):
        ss, rs = exchange_open("ag", aid, m)
        sc.ag[aid, m, p] = value
        own = sc.ag.at[aid, m, p]
        for off in range(1, 4):
            remote(own, own, ss, rs, (pipe_at(off), d)).start()

    def ag_wait(aid, m):
        exchange_wait(sc.ex_r, "ag", aid, m)

    def ag_value(aid, m):
        return jnp.concatenate([sc.ag[aid, m, q] for q in range(4)], axis=1)

    def finish_exchanges():
        for kind, i in exchange_order[-2:]:
            for m in range(2):
                exchange_wait(sc.ex_s, kind, i, m)

    finish.append(finish_exchanges)

    sum_order = [
        (False, 0), (False, 1), (True, 0), (False, 2), (False, 3), (True, 1),
        (True, 3), (False, 7), (False, 6), (True, 2), (False, 5), (False, 4),
    ]

    def st_buffer(wide, i, m):
        return (sc.stw if wide else sc.stm).at[i, m]

    def st_bytes(sems, wide, i, m):
        turn = sum_order.index((wide, i))
        bytes_wait(st_buffer(wide, i, m).at[pl.ds(0, n - 1)], sems.at[turn % 2, m])

    def st_start(wide, i, m):
        turn = sum_order.index((wide, i))
        if turn >= 2:
            st_bytes(sc.st_s, *sum_order[turn - 2], m)
        own = st_buffer(wide, i, m).at[d]
        ss, rs = sc.st_s.at[turn % 2, m], sc.st_r.at[turn % 2, m]

        def go(k):
            remote(own, own, ss, rs, (p, lax.rem(d + k, n))).start()

        if n > 8:
            each(n, 1, go)
            return
        high = lax.div(2 * z, n_z)
        for i in range(n_z - 1):
            low_far = n_z - 1 - i - lax.div(z + i + 1, n_z)
            high_far = i + lax.div(i - z + n_z, n_z)
            far = high * high_far + (1 - high) * low_far
            for e in range(2):
                remote(own, own, ss, rs, (p, 2 * far + e)).start()
        remote(own, own, ss, rs, sibling).start()

    def st_wait(wide, i, m):
        st_bytes(sc.st_r, wide, i, m)

    def finish_st():
        for wide, i in sum_order[-2:]:
            for m in range(2):
                st_bytes(sc.st_s, wide, i, m)

    finish.append(finish_st)

    def over_devices(body, init):
        if n <= 8:
            for j in range(n):
                init = body(j, init)
            return init
        return lax.fori_loop(0, n, body, init)

    def combine(wide, i, m):
        st_wait(wide, i, m)
        ref = sc.stw if wide else sc.stm
        blank = jnp.zeros((1, ref.shape[-1]), F32)
        mean = over_devices(
            lambda j, acc: acc + sc.cnt[m, j] * ref[i, m, j, 0:1, :], blank
        )
        mean = mean / totals[m]

        def spread(j, acc):
            gap = ref[i, m, j, 0:1, :] - mean
            return acc + ref[i, m, j, 1:2, :] + sc.cnt[m, j] * (gap * gap)

        var = over_devices(spread, blank) / totals[m]
        return mean, lax.rsqrt(var + EPS)

    def back_sums(wide, i, m):
        st_wait(wide, i, m)
        ref = sc.stw if wide else sc.stm
        return over_devices(
            lambda j, acc: acc + ref[i, m, j], jnp.zeros((2, ref.shape[-1]), F32)
        )

    def local_moments(v, m):
        mask = sc.msk[m]
        own = jnp.maximum(sc.cnt[m, d], 1.0)
        mean = jnp.sum(v * mask, 0, keepdims=True) / own
        gap = (v - mean) * mask
        return jnp.concatenate([mean, jnp.sum(gap * gap, 0, keepdims=True)], 0)

    def local_sums(dz, vhat):
        return jnp.concatenate(
            [jnp.sum(dz * vhat, 0, keepdims=True), jnp.sum(dz, 0, keepdims=True)], 0
        )

    def lanes(j):
        return slice(LANES * j, LANES * (j + 1))

    def stream(layer, m):
        return x_ref[m] if layer == 0 else sc.s1[m]

    def stream_part(layer, m, j):
        return (x_ref[m, :, lanes(j)] if layer == 0 else sc.s1[m, :, lanes(j)]).astype(F32)

    rs_par = {0: 0, 1: 1, 3: 0, 5: 1, 2: 0, 4: 1}

    def rs_send(rid, m, values):
        par = rs_par[rid]
        ss, rs = exchange_open("rs", rid, m)
        for j, value in enumerate(values):
            half = value.astype(BF16)
            sc.part[par, m, 2 * j] = half[:, :LANES]
            sc.part[par, m, 2 * j + 1] = half[:, LANES:]
        for off in range(1, 4):
            q = pipe_at(off)
            remote(sc.part.at[par, m, q], sc.rsr.at[rs_slot(rid), m, off - 1], ss, rs, (q, d)).start()

    def first_part(layer, m):
        s = stream(layer, m)
        rs_send(
            layer,
            m,
            [dot_nn(s, sc.wt[2 * layer, :, 256 * j : 256 * j + 256]) for j in range(2)],
        )

    def mid_moments(i, m, v):
        sc.midv[i, m] = v
        sc.stm[i, m, d] = local_moments(v, m)
        st_start(False, i, m)

    def first_norm(layer, m):
        mid_moments(2 * layer, m, rs_sum(layer, m, rs_par[layer]))

    def mid_hidden(i, m):
        mean, inv = combine(False, i, m)
        sc.inv_mid[i, m] = inv
        vhat = (sc.midv[i, m] - mean) * inv
        sc.midv[i, m] = vhat
        u = sc.gm[i, 0:1, :] * vhat + sc.gm[i, 1:2, :]
        return (sc.msk[m] * (u * sigmoid(u))).astype(BF16)

    def hidden_one(layer, m):
        i = 2 * layer
        mean, inv = combine(False, i, m)
        sc.inv_mid[i, m] = inv
        vhat = ((sc.midv[i, m] - mean) * inv).astype(BF16)
        sc.midv[i, m] = vhat.astype(F32)
        ag_start(layer, m, vhat)

    def taps_of(layer, taps):
        return jnp.concatenate(
            [
                jnp.concatenate([sc.k2[layer, 2 * k], sc.k2[layer, 2 * k + 1]], axis=0)
                for k in taps
            ],
            axis=1,
        )

    def second_part(layer, m):
        ag_wait(layer, m)
        for q in range(4):
            gain, bias = sc.gmf[2 * layer, 0:1, lanes(q)], sc.gmf[2 * layer, 1:2, lanes(q)]
            u = gain * sc.ag[layer, m, q].astype(F32) + bias
            sc.hf[layer, m, :, lanes(q)] = (sc.msk[m] * (u * sigmoid(u))).astype(BF16)
        h = sc.hf[layer, m]
        for j in range(5):
            width = 256 if j < 4 else 128
            y = dot_nn(h, taps_of(layer, [2 * j + e for e in range(width // LANES)]))
            for e in range(width // LANES):
                sc.yf[2 * j + e] = y[:, lanes(e)]

        def across(k):
            return (
                sc.yf[k + 1]
                + sc.beside[m, 0] * shifted(sc.yf[k], 1)
                + sc.beside[m, 1] * shifted(sc.yf[k + 2], -1)
            )

        total = across(3) + from_above(across(0), m) + from_below(across(6), m)
        mid_moments(2 * layer + 1, m, total)

    def hidden_two(layer, m):
        ag_start(2 + layer, m, mid_hidden(2 * layer + 1, m))

    def third_part(layer, m):
        ag_wait(2 + layer, m)
        h = ag_value(2 + layer, m)
        for j in range(2):
            sc.widv[layer, m, :, 256 * j : 256 * j + 256] = dot_nt(
                h, sc.wt[2 * layer + 1, 256 * j : 256 * j + 256, :]
            )
        for j in range(4):
            sc.stw[layer, m, d, :, lanes(j)] = local_moments(sc.widv[layer, m, :, lanes(j)], m)
        st_start(True, layer, m)

    def out_gain(layer, j):
        both = sc.go[2 * layer + lax.div(p, 2), lax.rem(p, 2)]
        return both[0:1, lanes(j)], both[1:2, lanes(j)]

    def pre_values(layer, m):
        mean, inv = combine(True, layer, m)
        sc.inv_wide[layer, m] = inv
        mask = sc.msk[m]
        for j in range(4):
            gain, bias = out_gain(layer, j)
            vhat = (sc.widv[layer, m, :, lanes(j)] - mean[:, lanes(j)]) * inv[:, lanes(j)]
            sc.widv[layer, m, :, lanes(j)] = vhat
            pre = gain * vhat + bias + stream_part(layer, m, j)
            sig = sigmoid(pre)
            out = (mask * (pre * sig)).astype(BF16)
            if layer == 0:
                sc.pre0[m, :, lanes(j)] = pre
                sc.s1[m, :, lanes(j)] = out
            else:
                sc.mix[m, :, lanes(j)] = out
                slope = sig * (1.0 + pre * (1.0 - sig))
                grad = (cot_ref[m, :, lanes(j)].astype(F32) * mask * slope).astype(BF16)
                sc.gp[1, m, :, lanes(j)] = grad
                sc.stw[3, m, d, :, lanes(j)] = local_sums(grad.astype(F32), vhat)
        if layer == 1:
            st_start(True, 3, m)

    def put_out(k, src, dst):
        copy = pltpu.make_async_copy(src, dst, sc.out.at[k])
        copy.start()
        return copy

    def grad_out_norm(layer, m):
        sums = back_sums(True, 2 + layer, m)
        if m == 0:
            sc.gsw[layer, p] = sums
        else:
            sc.gsw[layer, p] = sc.gsw[layer, p] + sums
        mask = sc.msk[m]
        inv = sc.inv_wide[layer, m]
        for j in range(4):
            gain, _ = out_gain(layer, j)
            dz = sc.gp[layer, m, :, lanes(j)].astype(F32)
            vhat = sc.widv[layer, m, :, lanes(j)]
            s1 = sums[0:1, lanes(j)] / totals[m]
            s0 = sums[1:2, lanes(j)] / totals[m]
            dv = mask * (gain * inv[:, lanes(j)]) * (dz - s0 - vhat * s1)
            sc.gt[m, :, lanes(j)] = dv.astype(BF16)
        g = sc.gt[m]
        rs_send(
            2 + layer,
            m,
            [dot_nn(g, sc.wt[2 * layer + 1, :, 256 * j : 256 * j + 256]) for j in range(2)],
        )

    def mid_grad(i, m, upstream):
        vhat = sc.midv[i, m]
        u = sc.gm[i, 0:1, :] * vhat + sc.gm[i, 1:2, :]
        sig = sigmoid(u)
        dz = upstream * sc.msk[m] * (sig * (1.0 + u * (1.0 - sig)))
        sc.dzm[m] = dz
        sc.stm[4 + i, m, d] = local_sums(dz, vhat)
        st_start(False, 4 + i, m)

    def mid_back(i, m):
        sums = back_sums(False, 4 + i, m)
        if m == 0:
            sc.gsm[i, p] = sums
        else:
            sc.gsm[i, p] = sc.gsm[i, p] + sums
        s1 = sums[0:1, :] / totals[m]
        s0 = sums[1:2, :] / totals[m]
        scale = sc.gm[i, 0:1, :] * sc.inv_mid[i, m]
        return (sc.msk[m] * scale * (sc.dzm[m] - s0 - sc.midv[i, m] * s1)).astype(BF16)

    def grad_two(layer, m):
        mid_grad(2 * layer + 1, m, rs_sum(2 + layer, m, rs_par[2 + layer]))

    def grad_second(layer, m):
        gs = mid_back(2 * layer + 1, m)
        own = gs.astype(F32)
        for du, moved in ((0, own), (1, from_above(own, m)), (-1, from_below(own, m))):
            k = 3 * (du + 1)
            sc.gb[m, :, lanes(k + 1)] = moved.astype(BF16)
            sc.gb[m, :, lanes(k + 2)] = (sc.beside[m, 0] * shifted(moved, 1)).astype(BF16)
            sc.gb[m, :, lanes(k)] = (sc.beside[m, 1] * shifted(moved, -1)).astype(BF16)
        g = sc.gb[m]
        rs_send(
            4 + layer,
            m,
            [
                dot_nt(
                    g, jnp.concatenate([sc.k2[layer, 2 * k + j] for k in range(9)], axis=1)
                )
                for j in range(2)
            ],
        )

    def grad_one(layer, m):
        mid_grad(2 * layer, m, rs_sum(4 + layer, m, rs_par[4 + layer]))
        ag_start(4 + layer, m, sc.dzm[m].astype(BF16))

    def small_copy(layer, m, off):
        own = sc.sml.at[layer, m, p]
        return remote(own, own, sc.sm_s.at[layer, m], sc.sm_r.at[layer, m], (pipe_at(off), d))

    def grad_first(layer, m):
        i = 2 * layer
        sums = back_sums(False, 4 + i, m)
        if m == 0:
            sc.gsm[i, p] = sums
        else:
            sc.gsm[i, p] = sc.gsm[i, p] + sums
        scale = sc.gm[i, 0:1, :] * sc.inv_mid[i, m]
        s1 = scale * (sums[0:1, :] / totals[m])
        s0 = scale * (sums[1:2, :] / totals[m])
        sc.sml[layer, m, p] = jnp.concatenate([scale, s0, s1, s1], 0)
        for off in range(1, 4):
            small_copy(layer, m, off).start()

    def finish_small():
        for layer in range(2):
            for m in range(2):
                bytes_wait(sc.sml.at[layer, m, pl.ds(0, 3)], sc.sm_s.at[layer, m])

    finish.append(finish_small)

    def slopes(m):
        for i in range(4):
            pre = sc.pre0[m, :, lanes(i)]
            sig = sigmoid(pre)
            sc.pre0[m, :, lanes(i)] = sc.msk[m] * (sig * (1.0 + pre * (1.0 - sig)))

    def conv_grad(layer, m):
        ag_wait(4 + layer, m)
        bytes_wait(sc.sml.at[layer, m, pl.ds(0, 3)], sc.sm_r.at[layer, m])
        for q in range(4):
            scale, s0, s1 = (sc.sml[layer, m, q, k : k + 1, :] for k in range(3))
            dz = sc.ag[4 + layer, m, q].astype(F32)
            vhat = sc.ag[layer, m, q].astype(F32)
            dv = sc.msk[m] * (scale * dz - s0 - s1 * vhat)
            sc.gff[layer, m, :, lanes(q)] = dv.astype(BF16)
        g = sc.gff[layer, m]
        for j in range(2):
            r = dot_nt(g, sc.wt[2 * layer, 256 * j : 256 * j + 256, :]).astype(BF16)
            if layer == 0:
                sc.cin[m, :, 256 * j : 256 * j + 256] = r
                continue
            for e in range(2):
                i = 2 * j + e
                up = sc.gp[1, m, :, lanes(i)].astype(F32) + r[:, lanes(e)].astype(F32)
                grad = (up * sc.pre0[m, :, lanes(i)]).astype(BF16)
                sc.gp[0, m, :, lanes(i)] = grad
                sc.stw[2, m, d, :, lanes(i)] = local_sums(
                    grad.astype(F32), sc.widv[0, m, :, lanes(i)]
                )
        if layer == 1:
            st_start(True, 2, m)

    def turned(blocks):
        for m, block in enumerate(blocks):
            sc.tb[:, rows * m : rows * (m + 1)] = block.T

    def both(get):
        return jnp.concatenate([get(0), get(1)], axis=0)

    def wide_grad(s, left, right):
        turned([left(0), left(1)])
        for j in range(2):
            cols = slice(256 * j, 256 * j + 256)
            rhs = both(lambda m: right(m)[:, cols])
            for h in range(2):
                r = dot_nn(sc.tb[256 * h : 256 * h + 256, :], rhs)
                sc.dw[s, h, :, cols] = r.astype(BF16)
        pair_copy("w", s).start()

    def wide_early():
        turned([x_ref[0], x_ref[1]])
        g = sc.gff[0, 0]
        for j in range(2):
            cols = slice(256 * j, 256 * j + 256)
            sc.ack[:, cols] = dot_nn(sc.tb[:, :rows], g[:, cols])

    def wide_late():
        g = sc.gff[0, 1]
        for j in range(2):
            cols = slice(256 * j, 256 * j + 256)
            for h in range(2):
                part = slice(256 * h, 256 * h + 256)
                r = sc.ack[part, cols] + dot_nn(sc.tb[part, rows:], g[:, cols])
                sc.dw[0, h, :, cols] = r.astype(BF16)
        pair_copy("w", 0).start()

    def taps_early():
        turned([sc.hf[0, 0], sc.hf[0, 1]])
        for j in range(5):
            cols = slice(256 * j, min(256 * j + 256, 1152))
            sc.ack[:, cols] = dot_nn(sc.tb[:, :rows], sc.gb[0, :, cols])

    def taps_late():
        for j in range(5):
            cols = slice(256 * j, min(256 * j + 256, 1152))
            r = (sc.ack[:, cols] + dot_nn(sc.tb[:, rows:], sc.gb[1, :, cols])).astype(BF16)
            for e in range(r.shape[1] // LANES):
                tap = 2 * j + e
                sc.dk[0, 512 * tap : 512 * tap + 512, :] = r[:, lanes(e)]
        pair_copy("k", 0).start()

    def taps_grad(layer):
        turned([sc.hf[layer, 0], sc.hf[layer, 1]])
        for j in range(5):
            width = 256 if j < 4 else 128
            rhs = both(lambda m: sc.gb[m, :, 256 * j : 256 * j + width])
            r = dot_nn(sc.tb[...], rhs).astype(BF16)
            for e in range(width // LANES):
                tap = 2 * j + e
                sc.dk[layer, 512 * tap : 512 * tap + 512, :] = r[:, lanes(e)]
        pair_copy("k", layer).start()

    def half_rows(which):
        return pl.ds(pl.multiple_of(2304 * which, 2304), 2304)

    def pair_copy(kind, t):
        if kind == "w":
            src, dst, i = sc.dw.at[t, 1 - c], sc.prw.at[t], t
        else:
            src, dst, i = sc.dk.at[t, half_rows(1 - c)], sc.prk.at[t], 4 + t
        return remote(src, dst, sc.pw_s.at[i], sc.pw_r.at[i], sibling)

    def pair_sum(kind, t):
        pair_copy(kind, t).wait_recv()
        if kind == "w":
            sc.zsw[t] = (sc.dw[t, c].astype(F32) + sc.prw[t].astype(F32)).astype(BF16)
            return
        for i in range(4):
            part = slice(576 * i, 576 * i + 576)
            mine = pl.ds(pl.multiple_of(2304 * c + 576 * i, 576), 576)
            sc.zsk[t, part] = (
                sc.dk[t, mine].astype(F32) + sc.prk[t, part].astype(F32)
            ).astype(BF16)

    items = gradient_items(n)
    line = n_z == 4
    inner = (z == 1) | (z == 2)

    def tile_sem(it):
        return it.t if it.kind == "w" else 4 + it.t

    def tile(it, name):
        return getattr(sc, name + it.kind)

    def some(it, name, start, count):
        return tile(it, name).at[it.t, pl.ds(start, count)]

    def part_rows(it, which):
        half = it.nr // 2
        return pl.ds(pl.multiple_of(it.r0 + half * which, half), half)

    def up_copy(it):
        rows_of = pl.ds(it.r0, it.nr)
        return remote(
            tile(it, "zs").at[it.t, rows_of],
            tile(it, "zo").at[it.t, rows_of],
            sc.it_s.at[tile_sem(it)],
            sc.one_r.at[it.i],
            (p, 2 * (1 + lax.div(z, 3)) + c),
        )

    def mid_copy(it):
        return remote(
            tile(it, "zs").at[it.t, part_rows(it, 2 - z)],
            tile(it, "zi").at[it.t, pl.ds(it.r0 // 2, it.nr // 2)],
            sc.it_s.at[tile_sem(it)],
            sc.mid_r.at[it.i],
            (p, 2 * (3 - z) + c),
        )

    def inn_copy(it):
        view = tile(it, "fz").at[it.t, part_rows(it, z - 1)]
        return remote(
            view, view, sc.it_s.at[tile_sem(it)], sc.inn_r.at[it.i], (p, 2 * (3 - z) + c)
        )

    def down_copy(it, e):
        view = tile(it, "fz").at[it.t, part_rows(it, z - 1 if e == 0 else 2 - z)]
        return remote(
            view, view, sc.it_s.at[tile_sem(it)], sc.one_r.at[it.i], (p, 2 * (3 * (z - 1)) + c)
        )

    def direct_rows(it, j):
        count = it.nr // n_own
        return pl.ds(pl.multiple_of(it.r0 + count * j, count), count)

    def owner(index, body):
        if n_own == n_z:
            body()
        else:
            pl.when(index < n_own)(body)

    def scatter_copy(it, k):
        j = lax.rem(z + k, n_z)
        return j, remote(
            tile(it, "zs").at[it.t, direct_rows(it, lax.rem(j, n_own))],
            tile(it, "zo").at[it.t, k - 1],
            sc.it_s.at[tile_sem(it)],
            sc.one_r.at[it.i],
            (p, 2 * j + c),
        )

    def gather_copy(it, k):
        j = lax.rem(z + k, n_z)
        view = tile(it, "fz").at[it.t, direct_rows(it, lax.rem(z, n_own))]
        return remote(view, view, sc.ga_s.at[tile_sem(it)], sc.mid_r.at[it.i], (p, 2 * j + c))

    def add_rows(target, first, second):
        target[...] = (first[...].astype(F32) + second[...].astype(F32)).astype(BF16)

    def step_up(it):
        if line:

            @pl.when((z == 0) | (z == 3))
            def _():
                up_copy(it).start()

        else:

            def go(k):
                j, copy = scatter_copy(it, k)
                owner(j, lambda: copy.start())

            each(n_z, 1, go)

    def step_mid(it):
        if not line:
            return

        @pl.when(inner)
        def _():
            up_copy(it).wait_recv()
            mine = some(it, "zs", it.r0, it.nr)
            add_rows(mine, mine, some(it, "zo", it.r0, it.nr))
            mid_copy(it).start()

    def step_down(it):
        if line:

            @pl.when(inner)
            def _():
                mid_copy(it).wait_recv()
                keep = part_rows(it, z - 1)
                add_rows(
                    tile(it, "fz").at[it.t, keep],
                    tile(it, "zs").at[it.t, keep],
                    some(it, "zi", it.r0 // 2, it.nr // 2),
                )
                inn_copy(it).start()
                down_copy(it, 0).start()

            return

        def go():
            bytes_wait(tile(it, "zo").at[it.t], sc.one_r.at[it.i])
            mine = direct_rows(it, z)
            total = tile(it, "zs")[it.t, mine].astype(F32)
            total = lax.fori_loop(
                0, n_z - 1, lambda k, acc: acc + tile(it, "zo")[it.t, k].astype(F32), total
            )
            tile(it, "fz")[it.t, mine] = total.astype(BF16)
            each(n_z, 1, lambda k: gather_copy(it, k).start())

        owner(z, go)

    def step_last(it):
        if not line:
            return

        @pl.when(inner)
        def _():
            inn_copy(it).wait_recv()
            down_copy(it, 1).start()

    def owner_of(it):
        return it.t if it.kind == "w" else 2 * it.t + c

    def landing(it, q, core):
        if it.kind == "w":
            return sc.ow.at[q, core, pl.ds(it.r0, it.nr)]
        lane = pl.ds(128 * q, 128) if isinstance(q, int) else columns_of(q)
        return sc.ok.at[pl.ds(it.r0, it.nr), lane]

    def to_sem(it, sems):
        return sems.at[0 if it.kind == "w" else 1, it.part]

    def to_copy(it):
        return remote(
            some(it, "fz", it.r0, it.nr),
            landing(it, p, c),
            sc.to_s.at[tile_sem(it)],
            to_sem(it, sc.to_r),
            (owner_of(it), d),
        )

    def shared(it):
        return line and it.kind == "w" and it.t == 0

    def in_charge(it):
        outer = (z == 0) | (z == 3)
        return outer if it.part % 2 == 0 else jnp.logical_not(outer)

    def sends_out(it):
        if shared(it):
            return (p == 1) | ((p > 1) & in_charge(it))
        return p != owner_of(it)

    def passes_on(it):
        if shared(it):
            return (p == 0) & in_charge(it)
        return p < 0

    def pass_copy(it):
        view = sc.ow.at[pl.ds(2, 2), c, pl.ds(it.r0, it.nr)]
        return remote(view, view, sc.sh_s.at[it.part], sc.sh_r.at[it.part], z_pair)

    def step_inner_out(it):
        if line:
            pl.when(inner)(lambda: deliver(it))

    def step_out(it):
        if line:

            @pl.when((z == 0) | (z == 3))
            def _():
                bytes_wait(some(it, "fz", it.r0, it.nr), sc.one_r.at[it.i])
                deliver(it)

        else:
            count = it.nr // n_own
            if n_own == n_z:
                bytes_wait(some(it, "fz", it.r0, count * (n_own - 1)), sc.mid_r.at[it.i])
            else:

                @pl.when(z < n_own)
                def _():
                    bytes_wait(some(it, "fz", it.r0, count * (n_own - 1)), sc.mid_r.at[it.i])

                @pl.when(z >= n_own)
                def _():
                    bytes_wait(some(it, "fz", it.r0, count * n_own), sc.mid_r.at[it.i])

            deliver(it)

    def deliver(it):
        @pl.when(sends_out(it))
        def _():
            to_copy(it).start()

        def place(q):
            landing(it, q, c)[...] = some(it, "fz", it.r0, it.nr)[...]

        if it.kind == "w":
            pl.when(p == it.t)(lambda: place(it.t))
        else:
            for core in range(2):
                pl.when((p == 2 * it.t + core) & (c == core))(
                    functools.partial(place, 2 * it.t + core)
                )

    def sibling_copy(it, q):
        view = landing(it, q, c)
        return remote(
            view, view, sc.sib_s.at[0 if it.kind == "w" else 1], to_sem(it, sc.sib_r), sibling
        )

    def slices(it, count):
        if it.kind == "w":
            return sc.ow.at[pl.ds(0, count), 0, pl.ds(it.r0, it.nr)]
        return sc.ok.at[pl.ds(it.r0, it.nr), pl.ds(0, 128 * count)]

    def step_sibling(it):
        def go():
            bytes_wait(slices(it, 3), to_sem(it, sc.to_r))
            for q in range(4):
                sibling_copy(it, q).start()

        if not shared(it):
            pl.when(p == owner_of(it))(go)
            return

        @pl.when((p == 0) & in_charge(it))
        def _():
            bytes_wait(slices(it, 3), to_sem(it, sc.to_r))
            pass_copy(it).start()
            for q in range(4):
                sibling_copy(it, q).start()

        @pl.when((p == 0) & jnp.logical_not(in_charge(it)))
        def _():
            bytes_wait(slices(it, 1), to_sem(it, sc.to_r))
            for q in range(2):
                sibling_copy(it, q).start()

    def step_rest(it):
        if not shared(it):
            return

        @pl.when((p == 0) & jnp.logical_not(in_charge(it)))
        def _():
            bytes_wait(slices(it, 2), sc.sh_r.at[it.part])
            for q in range(2, 4):
                sibling_copy(it, q).start()

    def step_done(it):
        def go():
            bytes_wait(slices(it, 4), to_sem(it, sc.sib_r))

        pl.when(p == (it.t if it.kind == "w" else 2 * it.t + 1 - c))(go)

    def finish_grads():
        for kind, t in [("w", s) for s in range(4)] + [("k", layer) for layer in range(2)]:
            pair_copy(kind, t).wait_send()
            whole = next(it for it in items if it.kind == kind and it.t == t)
            sends = sc.it_s.at[tile_sem(whole)]
            half = tile(whole, "zs").at[t]
            if line:

                @pl.when(inner)
                def _(kind=kind, t=t, sends=sends):
                    bytes_wait((sc.dw if kind == "w" else sc.dk).at[t], sends)

                @pl.when((z == 0) | (z == 3))
                def _(half=half, sends=sends):
                    bytes_wait(half, sends)

            else:

                def sent(k, it=whole):
                    j, copy = scatter_copy(it, k)
                    owner(j, lambda: copy.wait_send())

                each(n_z, 1, sent)
                owner(
                    z,
                    lambda it=whole: each(n_z, 1, lambda k: gather_copy(it, k).wait_send()),
                )

        for it in items:

            @pl.when(sends_out(it))
            def _(it=it):
                bytes_wait(some(it, "fz", it.r0, it.nr), sc.to_s.at[tile_sem(it)])

            @pl.when(passes_on(it))
            def _(it=it):
                bytes_wait(slices(it, 2), sc.sh_s.at[it.part])

        bytes_wait(sc.ow.at[:, 0], sc.sib_s.at[0])

        @pl.when(c == parity)
        def _():
            bytes_wait(sc.ok.at[...], sc.sib_s.at[1])

    finish.append(finish_grads)

    def gain_copies(off):
        dev = (pipe_at(off), d)
        return [
            remote(sc.gsm.at[:, p], sc.gsm.at[:, p], sc.g_s.at[0], sc.g_r.at[0], dev),
            remote(sc.gsw.at[:, p], sc.gsw.at[:, p], sc.g_s.at[1], sc.g_r.at[1], dev),
        ]

    def gains_wait(sems):
        bytes_wait(sc.gsm.at[:, pl.ds(0, 3)], sems.at[0])
        bytes_wait(sc.gsw.at[:, pl.ds(0, 3)], sems.at[1])

    def gains_start():
        for off in range(1, 4):
            for copy in gain_copies(off):
                copy.start()

    def gains_done():
        gains_wait(sc.g_r)
        for q in range(4):
            sc.gmo[0, :, lanes(q)] = sc.gsm[p, q]
        layer = lax.div(p, 2)
        for e in range(2):
            sc.goo[0, :, 512 * e : 512 * e + 512] = sc.gsw[layer, 2 * parity + e]
        outs.append(put_out(0, sc.gmo.at[...], gmid_ref.at[...]))
        outs.append(put_out(7, sc.goo.at[...], gout_ref.at[...]))

    def finish_gains():
        gains_wait(sc.g_s)

    finish.append(finish_gains)

    def of(kind, t):
        return [it for it in items if it.kind == kind and it.t == t]

    def one(step, kind, t, part):
        for it in of(kind, t)[part : part + 1]:
            step(it)

    def run(step, kind, t):
        for it in of(kind, t):
            step(it)

    def nothing():
        return None

    def paired(arrival, reply, layer, hooks=(nothing, nothing)):
        for m in range(2):
            arrival(layer, m)
            hooks[m]()
            reply(layer, m)

    def steps(*listed):
        def go():
            for body, *rest in listed:
                body(*rest)

        return go

    up, mid, down, last, out = step_up, step_mid, step_down, step_last, step_out
    inside = step_inner_out
    wide, taps = 0, 1
    spread_first(wide, 0)
    spread_second(wide, 0)
    ready(wide, 0)
    own_x.wait()
    first_part(0, 0)
    first_part(0, 1)
    own_n.wait()
    bytes_wait(sc.go.at[0], sc.loc.at[6])
    own_cot.wait()
    own_g.wait()
    norm_wait(sc.n_r)
    spread_first(taps, 0)
    spread_first(taps, 1)
    paired(
        first_norm,
        hidden_one,
        0,
        (
            steps((spread_second, taps, 0), (spread_second, taps, 1)),
            steps((spread_first, wide, 1)),
        ),
    )
    ready(taps, 0)
    ready(taps, 1)
    paired(
        second_part,
        hidden_two,
        0,
        (steps((spread_first, wide, 2), (spread_second, wide, 1)), steps((spread_first, taps, 2))),
    )
    ready(wide, 1)

    def turn(layer, m):
        pre_values(0, m)
        if m == 0:
            ready(wide, 2)
        first_part(1, m)

    paired(
        third_part,
        turn,
        0,
        (
            steps((spread_second, wide, 2), (spread_first, taps, 3), (spread_second, taps, 2)),
            steps((spread_first, wide, 3)),
        ),
    )
    paired(
        first_norm,
        hidden_one,
        1,
        (steps((spread_second, taps, 3)), steps((spread_second, wide, 3))),
    )
    ready(taps, 2)
    ready(taps, 3)
    paired(second_part, hidden_two, 1)
    ready(wide, 3)
    third_part(1, 0)
    pre_values(1, 0)
    third_part(1, 1)
    grad_out_norm(1, 0)
    pre_values(1, 1)
    outs = [put_out(2, sc.mix.at[...], mixed_ref.at[...])]
    grad_out_norm(1, 1)
    wide_grad(3, lambda m: sc.gt[m], lambda m: ag_value(3, m))
    paired(
        grad_two,
        grad_second,
        1,
        (
            steps((pair_sum, "w", 3), (one, up, "w", 3, 0), (slopes, 0)),
            steps((one, up, "w", 3, 1), (slopes, 1), (one, mid, "w", 3, 0)),
        ),
    )
    taps_grad(1)
    grad_one(1, 0)
    steps(
        (pair_sum, "k", 1),
        (one, up, "k", 1, 0),
        (one, mid, "w", 3, 1),
        (one, down, "w", 3, 0),
    )()
    grad_first(1, 0)
    grad_one(1, 1)
    conv_grad(1, 0)
    steps(
        (one, up, "k", 1, 1),
        (one, down, "w", 3, 1),
        (one, last, "w", 3, 0),
        (one, mid, "k", 1, 0),
    )()
    grad_first(1, 1)
    grad_out_norm(0, 0)
    conv_grad(1, 1)
    outs.append(put_out(3, sc.gp.at[0], gpre_ref.at[...]))
    steps(
        (one, up, "k", 1, 2),
        (one, last, "w", 3, 1),
        (one, mid, "k", 1, 1),
        (one, down, "k", 1, 0),
        (wide_grad, 2, lambda m: sc.s1[m], lambda m: sc.gff[1, m]),
    )()
    grad_out_norm(0, 1)
    wide_grad(1, lambda m: sc.gt[m], lambda m: ag_value(2, m))
    paired(
        grad_two,
        grad_second,
        0,
        (
            steps(
                (pair_sum, "w", 1),
                (one, up, "w", 1, 0),
                (one, mid, "k", 1, 2),
                (one, down, "k", 1, 1),
                (one, last, "k", 1, 0),
            ),
            steps(
                (one, up, "w", 1, 1),
                (pair_sum, "w", 2),
                (one, mid, "w", 1, 0),
                (one, down, "k", 1, 2),
                (one, last, "k", 1, 1),
                (taps_early,),
            ),
        ),
    )
    taps_late()
    grad_one(0, 0)
    steps(
        (pair_sum, "k", 0),
        (one, up, "k", 0, 0),
        (one, up, "k", 0, 1),
        (one, mid, "w", 1, 1),
        (one, down, "w", 1, 0),
        (one, last, "k", 1, 2),
    )()
    grad_first(0, 0)
    grad_one(0, 1)
    steps(
        (one, up, "k", 0, 2),
        (one, up, "k", 0, 3),
        (one, up, "k", 0, 4),
        (one, up, "k", 0, 5),
        (one, mid, "k", 0, 0),
        (one, mid, "k", 0, 1),
        (one, down, "w", 1, 1),
        (one, last, "w", 1, 0),
    )()
    one(down, "k", 0, 0)
    one(mid, "k", 0, 2)
    conv_grad(0, 0)
    one(down, "k", 0, 1)
    grad_first(0, 1)
    gains_start()
    one(mid, "k", 0, 3)
    one(last, "k", 0, 0)
    one(down, "k", 0, 2)
    one(last, "w", 1, 1)
    one(up, "w", 2, 0)
    one(last, "k", 0, 1)
    one(mid, "k", 0, 4)
    one(down, "k", 0, 3)
    run(inside, "k", 1)
    run(out, "k", 1)
    wide_early()
    conv_grad(0, 1)
    wide_late()
    run(inside, "w", 1)
    one(inside, "k", 0, 0)
    one(inside, "k", 0, 1)
    run(out, "w", 1)
    one(out, "k", 0, 0)
    one(out, "k", 0, 1)
    one(last, "k", 0, 2)
    one(inside, "k", 0, 2)
    one(mid, "k", 0, 5)
    one(down, "k", 0, 4)
    one(last, "k", 0, 3)
    one(inside, "k", 0, 3)
    outs.append(put_out(4, sc.cin.at[...], conv_ref.at[...]))
    pair_sum("w", 0)
    run(up, "w", 0)
    one(up, "w", 2, 1)
    one(out, "k", 0, 2)
    one(down, "k", 0, 5)
    one(last, "k", 0, 4)
    one(inside, "k", 0, 4)
    one(out, "k", 0, 3)
    one(mid, "w", 0, 0)
    one(mid, "w", 2, 0)
    run(inside, "w", 3)
    run(out, "w", 3)
    one(mid, "w", 0, 1)
    one(last, "k", 0, 5)
    one(inside, "k", 0, 5)
    one(out, "k", 0, 4)
    one(down, "w", 0, 0)
    one(mid, "w", 0, 2)
    one(down, "w", 0, 1)
    one(out, "k", 0, 5)
    one(down, "w", 2, 0)
    one(last, "w", 0, 0)
    one(inside, "w", 0, 0)
    one(mid, "w", 0, 3)
    one(down, "w", 0, 2)
    one(last, "w", 0, 1)
    one(inside, "w", 0, 1)
    one(out, "w", 0, 0)
    one(mid, "w", 2, 1)
    one(last, "w", 2, 0)
    one(inside, "w", 2, 0)
    one(down, "w", 0, 3)
    one(last, "w", 0, 2)
    one(inside, "w", 0, 2)
    one(out, "w", 0, 1)
    one(out, "w", 2, 0)
    one(down, "w", 2, 1)
    one(last, "w", 0, 3)
    one(inside, "w", 0, 3)
    one(out, "w", 0, 2)
    one(last, "w", 2, 1)
    one(inside, "w", 2, 1)
    for part in range(4):
        one(step_sibling, "k", 0, part)
    one(out, "w", 0, 3)
    one(step_sibling, "k", 0, 4)
    one(step_sibling, "k", 0, 5)
    one(out, "w", 2, 1)
    run(step_sibling, "w", 3)
    gains_done()
    run(step_sibling, "k", 1)
    run(step_sibling, "w", 2)
    run(step_sibling, "w", 1)
    one(step_sibling, "w", 0, 0)
    one(step_sibling, "w", 0, 1)
    run(step_done, "k", 1)
    run(step_done, "k", 0)
    outs.append(put_out(1, sc.ok.at[...], gtaps_ref.at[...]))
    for s in (3, 2, 1):
        run(step_done, "w", s)
    final = of("w", 0)
    for it in final[2:]:
        step_sibling(it)
    for it in final:
        step_rest(it)
    for group, part in enumerate((final[:-1], final[-1:]) if len(final) > 1 else (final,)):
        first, count = part[0].r0, sum(it.nr for it in part)
        for it in part:
            step_done(it)
        part_rows_of = pl.ds(first, count)
        outs.append(
            put_out(
                5 + group, sc.ow.at[:, :, part_rows_of], gwide_ref.at[:, :, part_rows_of]
            )
        )
    for copy in outs:
        copy.wait()
    for body in finish:
        body()


def cast_pieces(rows):
    pieces = [("taps", pl.ds(576 * i, 576)) for i in range(4)]
    pieces += [("wide", pl.ds(512 * i, 512)) for i in range(4)]
    return pieces + [("stream", m) for m in range(2)]


def cast_kernel(mixed, gpre, conv, gwide, gtaps, gmid, gout, *refs):
    o_mixed, o_input, o_wide, o_taps, o_mid, o_out = refs[:6]
    b_taps, b_wide, b_gpre, b_conv, f_taps, f_wide, f_stream = refs[6:13]
    b_mixed, b_mid, b_out, r_sem, w_sem, d_sem = refs[13:]
    pieces = cast_pieces(gpre.shape[1])
    same = ((mixed, b_mixed, o_mixed), (gmid, b_mid, o_mid), (gout, b_out, o_out))
    arrive = [pltpu.make_async_copy(a, b, d_sem.at[i]) for i, (a, b, _) in enumerate(same)]
    leave = [pltpu.make_async_copy(b, o, d_sem.at[i]) for i, (_, b, o) in enumerate(same)]
    reads, writes = [], []
    for i, (kind, part) in enumerate(pieces):
        if kind == "stream":
            reads.append(
                [
                    pltpu.make_async_copy(gpre.at[part], b_gpre.at[part], r_sem.at[i]),
                    pltpu.make_async_copy(conv.at[part], b_conv.at[part], r_sem.at[i + 2]),
                ]
            )
            writes.append(
                pltpu.make_async_copy(f_stream.at[part], o_input.at[part], w_sem.at[i])
            )
            continue
        src, low, high, dst = (
            (gtaps, b_taps, f_taps, o_taps)
            if kind == "taps"
            else (gwide, b_wide, f_wide, o_wide)
        )
        reads.append([pltpu.make_async_copy(src.at[part], low.at[part], r_sem.at[i])])
        writes.append(pltpu.make_async_copy(high.at[part], dst.at[part], w_sem.at[i]))
    for group in reads:
        for copy in group:
            copy.start()
    for copy in arrive:
        copy.start()
    for (kind, part), group, write in zip(pieces, reads, writes):
        for copy in group:
            copy.wait()
        size = 64

        def strip(i, carry, kind=kind, part=part):
            if kind == "stream":
                at = pl.ds(pl.multiple_of(i * size, size), size)
                f_stream[part, at] = b_gpre[part, at].astype(F32) + b_conv[part, at].astype(F32)
                return carry
            at = pl.ds(pl.multiple_of(part.start + i * size, size), size)
            if kind == "taps":
                f_taps[at] = b_taps[at].astype(F32)
            else:
                f_wide[at] = b_wide[at].astype(F32)
            return carry

        lax.fori_loop(0, (gpre.shape[1] if kind == "stream" else part.size) // size, strip, 0)
        write.start()
    for first, second in zip(arrive, leave):
        first.wait()
        second.start()
    for copy in writes + leave:
        copy.wait()


def cast_all(mixed, gpre, conv, gwide, gtaps, gmid, gout):
    anywhere = pl.BlockSpec(memory_space=pl.ANY)
    shape = jax.ShapeDtypeStruct
    count = len(cast_pieces(gpre.shape[1]))
    return pl.pallas_call(
        cast_kernel,
        in_specs=[anywhere] * 7,
        out_specs=[anywhere] * 6,
        out_shape=[
            shape(mixed.shape, BF16),
            shape(mixed.shape, F32),
            shape(gwide.shape, F32),
            shape(gtaps.shape, F32),
            shape(gmid.shape, F32),
            shape(gout.shape, F32),
        ],
        scratch_shapes=[
            pltpu.VMEM(gtaps.shape, BF16),
            pltpu.VMEM(gwide.shape, BF16),
            pltpu.VMEM(gpre.shape, BF16),
            pltpu.VMEM(gpre.shape, BF16),
            pltpu.VMEM(gtaps.shape, F32),
            pltpu.VMEM(gwide.shape, F32),
            pltpu.VMEM(gpre.shape, F32),
            pltpu.VMEM(mixed.shape, BF16),
            pltpu.VMEM(gmid.shape, F32),
            pltpu.VMEM(gout.shape, F32),
            pltpu.SemaphoreType.DMA((count + 2,)),
            pltpu.SemaphoreType.DMA((count,)),
            pltpu.SemaphoreType.DMA((3,)),
        ],
        compiler_params=pltpu.CompilerParams(vmem_limit_bytes=60 * 2**20),
        name="casts",
    )(mixed, gpre, conv, gwide, gtaps, gmid, gout)


def local(block_input, cotangent, weight_wide, weight_taps, norm_mid, norm_out, group_counts):
    n_dp = group_counts.shape[1]
    micro, rows, width = block_input.shape
    scratch = scratch_list(n_dp, rows)
    anywhere = pl.BlockSpec(memory_space=pl.ANY)

    def shape(dims, dtype):
        return jax.ShapeDtypeStruct(dims, dtype)

    stream = (micro, rows, width)
    mixed, gpre, conv, gwide, gtaps, gmid, gout = pl.pallas_call(
        functools.partial(kernel, list(scratch), n_dp),
        out_shape=[
            shape(stream, BF16),
            shape(stream, BF16),
            shape(stream, BF16),
            shape((4, 2, 256, 512), BF16),
            shape((2304, 512), BF16),
            shape(norm_mid.shape, F32),
            shape(norm_out.shape, F32),
        ],
        in_specs=[anywhere] * 7,
        out_specs=[anywhere] * 7,
        scratch_shapes=list(scratch.values()),
        compiler_params=pltpu.CompilerParams(
            collective_id=0, has_side_effects=True, vmem_limit_bytes=62 * 2**20
        ),
        name="layers",
    )(block_input, cotangent, weight_wide, weight_taps.reshape(9, 256, 512), norm_mid, norm_out, jnp.swapaxes(group_counts, 1, 2))
    results = cast_all(mixed, gpre, conv, gwide.reshape(2048, 512), gtaps, gmid, gout)
    mixed, grad_input, gwide, gtaps, gmid, gout = results
    return (
        mixed,
        grad_input,
        gwide.reshape(weight_wide.shape),
        gtaps.reshape(weight_taps.shape),
        gmid,
        gout,
    )


def solution(mesh):
    split = P(None, "dp", "pipe")
    section = P("pipe", None, None)
    return jax.shard_map(
        local,
        mesh=mesh,
        in_specs=(split, split, section, section, section, section, P()),
        out_specs=(split, split, section, section, section, section),
        check_vma=False,
    )
```

```python
import functools
from types import SimpleNamespace

import jax
import jax.numpy as jnp
from jax import lax
from jax.experimental import pallas as pl
from jax.experimental.pallas import tpu as pltpu
from jax.sharding import PartitionSpec as P

MESH = pl.DeviceIdType.MESH
F32 = jnp.float32
BF16 = jnp.bfloat16
EPS = 1e-05
LANES = 128
N_PIPE = 4
SIDES = (7, 6, 5, 2)


def dot_nn(a, b):
    return jnp.dot(a, b, preferred_element_type=F32)


def dot_nt(a, b):
    return lax.dot_general(a, b, (((1,), (1,)), ((), ())), preferred_element_type=F32)


def sigmoid(v):
    return jax.nn.sigmoid(v)


def sizes(n_dp):
    n_z = n_dp // 2
    n_own = min(n_z, 16)
    return n_z, n_own


def gradient_items(n_dp):
    line = n_dp // 2 == 4
    listed = []
    for kind, index, parts in (
        ("w", 3, [128, 128]),
        ("k", 1, [768] * 3),
        ("w", 2, [128, 128]),
        ("w", 1, [128, 128]),
        ("k", 0, [288, 288, 288, 288, 576, 576]),
        ("w", 0, [64] * 4),
    ):
        start = 0
        for part, rows in enumerate(parts if line else [sum(parts)]):
            listed.append(
                SimpleNamespace(
                    kind=kind, t=index, r0=start, nr=rows, i=len(listed), part=part
                )
            )
            start += rows
    return listed


def scratch_list(n_dp, rows):
    n_z, n_own = sizes(n_dp)
    items = len(gradient_items(n_dp))
    line = n_z == 4
    dma = pltpu.SemaphoreType.DMA

    def half(*shape):
        return pltpu.VMEM(shape, BF16)

    def full(*shape):
        return pltpu.VMEM(shape, F32)

    return dict(
        wt=half(4, 512, 512),
        k2=half(2, 18, 256, 128),
        gm=full(4, 2, 128),
        gmf=full(4, 2, 512),
        hf=half(2, 2, rows, 512),
        gff=half(2, 2, rows, 512),
        sml=full(2, 2, 4, 4, 128),
        go=full(4, 2, 2, 512),
        msk=full(2, rows, 128),
        beside=full(2, 2, rows, 128),
        above=full(2, 4, 2, rows, 128),
        yf=full(9, rows, 128),
        part=half(2, 2, 4, rows, 128),
        rsr=half(6 if line else 2, 2, 3, rows, 128),
        ag=half(6, 2, 4, rows, 128),
        stm=full(8, 2, n_dp, 2, 128),
        stw=full(4, 2, n_dp, 2, 512),
        midv=full(4, 2, rows, 128),
        dzm=full(2, rows, 128),
        inv_mid=full(4, 2, 1, 128),
        inv_wide=full(2, 2, 1, 512),
        widv=full(2, 2, rows, 512),
        pre0=full(2, rows, 512),
        s1=half(2, rows, 512),
        mix=half(2, rows, 512),
        gp=half(2, 2, rows, 512),
        gt=half(2, rows, 512),
        gb=half(2, rows, 1152),
        tb=half(512, 2 * rows),
        ack=full(512, 1152),
        dw=half(4, 2, 256, 512),
        prw=half(4, 256, 512),
        zsw=half(4, 256, 512),
        fzw=half(4, 256, 512),
        ow=half(4, 2, 256, 512),
        dk=half(2, 4608, 128),
        prk=half(2, 2304, 128),
        zsk=half(2, 2304, 128),
        fzk=half(2, 2304, 128),
        ok=half(2304, 512),
        zow=half(4, 256, 512) if line else half(4, n_z - 1, 256 // n_own, 512),
        ziw=half(4, 128, 512) if line else half(1, 16, 128),
        zok=half(2, 2304, 128) if line else half(2, n_z - 1, 2304 // n_own, 128),
        zik=half(2, 1152, 128) if line else half(1, 16, 128),
        gsm=full(4, 4, 2, 128),
        gsw=full(2, 4, 2, 512),
        cnt=pltpu.SMEM((2, n_dp), F32),
        xin=half(2, rows, 512),
        cin=half(2, rows, 512),
        gmo=full(1, 2, 512),
        goo=full(1, 2, 1024),
        counts=pltpu.SMEM((2, 4, n_dp), jnp.int32),
        f_s=dma((2,)),
        f_r=dma((2, 4)),
        z_r=dma((2, 4)),
        b_s=dma((2, 4)),
        b_r=dma((2, 4)),
        n_s=dma((3,)),
        n_r=dma((3,)),
        sm_s=dma((2, 2)),
        sm_r=dma((2, 2)),
        loc=dma((8,)),
        ex_s=dma((2, 2)),
        ex_r=dma((2, 2)),
        st_s=dma((2, 2)),
        st_r=dma((2, 2)),
        pw_s=dma((6,)),
        pw_r=dma((6,)),
        it_s=dma((6,)),
        one_r=dma((items,)),
        mid_r=dma((items,)),
        inn_r=dma((items,)),
        to_s=dma((6,)),
        ga_s=dma((6 if n_z != 4 else 1,)),
        sh_s=dma((4,)),
        sh_r=dma((4,)),
        to_r=dma((2, 6)),
        sib_s=dma((2,)),
        sib_r=dma((2, 6)),
        g_s=dma((2,)),
        g_r=dma((2,)),
        out=dma((8,)),
    )


def kernel(names, n, *refs):
    (x_hbm, cot_hbm, wide_ref, taps_ref, nmid_ref, nout_ref, counts_hbm) = refs[:7]
    (mixed_ref, gpre_ref, conv_ref, gwide_ref, gtaps_ref, gmid_ref, gout_ref) = refs[7:14]
    sc = SimpleNamespace(**dict(zip(names, refs[14:])))
    counts_ref = sc.counts
    x_ref, cot_ref = sc.xin, sc.cin
    rows = x_ref.shape[1]
    n_z, n_own = sizes(n)
    p = lax.axis_index("pipe")
    d = lax.axis_index("dp")
    z = lax.div(d, 2)
    c = lax.rem(d, 2)
    parity = lax.rem(p, 2)
    sibling = (p, 2 * z + 1 - c)
    z_odd = lax.rem(z, 2)
    z_pair = (p, 2 * (z + 1 - 2 * z_odd) + c)
    quarter = 2 * z_odd + c
    quarter_z = 2 * (1 - z_odd) + c
    finish = []

    def pipe_at(off):
        return lax.rem(p + N_PIPE + (2 * parity - 1) * off, N_PIPE)

    def remote(src, dst, ss, rs, dev):
        return pltpu.make_async_remote_copy(
            src_ref=src, dst_ref=dst, send_sem=ss, recv_sem=rs, device_id=dev, device_id_type=MESH
        )

    def each(count, first, body):
        if count - first <= 8:
            for k in range(first, count):
                body(k)
        else:

            def step(k, carry):
                body(k)
                return carry

            lax.fori_loop(first, count, step, 0)

    def bytes_wait(view, sem):
        pltpu.make_async_copy(view, view, sem).wait()

    barrier = pltpu.get_barrier_semaphore()
    for off in range(1, N_PIPE):
        pl.semaphore_signal(barrier, inc=1, device_id=(pipe_at(off), d), device_id_type=MESH)

    def greet(k):
        pl.semaphore_signal(
            barrier, inc=1, device_id=(p, lax.rem(d + k, n)), device_id_type=MESH
        )

    each(n, 1, greet)

    def columns_of(q):
        return pl.ds(pl.multiple_of(128 * q, 128), 128)

    own_w = pltpu.make_async_copy(
        wide_ref.at[0, pl.ds(pl.multiple_of(512 * p, 512), 512), :], sc.wt.at[p], sc.loc.at[0]
    )
    own_k = pltpu.make_async_copy(
        taps_ref.at[:, :, columns_of(p)],
        sc.k2.at[lax.div(p, 2), pl.ds(9 * parity, 9)],
        sc.loc.at[1],
    )
    own_c = pltpu.make_async_copy(counts_hbm, counts_ref, sc.loc.at[2])
    own_c.start()
    own_x = pltpu.make_async_copy(x_hbm, sc.xin, sc.loc.at[4])
    own_cot = pltpu.make_async_copy(cot_hbm, sc.cin, sc.loc.at[5])
    own_x.start()
    own_w.start()
    own_k.start()
    own_n = pltpu.make_async_copy(
        nmid_ref.at[0, :, columns_of(p)], sc.gm.at[p], sc.loc.at[3]
    )
    own_n.start()
    for e in range(2):
        pltpu.make_async_copy(
            nout_ref.at[0, :, pl.ds(512 * e, 512)], sc.go.at[p, e], sc.loc.at[6]
        ).start()
    own_cot.start()
    own_g = pltpu.make_async_copy(nmid_ref.at[0], sc.gmf.at[p], sc.loc.at[7])
    own_g.start()

    own_c.wait()

    def used_rows(m, j):
        return (
            49 * counts_ref[m, 0, j]
            + 36 * counts_ref[m, 1, j]
            + 25 * counts_ref[m, 2, j]
            + 4 * counts_ref[m, 3, j]
        )

    totals = []
    for m in range(2):

        def count_up(j, acc, m=m):
            used = used_rows(m, j)
            sc.cnt[m, j] = used.astype(F32)
            return acc + used

        totals.append(lax.fori_loop(0, n, count_up, jnp.int32(0)).astype(F32))

    pl.semaphore_wait(barrier, N_PIPE - 1 + n - 1)

    def held(kind, s, part):
        if kind == 0:
            return sc.wt.at[s, pl.ds(pl.multiple_of(128 * part, 128), 128)]
        layer, odd = (s // 2, s % 2) if isinstance(s, int) else (lax.div(s, 2), lax.rem(s, 2))
        return sc.k2.at[
            layer, pl.ds(9 * odd, 9), pl.ds(pl.multiple_of(64 * part, 64), 64)
        ]

    def fetch(kind, off):
        q = pipe_at(off)
        if kind == 0:
            src = wide_ref.at[0, pl.ds(pl.multiple_of(512 * q + 128 * quarter, 128), 128), :]
        else:
            src = taps_ref.at[:, pl.ds(pl.multiple_of(64 * quarter, 64), 64), columns_of(q)]
        return remote(
            src, held(kind, p, quarter), sc.f_s.at[kind], sc.f_r.at[kind, p], (q, d)
        )

    def send_norm(off):
        q = pipe_at(off)
        listed = [
            remote(
                nmid_ref.at[0, :, columns_of(q)],
                sc.gm.at[p],
                sc.n_s.at[0],
                sc.n_r.at[0],
                (q, d),
            ),
            remote(nmid_ref.at[0], sc.gmf.at[p], sc.n_s.at[2], sc.n_r.at[2], (q, d)),
        ]
        for e in range(2):
            listed.append(
                remote(
                    nout_ref.at[0, :, pl.ds(512 * e, 512)],
                    sc.go.at[p, e],
                    sc.n_s.at[1],
                    sc.n_r.at[1],
                    (q, d),
                )
            )
        return listed

    def norm_wait(sems):
        bytes_wait(sc.gm.at[pl.ds(0, 3)], sems.at[0])
        bytes_wait(sc.go.at[pl.ds(0, 3)], sems.at[1])
        bytes_wait(sc.gmf.at[pl.ds(0, 3)], sems.at[2])

    def pass_z(kind, s):
        view = held(kind, s, quarter)
        return remote(view, view, sc.b_s.at[kind, s], sc.z_r.at[kind, s], z_pair)

    def pass_sibling(kind, s, e):
        view = held(kind, s, quarter if e == 0 else quarter_z)
        return remote(view, view, sc.b_s.at[kind, s], sc.b_r.at[kind, s], sibling)

    def spread_first(kind, s):
        @pl.when(p != s)
        def _():
            view = held(kind, s, quarter)
            bytes_wait(view, sc.f_r.at[kind, s])
            pass_z(kind, s).start()
            pass_sibling(kind, s, 0).start()

    def spread_second(kind, s):
        @pl.when(p != s)
        def _():
            pass_z(kind, s).wait_recv()
            pass_sibling(kind, s, 1).start()

    def quarters(kind, s, count):
        if kind == 0:
            return sc.wt.at[s, pl.ds(0, 128 * count)]
        return sc.k2.at[s // 2, pl.ds(9 * (s % 2), 9), pl.ds(0, 64 * count)]

    def ready(kind, s):
        @pl.when(p != s)
        def _():
            bytes_wait(quarters(kind, s, 2), sc.b_r.at[kind, s])

        @pl.when(p == s)
        def _():
            (own_w if kind == 0 else own_k).wait()

    def finish_weights():
        for kind in range(2):
            bytes_wait(quarters(kind, 0, 3), sc.f_s.at[kind])
            for s in range(4):

                @pl.when(p != s)
                def _(kind=kind, s=s):
                    bytes_wait(quarters(kind, s, 3), sc.b_s.at[kind, s])

    finish.append(finish_weights)

    for even in range(2):

        @pl.when(parity == even)
        def _(even=even):
            for kind in (even, 1 - even):
                for off in range(1, 4):
                    fetch(kind, off).start()
                if kind == even:
                    for off in range(1, 4):
                        for copy in send_norm(off):
                            copy.start()

    def finish_norm():
        norm_wait(sc.n_s)

    finish.append(finish_norm)

    row_id = lax.broadcasted_iota(jnp.int32, (rows, LANES), 0).astype(F32)

    def build(m):
        ends = [jnp.float32(0.0)]
        total = jnp.int32(0)
        for g, side in enumerate(SIDES):
            total = total + side * side * counts_ref[m, g, d]
            ends.append(total.astype(F32))
        sc.msk[m] = jnp.where(row_id < ends[4], 1.0, 0.0)
        left = jnp.zeros((rows, LANES), F32)
        right = left
        for g, side in enumerate(SIDES):
            inside = (row_id >= ends[g]) & (row_id < ends[g + 1])
            within = row_id - ends[g]
            within = within - side * side * jnp.floor((within + 0.5) / (side * side))
            map_row = jnp.floor((within + 0.5) / side)
            map_col = within - side * map_row
            left = jnp.where(inside & (map_col > 0.5), 1.0, left)
            right = jnp.where(inside & (map_col < side - 1.5), 1.0, right)
            sc.above[m, g, 0] = jnp.where(inside & (map_row > 0.5), 1.0, 0.0)
            sc.above[m, g, 1] = jnp.where(inside & (map_row < side - 1.5), 1.0, 0.0)
        sc.beside[m, 0] = left
        sc.beside[m, 1] = right

    def shifted(values, count):
        return pltpu.roll(values, count % rows, 0)

    def from_above(values, m):
        return sum(
            sc.above[m, g, 0] * shifted(values, side) for g, side in enumerate(SIDES)
        )

    def from_below(values, m):
        return sum(
            sc.above[m, g, 1] * shifted(values, -side) for g, side in enumerate(SIDES)
        )

    for m in range(2):
        build(m)


    exchange_order = [
        ("rs", 0), ("ag", 0), ("ag", 2), ("rs", 1), ("ag", 1), ("ag", 3),
        ("rs", 3), ("rs", 5), ("ag", 5), ("rs", 2), ("rs", 4), ("ag", 4),
    ]

    def rs_slot(rid):
        return rid if sc.rsr.shape[0] == 6 else rs_par[rid]

    def three(kind, i, m):
        return sc.rsr.at[rs_slot(i), m] if kind == "rs" else sc.ag.at[i, m, pl.ds(0, 3)]

    def exchange_wait(sems, kind, i, m):
        turn = exchange_order.index((kind, i))
        bytes_wait(three(kind, i, m), sems.at[turn % 2, m])

    def exchange_open(kind, i, m):
        turn = exchange_order.index((kind, i))
        if turn >= 2:
            exchange_wait(sc.ex_s, *exchange_order[turn - 2], m)
        return sc.ex_s.at[turn % 2, m], sc.ex_r.at[turn % 2, m]

    def rs_sum(rid, m, par):
        exchange_wait(sc.ex_r, "rs", rid, m)
        total = sc.part[par, m, p].astype(F32)
        for k in range(3):
            total = total + sc.rsr[rs_slot(rid), m, k].astype(F32)
        return total

    def ag_start(aid, m, value):
        ss, rs = exchange_open("ag", aid, m)
        sc.ag[aid, m, p] = value
        own = sc.ag.at[aid, m, p]
        for off in range(1, 4):
            remote(own, own, ss, rs, (pipe_at(off), d)).start()

    def ag_wait(aid, m):
        exchange_wait(sc.ex_r, "ag", aid, m)

    def ag_value(aid, m):
        return jnp.concatenate([sc.ag[aid, m, q] for q in range(4)], axis=1)

    def finish_exchanges():
        for kind, i in exchange_order[-2:]:
            for m in range(2):
                exchange_wait(sc.ex_s, kind, i, m)

    finish.append(finish_exchanges)

    sum_order = [
        (False, 0), (False, 1), (True, 0), (False, 2), (False, 3), (True, 1),
        (True, 3), (False, 7), (False, 6), (True, 2), (False, 5), (False, 4),
    ]

    def st_buffer(wide, i, m):
        return (sc.stw if wide else sc.stm).at[i, m]

    def st_bytes(sems, wide, i, m):
        turn = sum_order.index((wide, i))
        bytes_wait(st_buffer(wide, i, m).at[pl.ds(0, n - 1)], sems.at[turn % 2, m])

    def st_start(wide, i, m):
        turn = sum_order.index((wide, i))
        if turn >= 2:
            st_bytes(sc.st_s, *sum_order[turn - 2], m)
        own = st_buffer(wide, i, m).at[d]
        ss, rs = sc.st_s.at[turn % 2, m], sc.st_r.at[turn % 2, m]

        def go(k):
            remote(own, own, ss, rs, (p, lax.rem(d + k, n))).start()

        if n > 8:
            each(n, 1, go)
            return
        high = lax.div(2 * z, n_z)
        for i in range(n_z - 1):
            low_far = n_z - 1 - i - lax.div(z + i + 1, n_z)
            high_far = i + lax.div(i - z + n_z, n_z)
            far = high * high_far + (1 - high) * low_far
            for e in range(2):
                remote(own, own, ss, rs, (p, 2 * far + e)).start()
        remote(own, own, ss, rs, sibling).start()

    def st_wait(wide, i, m):
        st_bytes(sc.st_r, wide, i, m)

    def finish_st():
        for wide, i in sum_order[-2:]:
            for m in range(2):
                st_bytes(sc.st_s, wide, i, m)

    finish.append(finish_st)

    def over_devices(body, init):
        if n <= 8:
            for j in range(n):
                init = body(j, init)
            return init
        return lax.fori_loop(0, n, body, init)

    def combine(wide, i, m):
        st_wait(wide, i, m)
        ref = sc.stw if wide else sc.stm
        blank = jnp.zeros((1, ref.shape[-1]), F32)
        mean = over_devices(
            lambda j, acc: acc + sc.cnt[m, j] * ref[i, m, j, 0:1, :], blank
        )
        mean = mean / totals[m]

        def spread(j, acc):
            gap = ref[i, m, j, 0:1, :] - mean
            return acc + ref[i, m, j, 1:2, :] + sc.cnt[m, j] * (gap * gap)

        var = over_devices(spread, blank) / totals[m]
        return mean, lax.rsqrt(var + EPS)

    def back_sums(wide, i, m):
        st_wait(wide, i, m)
        ref = sc.stw if wide else sc.stm
        return over_devices(
            lambda j, acc: acc + ref[i, m, j], jnp.zeros((2, ref.shape[-1]), F32)
        )

    def local_moments(v, m):
        mask = sc.msk[m]
        own = jnp.maximum(sc.cnt[m, d], 1.0)
        mean = jnp.sum(v * mask, 0, keepdims=True) / own
        gap = (v - mean) * mask
        return jnp.concatenate([mean, jnp.sum(gap * gap, 0, keepdims=True)], 0)

    def local_sums(dz, vhat):
        return jnp.concatenate(
            [jnp.sum(dz * vhat, 0, keepdims=True), jnp.sum(dz, 0, keepdims=True)], 0
        )

    def lanes(j):
        return slice(LANES * j, LANES * (j + 1))

    def stream(layer, m):
        return x_ref[m] if layer == 0 else sc.s1[m]

    def stream_part(layer, m, j):
        return (x_ref[m, :, lanes(j)] if layer == 0 else sc.s1[m, :, lanes(j)]).astype(F32)

    rs_par = {0: 0, 1: 1, 3: 0, 5: 1, 2: 0, 4: 1}

    def rs_send(rid, m, values):
        par = rs_par[rid]
        ss, rs = exchange_open("rs", rid, m)
        for j, value in enumerate(values):
            half = value.astype(BF16)
            sc.part[par, m, 2 * j] = half[:, :LANES]
            sc.part[par, m, 2 * j + 1] = half[:, LANES:]
        for off in range(1, 4):
            q = pipe_at(off)
            remote(sc.part.at[par, m, q], sc.rsr.at[rs_slot(rid), m, off - 1], ss, rs, (q, d)).start()

    def first_part(layer, m):
        s = stream(layer, m)
        rs_send(
            layer,
            m,
            [dot_nn(s, sc.wt[2 * layer, :, 256 * j : 256 * j + 256]) for j in range(2)],
        )

    def mid_moments(i, m, v):
        sc.midv[i, m] = v
        sc.stm[i, m, d] = local_moments(v, m)
        st_start(False, i, m)

    def first_norm(layer, m):
        mid_moments(2 * layer, m, rs_sum(layer, m, rs_par[layer]))

    def mid_hidden(i, m):
        mean, inv = combine(False, i, m)
        sc.inv_mid[i, m] = inv
        vhat = (sc.midv[i, m] - mean) * inv
        sc.midv[i, m] = vhat
        u = sc.gm[i, 0:1, :] * vhat + sc.gm[i, 1:2, :]
        return (sc.msk[m] * (u * sigmoid(u))).astype(BF16)

    def hidden_one(layer, m):
        i = 2 * layer
        mean, inv = combine(False, i, m)
        sc.inv_mid[i, m] = inv
        vhat = ((sc.midv[i, m] - mean) * inv).astype(BF16)
        sc.midv[i, m] = vhat.astype(F32)
        ag_start(layer, m, vhat)

    def taps_of(layer, taps):
        return jnp.concatenate(
            [
                jnp.concatenate([sc.k2[layer, 2 * k], sc.k2[layer, 2 * k + 1]], axis=0)
                for k in taps
            ],
            axis=1,
        )

    def second_part(layer, m):
        ag_wait(layer, m)
        for q in range(4):
            gain, bias = sc.gmf[2 * layer, 0:1, lanes(q)], sc.gmf[2 * layer, 1:2, lanes(q)]
            u = gain * sc.ag[layer, m, q].astype(F32) + bias
            sc.hf[layer, m, :, lanes(q)] = (sc.msk[m] * (u * sigmoid(u))).astype(BF16)
        h = sc.hf[layer, m]
        for j in range(5):
            width = 256 if j < 4 else 128
            y = dot_nn(h, taps_of(layer, [2 * j + e for e in range(width // LANES)]))
            for e in range(width // LANES):
                sc.yf[2 * j + e] = y[:, lanes(e)]

        def across(k):
            return (
                sc.yf[k + 1]
                + sc.beside[m, 0] * shifted(sc.yf[k], 1)
                + sc.beside[m, 1] * shifted(sc.yf[k + 2], -1)
            )

        total = across(3) + from_above(across(0), m) + from_below(across(6), m)
        mid_moments(2 * layer + 1, m, total)

    def hidden_two(layer, m):
        ag_start(2 + layer, m, mid_hidden(2 * layer + 1, m))

    def third_part(layer, m):
        ag_wait(2 + layer, m)
        h = ag_value(2 + layer, m)
        for j in range(2):
            sc.widv[layer, m, :, 256 * j : 256 * j + 256] = dot_nt(
                h, sc.wt[2 * layer + 1, 256 * j : 256 * j + 256, :]
            )
        for j in range(4):
            sc.stw[layer, m, d, :, lanes(j)] = local_moments(sc.widv[layer, m, :, lanes(j)], m)
        st_start(True, layer, m)

    def out_gain(layer, j):
        both = sc.go[2 * layer + lax.div(p, 2), lax.rem(p, 2)]
        return both[0:1, lanes(j)], both[1:2, lanes(j)]

    def pre_values(layer, m):
        mean, inv = combine(True, layer, m)
        sc.inv_wide[layer, m] = inv
        mask = sc.msk[m]
        for j in range(4):
            gain, bias = out_gain(layer, j)
            vhat = (sc.widv[layer, m, :, lanes(j)] - mean[:, lanes(j)]) * inv[:, lanes(j)]
            sc.widv[layer, m, :, lanes(j)] = vhat
            pre = gain * vhat + bias + stream_part(layer, m, j)
            sig = sigmoid(pre)
            out = (mask * (pre * sig)).astype(BF16)
            if layer == 0:
                sc.pre0[m, :, lanes(j)] = pre
                sc.s1[m, :, lanes(j)] = out
            else:
                sc.mix[m, :, lanes(j)] = out
                slope = sig * (1.0 + pre * (1.0 - sig))
                grad = (cot_ref[m, :, lanes(j)].astype(F32) * mask * slope).astype(BF16)
                sc.gp[1, m, :, lanes(j)] = grad
                sc.stw[3, m, d, :, lanes(j)] = local_sums(grad.astype(F32), vhat)
        if layer == 1:
            st_start(True, 3, m)

    def put_out(k, src, dst):
        copy = pltpu.make_async_copy(src, dst, sc.out.at[k])
        copy.start()
        return copy

    def grad_out_norm(layer, m):
        sums = back_sums(True, 2 + layer, m)
        if m == 0:
            sc.gsw[layer, p] = sums
        else:
            sc.gsw[layer, p] = sc.gsw[layer, p] + sums
        mask = sc.msk[m]
        inv = sc.inv_wide[layer, m]
        for j in range(4):
            gain, _ = out_gain(layer, j)
            dz = sc.gp[layer, m, :, lanes(j)].astype(F32)
            vhat = sc.widv[layer, m, :, lanes(j)]
            s1 = sums[0:1, lanes(j)] / totals[m]
            s0 = sums[1:2, lanes(j)] / totals[m]
            dv = mask * (gain * inv[:, lanes(j)]) * (dz - s0 - vhat * s1)
            sc.gt[m, :, lanes(j)] = dv.astype(BF16)
        g = sc.gt[m]
        rs_send(
            2 + layer,
            m,
            [dot_nn(g, sc.wt[2 * layer + 1, :, 256 * j : 256 * j + 256]) for j in range(2)],
        )

    def mid_grad(i, m, upstream):
        vhat = sc.midv[i, m]
        u = sc.gm[i, 0:1, :] * vhat + sc.gm[i, 1:2, :]
        sig = sigmoid(u)
        dz = upstream * sc.msk[m] * (sig * (1.0 + u * (1.0 - sig)))
        sc.dzm[m] = dz
        sc.stm[4 + i, m, d] = local_sums(dz, vhat)
        st_start(False, 4 + i, m)

    def mid_back(i, m):
        sums = back_sums(False, 4 + i, m)
        if m == 0:
            sc.gsm[i, p] = sums
        else:
            sc.gsm[i, p] = sc.gsm[i, p] + sums
        s1 = sums[0:1, :] / totals[m]
        s0 = sums[1:2, :] / totals[m]
        scale = sc.gm[i, 0:1, :] * sc.inv_mid[i, m]
        return (sc.msk[m] * scale * (sc.dzm[m] - s0 - sc.midv[i, m] * s1)).astype(BF16)

    def grad_two(layer, m):
        mid_grad(2 * layer + 1, m, rs_sum(2 + layer, m, rs_par[2 + layer]))

    def grad_second(layer, m):
        gs = mid_back(2 * layer + 1, m)
        own = gs.astype(F32)
        for du, moved in ((0, own), (1, from_above(own, m)), (-1, from_below(own, m))):
            k = 3 * (du + 1)
            sc.gb[m, :, lanes(k + 1)] = moved.astype(BF16)
            sc.gb[m, :, lanes(k + 2)] = (sc.beside[m, 0] * shifted(moved, 1)).astype(BF16)
            sc.gb[m, :, lanes(k)] = (sc.beside[m, 1] * shifted(moved, -1)).astype(BF16)
        g = sc.gb[m]
        rs_send(
            4 + layer,
            m,
            [
                dot_nt(
                    g, jnp.concatenate([sc.k2[layer, 2 * k + j] for k in range(9)], axis=1)
                )
                for j in range(2)
            ],
        )

    def grad_one(layer, m):
        mid_grad(2 * layer, m, rs_sum(4 + layer, m, rs_par[4 + layer]))
        ag_start(4 + layer, m, sc.dzm[m].astype(BF16))

    def small_copy(layer, m, off):
        own = sc.sml.at[layer, m, p]
        return remote(own, own, sc.sm_s.at[layer, m], sc.sm_r.at[layer, m], (pipe_at(off), d))

    def grad_first(layer, m):
        i = 2 * layer
        sums = back_sums(False, 4 + i, m)
        if m == 0:
            sc.gsm[i, p] = sums
        else:
            sc.gsm[i, p] = sc.gsm[i, p] + sums
        scale = sc.gm[i, 0:1, :] * sc.inv_mid[i, m]
        s1 = scale * (sums[0:1, :] / totals[m])
        s0 = scale * (sums[1:2, :] / totals[m])
        sc.sml[layer, m, p] = jnp.concatenate([scale, s0, s1, s1], 0)
        for off in range(1, 4):
            small_copy(layer, m, off).start()

    def finish_small():
        for layer in range(2):
            for m in range(2):
                bytes_wait(sc.sml.at[layer, m, pl.ds(0, 3)], sc.sm_s.at[layer, m])

    finish.append(finish_small)

    def slopes(m):
        for i in range(4):
            pre = sc.pre0[m, :, lanes(i)]
            sig = sigmoid(pre)
            sc.pre0[m, :, lanes(i)] = sc.msk[m] * (sig * (1.0 + pre * (1.0 - sig)))

    def conv_grad(layer, m):
        ag_wait(4 + layer, m)
        bytes_wait(sc.sml.at[layer, m, pl.ds(0, 3)], sc.sm_r.at[layer, m])
        for q in range(4):
            scale, s0, s1 = (sc.sml[layer, m, q, k : k + 1, :] for k in range(3))
            dz = sc.ag[4 + layer, m, q].astype(F32)
            vhat = sc.ag[layer, m, q].astype(F32)
            dv = sc.msk[m] * (scale * dz - s0 - s1 * vhat)
            sc.gff[layer, m, :, lanes(q)] = dv.astype(BF16)
        g = sc.gff[layer, m]
        for j in range(2):
            r = dot_nt(g, sc.wt[2 * layer, 256 * j : 256 * j + 256, :]).astype(BF16)
            if layer == 0:
                sc.cin[m, :, 256 * j : 256 * j + 256] = r
                continue
            for e in range(2):
                i = 2 * j + e
                up = sc.gp[1, m, :, lanes(i)].astype(F32) + r[:, lanes(e)].astype(F32)
                grad = (up * sc.pre0[m, :, lanes(i)]).astype(BF16)
                sc.gp[0, m, :, lanes(i)] = grad
                sc.stw[2, m, d, :, lanes(i)] = local_sums(
                    grad.astype(F32), sc.widv[0, m, :, lanes(i)]
                )
        if layer == 1:
            st_start(True, 2, m)

    def turned(blocks):
        for m, block in enumerate(blocks):
            sc.tb[:, rows * m : rows * (m + 1)] = block.T

    def both(get):
        return jnp.concatenate([get(0), get(1)], axis=0)

    def wide_grad(s, left, right):
        turned([left(0), left(1)])
        for j in range(2):
            cols = slice(256 * j, 256 * j + 256)
            rhs = both(lambda m: right(m)[:, cols])
            for h in range(2):
                r = dot_nn(sc.tb[256 * h : 256 * h + 256, :], rhs)
                sc.dw[s, h, :, cols] = r.astype(BF16)
        pair_copy("w", s).start()

    def wide_early():
        turned([x_ref[0], x_ref[1]])
        g = sc.gff[0, 0]
        for j in range(2):
            cols = slice(256 * j, 256 * j + 256)
            sc.ack[:, cols] = dot_nn(sc.tb[:, :rows], g[:, cols])

    def wide_late():
        g = sc.gff[0, 1]
        for j in range(2):
            cols = slice(256 * j, 256 * j + 256)
            for h in range(2):
                part = slice(256 * h, 256 * h + 256)
                r = sc.ack[part, cols] + dot_nn(sc.tb[part, rows:], g[:, cols])
                sc.dw[0, h, :, cols] = r.astype(BF16)
        pair_copy("w", 0).start()

    def taps_early():
        turned([sc.hf[0, 0], sc.hf[0, 1]])
        for j in range(5):
            cols = slice(256 * j, min(256 * j + 256, 1152))
            sc.ack[:, cols] = dot_nn(sc.tb[:, :rows], sc.gb[0, :, cols])

    def taps_late():
        for j in range(5):
            cols = slice(256 * j, min(256 * j + 256, 1152))
            r = (sc.ack[:, cols] + dot_nn(sc.tb[:, rows:], sc.gb[1, :, cols])).astype(BF16)
            for e in range(r.shape[1] // LANES):
                tap = 2 * j + e
                sc.dk[0, 512 * tap : 512 * tap + 512, :] = r[:, lanes(e)]
        pair_copy("k", 0).start()

    def taps_grad(layer):
        turned([sc.hf[layer, 0], sc.hf[layer, 1]])
        for j in range(5):
            width = 256 if j < 4 else 128
            rhs = both(lambda m: sc.gb[m, :, 256 * j : 256 * j + width])
            r = dot_nn(sc.tb[...], rhs).astype(BF16)
            for e in range(width // LANES):
                tap = 2 * j + e
                sc.dk[layer, 512 * tap : 512 * tap + 512, :] = r[:, lanes(e)]
        pair_copy("k", layer).start()

    def half_rows(which):
        return pl.ds(pl.multiple_of(2304 * which, 2304), 2304)

    def pair_copy(kind, t):
        if kind == "w":
            src, dst, i = sc.dw.at[t, 1 - c], sc.prw.at[t], t
        else:
            src, dst, i = sc.dk.at[t, half_rows(1 - c)], sc.prk.at[t], 4 + t
        return remote(src, dst, sc.pw_s.at[i], sc.pw_r.at[i], sibling)

    def pair_sum(kind, t):
        pair_copy(kind, t).wait_recv()
        if kind == "w":
            sc.zsw[t] = (sc.dw[t, c].astype(F32) + sc.prw[t].astype(F32)).astype(BF16)
            return
        for i in range(4):
            part = slice(576 * i, 576 * i + 576)
            mine = pl.ds(pl.multiple_of(2304 * c + 576 * i, 576), 576)
            sc.zsk[t, part] = (
                sc.dk[t, mine].astype(F32) + sc.prk[t, part].astype(F32)
            ).astype(BF16)

    items = gradient_items(n)
    line = n_z == 4
    inner = (z == 1) | (z == 2)

    def tile_sem(it):
        return it.t if it.kind == "w" else 4 + it.t

    def tile(it, name):
        return getattr(sc, name + it.kind)

    def some(it, name, start, count):
        return tile(it, name).at[it.t, pl.ds(start, count)]

    def part_rows(it, which):
        half = it.nr // 2
        return pl.ds(pl.multiple_of(it.r0 + half * which, half), half)

    def up_copy(it):
        rows_of = pl.ds(it.r0, it.nr)
        return remote(
            tile(it, "zs").at[it.t, rows_of],
            tile(it, "zo").at[it.t, rows_of],
            sc.it_s.at[tile_sem(it)],
            sc.one_r.at[it.i],
            (p, 2 * (1 + lax.div(z, 3)) + c),
        )

    def mid_copy(it):
        return remote(
            tile(it, "zs").at[it.t, part_rows(it, 2 - z)],
            tile(it, "zi").at[it.t, pl.ds(it.r0 // 2, it.nr // 2)],
            sc.it_s.at[tile_sem(it)],
            sc.mid_r.at[it.i],
            (p, 2 * (3 - z) + c),
        )

    def inn_copy(it):
        view = tile(it, "fz").at[it.t, part_rows(it, z - 1)]
        return remote(
            view, view, sc.it_s.at[tile_sem(it)], sc.inn_r.at[it.i], (p, 2 * (3 - z) + c)
        )

    def down_copy(it, e):
        view = tile(it, "fz").at[it.t, part_rows(it, z - 1 if e == 0 else 2 - z)]
        return remote(
            view, view, sc.it_s.at[tile_sem(it)], sc.one_r.at[it.i], (p, 2 * (3 * (z - 1)) + c)
        )

    def direct_rows(it, j):
        count = it.nr // n_own
        return pl.ds(pl.multiple_of(it.r0 + count * j, count), count)

    def owner(index, body):
        if n_own == n_z:
            body()
        else:
            pl.when(index < n_own)(body)

    def scatter_copy(it, k):
        j = lax.rem(z + k, n_z)
        return j, remote(
            tile(it, "zs").at[it.t, direct_rows(it, lax.rem(j, n_own))],
            tile(it, "zo").at[it.t, k - 1],
            sc.it_s.at[tile_sem(it)],
            sc.one_r.at[it.i],
            (p, 2 * j + c),
        )

    def gather_copy(it, k):
        j = lax.rem(z + k, n_z)
        view = tile(it, "fz").at[it.t, direct_rows(it, lax.rem(z, n_own))]
        return remote(view, view, sc.ga_s.at[tile_sem(it)], sc.mid_r.at[it.i], (p, 2 * j + c))

    def add_rows(target, first, second):
        target[...] = (first[...].astype(F32) + second[...].astype(F32)).astype(BF16)

    def step_up(it):
        if line:

            @pl.when((z == 0) | (z == 3))
            def _():
                up_copy(it).start()

        else:

            def go(k):
                j, copy = scatter_copy(it, k)
                owner(j, lambda: copy.start())

            each(n_z, 1, go)

    def step_mid(it):
        if not line:
            return

        @pl.when(inner)
        def _():
            up_copy(it).wait_recv()
            mine = some(it, "zs", it.r0, it.nr)
            add_rows(mine, mine, some(it, "zo", it.r0, it.nr))
            mid_copy(it).start()

    def step_down(it):
        if line:

            @pl.when(inner)
            def _():
                mid_copy(it).wait_recv()
                keep = part_rows(it, z - 1)
                add_rows(
                    tile(it, "fz").at[it.t, keep],
                    tile(it, "zs").at[it.t, keep],
                    some(it, "zi", it.r0 // 2, it.nr // 2),
                )
                inn_copy(it).start()
                down_copy(it, 0).start()

            return

        def go():
            bytes_wait(tile(it, "zo").at[it.t], sc.one_r.at[it.i])
            mine = direct_rows(it, z)
            total = tile(it, "zs")[it.t, mine].astype(F32)
            total = lax.fori_loop(
                0, n_z - 1, lambda k, acc: acc + tile(it, "zo")[it.t, k].astype(F32), total
            )
            tile(it, "fz")[it.t, mine] = total.astype(BF16)
            each(n_z, 1, lambda k: gather_copy(it, k).start())

        owner(z, go)

    def step_last(it):
        if not line:
            return

        @pl.when(inner)
        def _():
            inn_copy(it).wait_recv()
            down_copy(it, 1).start()

    def owner_of(it):
        return it.t if it.kind == "w" else 2 * it.t + c

    def landing(it, q, core):
        if it.kind == "w":
            return sc.ow.at[q, core, pl.ds(it.r0, it.nr)]
        lane = pl.ds(128 * q, 128) if isinstance(q, int) else columns_of(q)
        return sc.ok.at[pl.ds(it.r0, it.nr), lane]

    def to_sem(it, sems):
        return sems.at[0 if it.kind == "w" else 1, it.part]

    def to_copy(it):
        return remote(
            some(it, "fz", it.r0, it.nr),
            landing(it, p, c),
            sc.to_s.at[tile_sem(it)],
            to_sem(it, sc.to_r),
            (owner_of(it), d),
        )

    def shared(it):
        return line and it.kind == "w" and it.t == 0

    def in_charge(it):
        outer = (z == 0) | (z == 3)
        return outer if it.part % 2 == 0 else jnp.logical_not(outer)

    def sends_out(it):
        if shared(it):
            return (p == 1) | ((p > 1) & in_charge(it))
        return p != owner_of(it)

    def passes_on(it):
        if shared(it):
            return (p == 0) & in_charge(it)
        return p < 0

    def pass_copy(it):
        view = sc.ow.at[pl.ds(2, 2), c, pl.ds(it.r0, it.nr)]
        return remote(view, view, sc.sh_s.at[it.part], sc.sh_r.at[it.part], z_pair)

    def step_inner_out(it):
        if line:
            pl.when(inner)(lambda: deliver(it))

    def step_out(it):
        if line:

            @pl.when((z == 0) | (z == 3))
            def _():
                bytes_wait(some(it, "fz", it.r0, it.nr), sc.one_r.at[it.i])
                deliver(it)

        else:
            count = it.nr // n_own
            if n_own == n_z:
                bytes_wait(some(it, "fz", it.r0, count * (n_own - 1)), sc.mid_r.at[it.i])
            else:

                @pl.when(z < n_own)
                def _():
                    bytes_wait(some(it, "fz", it.r0, count * (n_own - 1)), sc.mid_r.at[it.i])

                @pl.when(z >= n_own)
                def _():
                    bytes_wait(some(it, "fz", it.r0, count * n_own), sc.mid_r.at[it.i])

            deliver(it)

    def deliver(it):
        @pl.when(sends_out(it))
        def _():
            to_copy(it).start()

        def place(q):
            landing(it, q, c)[...] = some(it, "fz", it.r0, it.nr)[...]

        if it.kind == "w":
            pl.when(p == it.t)(lambda: place(it.t))
        else:
            for core in range(2):
                pl.when((p == 2 * it.t + core) & (c == core))(
                    functools.partial(place, 2 * it.t + core)
                )

    def sibling_copy(it, q):
        view = landing(it, q, c)
        return remote(
            view, view, sc.sib_s.at[0 if it.kind == "w" else 1], to_sem(it, sc.sib_r), sibling
        )

    def slices(it, count):
        if it.kind == "w":
            return sc.ow.at[pl.ds(0, count), 0, pl.ds(it.r0, it.nr)]
        return sc.ok.at[pl.ds(it.r0, it.nr), pl.ds(0, 128 * count)]

    def step_sibling(it):
        def go():
            bytes_wait(slices(it, 3), to_sem(it, sc.to_r))
            for q in range(4):
                sibling_copy(it, q).start()

        if not shared(it):
            pl.when(p == owner_of(it))(go)
            return

        @pl.when((p == 0) & in_charge(it))
        def _():
            bytes_wait(slices(it, 3), to_sem(it, sc.to_r))
            pass_copy(it).start()
            for q in range(4):
                sibling_copy(it, q).start()

        @pl.when((p == 0) & jnp.logical_not(in_charge(it)))
        def _():
            bytes_wait(slices(it, 1), to_sem(it, sc.to_r))
            for q in range(2):
                sibling_copy(it, q).start()

    def step_rest(it):
        if not shared(it):
            return

        @pl.when((p == 0) & jnp.logical_not(in_charge(it)))
        def _():
            bytes_wait(slices(it, 2), sc.sh_r.at[it.part])
            for q in range(2, 4):
                sibling_copy(it, q).start()

    def step_done(it):
        def go():
            bytes_wait(slices(it, 4), to_sem(it, sc.sib_r))

        pl.when(p == (it.t if it.kind == "w" else 2 * it.t + 1 - c))(go)

    def finish_grads():
        for kind, t in [("w", s) for s in range(4)] + [("k", layer) for layer in range(2)]:
            pair_copy(kind, t).wait_send()
            whole = next(it for it in items if it.kind == kind and it.t == t)
            sends = sc.it_s.at[tile_sem(whole)]
            half = tile(whole, "zs").at[t]
            if line:

                @pl.when(inner)
                def _(kind=kind, t=t, sends=sends):
                    bytes_wait((sc.dw if kind == "w" else sc.dk).at[t], sends)

                @pl.when((z == 0) | (z == 3))
                def _(half=half, sends=sends):
                    bytes_wait(half, sends)

            else:

                def sent(k, it=whole):
                    j, copy = scatter_copy(it, k)
                    owner(j, lambda: copy.wait_send())

                each(n_z, 1, sent)
                owner(
                    z,
                    lambda it=whole: each(n_z, 1, lambda k: gather_copy(it, k).wait_send()),
                )

        for it in items:

            @pl.when(sends_out(it))
            def _(it=it):
                bytes_wait(some(it, "fz", it.r0, it.nr), sc.to_s.at[tile_sem(it)])

            @pl.when(passes_on(it))
            def _(it=it):
                bytes_wait(slices(it, 2), sc.sh_s.at[it.part])

        bytes_wait(sc.ow.at[:, 0], sc.sib_s.at[0])

        @pl.when(c == parity)
        def _():
            bytes_wait(sc.ok.at[...], sc.sib_s.at[1])

    finish.append(finish_grads)

    def gain_copies(off):
        dev = (pipe_at(off), d)
        return [
            remote(sc.gsm.at[:, p], sc.gsm.at[:, p], sc.g_s.at[0], sc.g_r.at[0], dev),
            remote(sc.gsw.at[:, p], sc.gsw.at[:, p], sc.g_s.at[1], sc.g_r.at[1], dev),
        ]

    def gains_wait(sems):
        bytes_wait(sc.gsm.at[:, pl.ds(0, 3)], sems.at[0])
        bytes_wait(sc.gsw.at[:, pl.ds(0, 3)], sems.at[1])

    def gains_start():
        for off in range(1, 4):
            for copy in gain_copies(off):
                copy.start()

    def gains_done():
        gains_wait(sc.g_r)
        for q in range(4):
            sc.gmo[0, :, lanes(q)] = sc.gsm[p, q]
        layer = lax.div(p, 2)
        for e in range(2):
            sc.goo[0, :, 512 * e : 512 * e + 512] = sc.gsw[layer, 2 * parity + e]
        outs.append(put_out(0, sc.gmo.at[...], gmid_ref.at[...]))
        outs.append(put_out(7, sc.goo.at[...], gout_ref.at[...]))

    def finish_gains():
        gains_wait(sc.g_s)

    finish.append(finish_gains)

    def of(kind, t):
        return [it for it in items if it.kind == kind and it.t == t]

    def one(step, kind, t, part):
        for it in of(kind, t)[part : part + 1]:
            step(it)

    def run(step, kind, t):
        for it in of(kind, t):
            step(it)

    def nothing():
        return None

    def paired(arrival, reply, layer, hooks=(nothing, nothing)):
        for m in range(2):
            arrival(layer, m)
            hooks[m]()
            reply(layer, m)

    def steps(*listed):
        def go():
            for body, *rest in listed:
                body(*rest)

        return go

    up, mid, down, last, out = step_up, step_mid, step_down, step_last, step_out
    inside = step_inner_out
    wide, taps = 0, 1
    spread_first(wide, 0)
    spread_second(wide, 0)
    ready(wide, 0)
    own_x.wait()
    first_part(0, 0)
    first_part(0, 1)
    own_n.wait()
    bytes_wait(sc.go.at[0], sc.loc.at[6])
    own_cot.wait()
    own_g.wait()
    norm_wait(sc.n_r)
    spread_first(taps, 0)
    spread_first(taps, 1)
    paired(
        first_norm,
        hidden_one,
        0,
        (
            steps((spread_second, taps, 0), (spread_second, taps, 1)),
            steps((spread_first, wide, 1)),
        ),
    )
    ready(taps, 0)
    ready(taps, 1)
    paired(
        second_part,
        hidden_two,
        0,
        (steps((spread_first, wide, 2), (spread_second, wide, 1)), steps((spread_first, taps, 2))),
    )
    ready(wide, 1)

    def turn(layer, m):
        pre_values(0, m)
        if m == 0:
            ready(wide, 2)
        first_part(1, m)

    paired(
        third_part,
        turn,
        0,
        (
            steps((spread_second, wide, 2), (spread_first, taps, 3), (spread_second, taps, 2)),
            steps((spread_first, wide, 3)),
        ),
    )
    paired(
        first_norm,
        hidden_one,
        1,
        (steps((spread_second, taps, 3)), steps((spread_second, wide, 3))),
    )
    ready(taps, 2)
    ready(taps, 3)
    paired(second_part, hidden_two, 1)
    ready(wide, 3)
    third_part(1, 0)
    pre_values(1, 0)
    third_part(1, 1)
    grad_out_norm(1, 0)
    pre_values(1, 1)
    outs = [put_out(2, sc.mix.at[...], mixed_ref.at[...])]
    grad_out_norm(1, 1)
    wide_grad(3, lambda m: sc.gt[m], lambda m: ag_value(3, m))
    paired(
        grad_two,
        grad_second,
        1,
        (
            steps((pair_sum, "w", 3), (one, up, "w", 3, 0), (slopes, 0)),
            steps((one, up, "w", 3, 1), (slopes, 1), (one, mid, "w", 3, 0)),
        ),
    )
    taps_grad(1)
    grad_one(1, 0)
    steps(
        (pair_sum, "k", 1),
        (one, up, "k", 1, 0),
        (one, mid, "w", 3, 1),
        (one, down, "w", 3, 0),
    )()
    grad_first(1, 0)
    grad_one(1, 1)
    conv_grad(1, 0)
    steps(
        (one, up, "k", 1, 1),
        (one, down, "w", 3, 1),
        (one, last, "w", 3, 0),
        (one, mid, "k", 1, 0),
    )()
    grad_first(1, 1)
    grad_out_norm(0, 0)
    conv_grad(1, 1)
    outs.append(put_out(3, sc.gp.at[0], gpre_ref.at[...]))
    steps(
        (one, up, "k", 1, 2),
        (one, last, "w", 3, 1),
        (one, mid, "k", 1, 1),
        (one, down, "k", 1, 0),
        (wide_grad, 2, lambda m: sc.s1[m], lambda m: sc.gff[1, m]),
    )()
    grad_out_norm(0, 1)
    wide_grad(1, lambda m: sc.gt[m], lambda m: ag_value(2, m))
    paired(
        grad_two,
        grad_second,
        0,
        (
            steps(
                (pair_sum, "w", 1),
                (one, up, "w", 1, 0),
                (one, mid, "k", 1, 2),
                (one, down, "k", 1, 1),
                (one, last, "k", 1, 0),
            ),
            steps(
                (one, up, "w", 1, 1),
                (pair_sum, "w", 2),
                (one, mid, "w", 1, 0),
                (one, down, "k", 1, 2),
                (one, last, "k", 1, 1),
                (taps_early,),
            ),
        ),
    )
    taps_late()
    grad_one(0, 0)
    steps(
        (pair_sum, "k", 0),
        (one, up, "k", 0, 0),
        (one, up, "k", 0, 1),
        (one, mid, "w", 1, 1),
        (one, down, "w", 1, 0),
        (one, last, "k", 1, 2),
    )()
    grad_first(0, 0)
    grad_one(0, 1)
    steps(
        (one, up, "k", 0, 2),
        (one, up, "k", 0, 3),
        (one, up, "k", 0, 4),
        (one, up, "k", 0, 5),
        (one, mid, "k", 0, 0),
        (one, mid, "k", 0, 1),
        (one, down, "w", 1, 1),
        (one, last, "w", 1, 0),
    )()
    one(down, "k", 0, 0)
    one(mid, "k", 0, 2)
    conv_grad(0, 0)
    one(down, "k", 0, 1)
    grad_first(0, 1)
    gains_start()
    one(mid, "k", 0, 3)
    one(last, "k", 0, 0)
    one(down, "k", 0, 2)
    one(last, "w", 1, 1)
    one(up, "w", 2, 0)
    one(last, "k", 0, 1)
    one(mid, "k", 0, 4)
    one(down, "k", 0, 3)
    wide_early()
    conv_grad(0, 1)
    wide_late()
    run(inside, "k", 1)
    run(out, "k", 1)
    run(inside, "w", 1)
    one(inside, "k", 0, 0)
    one(inside, "k", 0, 1)
    run(out, "w", 1)
    one(out, "k", 0, 0)
    one(out, "k", 0, 1)
    one(last, "k", 0, 2)
    one(inside, "k", 0, 2)
    one(mid, "k", 0, 5)
    one(down, "k", 0, 4)
    one(last, "k", 0, 3)
    one(inside, "k", 0, 3)
    outs.append(put_out(4, sc.cin.at[...], conv_ref.at[...]))
    pair_sum("w", 0)
    run(up, "w", 0)
    one(up, "w", 2, 1)
    one(out, "k", 0, 2)
    one(down, "k", 0, 5)
    one(last, "k", 0, 4)
    one(inside, "k", 0, 4)
    one(out, "k", 0, 3)
    one(mid, "w", 0, 0)
    one(mid, "w", 2, 0)
    run(inside, "w", 3)
    run(out, "w", 3)
    one(mid, "w", 0, 1)
    one(last, "k", 0, 5)
    one(inside, "k", 0, 5)
    one(out, "k", 0, 4)
    one(down, "w", 0, 0)
    one(mid, "w", 0, 2)
    one(down, "w", 0, 1)
    one(out, "k", 0, 5)
    one(down, "w", 2, 0)
    one(last, "w", 0, 0)
    one(inside, "w", 0, 0)
    one(mid, "w", 0, 3)
    one(down, "w", 0, 2)
    one(last, "w", 0, 1)
    one(inside, "w", 0, 1)
    one(out, "w", 0, 0)
    one(mid, "w", 2, 1)
    one(last, "w", 2, 0)
    one(inside, "w", 2, 0)
    one(down, "w", 0, 3)
    one(last, "w", 0, 2)
    one(inside, "w", 0, 2)
    one(out, "w", 0, 1)
    one(out, "w", 2, 0)
    one(down, "w", 2, 1)
    one(last, "w", 0, 3)
    one(inside, "w", 0, 3)
    one(out, "w", 0, 2)
    one(last, "w", 2, 1)
    one(inside, "w", 2, 1)
    for part in range(4):
        one(step_sibling, "k", 0, part)
    one(out, "w", 0, 3)
    one(step_sibling, "k", 0, 4)
    one(step_sibling, "k", 0, 5)
    one(out, "w", 2, 1)
    run(step_sibling, "w", 3)
    gains_done()
    run(step_sibling, "k", 1)
    run(step_sibling, "w", 2)
    run(step_sibling, "w", 1)
    one(step_sibling, "w", 0, 0)
    one(step_sibling, "w", 0, 1)
    run(step_done, "k", 1)
    run(step_done, "k", 0)
    outs.append(put_out(1, sc.ok.at[...], gtaps_ref.at[...]))
    for s in (3, 2, 1):
        run(step_done, "w", s)
    final = of("w", 0)
    for it in final[2:]:
        step_sibling(it)
    for it in final:
        step_rest(it)
    for group, part in enumerate((final[:-1], final[-1:]) if len(final) > 1 else (final,)):
        first, count = part[0].r0, sum(it.nr for it in part)
        for it in part:
            step_done(it)
        part_rows_of = pl.ds(first, count)
        outs.append(
            put_out(
                5 + group, sc.ow.at[:, :, part_rows_of], gwide_ref.at[:, :, part_rows_of]
            )
        )
    for copy in outs:
        copy.wait()
    for body in finish:
        body()


def cast_pieces(rows):
    pieces = [("taps", pl.ds(1152 * i, 1152)) for i in range(2)]
    pieces += [("wide", pl.ds(1024 * i, 1024)) for i in range(2)]
    return pieces + [("stream", m) for m in range(2)]


def cast_kernel(mixed, gpre, conv, gwide, gtaps, gmid, gout, *refs):
    o_mixed, o_input, o_wide, o_taps, o_mid, o_out = refs[:6]
    b_taps, b_wide, b_gpre, b_conv, f_taps, f_wide, f_stream = refs[6:13]
    b_mixed, b_mid, b_out, r_sem, w_sem, d_sem = refs[13:]
    pieces = cast_pieces(gpre.shape[1])
    same = ((mixed, b_mixed, o_mixed), (gmid, b_mid, o_mid), (gout, b_out, o_out))
    arrive = [pltpu.make_async_copy(a, b, d_sem.at[i]) for i, (a, b, _) in enumerate(same)]
    leave = [pltpu.make_async_copy(b, o, d_sem.at[i]) for i, (_, b, o) in enumerate(same)]
    reads, writes = [], []
    for i, (kind, part) in enumerate(pieces):
        if kind == "stream":
            reads.append(
                [
                    pltpu.make_async_copy(gpre.at[part], b_gpre.at[part], r_sem.at[i]),
                    pltpu.make_async_copy(conv.at[part], b_conv.at[part], r_sem.at[i + 2]),
                ]
            )
            writes.append(
                pltpu.make_async_copy(f_stream.at[part], o_input.at[part], w_sem.at[i])
            )
            continue
        src, low, high, dst = (
            (gtaps, b_taps, f_taps, o_taps)
            if kind == "taps"
            else (gwide, b_wide, f_wide, o_wide)
        )
        reads.append([pltpu.make_async_copy(src.at[part], low.at[part], r_sem.at[i])])
        writes.append(pltpu.make_async_copy(high.at[part], dst.at[part], w_sem.at[i]))
    for group in reads:
        for copy in group:
            copy.start()
    for copy in arrive:
        copy.start()
    for (kind, part), group, write in zip(pieces, reads, writes):
        for copy in group:
            copy.wait()
        size = 64

        def strip(i, carry, kind=kind, part=part):
            if kind == "stream":
                at = pl.ds(pl.multiple_of(i * size, size), size)
                f_stream[part, at] = b_gpre[part, at].astype(F32) + b_conv[part, at].astype(F32)
                return carry
            at = pl.ds(pl.multiple_of(part.start + i * size, size), size)
            if kind == "taps":
                f_taps[at] = b_taps[at].astype(F32)
            else:
                f_wide[at] = b_wide[at].astype(F32)
            return carry

        lax.fori_loop(0, (gpre.shape[1] if kind == "stream" else part.size) // size, strip, 0)
        write.start()
    for first, second in zip(arrive, leave):
        first.wait()
        second.start()
    for copy in writes + leave:
        copy.wait()


def cast_all(mixed, gpre, conv, gwide, gtaps, gmid, gout):
    anywhere = pl.BlockSpec(memory_space=pl.ANY)
    shape = jax.ShapeDtypeStruct
    count = len(cast_pieces(gpre.shape[1]))
    return pl.pallas_call(
        cast_kernel,
        in_specs=[anywhere] * 7,
        out_specs=[anywhere] * 6,
        out_shape=[
            shape(mixed.shape, BF16),
            shape(mixed.shape, F32),
            shape(gwide.shape, F32),
            shape(gtaps.shape, F32),
            shape(gmid.shape, F32),
            shape(gout.shape, F32),
        ],
        scratch_shapes=[
            pltpu.VMEM(gtaps.shape, BF16),
            pltpu.VMEM(gwide.shape, BF16),
            pltpu.VMEM(gpre.shape, BF16),
            pltpu.VMEM(gpre.shape, BF16),
            pltpu.VMEM(gtaps.shape, F32),
            pltpu.VMEM(gwide.shape, F32),
            pltpu.VMEM(gpre.shape, F32),
            pltpu.VMEM(mixed.shape, BF16),
            pltpu.VMEM(gmid.shape, F32),
            pltpu.VMEM(gout.shape, F32),
            pltpu.SemaphoreType.DMA((count + 2,)),
            pltpu.SemaphoreType.DMA((count,)),
            pltpu.SemaphoreType.DMA((3,)),
        ],
        compiler_params=pltpu.CompilerParams(vmem_limit_bytes=60 * 2**20),
        name="casts",
    )(mixed, gpre, conv, gwide, gtaps, gmid, gout)


def local(block_input, cotangent, weight_wide, weight_taps, norm_mid, norm_out, group_counts):
    n_dp = group_counts.shape[1]
    micro, rows, width = block_input.shape
    scratch = scratch_list(n_dp, rows)
    anywhere = pl.BlockSpec(memory_space=pl.ANY)

    def shape(dims, dtype):
        return jax.ShapeDtypeStruct(dims, dtype)

    stream = (micro, rows, width)
    mixed, gpre, conv, gwide, gtaps, gmid, gout = pl.pallas_call(
        functools.partial(kernel, list(scratch), n_dp),
        out_shape=[
            shape(stream, BF16),
            shape(stream, BF16),
            shape(stream, BF16),
            shape((4, 2, 256, 512), BF16),
            shape((2304, 512), BF16),
            shape(norm_mid.shape, F32),
            shape(norm_out.shape, F32),
        ],
        in_specs=[anywhere] * 7,
        out_specs=[anywhere] * 7,
        scratch_shapes=list(scratch.values()),
        compiler_params=pltpu.CompilerParams(
            collective_id=0, has_side_effects=True, vmem_limit_bytes=62 * 2**20
        ),
        name="layers",
    )(block_input, cotangent, weight_wide, weight_taps.reshape(9, 256, 512), norm_mid, norm_out, jnp.swapaxes(group_counts, 1, 2))
    results = cast_all(mixed, gpre, conv, gwide.reshape(2048, 512), gtaps, gmid, gout)
    mixed, grad_input, gwide, gtaps, gmid, gout = results
    return (
        mixed,
        grad_input,
        gwide.reshape(weight_wide.shape),
        gtaps.reshape(weight_taps.shape),
        gmid,
        gout,
    )


def solution(mesh):
    split = P(None, "dp", "pipe")
    section = P("pipe", None, None)
    return jax.shard_map(
        local,
        mesh=mesh,
        in_specs=(split, split, section, section, section, section, P()),
        out_specs=(split, split, section, section, section, section),
        check_vma=False,
    )
```

```python
import functools
from types import SimpleNamespace

import jax
import jax.numpy as jnp
from jax import lax
from jax.experimental import pallas as pl
from jax.experimental.pallas import tpu as pltpu
from jax.sharding import PartitionSpec as P

MESH = pl.DeviceIdType.MESH
F32 = jnp.float32
BF16 = jnp.bfloat16
EPS = 1e-05
LANES = 128
N_PIPE = 4
SIDES = (7, 6, 5, 2)


def dot_nn(a, b):
    return jnp.dot(a, b, preferred_element_type=F32)


def dot_nt(a, b):
    return lax.dot_general(a, b, (((1,), (1,)), ((), ())), preferred_element_type=F32)


def sigmoid(v):
    return jax.nn.sigmoid(v)


def sizes(n_dp):
    n_z = n_dp // 2
    n_own = min(n_z, 16)
    return n_z, n_own


def gradient_items(n_dp):
    line = n_dp // 2 == 4
    listed = []
    for kind, index, parts in (
        ("w", 3, [128, 128]),
        ("k", 1, [768] * 3),
        ("w", 2, [128, 128]),
        ("w", 1, [128, 128]),
        ("k", 0, [288, 288, 288, 288, 576, 576]),
        ("w", 0, [64] * 4),
    ):
        start = 0
        for part, rows in enumerate(parts if line else [sum(parts)]):
            listed.append(
                SimpleNamespace(
                    kind=kind, t=index, r0=start, nr=rows, i=len(listed), part=part
                )
            )
            start += rows
    return listed


def scratch_list(n_dp, rows):
    n_z, n_own = sizes(n_dp)
    items = len(gradient_items(n_dp))
    line = n_z == 4
    dma = pltpu.SemaphoreType.DMA

    def half(*shape):
        return pltpu.VMEM(shape, BF16)

    def full(*shape):
        return pltpu.VMEM(shape, F32)

    return dict(
        wt=half(4, 512, 512),
        k2=half(2, 18, 256, 128),
        gm=full(4, 2, 128),
        gmf=full(4, 2, 512),
        hf=half(2, 2, rows, 512),
        gff=half(2, 2, rows, 512),
        sml=full(2, 2, 4, 4, 128),
        go=full(4, 2, 2, 512),
        msk=full(2, rows, 128),
        beside=full(2, 2, rows, 128),
        above=full(2, 4, 2, rows, 128),
        yf=full(9, rows, 128),
        part=half(2, 2, 4, rows, 128),
        rsr=half(6 if line else 2, 2, 3, rows, 128),
        ag=half(6, 2, 4, rows, 128),
        stm=full(8, 2, n_dp, 2, 128),
        stw=full(4, 2, n_dp, 2, 512),
        midv=full(4, 2, rows, 128),
        dzm=full(2, rows, 128),
        inv_mid=full(4, 2, 1, 128),
        inv_wide=full(2, 2, 1, 512),
        widv=full(2, 2, rows, 512),
        pre0=full(2, rows, 512),
        s1=half(2, rows, 512),
        mix=half(2, rows, 512),
        gp=half(2, 2, rows, 512),
        gt=half(2, rows, 512),
        gb=half(2, rows, 1152),
        tb=half(512, 2 * rows),
        ack=full(512, 1152),
        dw=half(4, 2, 256, 512),
        prw=half(4, 256, 512),
        zsw=half(4, 256, 512),
        fzw=half(4, 256, 512),
        ow=half(4, 2, 256, 512),
        dk=half(2, 4608, 128),
        prk=half(2, 2304, 128),
        zsk=half(2, 2304, 128),
        fzk=half(2, 2304, 128),
        ok=half(2304, 512),
        zow=half(4, 256, 512) if line else half(4, n_z - 1, 256 // n_own, 512),
        ziw=half(4, 128, 512) if line else half(1, 16, 128),
        zok=half(2, 2304, 128) if line else half(2, n_z - 1, 2304 // n_own, 128),
        zik=half(2, 1152, 128) if line else half(1, 16, 128),
        gsm=full(4, 4, 2, 128),
        gsw=full(2, 4, 2, 512),
        cnt=pltpu.SMEM((2, n_dp), F32),
        xin=half(2, rows, 512),
        cin=half(2, rows, 512),
        gmo=full(1, 2, 512),
        goo=full(1, 2, 1024),
        counts=pltpu.SMEM((2, 4, n_dp), jnp.int32),
        f_s=dma((2,)),
        f_r=dma((2, 4)),
        z_r=dma((2, 4)),
        b_s=dma((2, 4)),
        b_r=dma((2, 4)),
        n_s=dma((3,)),
        n_r=dma((3,)),
        sm_s=dma((2, 2)),
        sm_r=dma((2, 2)),
        loc=dma((8,)),
        ex_s=dma((2, 2)),
        ex_r=dma((2, 2)),
        st_s=dma((2, 2)),
        st_r=dma((2, 2)),
        pw_s=dma((2,)),
        pw_r=dma((6,)),
        it_s=dma((6,)),
        one_r=dma((items,)),
        mid_r=dma((items,)),
        inn_r=dma((items,)),
        to_s=dma((6,)),
        ga_s=dma((6 if n_z != 4 else 1,)),
        sh_s=dma((4,)),
        sh_r=dma((4,)),
        to_r=dma((2, 6)),
        sib_s=dma((2,)),
        sib_r=dma((2, 6)),
        g_s=dma((2,)),
        g_r=dma((2,)),
        out=dma((8,)),
    )


def kernel(names, n, *refs):
    (x_hbm, cot_hbm, wide_ref, taps_ref, nmid_ref, nout_ref, counts_hbm) = refs[:7]
    (mixed_ref, gpre_ref, conv_ref, gwide_ref, gtaps_ref, gmid_ref, gout_ref) = refs[7:14]
    sc = SimpleNamespace(**dict(zip(names, refs[14:])))
    counts_ref = sc.counts
    x_ref, cot_ref = sc.xin, sc.cin
    rows = x_ref.shape[1]
    n_z, n_own = sizes(n)
    p = lax.axis_index("pipe")
    d = lax.axis_index("dp")
    z = lax.div(d, 2)
    c = lax.rem(d, 2)
    parity = lax.rem(p, 2)
    sibling = (p, 2 * z + 1 - c)
    z_odd = lax.rem(z, 2)
    z_pair = (p, 2 * (z + 1 - 2 * z_odd) + c)
    quarter = 2 * z_odd + c
    quarter_z = 2 * (1 - z_odd) + c
    finish = []

    def pipe_at(off):
        return lax.rem(p + N_PIPE + (2 * parity - 1) * off, N_PIPE)

    def remote(src, dst, ss, rs, dev):
        return pltpu.make_async_remote_copy(
            src_ref=src, dst_ref=dst, send_sem=ss, recv_sem=rs, device_id=dev, device_id_type=MESH
        )

    def each(count, first, body):
        if count - first <= 8:
            for k in range(first, count):
                body(k)
        else:

            def step(k, carry):
                body(k)
                return carry

            lax.fori_loop(first, count, step, 0)

    def bytes_wait(view, sem):
        pltpu.make_async_copy(view, view, sem).wait()

    barrier = pltpu.get_barrier_semaphore()
    for off in range(1, N_PIPE):
        pl.semaphore_signal(barrier, inc=1, device_id=(pipe_at(off), d), device_id_type=MESH)

    def greet(k):
        pl.semaphore_signal(
            barrier, inc=1, device_id=(p, lax.rem(d + k, n)), device_id_type=MESH
        )

    each(n, 1, greet)

    def columns_of(q):
        return pl.ds(pl.multiple_of(128 * q, 128), 128)

    own_w = pltpu.make_async_copy(
        wide_ref.at[0, pl.ds(pl.multiple_of(512 * p, 512), 512), :], sc.wt.at[p], sc.loc.at[0]
    )
    own_k = pltpu.make_async_copy(
        taps_ref.at[:, :, columns_of(p)],
        sc.k2.at[lax.div(p, 2), pl.ds(9 * parity, 9)],
        sc.loc.at[1],
    )
    own_c = pltpu.make_async_copy(counts_hbm, counts_ref, sc.loc.at[2])
    own_c.start()
    own_x = pltpu.make_async_copy(x_hbm, sc.xin, sc.loc.at[4])
    own_cot = pltpu.make_async_copy(cot_hbm, sc.cin, sc.loc.at[5])
    own_x.start()
    own_w.start()
    own_k.start()
    own_n = pltpu.make_async_copy(
        nmid_ref.at[0, :, columns_of(p)], sc.gm.at[p], sc.loc.at[3]
    )
    own_n.start()
    for e in range(2):
        pltpu.make_async_copy(
            nout_ref.at[0, :, pl.ds(512 * e, 512)], sc.go.at[p, e], sc.loc.at[6]
        ).start()
    own_cot.start()
    own_g = pltpu.make_async_copy(nmid_ref.at[0], sc.gmf.at[p], sc.loc.at[7])
    own_g.start()

    own_c.wait()

    def used_rows(m, j):
        return (
            49 * counts_ref[m, 0, j]
            + 36 * counts_ref[m, 1, j]
            + 25 * counts_ref[m, 2, j]
            + 4 * counts_ref[m, 3, j]
        )

    totals = []
    for m in range(2):

        def count_up(j, acc, m=m):
            used = used_rows(m, j)
            sc.cnt[m, j] = used.astype(F32)
            return acc + used

        totals.append(lax.fori_loop(0, n, count_up, jnp.int32(0)).astype(F32))

    pl.semaphore_wait(barrier, N_PIPE - 1 + n - 1)

    def held(kind, s, part):
        if kind == 0:
            return sc.wt.at[s, pl.ds(pl.multiple_of(128 * part, 128), 128)]
        layer, odd = (s // 2, s % 2) if isinstance(s, int) else (lax.div(s, 2), lax.rem(s, 2))
        return sc.k2.at[
            layer, pl.ds(9 * odd, 9), pl.ds(pl.multiple_of(64 * part, 64), 64)
        ]

    def fetch(kind, off):
        q = pipe_at(off)
        if kind == 0:
            src = wide_ref.at[0, pl.ds(pl.multiple_of(512 * q + 128 * quarter, 128), 128), :]
        else:
            src = taps_ref.at[:, pl.ds(pl.multiple_of(64 * quarter, 64), 64), columns_of(q)]
        return remote(
            src, held(kind, p, quarter), sc.f_s.at[kind], sc.f_r.at[kind, p], (q, d)
        )

    def send_norm(off):
        q = pipe_at(off)
        listed = [
            remote(
                nmid_ref.at[0, :, columns_of(q)],
                sc.gm.at[p],
                sc.n_s.at[0],
                sc.n_r.at[0],
                (q, d),
            ),
            remote(nmid_ref.at[0], sc.gmf.at[p], sc.n_s.at[2], sc.n_r.at[2], (q, d)),
        ]
        for e in range(2):
            listed.append(
                remote(
                    nout_ref.at[0, :, pl.ds(512 * e, 512)],
                    sc.go.at[p, e],
                    sc.n_s.at[1],
                    sc.n_r.at[1],
                    (q, d),
                )
            )
        return listed

    def norm_wait(sems):
        bytes_wait(sc.gm.at[pl.ds(0, 3)], sems.at[0])
        bytes_wait(sc.go.at[pl.ds(0, 3)], sems.at[1])
        bytes_wait(sc.gmf.at[pl.ds(0, 3)], sems.at[2])

    def pass_z(kind, s):
        view = held(kind, s, quarter)
        return remote(view, view, sc.b_s.at[kind, s], sc.z_r.at[kind, s], z_pair)

    def pass_sibling(kind, s, e):
        view = held(kind, s, quarter if e == 0 else quarter_z)
        return remote(view, view, sc.b_s.at[kind, s], sc.b_r.at[kind, s], sibling)

    def spread_first(kind, s):
        @pl.when(p != s)
        def _():
            view = held(kind, s, quarter)
            bytes_wait(view, sc.f_r.at[kind, s])
            pass_z(kind, s).start()
            pass_sibling(kind, s, 0).start()

    def spread_second(kind, s):
        @pl.when(p != s)
        def _():
            pass_z(kind, s).wait_recv()
            pass_sibling(kind, s, 1).start()

    def quarters(kind, s, count):
        if kind == 0:
            return sc.wt.at[s, pl.ds(0, 128 * count)]
        return sc.k2.at[s // 2, pl.ds(9 * (s % 2), 9), pl.ds(0, 64 * count)]

    def ready(kind, s):
        @pl.when(p != s)
        def _():
            bytes_wait(quarters(kind, s, 2), sc.b_r.at[kind, s])

        @pl.when(p == s)
        def _():
            (own_w if kind == 0 else own_k).wait()

    def finish_weights():
        for kind in range(2):
            bytes_wait(quarters(kind, 0, 3), sc.f_s.at[kind])
            for s in range(4):

                @pl.when(p != s)
                def _(kind=kind, s=s):
                    bytes_wait(quarters(kind, s, 3), sc.b_s.at[kind, s])

    finish.append(finish_weights)

    for even in range(2):

        @pl.when(parity == even)
        def _(even=even):
            for kind in (even, 1 - even):
                for off in range(1, 4):
                    fetch(kind, off).start()
                if kind == even:
                    for off in range(1, 4):
                        for copy in send_norm(off):
                            copy.start()

    def finish_norm():
        norm_wait(sc.n_s)

    finish.append(finish_norm)

    row_id = lax.broadcasted_iota(jnp.int32, (rows, LANES), 0).astype(F32)

    def build(m):
        ends = [jnp.float32(0.0)]
        total = jnp.int32(0)
        for g, side in enumerate(SIDES):
            total = total + side * side * counts_ref[m, g, d]
            ends.append(total.astype(F32))
        sc.msk[m] = jnp.where(row_id < ends[4], 1.0, 0.0)
        left = jnp.zeros((rows, LANES), F32)
        right = left
        for g, side in enumerate(SIDES):
            inside = (row_id >= ends[g]) & (row_id < ends[g + 1])
            within = row_id - ends[g]
            within = within - side * side * jnp.floor((within + 0.5) / (side * side))
            map_row = jnp.floor((within + 0.5) / side)
            map_col = within - side * map_row
            left = jnp.where(inside & (map_col > 0.5), 1.0, left)
            right = jnp.where(inside & (map_col < side - 1.5), 1.0, right)
            sc.above[m, g, 0] = jnp.where(inside & (map_row > 0.5), 1.0, 0.0)
            sc.above[m, g, 1] = jnp.where(inside & (map_row < side - 1.5), 1.0, 0.0)
        sc.beside[m, 0] = left
        sc.beside[m, 1] = right

    def shifted(values, count):
        return pltpu.roll(values, count % rows, 0)

    def from_above(values, m):
        return sum(
            sc.above[m, g, 0] * shifted(values, side) for g, side in enumerate(SIDES)
        )

    def from_below(values, m):
        return sum(
            sc.above[m, g, 1] * shifted(values, -side) for g, side in enumerate(SIDES)
        )

    for m in range(2):
        build(m)


    exchange_order = [
        ("rs", 0), ("ag", 0), ("ag", 2), ("rs", 1), ("ag", 1), ("ag", 3),
        ("rs", 3), ("rs", 5), ("ag", 5), ("rs", 2), ("rs", 4), ("ag", 4),
    ]

    def rs_slot(rid):
        return rid if sc.rsr.shape[0] == 6 else rs_par[rid]

    def three(kind, i, m):
        return sc.rsr.at[rs_slot(i), m] if kind == "rs" else sc.ag.at[i, m, pl.ds(0, 3)]

    def exchange_wait(sems, kind, i, m):
        turn = exchange_order.index((kind, i))
        bytes_wait(three(kind, i, m), sems.at[turn % 2, m])

    def exchange_open(kind, i, m):
        turn = exchange_order.index((kind, i))
        if turn >= 2:
            exchange_wait(sc.ex_s, *exchange_order[turn - 2], m)
        return sc.ex_s.at[turn % 2, m], sc.ex_r.at[turn % 2, m]

    def rs_sum(rid, m, par):
        exchange_wait(sc.ex_r, "rs", rid, m)
        total = sc.part[par, m, p].astype(F32)
        for k in range(3):
            total = total + sc.rsr[rs_slot(rid), m, k].astype(F32)
        return total

    def ag_start(aid, m, value):
        ss, rs = exchange_open("ag", aid, m)
        sc.ag[aid, m, p] = value
        own = sc.ag.at[aid, m, p]
        for off in range(1, 4):
            remote(own, own, ss, rs, (pipe_at(off), d)).start()

    def ag_wait(aid, m):
        exchange_wait(sc.ex_r, "ag", aid, m)

    def ag_value(aid, m):
        return jnp.concatenate([sc.ag[aid, m, q] for q in range(4)], axis=1)

    def finish_exchanges():
        for kind, i in exchange_order[-2:]:
            for m in range(2):
                exchange_wait(sc.ex_s, kind, i, m)

    finish.append(finish_exchanges)

    sum_order = [
        (False, 0), (False, 1), (True, 0), (False, 2), (False, 3), (True, 1),
        (True, 3), (False, 7), (False, 6), (True, 2), (False, 5), (False, 4),
    ]

    def st_buffer(wide, i, m):
        return (sc.stw if wide else sc.stm).at[i, m]

    def st_bytes(sems, wide, i, m):
        turn = sum_order.index((wide, i))
        bytes_wait(st_buffer(wide, i, m).at[pl.ds(0, n - 1)], sems.at[turn % 2, m])

    def st_start(wide, i, m):
        turn = sum_order.index((wide, i))
        if turn >= 2:
            st_bytes(sc.st_s, *sum_order[turn - 2], m)
        own = st_buffer(wide, i, m).at[d]
        ss, rs = sc.st_s.at[turn % 2, m], sc.st_r.at[turn % 2, m]

        def go(k):
            remote(own, own, ss, rs, (p, lax.rem(d + k, n))).start()

        if n > 8:
            each(n, 1, go)
            return
        high = lax.div(2 * z, n_z)
        for i in range(n_z - 1):
            low_far = n_z - 1 - i - lax.div(z + i + 1, n_z)
            high_far = i + lax.div(i - z + n_z, n_z)
            far = high * high_far + (1 - high) * low_far
            for e in range(2):
                remote(own, own, ss, rs, (p, 2 * far + e)).start()
        remote(own, own, ss, rs, sibling).start()

    def st_wait(wide, i, m):
        st_bytes(sc.st_r, wide, i, m)

    def finish_st():
        for wide, i in sum_order[-2:]:
            for m in range(2):
                st_bytes(sc.st_s, wide, i, m)

    finish.append(finish_st)

    def over_devices(body, init):
        if n <= 8:
            for j in range(n):
                init = body(j, init)
            return init
        return lax.fori_loop(0, n, body, init)

    def combine(wide, i, m):
        st_wait(wide, i, m)
        ref = sc.stw if wide else sc.stm
        blank = jnp.zeros((1, ref.shape[-1]), F32)
        mean = over_devices(
            lambda j, acc: acc + sc.cnt[m, j] * ref[i, m, j, 0:1, :], blank
        )
        mean = mean / totals[m]

        def spread(j, acc):
            gap = ref[i, m, j, 0:1, :] - mean
            return acc + ref[i, m, j, 1:2, :] + sc.cnt[m, j] * (gap * gap)

        var = over_devices(spread, blank) / totals[m]
        return mean, lax.rsqrt(var + EPS)

    def back_sums(wide, i, m):
        st_wait(wide, i, m)
        ref = sc.stw if wide else sc.stm
        return over_devices(
            lambda j, acc: acc + ref[i, m, j], jnp.zeros((2, ref.shape[-1]), F32)
        )

    def local_moments(v, m):
        mask = sc.msk[m]
        own = jnp.maximum(sc.cnt[m, d], 1.0)
        mean = jnp.sum(v * mask, 0, keepdims=True) / own
        gap = (v - mean) * mask
        return jnp.concatenate([mean, jnp.sum(gap * gap, 0, keepdims=True)], 0)

    def local_sums(dz, vhat):
        return jnp.concatenate(
            [jnp.sum(dz * vhat, 0, keepdims=True), jnp.sum(dz, 0, keepdims=True)], 0
        )

    def lanes(j):
        return slice(LANES * j, LANES * (j + 1))

    def stream(layer, m):
        return x_ref[m] if layer == 0 else sc.s1[m]

    def stream_part(layer, m, j):
        return (x_ref[m, :, lanes(j)] if layer == 0 else sc.s1[m, :, lanes(j)]).astype(F32)

    rs_par = {0: 0, 1: 1, 3: 0, 5: 1, 2: 0, 4: 1}

    def rs_send(rid, m, values):
        par = rs_par[rid]
        ss, rs = exchange_open("rs", rid, m)
        for j, value in enumerate(values):
            half = value.astype(BF16)
            sc.part[par, m, 2 * j] = half[:, :LANES]
            sc.part[par, m, 2 * j + 1] = half[:, LANES:]
        for off in range(1, 4):
            q = pipe_at(off)
            remote(sc.part.at[par, m, q], sc.rsr.at[rs_slot(rid), m, off - 1], ss, rs, (q, d)).start()

    def first_part(layer, m):
        s = stream(layer, m)
        rs_send(
            layer,
            m,
            [dot_nn(s, sc.wt[2 * layer, :, 256 * j : 256 * j + 256]) for j in range(2)],
        )

    def mid_moments(i, m, v):
        sc.midv[i, m] = v
        sc.stm[i, m, d] = local_moments(v, m)
        st_start(False, i, m)

    def first_norm(layer, m):
        mid_moments(2 * layer, m, rs_sum(layer, m, rs_par[layer]))

    def mid_hidden(i, m):
        mean, inv = combine(False, i, m)
        sc.inv_mid[i, m] = inv
        vhat = (sc.midv[i, m] - mean) * inv
        sc.midv[i, m] = vhat
        u = sc.gm[i, 0:1, :] * vhat + sc.gm[i, 1:2, :]
        return (sc.msk[m] * (u * sigmoid(u))).astype(BF16)

    def hidden_one(layer, m):
        i = 2 * layer
        mean, inv = combine(False, i, m)
        sc.inv_mid[i, m] = inv
        vhat = ((sc.midv[i, m] - mean) * inv).astype(BF16)
        sc.midv[i, m] = vhat.astype(F32)
        ag_start(layer, m, vhat)

    def taps_of(layer, taps):
        return jnp.concatenate(
            [
                jnp.concatenate([sc.k2[layer, 2 * k], sc.k2[layer, 2 * k + 1]], axis=0)
                for k in taps
            ],
            axis=1,
        )

    def second_part(layer, m):
        ag_wait(layer, m)
        for q in range(4):
            gain, bias = sc.gmf[2 * layer, 0:1, lanes(q)], sc.gmf[2 * layer, 1:2, lanes(q)]
            u = gain * sc.ag[layer, m, q].astype(F32) + bias
            sc.hf[layer, m, :, lanes(q)] = (sc.msk[m] * (u * sigmoid(u))).astype(BF16)
        h = sc.hf[layer, m]
        for j in range(5):
            width = 256 if j < 4 else 128
            y = dot_nn(h, taps_of(layer, [2 * j + e for e in range(width // LANES)]))
            for e in range(width // LANES):
                sc.yf[2 * j + e] = y[:, lanes(e)]

        def across(k):
            return (
                sc.yf[k + 1]
                + sc.beside[m, 0] * shifted(sc.yf[k], 1)
                + sc.beside[m, 1] * shifted(sc.yf[k + 2], -1)
            )

        total = across(3) + from_above(across(0), m) + from_below(across(6), m)
        mid_moments(2 * layer + 1, m, total)

    def hidden_two(layer, m):
        ag_start(2 + layer, m, mid_hidden(2 * layer + 1, m))

    def third_part(layer, m):
        ag_wait(2 + layer, m)
        h = ag_value(2 + layer, m)
        for j in range(2):
            sc.widv[layer, m, :, 256 * j : 256 * j + 256] = dot_nt(
                h, sc.wt[2 * layer + 1, 256 * j : 256 * j + 256, :]
            )
        for j in range(4):
            sc.stw[layer, m, d, :, lanes(j)] = local_moments(sc.widv[layer, m, :, lanes(j)], m)
        st_start(True, layer, m)

    def out_gain(layer, j):
        both = sc.go[2 * layer + lax.div(p, 2), lax.rem(p, 2)]
        return both[0:1, lanes(j)], both[1:2, lanes(j)]

    def pre_values(layer, m):
        mean, inv = combine(True, layer, m)
        sc.inv_wide[layer, m] = inv
        mask = sc.msk[m]
        for j in range(4):
            gain, bias = out_gain(layer, j)
            vhat = (sc.widv[layer, m, :, lanes(j)] - mean[:, lanes(j)]) * inv[:, lanes(j)]
            sc.widv[layer, m, :, lanes(j)] = vhat
            pre = gain * vhat + bias + stream_part(layer, m, j)
            sig = sigmoid(pre)
            out = (mask * (pre * sig)).astype(BF16)
            if layer == 0:
                sc.pre0[m, :, lanes(j)] = pre
                sc.s1[m, :, lanes(j)] = out
            else:
                sc.mix[m, :, lanes(j)] = out
                slope = sig * (1.0 + pre * (1.0 - sig))
                grad = (cot_ref[m, :, lanes(j)].astype(F32) * mask * slope).astype(BF16)
                sc.gp[1, m, :, lanes(j)] = grad
                sc.stw[3, m, d, :, lanes(j)] = local_sums(grad.astype(F32), vhat)
        if layer == 1:
            st_start(True, 3, m)

    def put_out(k, src, dst):
        copy = pltpu.make_async_copy(src, dst, sc.out.at[k])
        copy.start()
        return copy

    def grad_out_norm(layer, m):
        sums = back_sums(True, 2 + layer, m)
        if m == 0:
            sc.gsw[layer, p] = sums
        else:
            sc.gsw[layer, p] = sc.gsw[layer, p] + sums
        mask = sc.msk[m]
        inv = sc.inv_wide[layer, m]
        for j in range(4):
            gain, _ = out_gain(layer, j)
            dz = sc.gp[layer, m, :, lanes(j)].astype(F32)
            vhat = sc.widv[layer, m, :, lanes(j)]
            s1 = sums[0:1, lanes(j)] / totals[m]
            s0 = sums[1:2, lanes(j)] / totals[m]
            dv = mask * (gain * inv[:, lanes(j)]) * (dz - s0 - vhat * s1)
            sc.gt[m, :, lanes(j)] = dv.astype(BF16)
        g = sc.gt[m]
        rs_send(
            2 + layer,
            m,
            [dot_nn(g, sc.wt[2 * layer + 1, :, 256 * j : 256 * j + 256]) for j in range(2)],
        )

    def mid_grad(i, m, upstream):
        vhat = sc.midv[i, m]
        u = sc.gm[i, 0:1, :] * vhat + sc.gm[i, 1:2, :]
        sig = sigmoid(u)
        dz = upstream * sc.msk[m] * (sig * (1.0 + u * (1.0 - sig)))
        sc.dzm[m] = dz
        sc.stm[4 + i, m, d] = local_sums(dz, vhat)
        st_start(False, 4 + i, m)

    def mid_back(i, m):
        sums = back_sums(False, 4 + i, m)
        if m == 0:
            sc.gsm[i, p] = sums
        else:
            sc.gsm[i, p] = sc.gsm[i, p] + sums
        s1 = sums[0:1, :] / totals[m]
        s0 = sums[1:2, :] / totals[m]
        scale = sc.gm[i, 0:1, :] * sc.inv_mid[i, m]
        return (sc.msk[m] * scale * (sc.dzm[m] - s0 - sc.midv[i, m] * s1)).astype(BF16)

    def grad_two(layer, m):
        mid_grad(2 * layer + 1, m, rs_sum(2 + layer, m, rs_par[2 + layer]))

    def grad_second(layer, m):
        gs = mid_back(2 * layer + 1, m)
        own = gs.astype(F32)
        for du, moved in ((0, own), (1, from_above(own, m)), (-1, from_below(own, m))):
            k = 3 * (du + 1)
            sc.gb[m, :, lanes(k + 1)] = moved.astype(BF16)
            sc.gb[m, :, lanes(k + 2)] = (sc.beside[m, 0] * shifted(moved, 1)).astype(BF16)
            sc.gb[m, :, lanes(k)] = (sc.beside[m, 1] * shifted(moved, -1)).astype(BF16)
        g = sc.gb[m]
        rs_send(
            4 + layer,
            m,
            [
                dot_nt(
                    g, jnp.concatenate([sc.k2[layer, 2 * k + j] for k in range(9)], axis=1)
                )
                for j in range(2)
            ],
        )

    def grad_one(layer, m):
        mid_grad(2 * layer, m, rs_sum(4 + layer, m, rs_par[4 + layer]))
        ag_start(4 + layer, m, sc.dzm[m].astype(BF16))

    def small_copy(layer, m, off):
        own = sc.sml.at[layer, m, p]
        return remote(own, own, sc.sm_s.at[layer, m], sc.sm_r.at[layer, m], (pipe_at(off), d))

    def grad_first(layer, m):
        i = 2 * layer
        sums = back_sums(False, 4 + i, m)
        if m == 0:
            sc.gsm[i, p] = sums
        else:
            sc.gsm[i, p] = sc.gsm[i, p] + sums
        scale = sc.gm[i, 0:1, :] * sc.inv_mid[i, m]
        s1 = scale * (sums[0:1, :] / totals[m])
        s0 = scale * (sums[1:2, :] / totals[m])
        sc.sml[layer, m, p] = jnp.concatenate([scale, s0, s1, s1], 0)
        for off in range(1, 4):
            small_copy(layer, m, off).start()

    def finish_small():
        for layer in range(2):
            for m in range(2):
                bytes_wait(sc.sml.at[layer, m, pl.ds(0, 3)], sc.sm_s.at[layer, m])

    finish.append(finish_small)

    def slopes(m):
        for i in range(4):
            pre = sc.pre0[m, :, lanes(i)]
            sig = sigmoid(pre)
            sc.pre0[m, :, lanes(i)] = sc.msk[m] * (sig * (1.0 + pre * (1.0 - sig)))

    def conv_grad(layer, m):
        ag_wait(4 + layer, m)
        bytes_wait(sc.sml.at[layer, m, pl.ds(0, 3)], sc.sm_r.at[layer, m])
        for q in range(4):
            scale, s0, s1 = (sc.sml[layer, m, q, k : k + 1, :] for k in range(3))
            dz = sc.ag[4 + layer, m, q].astype(F32)
            vhat = sc.ag[layer, m, q].astype(F32)
            dv = sc.msk[m] * (scale * dz - s0 - s1 * vhat)
            sc.gff[layer, m, :, lanes(q)] = dv.astype(BF16)
        g = sc.gff[layer, m]
        for j in range(2):
            r = dot_nt(g, sc.wt[2 * layer, 256 * j : 256 * j + 256, :]).astype(BF16)
            if layer == 0:
                sc.cin[m, :, 256 * j : 256 * j + 256] = r
                continue
            for e in range(2):
                i = 2 * j + e
                up = sc.gp[1, m, :, lanes(i)].astype(F32) + r[:, lanes(e)].astype(F32)
                grad = (up * sc.pre0[m, :, lanes(i)]).astype(BF16)
                sc.gp[0, m, :, lanes(i)] = grad
                sc.stw[2, m, d, :, lanes(i)] = local_sums(
                    grad.astype(F32), sc.widv[0, m, :, lanes(i)]
                )
        if layer == 1:
            st_start(True, 2, m)

    def turned(blocks):
        for m, block in enumerate(blocks):
            sc.tb[:, rows * m : rows * (m + 1)] = block.T

    def both(get):
        return jnp.concatenate([get(0), get(1)], axis=0)

    def wide_grad(s, left, right):
        turned([left(0), left(1)])
        for j in range(2):
            cols = slice(256 * j, 256 * j + 256)
            rhs = both(lambda m: right(m)[:, cols])
            for h in range(2):
                r = dot_nn(sc.tb[256 * h : 256 * h + 256, :], rhs)
                sc.dw[s, h, :, cols] = r.astype(BF16)
        pair_copy("w", s).start()

    def wide_early():
        turned([x_ref[0], x_ref[1]])
        g = sc.gff[0, 0]
        for j in range(2):
            cols = slice(256 * j, 256 * j + 256)
            sc.ack[:, cols] = dot_nn(sc.tb[:, :rows], g[:, cols])

    def wide_late():
        g = sc.gff[0, 1]
        for j in range(2):
            cols = slice(256 * j, 256 * j + 256)
            for h in range(2):
                part = slice(256 * h, 256 * h + 256)
                r = sc.ack[part, cols] + dot_nn(sc.tb[part, rows:], g[:, cols])
                sc.dw[0, h, :, cols] = r.astype(BF16)
        pair_copy("w", 0).start()

    def taps_early():
        turned([sc.hf[0, 0], sc.hf[0, 1]])
        for j in range(5):
            cols = slice(256 * j, min(256 * j + 256, 1152))
            sc.ack[:, cols] = dot_nn(sc.tb[:, :rows], sc.gb[0, :, cols])

    def taps_late():
        for j in range(5):
            cols = slice(256 * j, min(256 * j + 256, 1152))
            r = (sc.ack[:, cols] + dot_nn(sc.tb[:, rows:], sc.gb[1, :, cols])).astype(BF16)
            for e in range(r.shape[1] // LANES):
                tap = 2 * j + e
                sc.dk[0, 512 * tap : 512 * tap + 512, :] = r[:, lanes(e)]
        pair_copy("k", 0).start()

    def taps_grad(layer):
        turned([sc.hf[layer, 0], sc.hf[layer, 1]])
        for j in range(5):
            width = 256 if j < 4 else 128
            rhs = both(lambda m: sc.gb[m, :, 256 * j : 256 * j + width])
            r = dot_nn(sc.tb[...], rhs).astype(BF16)
            for e in range(width // LANES):
                tap = 2 * j + e
                sc.dk[layer, 512 * tap : 512 * tap + 512, :] = r[:, lanes(e)]
        pair_copy("k", layer).start()

    def half_rows(which):
        return pl.ds(pl.multiple_of(2304 * which, 2304), 2304)

    def pair_copy(kind, t):
        if kind == "w":
            src, dst, i = sc.dw.at[t, 1 - c], sc.prw.at[t], t
        else:
            src, dst, i = sc.dk.at[t, half_rows(1 - c)], sc.prk.at[t], 4 + t
        return remote(src, dst, sc.pw_s.at[0 if kind == "w" else 1], sc.pw_r.at[i], sibling)

    def pair_sum(kind, t):
        pair_copy(kind, t).wait_recv()
        if kind == "w":
            sc.zsw[t] = (sc.dw[t, c].astype(F32) + sc.prw[t].astype(F32)).astype(BF16)
            return
        for i in range(4):
            part = slice(576 * i, 576 * i + 576)
            mine = pl.ds(pl.multiple_of(2304 * c + 576 * i, 576), 576)
            sc.zsk[t, part] = (
                sc.dk[t, mine].astype(F32) + sc.prk[t, part].astype(F32)
            ).astype(BF16)

    items = gradient_items(n)
    line = n_z == 4
    inner = (z == 1) | (z == 2)

    def tile_sem(it):
        return it.t if it.kind == "w" else 4 + it.t

    def tile(it, name):
        return getattr(sc, name + it.kind)

    def some(it, name, start, count):
        return tile(it, name).at[it.t, pl.ds(start, count)]

    def part_rows(it, which):
        half = it.nr // 2
        return pl.ds(pl.multiple_of(it.r0 + half * which, half), half)

    def up_copy(it):
        rows_of = pl.ds(it.r0, it.nr)
        return remote(
            tile(it, "zs").at[it.t, rows_of],
            tile(it, "zo").at[it.t, rows_of],
            sc.it_s.at[tile_sem(it)],
            sc.one_r.at[it.i],
            (p, 2 * (1 + lax.div(z, 3)) + c),
        )

    def mid_copy(it):
        return remote(
            tile(it, "zs").at[it.t, part_rows(it, 2 - z)],
            tile(it, "zi").at[it.t, pl.ds(it.r0 // 2, it.nr // 2)],
            sc.it_s.at[tile_sem(it)],
            sc.mid_r.at[it.i],
            (p, 2 * (3 - z) + c),
        )

    def inn_copy(it):
        view = tile(it, "fz").at[it.t, part_rows(it, z - 1)]
        return remote(
            view, view, sc.it_s.at[tile_sem(it)], sc.inn_r.at[it.i], (p, 2 * (3 - z) + c)
        )

    def down_copy(it, e):
        view = tile(it, "fz").at[it.t, part_rows(it, z - 1 if e == 0 else 2 - z)]
        return remote(
            view, view, sc.it_s.at[tile_sem(it)], sc.one_r.at[it.i], (p, 2 * (3 * (z - 1)) + c)
        )

    def direct_rows(it, j):
        count = it.nr // n_own
        return pl.ds(pl.multiple_of(it.r0 + count * j, count), count)

    def owner(index, body):
        if n_own == n_z:
            body()
        else:
            pl.when(index < n_own)(body)

    def scatter_copy(it, k):
        j = lax.rem(z + k, n_z)
        return j, remote(
            tile(it, "zs").at[it.t, direct_rows(it, lax.rem(j, n_own))],
            tile(it, "zo").at[it.t, k - 1],
            sc.it_s.at[tile_sem(it)],
            sc.one_r.at[it.i],
            (p, 2 * j + c),
        )

    def gather_copy(it, k):
        j = lax.rem(z + k, n_z)
        view = tile(it, "fz").at[it.t, direct_rows(it, lax.rem(z, n_own))]
        return remote(view, view, sc.ga_s.at[tile_sem(it)], sc.mid_r.at[it.i], (p, 2 * j + c))

    def add_rows(target, first, second):
        target[...] = (first[...].astype(F32) + second[...].astype(F32)).astype(BF16)

    def step_up(it):
        if line:

            @pl.when((z == 0) | (z == 3))
            def _():
                up_copy(it).start()

        else:

            def go(k):
                j, copy = scatter_copy(it, k)
                owner(j, lambda: copy.start())

            each(n_z, 1, go)

    def step_mid(it):
        if not line:
            return

        @pl.when(inner)
        def _():
            up_copy(it).wait_recv()
            mine = some(it, "zs", it.r0, it.nr)
            add_rows(mine, mine, some(it, "zo", it.r0, it.nr))
            mid_copy(it).start()

    def step_down(it):
        if line:

            @pl.when(inner)
            def _():
                mid_copy(it).wait_recv()
                keep = part_rows(it, z - 1)
                add_rows(
                    tile(it, "fz").at[it.t, keep],
                    tile(it, "zs").at[it.t, keep],
                    some(it, "zi", it.r0 // 2, it.nr // 2),
                )
                inn_copy(it).start()
                down_copy(it, 0).start()

            return

        def go():
            bytes_wait(tile(it, "zo").at[it.t], sc.one_r.at[it.i])
            mine = direct_rows(it, z)
            total = tile(it, "zs")[it.t, mine].astype(F32)
            total = lax.fori_loop(
                0, n_z - 1, lambda k, acc: acc + tile(it, "zo")[it.t, k].astype(F32), total
            )
            tile(it, "fz")[it.t, mine] = total.astype(BF16)
            each(n_z, 1, lambda k: gather_copy(it, k).start())

        owner(z, go)

    def step_last(it):
        if not line:
            return

        @pl.when(inner)
        def _():
            inn_copy(it).wait_recv()
            down_copy(it, 1).start()

    def owner_of(it):
        return it.t if it.kind == "w" else 2 * it.t + c

    def landing(it, q, core):
        if it.kind == "w":
            return sc.ow.at[q, core, pl.ds(it.r0, it.nr)]
        lane = pl.ds(128 * q, 128) if isinstance(q, int) else columns_of(q)
        return sc.ok.at[pl.ds(it.r0, it.nr), lane]

    def to_sem(it, sems):
        return sems.at[0 if it.kind == "w" else 1, it.part]

    def to_copy(it):
        return remote(
            some(it, "fz", it.r0, it.nr),
            landing(it, p, c),
            sc.to_s.at[tile_sem(it)],
            to_sem(it, sc.to_r),
            (owner_of(it), d),
        )

    def shared(it):
        return line and it.kind == "w" and it.t == 0

    def in_charge(it):
        outer = (z == 0) | (z == 3)
        return outer if it.part % 2 == 0 else jnp.logical_not(outer)

    def sends_out(it):
        if shared(it):
            return (p == 1) | ((p > 1) & in_charge(it))
        return p != owner_of(it)

    def passes_on(it):
        if shared(it):
            return (p == 0) & in_charge(it)
        return p < 0

    def pass_copy(it):
        view = sc.ow.at[pl.ds(2, 2), c, pl.ds(it.r0, it.nr)]
        return remote(view, view, sc.sh_s.at[it.part], sc.sh_r.at[it.part], z_pair)

    def step_inner_out(it):
        if line:
            pl.when(inner)(lambda: deliver(it))

    def step_out(it):
        if line:

            @pl.when((z == 0) | (z == 3))
            def _():
                bytes_wait(some(it, "fz", it.r0, it.nr), sc.one_r.at[it.i])
                deliver(it)

        else:
            count = it.nr // n_own
            if n_own == n_z:
                bytes_wait(some(it, "fz", it.r0, count * (n_own - 1)), sc.mid_r.at[it.i])
            else:

                @pl.when(z < n_own)
                def _():
                    bytes_wait(some(it, "fz", it.r0, count * (n_own - 1)), sc.mid_r.at[it.i])

                @pl.when(z >= n_own)
                def _():
                    bytes_wait(some(it, "fz", it.r0, count * n_own), sc.mid_r.at[it.i])

            deliver(it)

    def deliver(it):
        @pl.when(sends_out(it))
        def _():
            to_copy(it).start()

        def place(q):
            landing(it, q, c)[...] = some(it, "fz", it.r0, it.nr)[...]

        if it.kind == "w":
            pl.when(p == it.t)(lambda: place(it.t))
        else:
            for core in range(2):
                pl.when((p == 2 * it.t + core) & (c == core))(
                    functools.partial(place, 2 * it.t + core)
                )

    def sibling_copy(it, q):
        view = landing(it, q, c)
        return remote(
            view, view, sc.sib_s.at[0 if it.kind == "w" else 1], to_sem(it, sc.sib_r), sibling
        )

    def slices(it, count):
        if it.kind == "w":
            return sc.ow.at[pl.ds(0, count), 0, pl.ds(it.r0, it.nr)]
        return sc.ok.at[pl.ds(it.r0, it.nr), pl.ds(0, 128 * count)]

    def step_sibling(it):
        def go():
            bytes_wait(slices(it, 3), to_sem(it, sc.to_r))
            for q in range(4):
                sibling_copy(it, q).start()

        if not shared(it):
            pl.when(p == owner_of(it))(go)
            return

        @pl.when((p == 0) & in_charge(it))
        def _():
            bytes_wait(slices(it, 3), to_sem(it, sc.to_r))
            pass_copy(it).start()
            for q in range(4):
                sibling_copy(it, q).start()

        @pl.when((p == 0) & jnp.logical_not(in_charge(it)))
        def _():
            bytes_wait(slices(it, 1), to_sem(it, sc.to_r))
            for q in range(2):
                sibling_copy(it, q).start()

    def step_rest(it):
        if not shared(it):
            return

        @pl.when((p == 0) & jnp.logical_not(in_charge(it)))
        def _():
            bytes_wait(slices(it, 2), sc.sh_r.at[it.part])
            for q in range(2, 4):
                sibling_copy(it, q).start()

    def step_done(it):
        def go():
            bytes_wait(slices(it, 4), to_sem(it, sc.sib_r))

        pl.when(p == (it.t if it.kind == "w" else 2 * it.t + 1 - c))(go)

    def finish_grads():
        bytes_wait(sc.dw.at[:, 0], sc.pw_s.at[0])
        bytes_wait(sc.dk.at[0], sc.pw_s.at[1])
        for kind, t in [("w", s) for s in range(4)] + [("k", layer) for layer in range(2)]:
            whole = next(it for it in items if it.kind == kind and it.t == t)
            sends = sc.it_s.at[tile_sem(whole)]
            half = tile(whole, "zs").at[t]
            if line:

                @pl.when(inner)
                def _(kind=kind, t=t, sends=sends):
                    bytes_wait((sc.dw if kind == "w" else sc.dk).at[t], sends)

                @pl.when((z == 0) | (z == 3))
                def _(half=half, sends=sends):
                    bytes_wait(half, sends)

            else:

                def sent(k, it=whole):
                    j, copy = scatter_copy(it, k)
                    owner(j, lambda: copy.wait_send())

                each(n_z, 1, sent)
                owner(
                    z,
                    lambda it=whole: each(n_z, 1, lambda k: gather_copy(it, k).wait_send()),
                )

        for it in items:

            @pl.when(sends_out(it))
            def _(it=it):
                bytes_wait(some(it, "fz", it.r0, it.nr), sc.to_s.at[tile_sem(it)])

            @pl.when(passes_on(it))
            def _(it=it):
                bytes_wait(slices(it, 2), sc.sh_s.at[it.part])

        bytes_wait(sc.ow.at[:, 0], sc.sib_s.at[0])

        @pl.when(c == parity)
        def _():
            bytes_wait(sc.ok.at[...], sc.sib_s.at[1])

    finish.append(finish_grads)

    def gain_copies(off):
        dev = (pipe_at(off), d)
        return [
            remote(sc.gsm.at[:, p], sc.gsm.at[:, p], sc.g_s.at[0], sc.g_r.at[0], dev),
            remote(sc.gsw.at[:, p], sc.gsw.at[:, p], sc.g_s.at[1], sc.g_r.at[1], dev),
        ]

    def gains_wait(sems):
        bytes_wait(sc.gsm.at[:, pl.ds(0, 3)], sems.at[0])
        bytes_wait(sc.gsw.at[:, pl.ds(0, 3)], sems.at[1])

    def gains_start():
        for off in range(1, 4):
            for copy in gain_copies(off):
                copy.start()

    def gains_done():
        gains_wait(sc.g_r)
        for q in range(4):
            sc.gmo[0, :, lanes(q)] = sc.gsm[p, q]
        layer = lax.div(p, 2)
        for e in range(2):
            sc.goo[0, :, 512 * e : 512 * e + 512] = sc.gsw[layer, 2 * parity + e]
        outs.append(put_out(0, sc.gmo.at[...], gmid_ref.at[...]))
        outs.append(put_out(7, sc.goo.at[...], gout_ref.at[...]))

    def finish_gains():
        gains_wait(sc.g_s)

    finish.append(finish_gains)

    def of(kind, t):
        return [it for it in items if it.kind == kind and it.t == t]

    def one(step, kind, t, part):
        for it in of(kind, t)[part : part + 1]:
            step(it)

    def run(step, kind, t):
        for it in of(kind, t):
            step(it)

    def nothing():
        return None

    def paired(arrival, reply, layer, hooks=(nothing, nothing)):
        for m in range(2):
            arrival(layer, m)
            hooks[m]()
            reply(layer, m)

    def steps(*listed):
        def go():
            for body, *rest in listed:
                body(*rest)

        return go

    up, mid, down, last, out = step_up, step_mid, step_down, step_last, step_out
    inside = step_inner_out
    wide, taps = 0, 1
    spread_first(wide, 0)
    spread_second(wide, 0)
    ready(wide, 0)
    own_x.wait()
    first_part(0, 0)
    first_part(0, 1)
    own_n.wait()
    bytes_wait(sc.go.at[0], sc.loc.at[6])
    own_cot.wait()
    own_g.wait()
    norm_wait(sc.n_r)
    spread_first(taps, 0)
    spread_first(taps, 1)
    paired(
        first_norm,
        hidden_one,
        0,
        (
            steps((spread_second, taps, 0), (spread_second, taps, 1)),
            steps((spread_first, wide, 1)),
        ),
    )
    ready(taps, 0)
    ready(taps, 1)
    paired(
        second_part,
        hidden_two,
        0,
        (steps((spread_first, wide, 2), (spread_second, wide, 1)), steps((spread_first, taps, 2))),
    )
    ready(wide, 1)

    def turn(layer, m):
        pre_values(0, m)
        if m == 0:
            ready(wide, 2)
        first_part(1, m)

    paired(
        third_part,
        turn,
        0,
        (
            steps((spread_second, wide, 2), (spread_first, taps, 3), (spread_second, taps, 2)),
            steps((spread_first, wide, 3)),
        ),
    )
    paired(
        first_norm,
        hidden_one,
        1,
        (steps((spread_second, taps, 3)), steps((spread_second, wide, 3))),
    )
    ready(taps, 2)
    ready(taps, 3)
    paired(second_part, hidden_two, 1)
    ready(wide, 3)
    third_part(1, 0)
    pre_values(1, 0)
    third_part(1, 1)
    grad_out_norm(1, 0)
    pre_values(1, 1)
    outs = [put_out(2, sc.mix.at[...], mixed_ref.at[...])]
    grad_out_norm(1, 1)
    wide_grad(3, lambda m: sc.gt[m], lambda m: ag_value(3, m))
    paired(
        grad_two,
        grad_second,
        1,
        (
            steps((pair_sum, "w", 3), (one, up, "w", 3, 0), (slopes, 0)),
            steps((one, up, "w", 3, 1), (slopes, 1), (one, mid, "w", 3, 0)),
        ),
    )
    taps_grad(1)
    grad_one(1, 0)
    steps(
        (pair_sum, "k", 1),
        (one, up, "k", 1, 0),
        (one, mid, "w", 3, 1),
        (one, down, "w", 3, 0),
    )()
    grad_first(1, 0)
    grad_one(1, 1)
    conv_grad(1, 0)
    steps(
        (one, up, "k", 1, 1),
        (one, down, "w", 3, 1),
        (one, last, "w", 3, 0),
        (one, mid, "k", 1, 0),
    )()
    grad_first(1, 1)
    grad_out_norm(0, 0)
    conv_grad(1, 1)
    outs.append(put_out(3, sc.gp.at[0], gpre_ref.at[...]))
    steps(
        (one, up, "k", 1, 2),
        (one, last, "w", 3, 1),
        (one, mid, "k", 1, 1),
        (one, down, "k", 1, 0),
        (wide_grad, 2, lambda m: sc.s1[m], lambda m: sc.gff[1, m]),
    )()
    grad_out_norm(0, 1)
    wide_grad(1, lambda m: sc.gt[m], lambda m: ag_value(2, m))
    paired(
        grad_two,
        grad_second,
        0,
        (
            steps(
                (pair_sum, "w", 1),
                (one, up, "w", 1, 0),
                (one, mid, "k", 1, 2),
                (one, down, "k", 1, 1),
                (one, last, "k", 1, 0),
            ),
            steps(
                (one, up, "w", 1, 1),
                (pair_sum, "w", 2),
                (one, mid, "w", 1, 0),
                (one, down, "k", 1, 2),
                (one, last, "k", 1, 1),
                (taps_early,),
            ),
        ),
    )
    taps_late()
    grad_one(0, 0)
    steps(
        (pair_sum, "k", 0),
        (one, up, "k", 0, 0),
        (one, up, "k", 0, 1),
        (one, mid, "w", 1, 1),
        (one, down, "w", 1, 0),
        (one, last, "k", 1, 2),
    )()
    grad_first(0, 0)
    grad_one(0, 1)
    steps(
        (one, up, "k", 0, 2),
        (one, up, "k", 0, 3),
        (one, up, "k", 0, 4),
        (one, up, "k", 0, 5),
        (one, mid, "k", 0, 0),
        (one, mid, "k", 0, 1),
        (one, down, "w", 1, 1),
        (one, last, "w", 1, 0),
    )()
    one(down, "k", 0, 0)
    one(mid, "k", 0, 2)
    conv_grad(0, 0)
    one(down, "k", 0, 1)
    grad_first(0, 1)
    gains_start()
    one(mid, "k", 0, 3)
    one(last, "k", 0, 0)
    one(down, "k", 0, 2)
    one(last, "w", 1, 1)
    one(up, "w", 2, 0)
    one(last, "k", 0, 1)
    one(mid, "k", 0, 4)
    one(down, "k", 0, 3)
    wide_early()
    conv_grad(0, 1)
    wide_late()
    run(inside, "k", 1)
    run(out, "k", 1)
    run(inside, "w", 1)
    one(inside, "k", 0, 0)
    one(inside, "k", 0, 1)
    run(out, "w", 1)
    one(out, "k", 0, 0)
    one(out, "k", 0, 1)
    one(last, "k", 0, 2)
    one(inside, "k", 0, 2)
    one(mid, "k", 0, 5)
    one(down, "k", 0, 4)
    one(last, "k", 0, 3)
    one(inside, "k", 0, 3)
    outs.append(put_out(4, sc.cin.at[...], conv_ref.at[...]))
    pair_sum("w", 0)
    run(up, "w", 0)
    one(up, "w", 2, 1)
    one(out, "k", 0, 2)
    one(down, "k", 0, 5)
    one(last, "k", 0, 4)
    one(inside, "k", 0, 4)
    one(out, "k", 0, 3)
    one(mid, "w", 0, 0)
    one(mid, "w", 2, 0)
    run(inside, "w", 3)
    run(out, "w", 3)
    one(mid, "w", 0, 1)
    one(last, "k", 0, 5)
    one(inside, "k", 0, 5)
    one(out, "k", 0, 4)
    one(down, "w", 0, 0)
    one(mid, "w", 0, 2)
    one(down, "w", 0, 1)
    one(out, "k", 0, 5)
    one(down, "w", 2, 0)
    one(last, "w", 0, 0)
    one(inside, "w", 0, 0)
    one(mid, "w", 0, 3)
    one(down, "w", 0, 2)
    one(last, "w", 0, 1)
    one(inside, "w", 0, 1)
    one(out, "w", 0, 0)
    one(mid, "w", 2, 1)
    one(last, "w", 2, 0)
    one(inside, "w", 2, 0)
    one(down, "w", 0, 3)
    one(last, "w", 0, 2)
    one(inside, "w", 0, 2)
    one(out, "w", 0, 1)
    one(out, "w", 2, 0)
    one(down, "w", 2, 1)
    one(last, "w", 0, 3)
    one(inside, "w", 0, 3)
    one(out, "w", 0, 2)
    one(last, "w", 2, 1)
    one(inside, "w", 2, 1)
    for part in range(4):
        one(step_sibling, "k", 0, part)
    one(out, "w", 0, 3)
    one(step_sibling, "k", 0, 4)
    one(step_sibling, "k", 0, 5)
    one(out, "w", 2, 1)
    run(step_sibling, "w", 3)
    gains_done()
    run(step_sibling, "k", 1)
    run(step_sibling, "w", 2)
    run(step_sibling, "w", 1)
    one(step_sibling, "w", 0, 0)
    one(step_sibling, "w", 0, 1)
    run(step_done, "k", 1)
    run(step_done, "k", 0)
    outs.append(put_out(1, sc.ok.at[...], gtaps_ref.at[...]))
    for s in (3, 2, 1):
        run(step_done, "w", s)
    final = of("w", 0)
    for it in final[2:]:
        step_sibling(it)
    for it in final:
        step_rest(it)
    for group, part in enumerate((final[:-1], final[-1:]) if len(final) > 1 else (final,)):
        first, count = part[0].r0, sum(it.nr for it in part)
        for it in part:
            step_done(it)
        part_rows_of = pl.ds(first, count)
        outs.append(
            put_out(
                5 + group, sc.ow.at[:, :, part_rows_of], gwide_ref.at[:, :, part_rows_of]
            )
        )
    for copy in outs:
        copy.wait()
    for body in finish:
        body()


def cast_pieces(rows):
    pieces = [("taps", pl.ds(1152 * i, 1152)) for i in range(2)]
    pieces += [("wide", pl.ds(1024 * i, 1024)) for i in range(2)]
    return pieces + [("stream", m) for m in range(2)]


def cast_kernel(mixed, gpre, conv, gwide, gtaps, gmid, gout, *refs):
    o_mixed, o_input, o_wide, o_taps, o_mid, o_out = refs[:6]
    b_taps, b_wide, b_gpre, b_conv, f_taps, f_wide, f_stream = refs[6:13]
    b_mixed, b_mid, b_out, r_sem, w_sem, d_sem = refs[13:]
    pieces = cast_pieces(gpre.shape[1])
    same = ((mixed, b_mixed, o_mixed), (gmid, b_mid, o_mid), (gout, b_out, o_out))
    arrive = [pltpu.make_async_copy(a, b, d_sem.at[i]) for i, (a, b, _) in enumerate(same)]
    leave = [pltpu.make_async_copy(b, o, d_sem.at[i]) for i, (_, b, o) in enumerate(same)]
    reads, writes = [], []
    for i, (kind, part) in enumerate(pieces):
        if kind == "stream":
            reads.append(
                [
                    pltpu.make_async_copy(gpre.at[part], b_gpre.at[part], r_sem.at[i]),
                    pltpu.make_async_copy(conv.at[part], b_conv.at[part], r_sem.at[i + 2]),
                ]
            )
            writes.append(
                pltpu.make_async_copy(f_stream.at[part], o_input.at[part], w_sem.at[i])
            )
            continue
        src, low, high, dst = (
            (gtaps, b_taps, f_taps, o_taps)
            if kind == "taps"
            else (gwide, b_wide, f_wide, o_wide)
        )
        reads.append([pltpu.make_async_copy(src.at[part], low.at[part], r_sem.at[i])])
        writes.append(pltpu.make_async_copy(high.at[part], dst.at[part], w_sem.at[i]))
    for group in reads:
        for copy in group:
            copy.start()
    for copy in arrive:
        copy.start()
    for (kind, part), group, write in zip(pieces, reads, writes):
        for copy in group:
            copy.wait()
        size = 64

        def strip(i, carry, kind=kind, part=part):
            if kind == "stream":
                at = pl.ds(pl.multiple_of(i * size, size), size)
                f_stream[part, at] = b_gpre[part, at].astype(F32) + b_conv[part, at].astype(F32)
                return carry
            at = pl.ds(pl.multiple_of(part.start + i * size, size), size)
            if kind == "taps":
                f_taps[at] = b_taps[at].astype(F32)
            else:
                f_wide[at] = b_wide[at].astype(F32)
            return carry

        lax.fori_loop(0, (gpre.shape[1] if kind == "stream" else part.size) // size, strip, 0)
        write.start()
    for first, second in zip(arrive, leave):
        first.wait()
        second.start()
    for copy in writes + leave:
        copy.wait()


def cast_all(mixed, gpre, conv, gwide, gtaps, gmid, gout):
    anywhere = pl.BlockSpec(memory_space=pl.ANY)
    shape = jax.ShapeDtypeStruct
    count = len(cast_pieces(gpre.shape[1]))
    return pl.pallas_call(
        cast_kernel,
        in_specs=[anywhere] * 7,
        out_specs=[anywhere] * 6,
        out_shape=[
            shape(mixed.shape, BF16),
            shape(mixed.shape, F32),
            shape(gwide.shape, F32),
            shape(gtaps.shape, F32),
            shape(gmid.shape, F32),
            shape(gout.shape, F32),
        ],
        scratch_shapes=[
            pltpu.VMEM(gtaps.shape, BF16),
            pltpu.VMEM(gwide.shape, BF16),
            pltpu.VMEM(gpre.shape, BF16),
            pltpu.VMEM(gpre.shape, BF16),
            pltpu.VMEM(gtaps.shape, F32),
            pltpu.VMEM(gwide.shape, F32),
            pltpu.VMEM(gpre.shape, F32),
            pltpu.VMEM(mixed.shape, BF16),
            pltpu.VMEM(gmid.shape, F32),
            pltpu.VMEM(gout.shape, F32),
            pltpu.SemaphoreType.DMA((count + 2,)),
            pltpu.SemaphoreType.DMA((count,)),
            pltpu.SemaphoreType.DMA((3,)),
        ],
        compiler_params=pltpu.CompilerParams(vmem_limit_bytes=60 * 2**20),
        name="casts",
    )(mixed, gpre, conv, gwide, gtaps, gmid, gout)


def local(block_input, cotangent, weight_wide, weight_taps, norm_mid, norm_out, group_counts):
    n_dp = group_counts.shape[1]
    micro, rows, width = block_input.shape
    scratch = scratch_list(n_dp, rows)
    anywhere = pl.BlockSpec(memory_space=pl.ANY)

    def shape(dims, dtype):
        return jax.ShapeDtypeStruct(dims, dtype)

    stream = (micro, rows, width)
    mixed, gpre, conv, gwide, gtaps, gmid, gout = pl.pallas_call(
        functools.partial(kernel, list(scratch), n_dp),
        out_shape=[
            shape(stream, BF16),
            shape(stream, BF16),
            shape(stream, BF16),
            shape((4, 2, 256, 512), BF16),
            shape((2304, 512), BF16),
            shape(norm_mid.shape, F32),
            shape(norm_out.shape, F32),
        ],
        in_specs=[anywhere] * 7,
        out_specs=[anywhere] * 7,
        scratch_shapes=list(scratch.values()),
        compiler_params=pltpu.CompilerParams(
            collective_id=0, has_side_effects=True, vmem_limit_bytes=62 * 2**20
        ),
        name="layers",
    )(block_input, cotangent, weight_wide, weight_taps.reshape(9, 256, 512), norm_mid, norm_out, jnp.swapaxes(group_counts, 1, 2))
    results = cast_all(mixed, gpre, conv, gwide.reshape(2048, 512), gtaps, gmid, gout)
    mixed, grad_input, gwide, gtaps, gmid, gout = results
    return (
        mixed,
        grad_input,
        gwide.reshape(weight_wide.shape),
        gtaps.reshape(weight_taps.shape),
        gmid,
        gout,
    )


def solution(mesh):
    split = P(None, "dp", "pipe")
    section = P("pipe", None, None)
    return jax.shard_map(
        local,
        mesh=mesh,
        in_specs=(split, split, section, section, section, section, P()),
        out_specs=(split, split, section, section, section, section),
        check_vma=False,
    )
```
